32 devices in a mesh: groups: 2 (over y), tm: 4 (over z), head: 4 (over x, core).
Axes of the slice: x: 2, y: 2, z: 4, core: 2. Of those that a mesh axis runs over, the one named last changes fastest.
Arguments:
- queries: bfloat16 [8, 256, 3072], P(('groups', 'tm'), 'head'), parts along dimension 0, may hold values from -128 to 128
- keys: bfloat16 [8, 256, 3072], P(('groups', 'tm'), 'head'), parts along dimension 0, may hold values from -6 to 6
- values: bfloat16 [8, 256, 3072], P(('groups', 'tm'), 'head'), parts along dimension 0, may hold values from -6 to 6
- residual: bfloat16 [8, 256, 5120], P(('groups', 'tm'), None, 'head'), parts along dimension 0, may hold values from -3 to 3
- fresh_frame: bfloat16 [512, 5120], P('groups', 'head'), parts along dimension 0, may hold values from -6 to 6
- out_weight: bfloat16 [3072, 5120], P('tm', 'head'), may hold values from -0.875 to 0.875
- time_weight: bfloat16 [256, 5120], P(None, 'head'), may hold values from -0.375 to 0.375
- noise_steps: int32 [8], P(('groups', 'tm')), parts along dimension 0, may hold values from 0 to 49, as said below
- frame_mask: int32 [8, 4], P(('groups', 'tm')), parts along dimension 0, may hold values from 0 to 1, as said below
Outputs:
- rolled: bfloat16 [8, 256, 5120], P(('groups', 'tm'), None, 'head'), parts along dimension 0
The draws below stay inside these ranges and needn't reach their ends.
There are 2 independent parts, one for each index of `groups`. The reference program is written for one: setup_inputs(seed, part) draws one part's arguments, and reference() takes and returns one part's arrays. A program takes and returns all parts, laid end to end along the dimension named above; an argument that names none is the same for every part. Nothing has to cross between parts.
Inputs may be any that keep to these rules, and one draw needn't show every extreme that they name: frame_mask[i, j] is 1 exactly for i - L_i < j <= i, with a whole number L_i from 1 to 4 for each frame i; the last frame has L_i = 4. `noise_steps`: never falling along the frames; the first frame has 0 and the last 49.
All inputs are finite; a program needn't handle non-finite values.
Results may differ from the reference program's by a relative error of at most 0.0065.
Values may be sent and summed in bfloat16 or wider, within the bound.
No kernel may reach another device: no remote copies, remote signals or barrier semaphores. Data moves between devices by JAX's collectives and lax.ppermute only.
A program may use at most 64 MiB of HBM per device.

```python
import math
import jax
import jax.numpy as jnp
from jax import lax

D = 5120
HD = 128
HEADS = 24
FREQ = 256
STEPS = 50
TOK = 256
FRAMES = 4
WIN = 4


def draw_pair(key):
    base = jax.random.fold_in(key, 11)
    key_normal, key_query = jax.random.split(base, 2)
    shape = (FRAMES, TOK, HEADS * HD)
    keys_raw = jnp.clip(jax.random.normal(key_normal, shape, jnp.float32), -6.0, 6.0)
    query_raw = jnp.clip(2.0 * jax.random.normal(key_query, shape, jnp.float32), -12.0, 12.0)
    return (query_raw, keys_raw)


def draw_queries(key, part):
    return draw_pair(key)[0].astype(jnp.bfloat16)


def draw_keys(key, part):
    return draw_pair(key)[1].astype(jnp.bfloat16)


def draw_noise_steps(key, part):
    picks = jax.random.randint(jax.random.fold_in(key, 23), (FRAMES,), 0, STEPS)
    ordered = jnp.sort(picks)
    position = jnp.arange(FRAMES)
    ordered = jnp.where(position == 0, 0, jnp.where(position == FRAMES - 1, STEPS - 1, ordered))
    return ordered.astype(jnp.int32)


def draw_frame_mask(key, part):
    spans = jax.random.randint(jax.random.fold_in(key, 31), (FRAMES,), 1, WIN + 1)
    position = jnp.arange(FRAMES)
    spans = jnp.where(position == FRAMES - 1, WIN, spans)
    spans = jnp.minimum(spans, position + 1)
    rows = position[:, None]
    cols = position[None, :]
    return ((cols <= rows) & (cols > rows - spans[:, None])).astype(jnp.int32)


def steps_of(stream_key, dims, cuts, least, high):
    factor_of, own = 1.0, jax.random.fold_in(stream_key, 6)
    for dim, shards_of in cuts:
        draws = jnp.exp(jax.random.uniform(jax.random.fold_in(own, dim), (shards_of,), jnp.float32, least / len(cuts), high / len(cuts)))
        factor_of = factor_of * jnp.repeat(draws, dims[dim] // shards_of).reshape([-1 if axis == dim else 1 for axis in range(len(dims))])
    return factor_of


def scatter_about(key, dims, scale, reach, cuts=(), kind=jnp.bfloat16):
    gain = steps_of(key, dims, cuts, -0.22, 0.18) if cuts else 1.0
    drawn = jax.random.normal(key, dims, jnp.float32) * scale * gain
    return jnp.minimum(jnp.maximum(drawn, -reach), reach).astype(kind)


def setup_inputs(seed: int = 0, part: int = 0) -> dict:
    arg_keys = jax.random.split(jax.random.key(seed), 10)
    part_splits = jax.random.split(jax.random.fold_in(arg_keys[9], part), 10)
    queries = draw_queries(jax.random.fold_in(jax.random.fold_in(arg_keys[9], part), 71), part)
    keys = draw_keys(jax.random.fold_in(jax.random.fold_in(arg_keys[9], part), 71), part)
    values = scatter_about(part_splits[2], (FRAMES, TOK, HEADS * HD), 1.0, 6.0, ((0, 4), (1, 4)))
    residual = scatter_about(part_splits[3], (FRAMES, TOK, D), 0.5, 3.0, ((0, 4), (2, 4)))
    fresh_frame = scatter_about(part_splits[4], (TOK, D), 1.0, 6.0, ((1, 4),))
    out_weight = scatter_about(arg_keys[5], (HEADS * HD, D), (HEADS * HD // 64) ** -0.5, 0.875, ((0, 4), (1, 4)))
    time_weight = scatter_about(arg_keys[6], (FREQ, D), FREQ ** -0.5, 0.375, ((1, 4),))
    noise_steps = draw_noise_steps(jax.random.fold_in(jax.random.fold_in(arg_keys[9], part), 71), part)
    frame_mask = draw_frame_mask(jax.random.fold_in(jax.random.fold_in(arg_keys[9], part), 71), part)
    return dict(queries=queries, keys=keys, values=values, residual=residual, fresh_frame=fresh_frame, out_weight=out_weight, time_weight=time_weight, noise_steps=noise_steps, frame_mask=frame_mask)


def time_features(noise_steps):
    timestep = 1000.0 * (noise_steps.astype(jnp.float32) + 1.0) / STEPS
    half = FREQ // 2
    rates = jnp.exp(-math.log(10000.0) * jnp.arange(half).astype(jnp.float32) / half)
    angles = timestep[:, None] * rates[None, :]
    return jnp.concatenate([jnp.cos(angles), jnp.sin(angles)], axis=1)

def reference(queries, keys, values, residual, fresh_frame, out_weight, time_weight, noise_steps, frame_mask):
    width = HEADS * HD
    scale = 1.0 / math.sqrt(HD)
    blank = jnp.zeros((WIN - 1, TOK, width), keys.dtype)
    keys_padded = jnp.concatenate([blank, keys], axis=0)
    values_padded = jnp.concatenate([blank, values], axis=0)
    mask_padded = jnp.concatenate([jnp.zeros((FRAMES, WIN - 1), jnp.int32), frame_mask.astype(jnp.int32)], axis=1)

    def one_frame(frame):
        query_rows = lax.dynamic_index_in_dim(queries, frame, 0, keepdims=False).astype(jnp.float32).reshape(TOK, HEADS, HD)
        key_rows = lax.dynamic_slice_in_dim(keys_padded, frame, WIN, 0).astype(jnp.float32).reshape(WIN * TOK, HEADS, HD)
        value_rows = lax.dynamic_slice_in_dim(values_padded, frame, WIN, 0).astype(jnp.float32).reshape(WIN * TOK, HEADS, HD)
        mask_row = lax.dynamic_index_in_dim(mask_padded, frame, 0, keepdims=False)
        allowed = jnp.repeat(lax.dynamic_slice_in_dim(mask_row, frame, WIN, 0), TOK)
        scores = jnp.einsum('qhd,khd->hqk', query_rows, key_rows) * scale
        scores = jnp.where(allowed[None, None, :] > 0, scores, -1e+30)
        peak = lax.optimization_barrier(jnp.max(scores, axis=2, keepdims=True))
        lifted = jnp.exp(scores - peak)
        totals = lax.optimization_barrier(jnp.sum(lifted, axis=2))
        rounded = lax.optimization_barrier(lifted.astype(jnp.bfloat16)).astype(jnp.float32)
        mixed = jnp.einsum('hqk,khd->qhd', rounded, value_rows) / jnp.transpose(totals)[:, :, None]
        return mixed.reshape(TOK, width).astype(jnp.bfloat16)
    attention = lax.map(one_frame, jnp.arange(FRAMES, dtype=jnp.int32))
    projected = jnp.dot(attention.reshape(FRAMES * TOK, width), out_weight, preferred_element_type=jnp.float32).reshape(FRAMES, TOK, D)
    gate = jnp.dot(time_features(noise_steps), time_weight.astype(jnp.float32), precision=lax.Precision.HIGHEST)
    updated = (residual.astype(jnp.float32) + gate[:, None, :] * projected).astype(jnp.bfloat16)
    return jnp.concatenate([updated[1:], fresh_frame[None]], axis=0)
```

```python
import math

import jax
import jax.numpy as jnp
import numpy as np
from jax import lax
from jax.experimental import pallas as pl
from jax.experimental.pallas import tpu as pltpu
from jax.sharding import PartitionSpec as P

HD = 128
FREQ = 256
STEPS = 50
VMEM_BYTES = 40 * 1024 * 1024


def shifted(value, axis, steps):
    count = lax.axis_size(axis)
    leading, last = (max(0, -steps), min(count, count - steps))
    return lax.ppermute(value, axis, [(source, source + steps) for source in range(leading, last)])


def time_features(noise_steps):
    timestep = 1000.0 * (noise_steps.astype(jnp.float32) + 1.0) / STEPS
    half = FREQ // 2
    rates = jnp.exp(-math.log(10000.0) * jnp.arange(half).astype(jnp.float32) / half)
    angles = timestep[:, None] * rates[None, :]
    return jnp.concatenate([jnp.cos(angles), jnp.sin(angles)], axis=1)


def frame_plan(
    queries, keys, values, residual, fresh_frame, out_weight, time_weight, noise_steps, frame_mask
):
    query_local, key_local, value_local = (
        lax.all_to_all(queries, "head", split_axis=2, concat_axis=1, tiled=True),
        lax.all_to_all(keys, "head", split_axis=2, concat_axis=1, tiled=True),
        lax.all_to_all(values, "head", split_axis=2, concat_axis=1, tiled=True),
    )
    tokens = query_local.shape[1]
    heads_here = query_local.shape[2] // HD
    scale = 1.0 / math.sqrt(HD)
    query_heads = query_local[0].reshape(tokens, heads_here, HD)
    key_value = jnp.stack([key_local[0], value_local[0]], axis=0)
    frame = lax.axis_index("tm")
    frames_total = lax.axis_size("tm")
    window = min(8, frames_total)
    mask_row = frame_mask[0]
    columns = jnp.arange(mask_row.shape[0], dtype=jnp.int32)

    def allowed_at(offset):
        hits = jnp.sum(jnp.where(columns == frame - offset, mask_row, 0))
        return hits > 0

    def absorb(state, block, allowed):
        running_max, weight_sum, accumulated = state
        key_heads = block[0].reshape(tokens, heads_here, HD)
        value_heads = block[1].reshape(tokens, heads_here, HD)
        scores = (
            jnp.einsum("qhd,khd->hqk", query_heads, key_heads, preferred_element_type=jnp.float32)
            * scale
        )
        new_max = jnp.where(allowed, jnp.maximum(running_max, jnp.max(scores, axis=2)), running_max)
        lifted = jnp.where(allowed, jnp.exp(jnp.minimum(scores - new_max[:, :, None], 0.0)), 0.0)
        factor = jnp.exp(running_max - new_max)
        weight_sum = weight_sum * factor + jnp.sum(lifted, axis=2)
        rounded = lifted.astype(jnp.bfloat16)
        accumulated = accumulated * jnp.transpose(factor)[:, :, None] + jnp.einsum(
            "hqk,khd->qhd", rounded, value_heads, preferred_element_type=jnp.float32
        )
        return (new_max, weight_sum, accumulated)

    state = (
        jnp.full((heads_here, tokens), -1e30, jnp.float32),
        jnp.zeros((heads_here, tokens), jnp.float32),
        jnp.zeros((tokens, heads_here, HD), jnp.float32),
    )
    state = absorb(state, key_value, allowed_at(0))
    moving = key_value
    for offset in range(1, window):
        moving = shifted(moving, "tm", 1)
        state = absorb(state, moving, allowed_at(offset))
    running_max, weight_sum, accumulated = state
    attention = (
        (accumulated / jnp.transpose(weight_sum)[:, :, None])
        .reshape(tokens, heads_here * HD)
        .astype(jnp.bfloat16)
    )
    weight_cols = lax.all_gather(out_weight, "tm", axis=0, tiled=True)
    projected = jnp.dot(
        lax.all_gather(attention, "head", axis=1, tiled=True),
        weight_cols,
        preferred_element_type=jnp.float32,
    )
    gate = jnp.dot(
        time_features(noise_steps), time_weight.astype(jnp.float32), precision=lax.Precision.HIGHEST
    )
    updated = (residual[0].astype(jnp.float32) + gate * projected).astype(jnp.bfloat16)
    moved = shifted(updated, "tm", -1)
    rolled = jnp.where(frame == frames_total - 1, fresh_frame, moved)
    return rolled[None]


def whole_in_vmem(count):
    return [pl.BlockSpec(memory_space=pltpu.VMEM)] * count


def pack(queries, keys, values, moves, pairs, width):
    tokens = queries.shape[0]

    def kernel(query_ref, key_ref, value_ref, *pieces):
        frame, pair = (lax.axis_index("tm"), lax.axis_index("head") // 2)
        for piece, (a, b) in zip(pieces, moves):
            block = (frame ^ a) * pairs + (pair ^ b)
            columns = pl.ds(pl.multiple_of(block * width, HD), width)
            for place, source in enumerate((query_ref, key_ref, value_ref)):
                piece[:, place * width : (place + 1) * width] = source[:, columns]

    return pl.pallas_call(
        kernel,
        out_shape=[jax.ShapeDtypeStruct((tokens, 3 * width), queries.dtype)] * len(moves),
        in_specs=whole_in_vmem(3),
        out_specs=whole_in_vmem(len(moves)),
        compiler_params=pltpu.CompilerParams(vmem_limit_bytes=VMEM_BYTES),
        name="pack",
    )(queries, keys, values)


def attend(mask, order, own, mate, moves, pairs, frames, width):
    tokens = own[0].shape[0]
    rows, keys_rows = (pairs * tokens, 2 * pairs * tokens)
    slots = frames - 1
    scale = 1.0 / math.sqrt(HD)

    def kernel(mask_ref, order_ref, *refs):
        own_refs, mate_refs = (refs[: len(moves)], refs[len(moves) : 2 * len(moves)])
        outs = refs[2 * len(moves) : 2 * len(moves) + slots]
        query_buf, key_buf, value_buf = refs[2 * len(moves) + slots :]
        here = lax.axis_index("tm")
        for own_ref, mate_ref, (a, b) in zip(own_refs, mate_refs, moves):
            frame = here ^ a
            query_buf[frame, b * tokens : (b + 1) * tokens, :] = own_ref[:, :width]
            for side, ref in enumerate((own_ref, mate_ref)):
                span = slice((2 * b + side) * tokens, (2 * b + side + 1) * tokens)
                key_buf[frame, span, :] = ref[:, width : 2 * width]
                value_buf[frame, span, :] = ref[:, 2 * width :]
        for slot in range(slots):
            frame = order_ref[slot]
            for start in range(0, width, HD):
                channels = slice(start, start + HD)
                query = query_buf[frame, :, channels]
                blocks = []
                for other in range(frames):
                    scores = (
                        lax.dot_general(
                            query,
                            key_buf[other, :, channels],
                            (((1,), (1,)), ((), ())),
                            preferred_element_type=jnp.float32,
                        )
                        * scale
                    )
                    blocks.append(jnp.where(mask_ref[frame, other] > 0, scores, -1e30))
                scores = jnp.concatenate(blocks, axis=1)
                lifted = jnp.exp(scores - jnp.max(scores, axis=1, keepdims=True))
                totals = jnp.sum(lifted, axis=1, keepdims=True)
                values = value_buf[:, :, channels].reshape(frames * keys_rows, HD)
                mixed = jnp.dot(
                    lifted.astype(jnp.bfloat16), values, preferred_element_type=jnp.float32
                )
                outs[slot][:, channels] = (mixed / totals).astype(jnp.bfloat16)

    kind = own[0].dtype
    return pl.pallas_call(
        kernel,
        out_shape=[jax.ShapeDtypeStruct((rows, width), jnp.bfloat16)] * slots,
        in_specs=[pl.BlockSpec(memory_space=pltpu.SMEM)] * 2 + whole_in_vmem(2 * len(moves)),
        out_specs=whole_in_vmem(slots),
        scratch_shapes=[
            pltpu.VMEM((frames, rows, width), kind),
            pltpu.VMEM((frames, keys_rows, width), kind),
            pltpu.VMEM((frames, keys_rows, width), kind),
        ],
        compiler_params=pltpu.CompilerParams(vmem_limit_bytes=VMEM_BYTES),
        name="attend",
    )(mask, order, *own, *mate)


def project(pieces, weight, pairs):
    rows, width = pieces[0].shape
    tokens = rows // pairs
    depth, columns = weight.shape
    step = math.gcd(columns, 256)

    def kernel(*refs):
        piece_refs, (weight_ref, out_ref, whole) = (refs[: len(pieces)], refs[len(pieces) :])
        here = lax.axis_index("head")
        for j, ref in enumerate(piece_refs):
            source = here ^ j
            pair, core = (source // 2, source % 2)
            channels = pl.ds(pl.multiple_of(pair * width, HD), width)
            for b in range(pairs):
                first = ((pair ^ b) * 2 + core) * tokens
                whole[pl.ds(pl.multiple_of(first, 16), tokens), channels] = ref[
                    b * tokens : (b + 1) * tokens, :
                ]
        for start in range(0, columns, step):
            out_ref[:, start : start + step] = jnp.dot(
                whole[...], weight_ref[:, start : start + step], preferred_element_type=jnp.float32
            )

    return pl.pallas_call(
        kernel,
        out_shape=jax.ShapeDtypeStruct((2 * rows, columns), jnp.float32),
        in_specs=whole_in_vmem(len(pieces) + 1),
        out_specs=whole_in_vmem(1)[0],
        scratch_shapes=[pltpu.VMEM((2 * rows, depth), jnp.bfloat16)],
        compiler_params=pltpu.CompilerParams(vmem_limit_bytes=VMEM_BYTES),
        name="project",
    )(*pieces, weight)


def line_schedule(frames):
    steps = []
    for step in range(frames - 1):
        down = {z: step + 1 - (frames - 1 - z) for z in range(1, frames)}
        up = {z: frames - 1 - step + z for z in range(frames)}
        down = {z: f for z, f in down.items() if 1 <= f <= z}
        up = {z: f for z, f in up.items() if z + 2 <= f < frames}
        steps.append((down, up))
    order = []
    for z in range(frames):
        sent = [f for down, up in steps for f in (down.get(z), up.get(z)) if f is not None]
        order.append((sent + [z + 1])[: frames - 1])
    return steps, order


def by_place(table, values):
    here = lax.axis_index("tm")
    result = values[table[0]]
    for slot in sorted(set(table) - {table[0]}):
        hits = [here == z for z, entry in enumerate(table) if entry == slot]
        result = jnp.where(jnp.stack(hits).any(), values[slot], result)
    return result


def head_plan(
    queries, keys, values, residual, fresh_frame, out_weight, time_weight, noise_steps, frame_mask
):
    frames, across = (lax.axis_size("tm"), lax.axis_size("head"))
    pairs = across // 2
    width = queries.shape[2] // (frames * pairs)
    here = lax.axis_index("tm")
    moves = [(a, b) for a in range(frames) for b in range(pairs)]
    plans = lax.all_gather(
        jnp.concatenate([frame_mask[0], noise_steps]), "tm", axis=0, tiled=False
    )
    packed = pack(queries[0], keys[0], values[0], moves, pairs, width)

    own = []
    for piece, (a, b) in zip(packed, moves):
        if (a, b) != (0, 0):
            links = [
                (z * across + h, (z ^ a) * across + (h ^ (2 * b)))
                for z in range(frames)
                for h in range(across)
            ]
            piece = lax.ppermute(piece, ("tm", "head"), links)
        own.append(piece)
    swap = [(h, h ^ 1) for h in range(across)]
    mate = [lax.ppermute(piece, "head", swap) for piece in own]

    steps, order = line_schedule(frames)
    slots = frames - 1
    order_here = jnp.asarray(np.array(order, np.int32))[here]
    mixed = attend(plans[:, :-1], order_here, own, mate, moves, pairs, frames, width)

    later, _ = lax.optimization_barrier((residual[0], mate[-1]))
    residual_next = shifted(later, "tm", -1)
    noise_next = lax.dynamic_index_in_dim(plans[:, -1], jnp.minimum(here + 1, frames - 1), 0)
    gate = jnp.dot(
        time_features(noise_next), time_weight.astype(jnp.float32), precision=lax.Precision.HIGHEST
    )

    partial = []
    for part in mixed:
        pieces = [part] + [
            lax.ppermute(part, "head", [(h, h ^ j) for h in range(across)])
            for j in range(1, across)
        ]
        partial.append(project(pieces, out_weight, pairs))

    from_above, from_below = (None, None)
    total = partial[-1]
    for step, (down, up) in enumerate(steps):

        def outgoing(sends, arrived):
            table = [order[z].index(sends[z]) if z in sends else 0 for z in range(frames)]
            chosen = by_place(table, partial)
            if arrived is not None:
                chosen = chosen + arrived.astype(jnp.float32)
            return chosen.astype(jnp.bfloat16)

        next_above, next_below = (None, None)
        if down:
            payload = outgoing(down, from_above)
            next_above = lax.ppermute(payload, "tm", [(z, z - 1) for z in down])
        if up:
            payload = outgoing(up, from_below)
            next_below = lax.ppermute(payload, "tm", [(z, z + 1) for z in up])
        from_above, from_below = (next_above, next_below)
        if next_below is not None:
            last = [z for z in up if up[z] == z + 2]
            arrives = jnp.isin(here, jnp.array([z + 1 for z in last])) if last else None
            if last:
                total = total + jnp.where(arrives, next_below.astype(jnp.float32), 0.0)
    total = total + from_above.astype(jnp.float32)
    updated = (residual_next.astype(jnp.float32) + gate * total).astype(jnp.bfloat16)
    rolled = jnp.where(here == frames - 1, fresh_frame, updated)
    return rolled[None]


def power_of_two(number):
    return number & (number - 1) == 0


def on_device(queries, *others):
    frames, across = (lax.axis_size("tm"), lax.axis_size("head"))
    heads = queries.shape[2] // HD
    even = across % 2 == 0 and power_of_two(across) and power_of_two(frames)
    if even and 2 < frames <= others[-1].shape[1] <= 8 and heads % (frames * across // 2) == 0:
        return head_plan(queries, *others)
    return frame_plan(queries, *others)


def solution(mesh):
    placed = (
        P(("groups", "tm"), "head", None),
        P(("groups", "tm"), "head", None),
        P(("groups", "tm"), "head", None),
        P(("groups", "tm"), None, "head"),
        P("groups", "head"),
        P("tm", "head"),
        P(None, "head"),
        P(("groups", "tm")),
        P(("groups", "tm"), None),
    )
    return jax.shard_map(
        on_device,
        mesh=mesh,
        in_specs=placed,
        out_specs=P(("groups", "tm"), None, "head"),
        check_vma=False,
    )
```

```python
import math

import jax
import jax.numpy as jnp
import numpy as np
from jax import lax
from jax.experimental import pallas as pl
from jax.experimental.pallas import tpu as pltpu
from jax.sharding import PartitionSpec as P

HD = 128
FREQ = 256
STEPS = 50
VMEM_BYTES = 24 * 1024 * 1024
PACK_BYTES = 60 * 1024 * 1024


def shifted(value, axis, steps):
    count = lax.axis_size(axis)
    leading, last = (max(0, -steps), min(count, count - steps))
    return lax.ppermute(value, axis, [(source, source + steps) for source in range(leading, last)])


def time_features(noise_steps):
    timestep = 1000.0 * (noise_steps.astype(jnp.float32) + 1.0) / STEPS
    half = FREQ // 2
    rates = jnp.exp(-math.log(10000.0) * jnp.arange(half).astype(jnp.float32) / half)
    angles = timestep[:, None] * rates[None, :]
    return jnp.concatenate([jnp.cos(angles), jnp.sin(angles)], axis=1)


def frame_plan(
    queries, keys, values, residual, fresh_frame, out_weight, time_weight, noise_steps, frame_mask
):
    query_local, key_local, value_local = (
        lax.all_to_all(queries, "head", split_axis=2, concat_axis=1, tiled=True),
        lax.all_to_all(keys, "head", split_axis=2, concat_axis=1, tiled=True),
        lax.all_to_all(values, "head", split_axis=2, concat_axis=1, tiled=True),
    )
    tokens = query_local.shape[1]
    heads_here = query_local.shape[2] // HD
    scale = 1.0 / math.sqrt(HD)
    query_heads = query_local[0].reshape(tokens, heads_here, HD)
    key_value = jnp.stack([key_local[0], value_local[0]], axis=0)
    frame = lax.axis_index("tm")
    frames_total = lax.axis_size("tm")
    window = min(8, frames_total)
    mask_row = frame_mask[0]
    columns = jnp.arange(mask_row.shape[0], dtype=jnp.int32)

    def allowed_at(offset):
        hits = jnp.sum(jnp.where(columns == frame - offset, mask_row, 0))
        return hits > 0

    def absorb(state, block, allowed):
        running_max, weight_sum, accumulated = state
        key_heads = block[0].reshape(tokens, heads_here, HD)
        value_heads = block[1].reshape(tokens, heads_here, HD)
        scores = (
            jnp.einsum("qhd,khd->hqk", query_heads, key_heads, preferred_element_type=jnp.float32)
            * scale
        )
        new_max = jnp.where(allowed, jnp.maximum(running_max, jnp.max(scores, axis=2)), running_max)
        lifted = jnp.where(allowed, jnp.exp(jnp.minimum(scores - new_max[:, :, None], 0.0)), 0.0)
        factor = jnp.exp(running_max - new_max)
        weight_sum = weight_sum * factor + jnp.sum(lifted, axis=2)
        rounded = lifted.astype(jnp.bfloat16)
        accumulated = accumulated * jnp.transpose(factor)[:, :, None] + jnp.einsum(
            "hqk,khd->qhd", rounded, value_heads, preferred_element_type=jnp.float32
        )
        return (new_max, weight_sum, accumulated)

    state = (
        jnp.full((heads_here, tokens), -1e30, jnp.float32),
        jnp.zeros((heads_here, tokens), jnp.float32),
        jnp.zeros((tokens, heads_here, HD), jnp.float32),
    )
    state = absorb(state, key_value, allowed_at(0))
    moving = key_value
    for offset in range(1, window):
        moving = shifted(moving, "tm", 1)
        state = absorb(state, moving, allowed_at(offset))
    running_max, weight_sum, accumulated = state
    attention = (
        (accumulated / jnp.transpose(weight_sum)[:, :, None])
        .reshape(tokens, heads_here * HD)
        .astype(jnp.bfloat16)
    )
    weight_cols = lax.all_gather(out_weight, "tm", axis=0, tiled=True)
    projected = jnp.dot(
        lax.all_gather(attention, "head", axis=1, tiled=True),
        weight_cols,
        preferred_element_type=jnp.float32,
    )
    gate = jnp.dot(
        time_features(noise_steps), time_weight.astype(jnp.float32), precision=lax.Precision.HIGHEST
    )
    updated = (residual[0].astype(jnp.float32) + gate * projected).astype(jnp.bfloat16)
    moved = shifted(updated, "tm", -1)
    rolled = jnp.where(frame == frames_total - 1, fresh_frame, moved)
    return rolled[None]


def whole_in_vmem(count):
    return [pl.BlockSpec(memory_space=pltpu.VMEM)] * count


def roomy():
    return pltpu.CompilerParams(vmem_limit_bytes=VMEM_BYTES)


def pack(queries, keys, values, moves, pairs, width):
    tokens = queries.shape[0]
    count = len(moves)

    def kernel(*refs):
        sources, pieces, sems = (refs[:3], refs[3 : 3 + count], refs[3 + count])
        frame, pair = (lax.axis_index("tm"), lax.axis_index("head") // 2)
        copies = []
        for number, (a, b) in enumerate(moves):
            block = (frame ^ a) * pairs + (pair ^ b)
            columns = pl.ds(pl.multiple_of(block * width, HD), width)
            for place, source in enumerate(sources):
                target = pieces[number].at[:, place * width : (place + 1) * width]
                copy = pltpu.make_async_copy(source.at[:, columns], target, sems.at[number, place])
                copy.start()
                copies.append(copy)
        for copy in copies:
            copy.wait()

    return pl.pallas_call(
        kernel,
        out_shape=[jax.ShapeDtypeStruct((tokens, 3 * width), queries.dtype)] * count,
        in_specs=[pl.BlockSpec(memory_space=pltpu.HBM)] * 3,
        out_specs=[pl.BlockSpec(memory_space=pltpu.HBM)] * count,
        scratch_shapes=[pltpu.SemaphoreType.DMA((count, 3))],
        compiler_params=pltpu.CompilerParams(vmem_limit_bytes=PACK_BYTES),
        name="pack",
    )(queries, keys, values)


def pick(table, here):
    result = table[0]
    for place, entry in enumerate(table[1:], 1):
        result = jnp.where(here == place, entry, result)
    return result


def attend(masks, frames_of_slot, own, mate, moves, pairs, frames, width):
    tokens = own[0].shape[0]
    rows, keys_rows = (pairs * tokens, 2 * pairs * tokens)
    scale = 1.0 / math.sqrt(HD)

    def kernel(*refs):
        mask_refs, refs = (refs[:frames], refs[frames:])
        own_refs, refs = (refs[: len(moves)], refs[len(moves) :])
        mate_refs, refs = (refs[: len(moves)], refs[len(moves) :])
        out_ref, query_buf, key_buf, value_buf = refs
        here = lax.axis_index("tm")
        for own_ref, mate_ref, (a, b) in zip(own_refs, mate_refs, moves):
            query_buf[here ^ a, b * tokens : (b + 1) * tokens, :] = own_ref[:, :width]
            for side, ref in enumerate((own_ref, mate_ref)):
                span = slice((2 * b + side) * tokens, (2 * b + side + 1) * tokens)
                key_buf[a, span, :] = ref[:, width : 2 * width]
                value_buf[a, span, :] = ref[:, 2 * width :]
        frame = pick(frames_of_slot, here)
        allowed = []
        for a in range(frames):
            entry = 0
            for source in range(frames):
                entry = jnp.where(here ^ source == frame, mask_refs[source][0, here ^ a], entry)
            allowed.append(entry)
        for start in range(0, width, HD):
            channels = slice(start, start + HD)
            query = query_buf[frame, :, channels]
            blocks = []
            for a in range(frames):
                scores = (
                    lax.dot_general(
                        query,
                        key_buf[a, :, channels],
                        (((1,), (1,)), ((), ())),
                        preferred_element_type=jnp.float32,
                    )
                    * scale
                )
                blocks.append(jnp.where(allowed[a] > 0, scores, -1e30))
            scores = jnp.concatenate(blocks, axis=1)
            lifted = jnp.exp(scores - jnp.max(scores, axis=1, keepdims=True))
            totals = jnp.sum(lifted, axis=1, keepdims=True)
            values = value_buf[:, :, channels].reshape(frames * keys_rows, HD)
            mixed = jnp.dot(
                lifted.astype(jnp.bfloat16), values, preferred_element_type=jnp.float32
            )
            out_ref[:, channels] = (mixed / totals).astype(jnp.bfloat16)

    kind = own[0].dtype
    return pl.pallas_call(
        kernel,
        out_shape=jax.ShapeDtypeStruct((rows, width), jnp.bfloat16),
        in_specs=[pl.BlockSpec(memory_space=pltpu.SMEM)] * frames + whole_in_vmem(2 * len(moves)),
        out_specs=whole_in_vmem(1)[0],
        scratch_shapes=[
            pltpu.VMEM((frames, rows, width), kind),
            pltpu.VMEM((frames, keys_rows, width), kind),
            pltpu.VMEM((frames, keys_rows, width), kind),
        ],
        compiler_params=roomy(),
        name="attend",
    )(*masks, *own, *mate)


def project(pieces, weight, pairs):
    rows, width = pieces[0].shape
    tokens = rows // pairs
    depth, columns = weight.shape
    step = math.gcd(columns, 256)

    def kernel(*refs):
        piece_refs, (weight_ref, out_ref, short_ref, whole) = (
            refs[: len(pieces)],
            refs[len(pieces) :],
        )
        here = lax.axis_index("head")
        for j, ref in enumerate(piece_refs):
            source = here ^ j
            pair, core = (source // 2, source % 2)
            channels = pl.ds(pl.multiple_of(pair * width, HD), width)
            for b in range(pairs):
                first = ((pair ^ b) * 2 + core) * tokens
                whole[pl.ds(pl.multiple_of(first, 16), tokens), channels] = ref[
                    b * tokens : (b + 1) * tokens, :
                ]
        for start in range(0, columns, step):
            product = jnp.dot(
                whole[...], weight_ref[:, start : start + step], preferred_element_type=jnp.float32
            )
            out_ref[:, start : start + step] = product
            short_ref[:, start : start + step] = product.astype(jnp.bfloat16)

    return pl.pallas_call(
        kernel,
        out_shape=[
            jax.ShapeDtypeStruct((2 * rows, columns), jnp.float32),
            jax.ShapeDtypeStruct((2 * rows, columns), jnp.bfloat16),
        ],
        in_specs=whole_in_vmem(len(pieces) + 1),
        out_specs=whole_in_vmem(2),
        scratch_shapes=[pltpu.VMEM((2 * rows, depth), jnp.bfloat16)],
        compiler_params=roomy(),
        name="project",
    )(*pieces, weight)


def join(partial, table, arrived, residual=None, gate=None):
    rows, columns = partial[0].shape
    step = math.gcd(columns, 256)
    slots = sorted(set(table))
    extras = [] if residual is None else [residual, gate]

    def kernel(*refs):
        own_refs, refs = (refs[: len(slots)], refs[len(slots) :])
        arrived_refs, refs = (refs[: len(arrived)], refs[len(arrived) :])
        out_ref = refs[-1]
        here = lax.axis_index("tm")
        for slot, own_ref in zip(slots, own_refs):
            mine = pick([entry == slot for entry in table], here)

            @pl.when(mine)
            def _():
                for start in range(0, columns, step):
                    part = slice(start, start + step)
                    total = own_ref[:, part]
                    for ref in arrived_refs:
                        total += ref[:, part].astype(jnp.float32)
                    if extras:
                        total = refs[0][:, part].astype(jnp.float32) + refs[1][:, part] * total
                    out_ref[:, part] = total.astype(jnp.bfloat16)

    operands = [partial[slot] for slot in slots] + list(arrived) + extras
    return pl.pallas_call(
        kernel,
        out_shape=jax.ShapeDtypeStruct((rows, columns), jnp.bfloat16),
        in_specs=whole_in_vmem(len(operands)),
        out_specs=whole_in_vmem(1)[0],
        compiler_params=roomy(),
        name="join",
    )(*operands)


def finish(arrived, partial, below, gate, fresh_frame):
    rows, columns = partial.shape
    step = math.gcd(columns, 256)

    def kernel(arrived_ref, partial_ref, below_ref, gate_ref, fresh_ref, out_ref):
        last = lax.axis_index("tm") == lax.axis_size("tm") - 1

        @pl.when(last)
        def _():
            out_ref[...] = fresh_ref[...]

        @pl.when(jnp.logical_not(last))
        def _():
            for start in range(0, columns, step):
                part = slice(start, start + step)
                total = partial_ref[:, part] + below_ref[:, part].astype(jnp.float32)
                total = arrived_ref[:, part].astype(jnp.float32) + gate_ref[:, part] * total
                out_ref[:, part] = total.astype(jnp.bfloat16)

    return pl.pallas_call(
        kernel,
        out_shape=jax.ShapeDtypeStruct((rows, columns), jnp.bfloat16),
        in_specs=whole_in_vmem(5),
        out_specs=whole_in_vmem(1)[0],
        compiler_params=roomy(),
        name="finish",
    )(arrived, partial, below, gate, fresh_frame)


def line_schedule(frames):
    steps = []
    for step in range(frames - 1):
        down = {z: step + 1 - (frames - 1 - z) for z in range(1, frames)}
        up = {z: frames - 1 - step + z for z in range(frames)}
        down = {z: f for z, f in down.items() if 1 <= f <= z}
        up = {z: f for z, f in up.items() if z + 2 <= f < frames}
        steps.append((down, up))
    order = []
    for z in range(frames):
        sent = [f for down, up in steps for f in (down.get(z), up.get(z)) if f is not None]
        order.append((sent + [z + 1])[: frames - 1])
    return steps, order


def head_plan(
    queries, keys, values, residual, fresh_frame, out_weight, time_weight, noise_steps, frame_mask
):
    frames, across = (lax.axis_size("tm"), lax.axis_size("head"))
    pairs = across // 2
    width = queries.shape[2] // (frames * pairs)
    here = lax.axis_index("tm")
    moves = [(a, b) for a in reversed(range(frames)) for b in range(pairs)]
    packed = pack(queries[0], keys[0], values[0], moves, pairs, width)

    own = []
    for piece, (a, b) in zip(packed, moves):
        if (a, b) != (0, 0):
            links = [
                (z * across + h, (z ^ a) * across + (h ^ (2 * b)))
                for z in range(frames)
                for h in range(across)
            ]
            piece = lax.ppermute(piece, ("tm", "head"), links)
        own.append(piece)
    swap = [(h, h ^ 1) for h in range(across)]
    mate = [lax.ppermute(piece, "head", swap) for piece in own]
    masks = [frame_mask] + [
        lax.ppermute(frame_mask, "tm", [(z, z ^ a) for z in range(frames)])
        for a in range(1, frames)
    ]
    noise = jnp.concatenate([noise_steps, shifted(noise_steps, "tm", -1)])
    gates = jnp.dot(
        time_features(noise), time_weight.astype(jnp.float32), precision=lax.Precision.HIGHEST
    )
    masks[0], gates = lax.optimization_barrier((masks[0], gates))
    gate_here, gate_next = (gates[:1], gates[1:])

    steps, order = line_schedule(frames)
    partial, short = ([], [])
    for slot in range(frames - 1):
        frames_of_slot = [order[z][slot] for z in range(frames)]
        part = attend(masks, frames_of_slot, own, mate, moves, pairs, frames, width)
        pieces = [part] + [
            lax.ppermute(part, "head", [(h, h ^ j) for h in range(across)])
            for j in range(1, across)
        ]
        product, rounded = project(pieces, out_weight, pairs)
        partial.append(product)
        short.append(rounded)

    above, below, payload = (None, None, short[0])
    for number, (down, up) in enumerate(steps):
        if number > 0:
            sends = {**down, **up}
            table = [order[z].index(sends[z]) if z in sends else 0 for z in range(frames)]
            final = number == len(steps) - 1
            arrived = [above] if final else [ref for ref in (above, below) if ref is not None]
            payload = join(
                partial, table, arrived, *((residual[0], gate_here) if final else ())
            )
        apart = not {z - 1 for z in down} & {z + 1 for z in up}
        if apart:
            links = [(z, z - 1) for z in down] + [(z, z + 1) for z in up]
            above, below = (lax.ppermute(payload, "tm", links), None if up else below)
        else:
            above = lax.ppermute(payload, "tm", [(z, z - 1) for z in down])
            below = lax.ppermute(payload, "tm", [(z, z + 1) for z in up])
    return finish(above, partial[-1], below, gate_next, fresh_frame)[None]


def power_of_two(number):
    return number & (number - 1) == 0


def suits_line(frames, window):
    apart = all(not set(down) & set(up) for down, up in line_schedule(frames)[0])
    return 2 < frames <= window and power_of_two(frames) and apart


def on_device(queries, *others):
    frames, across = (lax.axis_size("tm"), lax.axis_size("head"))
    heads = queries.shape[2] // HD
    even = across % 2 == 0 and power_of_two(across)
    if even and suits_line(frames, others[-1].shape[1]) and heads % (frames * across // 2) == 0:
        return head_plan(queries, *others)
    return frame_plan(queries, *others)


def solution(mesh):
    placed = (
        P(("groups", "tm"), "head", None),
        P(("groups", "tm"), "head", None),
        P(("groups", "tm"), "head", None),
        P(("groups", "tm"), None, "head"),
        P("groups", "head"),
        P("tm", "head"),
        P(None, "head"),
        P(("groups", "tm")),
        P(("groups", "tm"), None),
    )
    return jax.shard_map(
        on_device,
        mesh=mesh,
        in_specs=placed,
        out_specs=P(("groups", "tm"), None, "head"),
        check_vma=False,
    )
```

```python
import math

import jax
import jax.numpy as jnp
import numpy as np
from jax import lax
from jax.experimental import pallas as pl
from jax.experimental.pallas import tpu as pltpu
from jax.sharding import PartitionSpec as P

HD = 128
FREQ = 256
STEPS = 50
VMEM_BYTES = 24 * 1024 * 1024
PACK_BYTES = 60 * 1024 * 1024


def shifted(value, axis, steps):
    count = lax.axis_size(axis)
    leading, last = (max(0, -steps), min(count, count - steps))
    return lax.ppermute(value, axis, [(source, source + steps) for source in range(leading, last)])


def time_features(noise_steps):
    timestep = 1000.0 * (noise_steps.astype(jnp.float32) + 1.0) / STEPS
    half = FREQ // 2
    rates = jnp.exp(-math.log(10000.0) * jnp.arange(half).astype(jnp.float32) / half)
    angles = timestep[:, None] * rates[None, :]
    return jnp.concatenate([jnp.cos(angles), jnp.sin(angles)], axis=1)


def frame_plan(
    queries, keys, values, residual, fresh_frame, out_weight, time_weight, noise_steps, frame_mask
):
    query_local, key_local, value_local = (
        lax.all_to_all(queries, "head", split_axis=2, concat_axis=1, tiled=True),
        lax.all_to_all(keys, "head", split_axis=2, concat_axis=1, tiled=True),
        lax.all_to_all(values, "head", split_axis=2, concat_axis=1, tiled=True),
    )
    tokens = query_local.shape[1]
    heads_here = query_local.shape[2] // HD
    scale = 1.0 / math.sqrt(HD)
    query_heads = query_local[0].reshape(tokens, heads_here, HD)
    key_value = jnp.stack([key_local[0], value_local[0]], axis=0)
    frame = lax.axis_index("tm")
    frames_total = lax.axis_size("tm")
    window = min(8, frames_total)
    mask_row = frame_mask[0]
    columns = jnp.arange(mask_row.shape[0], dtype=jnp.int32)

    def allowed_at(offset):
        hits = jnp.sum(jnp.where(columns == frame - offset, mask_row, 0))
        return hits > 0

    def absorb(state, block, allowed):
        running_max, weight_sum, accumulated = state
        key_heads = block[0].reshape(tokens, heads_here, HD)
        value_heads = block[1].reshape(tokens, heads_here, HD)
        scores = (
            jnp.einsum("qhd,khd->hqk", query_heads, key_heads, preferred_element_type=jnp.float32)
            * scale
        )
        new_max = jnp.where(allowed, jnp.maximum(running_max, jnp.max(scores, axis=2)), running_max)
        lifted = jnp.where(allowed, jnp.exp(jnp.minimum(scores - new_max[:, :, None], 0.0)), 0.0)
        factor = jnp.exp(running_max - new_max)
        weight_sum = weight_sum * factor + jnp.sum(lifted, axis=2)
        rounded = lifted.astype(jnp.bfloat16)
        accumulated = accumulated * jnp.transpose(factor)[:, :, None] + jnp.einsum(
            "hqk,khd->qhd", rounded, value_heads, preferred_element_type=jnp.float32
        )
        return (new_max, weight_sum, accumulated)

    state = (
        jnp.full((heads_here, tokens), -1e30, jnp.float32),
        jnp.zeros((heads_here, tokens), jnp.float32),
        jnp.zeros((tokens, heads_here, HD), jnp.float32),
    )
    state = absorb(state, key_value, allowed_at(0))
    moving = key_value
    for offset in range(1, window):
        moving = shifted(moving, "tm", 1)
        state = absorb(state, moving, allowed_at(offset))
    running_max, weight_sum, accumulated = state
    attention = (
        (accumulated / jnp.transpose(weight_sum)[:, :, None])
        .reshape(tokens, heads_here * HD)
        .astype(jnp.bfloat16)
    )
    weight_cols = lax.all_gather(out_weight, "tm", axis=0, tiled=True)
    projected = jnp.dot(
        lax.all_gather(attention, "head", axis=1, tiled=True),
        weight_cols,
        preferred_element_type=jnp.float32,
    )
    gate = jnp.dot(
        time_features(noise_steps), time_weight.astype(jnp.float32), precision=lax.Precision.HIGHEST
    )
    updated = (residual[0].astype(jnp.float32) + gate * projected).astype(jnp.bfloat16)
    moved = shifted(updated, "tm", -1)
    rolled = jnp.where(frame == frames_total - 1, fresh_frame, moved)
    return rolled[None]


def whole_in_vmem(count):
    return [pl.BlockSpec(memory_space=pltpu.VMEM)] * count


def roomy():
    return pltpu.CompilerParams(vmem_limit_bytes=VMEM_BYTES)


def pack(queries, keys, values, moves, pairs, width):
    tokens = queries.shape[0]
    count = len(moves)

    def kernel(*refs):
        sources, pieces, (loaded, packed, in_sems, out_sems) = (
            refs[:3],
            refs[3 : 3 + count],
            refs[3 + count :],
        )
        frame, pair = (lax.axis_index("tm"), lax.axis_index("head") // 2)
        loads = [
            pltpu.make_async_copy(source, loaded.at[place], in_sems.at[place])
            for place, source in enumerate(sources)
        ]
        for load in loads:
            load.start()
        for load in loads:
            load.wait()
        stores = []
        for number, (a, b) in enumerate(moves):
            block = (frame ^ a) * pairs + (pair ^ b)
            columns = pl.ds(pl.multiple_of(block * width, HD), width)
            for place in range(3):
                packed[number, :, place * width : (place + 1) * width] = loaded[place, :, columns]
            store = pltpu.make_async_copy(packed.at[number], pieces[number], out_sems.at[number])
            store.start()
            stores.append(store)
        for store in stores:
            store.wait()

    return pl.pallas_call(
        kernel,
        out_shape=[jax.ShapeDtypeStruct((tokens, 3 * width), queries.dtype)] * count,
        in_specs=[pl.BlockSpec(memory_space=pltpu.HBM)] * 3,
        out_specs=[pl.BlockSpec(memory_space=pltpu.HBM)] * count,
        scratch_shapes=[
            pltpu.VMEM((3, *queries.shape), queries.dtype),
            pltpu.VMEM((count, tokens, 3 * width), queries.dtype),
            pltpu.SemaphoreType.DMA((3,)),
            pltpu.SemaphoreType.DMA((count,)),
        ],
        compiler_params=pltpu.CompilerParams(vmem_limit_bytes=PACK_BYTES),
        name="pack",
    )(queries, keys, values)


def pick(table, here):
    result = table[0]
    for place, entry in enumerate(table[1:], 1):
        result = jnp.where(here == place, entry, result)
    return result


def attend(masks, frames_of_slot, own, mate, moves, pairs, frames, width):
    tokens = own[0].shape[0]
    rows, keys_rows = (pairs * tokens, 2 * pairs * tokens)
    scale = 1.0 / math.sqrt(HD)

    def kernel(*refs):
        mask_refs, refs = (refs[:frames], refs[frames:])
        own_refs, refs = (refs[: len(moves)], refs[len(moves) :])
        mate_refs, refs = (refs[: len(moves)], refs[len(moves) :])
        out_ref, query_buf, key_buf, value_buf = refs
        here = lax.axis_index("tm")
        for own_ref, mate_ref, (a, b) in zip(own_refs, mate_refs, moves):
            query_buf[here ^ a, b * tokens : (b + 1) * tokens, :] = own_ref[:, :width]
            for side, ref in enumerate((own_ref, mate_ref)):
                span = slice((2 * b + side) * tokens, (2 * b + side + 1) * tokens)
                key_buf[a, span, :] = ref[:, width : 2 * width]
                value_buf[a, span, :] = ref[:, 2 * width :]
        frame = pick(frames_of_slot, here)
        allowed = []
        for a in range(frames):
            entry = 0
            for source in range(frames):
                entry = jnp.where(here ^ source == frame, mask_refs[source][0, here ^ a], entry)
            allowed.append(entry)
        for start in range(0, width, HD):
            channels = slice(start, start + HD)
            query = query_buf[frame, :, channels]
            blocks = []
            for a in range(frames):
                scores = (
                    lax.dot_general(
                        query,
                        key_buf[a, :, channels],
                        (((1,), (1,)), ((), ())),
                        preferred_element_type=jnp.float32,
                    )
                    * scale
                )
                blocks.append(jnp.where(allowed[a] > 0, scores, -1e30))
            scores = jnp.concatenate(blocks, axis=1)
            lifted = jnp.exp(scores - jnp.max(scores, axis=1, keepdims=True))
            totals = jnp.sum(lifted, axis=1, keepdims=True)
            values = value_buf[:, :, channels].reshape(frames * keys_rows, HD)
            mixed = jnp.dot(
                lifted.astype(jnp.bfloat16), values, preferred_element_type=jnp.float32
            )
            out_ref[:, channels] = (mixed / totals).astype(jnp.bfloat16)

    kind = own[0].dtype
    return pl.pallas_call(
        kernel,
        out_shape=jax.ShapeDtypeStruct((rows, width), jnp.bfloat16),
        in_specs=[pl.BlockSpec(memory_space=pltpu.SMEM)] * frames + whole_in_vmem(2 * len(moves)),
        out_specs=whole_in_vmem(1)[0],
        scratch_shapes=[
            pltpu.VMEM((frames, rows, width), kind),
            pltpu.VMEM((frames, keys_rows, width), kind),
            pltpu.VMEM((frames, keys_rows, width), kind),
        ],
        compiler_params=roomy(),
        name="attend",
    )(*masks, *own, *mate)


def project(pieces, weight, pairs):
    rows, width = pieces[0].shape
    tokens = rows // pairs
    depth, columns = weight.shape
    step = math.gcd(columns, 256)

    def kernel(*refs):
        piece_refs, (weight_ref, out_ref, short_ref, whole) = (
            refs[: len(pieces)],
            refs[len(pieces) :],
        )
        here = lax.axis_index("head")
        for j, ref in enumerate(piece_refs):
            source = here ^ j
            pair, core = (source // 2, source % 2)
            channels = pl.ds(pl.multiple_of(pair * width, HD), width)
            for b in range(pairs):
                first = ((pair ^ b) * 2 + core) * tokens
                whole[pl.ds(pl.multiple_of(first, 16), tokens), channels] = ref[
                    b * tokens : (b + 1) * tokens, :
                ]
        for start in range(0, columns, step):
            product = jnp.dot(
                whole[...], weight_ref[:, start : start + step], preferred_element_type=jnp.float32
            )
            out_ref[:, start : start + step] = product
            short_ref[:, start : start + step] = product.astype(jnp.bfloat16)

    return pl.pallas_call(
        kernel,
        out_shape=[
            jax.ShapeDtypeStruct((2 * rows, columns), jnp.float32),
            jax.ShapeDtypeStruct((2 * rows, columns), jnp.bfloat16),
        ],
        in_specs=whole_in_vmem(len(pieces) + 1),
        out_specs=whole_in_vmem(2),
        scratch_shapes=[pltpu.VMEM((2 * rows, depth), jnp.bfloat16)],
        compiler_params=roomy(),
        name="project",
    )(*pieces, weight)


def join(partial, table, arrived, residual=None, gate=None):
    rows, columns = partial[0].shape
    step = math.gcd(columns, 256)
    slots = sorted(set(table))
    extras = [] if residual is None else [residual, gate]

    def kernel(*refs):
        own_refs, refs = (refs[: len(slots)], refs[len(slots) :])
        arrived_refs, refs = (refs[: len(arrived)], refs[len(arrived) :])
        out_ref = refs[-1]
        here = lax.axis_index("tm")
        for slot, own_ref in zip(slots, own_refs):
            mine = pick([entry == slot for entry in table], here)

            @pl.when(mine)
            def _():
                for start in range(0, columns, step):
                    part = slice(start, start + step)
                    total = own_ref[:, part]
                    for ref in arrived_refs:
                        total += ref[:, part].astype(jnp.float32)
                    if extras:
                        total = refs[0][:, part].astype(jnp.float32) + refs[1][:, part] * total
                    out_ref[:, part] = total.astype(jnp.bfloat16)

    operands = [partial[slot] for slot in slots] + list(arrived) + extras
    return pl.pallas_call(
        kernel,
        out_shape=jax.ShapeDtypeStruct((rows, columns), jnp.bfloat16),
        in_specs=whole_in_vmem(len(operands)),
        out_specs=whole_in_vmem(1)[0],
        compiler_params=roomy(),
        name="join",
    )(*operands)


def finish(arrived, partial, below, gate, fresh_frame):
    rows, columns = partial.shape
    step = math.gcd(columns, 256)

    def kernel(arrived_ref, partial_ref, below_ref, gate_ref, fresh_ref, out_ref):
        last = lax.axis_index("tm") == lax.axis_size("tm") - 1

        @pl.when(last)
        def _():
            out_ref[...] = fresh_ref[...]

        @pl.when(jnp.logical_not(last))
        def _():
            for start in range(0, columns, step):
                part = slice(start, start + step)
                total = partial_ref[:, part] + below_ref[:, part].astype(jnp.float32)
                total = arrived_ref[:, part].astype(jnp.float32) + gate_ref[:, part] * total
                out_ref[:, part] = total.astype(jnp.bfloat16)

    return pl.pallas_call(
        kernel,
        out_shape=jax.ShapeDtypeStruct((rows, columns), jnp.bfloat16),
        in_specs=whole_in_vmem(5),
        out_specs=whole_in_vmem(1)[0],
        compiler_params=roomy(),
        name="finish",
    )(arrived, partial, below, gate, fresh_frame)


def line_schedule(frames):
    steps = []
    for step in range(frames - 1):
        down = {z: step + 1 - (frames - 1 - z) for z in range(1, frames)}
        up = {z: frames - 1 - step + z for z in range(frames)}
        down = {z: f for z, f in down.items() if 1 <= f <= z}
        up = {z: f for z, f in up.items() if z + 2 <= f < frames}
        steps.append((down, up))
    order = []
    for z in range(frames):
        sent = [f for down, up in steps for f in (down.get(z), up.get(z)) if f is not None]
        order.append((sent + [z + 1])[: frames - 1])
    return steps, order


def head_plan(
    queries, keys, values, residual, fresh_frame, out_weight, time_weight, noise_steps, frame_mask
):
    frames, across = (lax.axis_size("tm"), lax.axis_size("head"))
    pairs = across // 2
    width = queries.shape[2] // (frames * pairs)
    here = lax.axis_index("tm")
    moves = [(a, b) for a in reversed(range(frames)) for b in range(pairs)]
    packed = pack(queries[0], keys[0], values[0], moves, pairs, width)

    own = []
    for piece, (a, b) in zip(packed, moves):
        if (a, b) != (0, 0):
            links = [
                (z * across + h, (z ^ a) * across + (h ^ (2 * b)))
                for z in range(frames)
                for h in range(across)
            ]
            piece = lax.ppermute(piece, ("tm", "head"), links)
        own.append(piece)
    own[0], frame_mask, noise_steps = lax.optimization_barrier((own[0], frame_mask, noise_steps))
    swap = [(h, h ^ 1) for h in range(across)]
    mate = [lax.ppermute(piece, "head", swap) for piece in own]
    masks = [frame_mask] + [
        lax.ppermute(frame_mask, "tm", [(z, z ^ a) for z in range(frames)])
        for a in range(1, frames)
    ]
    noise = jnp.concatenate([noise_steps, shifted(noise_steps, "tm", -1)])
    gates = jnp.dot(
        time_features(noise), time_weight.astype(jnp.float32), precision=lax.Precision.HIGHEST
    )
    masks[0], gates = lax.optimization_barrier((masks[0], gates))
    gate_here, gate_next = (gates[:1], gates[1:])

    steps, order = line_schedule(frames)
    partial, short = ([], [])
    for slot in range(frames - 1):
        frames_of_slot = [order[z][slot] for z in range(frames)]
        part = attend(masks, frames_of_slot, own, mate, moves, pairs, frames, width)
        pieces = [part] + [
            lax.ppermute(part, "head", [(h, h ^ j) for h in range(across)])
            for j in range(1, across)
        ]
        product, rounded = project(pieces, out_weight, pairs)
        partial.append(product)
        short.append(rounded)

    above, below, payload = (None, None, short[0])
    for number, (down, up) in enumerate(steps):
        if number > 0:
            sends = {**down, **up}
            table = [order[z].index(sends[z]) if z in sends else 0 for z in range(frames)]
            final = number == len(steps) - 1
            arrived = [above] if final else [ref for ref in (above, below) if ref is not None]
            payload = join(
                partial, table, arrived, *((residual[0], gate_here) if final else ())
            )
        apart = not {z - 1 for z in down} & {z + 1 for z in up}
        if apart:
            links = [(z, z - 1) for z in down] + [(z, z + 1) for z in up]
            above, below = (lax.ppermute(payload, "tm", links), None if up else below)
        else:
            above = lax.ppermute(payload, "tm", [(z, z - 1) for z in down])
            below = lax.ppermute(payload, "tm", [(z, z + 1) for z in up])
    return finish(above, partial[-1], below, gate_next, fresh_frame)[None]


def power_of_two(number):
    return number & (number - 1) == 0


def suits_line(frames, window):
    apart = all(not set(down) & set(up) for down, up in line_schedule(frames)[0])
    return 2 < frames <= window and power_of_two(frames) and apart


def on_device(queries, *others):
    frames, across = (lax.axis_size("tm"), lax.axis_size("head"))
    heads = queries.shape[2] // HD
    even = across % 2 == 0 and power_of_two(across)
    if even and suits_line(frames, others[-1].shape[1]) and heads % (frames * across // 2) == 0:
        return head_plan(queries, *others)
    return frame_plan(queries, *others)


def solution(mesh):
    placed = (
        P(("groups", "tm"), "head", None),
        P(("groups", "tm"), "head", None),
        P(("groups", "tm"), "head", None),
        P(("groups", "tm"), None, "head"),
        P("groups", "head"),
        P("tm", "head"),
        P(None, "head"),
        P(("groups", "tm")),
        P(("groups", "tm"), None),
    )
    return jax.shard_map(
        on_device,
        mesh=mesh,
        in_specs=placed,
        out_specs=P(("groups", "tm"), None, "head"),
        check_vma=False,
    )
```

```python
import math

import jax
import jax.numpy as jnp
import numpy as np
from jax import lax
from jax.experimental import pallas as pl
from jax.experimental.pallas import tpu as pltpu
from jax.sharding import PartitionSpec as P

HD = 128
FREQ = 256
STEPS = 50
VMEM_BYTES = 16 * 1024 * 1024
PACK_BYTES = 60 * 1024 * 1024


def shifted(value, axis, steps):
    count = lax.axis_size(axis)
    leading, last = (max(0, -steps), min(count, count - steps))
    return lax.ppermute(value, axis, [(source, source + steps) for source in range(leading, last)])


def time_features(noise_steps):
    timestep = 1000.0 * (noise_steps.astype(jnp.float32) + 1.0) / STEPS
    half = FREQ // 2
    rates = jnp.exp(-math.log(10000.0) * jnp.arange(half).astype(jnp.float32) / half)
    angles = timestep[:, None] * rates[None, :]
    return jnp.concatenate([jnp.cos(angles), jnp.sin(angles)], axis=1)


def frame_plan(
    queries, keys, values, residual, fresh_frame, out_weight, time_weight, noise_steps, frame_mask
):
    query_local, key_local, value_local = (
        lax.all_to_all(queries, "head", split_axis=2, concat_axis=1, tiled=True),
        lax.all_to_all(keys, "head", split_axis=2, concat_axis=1, tiled=True),
        lax.all_to_all(values, "head", split_axis=2, concat_axis=1, tiled=True),
    )
    tokens = query_local.shape[1]
    heads_here = query_local.shape[2] // HD
    scale = 1.0 / math.sqrt(HD)
    query_heads = query_local[0].reshape(tokens, heads_here, HD)
    key_value = jnp.stack([key_local[0], value_local[0]], axis=0)
    frame = lax.axis_index("tm")
    frames_total = lax.axis_size("tm")
    window = min(8, frames_total)
    mask_row = frame_mask[0]
    columns = jnp.arange(mask_row.shape[0], dtype=jnp.int32)

    def allowed_at(offset):
        hits = jnp.sum(jnp.where(columns == frame - offset, mask_row, 0))
        return hits > 0

    def absorb(state, block, allowed):
        running_max, weight_sum, accumulated = state
        key_heads = block[0].reshape(tokens, heads_here, HD)
        value_heads = block[1].reshape(tokens, heads_here, HD)
        scores = (
            jnp.einsum("qhd,khd->hqk", query_heads, key_heads, preferred_element_type=jnp.float32)
            * scale
        )
        new_max = jnp.where(allowed, jnp.maximum(running_max, jnp.max(scores, axis=2)), running_max)
        lifted = jnp.where(allowed, jnp.exp(jnp.minimum(scores - new_max[:, :, None], 0.0)), 0.0)
        factor = jnp.exp(running_max - new_max)
        weight_sum = weight_sum * factor + jnp.sum(lifted, axis=2)
        rounded = lifted.astype(jnp.bfloat16)
        accumulated = accumulated * jnp.transpose(factor)[:, :, None] + jnp.einsum(
            "hqk,khd->qhd", rounded, value_heads, preferred_element_type=jnp.float32
        )
        return (new_max, weight_sum, accumulated)

    state = (
        jnp.full((heads_here, tokens), -1e30, jnp.float32),
        jnp.zeros((heads_here, tokens), jnp.float32),
        jnp.zeros((tokens, heads_here, HD), jnp.float32),
    )
    state = absorb(state, key_value, allowed_at(0))
    moving = key_value
    for offset in range(1, window):
        moving = shifted(moving, "tm", 1)
        state = absorb(state, moving, allowed_at(offset))
    running_max, weight_sum, accumulated = state
    attention = (
        (accumulated / jnp.transpose(weight_sum)[:, :, None])
        .reshape(tokens, heads_here * HD)
        .astype(jnp.bfloat16)
    )
    weight_cols = lax.all_gather(out_weight, "tm", axis=0, tiled=True)
    projected = jnp.dot(
        lax.all_gather(attention, "head", axis=1, tiled=True),
        weight_cols,
        preferred_element_type=jnp.float32,
    )
    gate = jnp.dot(
        time_features(noise_steps), time_weight.astype(jnp.float32), precision=lax.Precision.HIGHEST
    )
    updated = (residual[0].astype(jnp.float32) + gate * projected).astype(jnp.bfloat16)
    moved = shifted(updated, "tm", -1)
    rolled = jnp.where(frame == frames_total - 1, fresh_frame, moved)
    return rolled[None]


def whole_in_vmem(count):
    return [pl.BlockSpec(memory_space=pltpu.VMEM)] * count


def in_hbm(count):
    return [pl.BlockSpec(memory_space=pltpu.HBM)] * count


def roomy():
    return pltpu.CompilerParams(vmem_limit_bytes=VMEM_BYTES)


def pack(queries, keys, values, frame_mask, noise_steps, moves, pairs, width):
    tokens = queries.shape[0]
    window = frame_mask.shape[1]
    widths = [3 * width + (HD if b == 0 else 0) for a, b in moves]
    count = len(moves)

    def kernel(*refs):
        sources, small, pieces, scratch = (refs[:3], refs[3:5], refs[5 : 5 + count], refs[5 + count :])
        loaded, packed, mask_ref, noise_ref, in_sems, out_sems = scratch
        frame, pair = (lax.axis_index("tm"), lax.axis_index("head") // 2)
        targets = [loaded.at[place] for place in range(3)] + [mask_ref, noise_ref]
        loads = [
            pltpu.make_async_copy(source, target, in_sems.at[place])
            for place, (source, target) in enumerate(zip((*sources, *small), targets))
        ]
        for load in loads:
            load.start()
        for load in loads:
            load.wait()
        lane = lax.broadcasted_iota(jnp.int32, (tokens, HD), 1)
        note = jnp.where(lane == window, noise_ref[0], 0)
        for column in range(window):
            note = jnp.where(lane == column, mask_ref[0, column], note)
        note = note.astype(jnp.float32).astype(queries.dtype)
        stores = []
        for number, (a, b) in enumerate(moves):
            block = (frame ^ a) * pairs + (pair ^ b)
            columns = pl.ds(pl.multiple_of(block * width, HD), width)
            for place in range(3):
                packed[number, :, place * width : (place + 1) * width] = loaded[place, :, columns]
            if b == 0:
                packed[number, :, 3 * width :] = note
            store = pltpu.make_async_copy(
                packed.at[number, :, : widths[number]], pieces[number], out_sems.at[number]
            )
            store.start()
            stores.append(store)
        for store in stores:
            store.wait()

    return pl.pallas_call(
        kernel,
        out_shape=[jax.ShapeDtypeStruct((tokens, size), queries.dtype) for size in widths],
        in_specs=in_hbm(5),
        out_specs=in_hbm(count),
        scratch_shapes=[
            pltpu.VMEM((3, *queries.shape), queries.dtype),
            pltpu.VMEM((count, tokens, 3 * width + HD), queries.dtype),
            pltpu.SMEM(frame_mask.shape, frame_mask.dtype),
            pltpu.SMEM(noise_steps.shape, noise_steps.dtype),
            pltpu.SemaphoreType.DMA((5,)),
            pltpu.SemaphoreType.DMA((count,)),
        ],
        compiler_params=pltpu.CompilerParams(vmem_limit_bytes=PACK_BYTES),
        name="pack",
    )(queries, keys, values, frame_mask, noise_steps)


def pick(table, here):
    result = table[0]
    for place, entry in enumerate(table[1:], 1):
        result = jnp.where(here == place, entry, result)
    return result


def collect(pieces, width):
    flat = [piece for frame in pieces for options in frame for piece, _ in options]
    tokens, kind = (flat[0].shape[0], flat[0].dtype)
    pairs, count = (len(pieces[0]), len(pieces))

    def kernel(*refs):
        query_ref, pair_ref, note_ref = refs[len(flat) :]
        sources = iter(refs[: len(flat)])
        here = lax.axis_index("tm")
        for i, frame in enumerate(pieces):
            for b, options in enumerate(frame):
                for _, places in options:
                    source = next(sources)

                    def fill(i=i, b=b, source=source):
                        rows = slice(b * tokens, (b + 1) * tokens)
                        query_ref[i, rows, :] = source[:, :width]
                        pair_ref[i, rows, :] = source[:, width : 3 * width]
                        if b == 0:
                            note_ref[i] = source[:16, 3 * width :]

                    if places is None:
                        fill()
                    else:
                        pl.when(pick([z in places for z in range(lax.axis_size("tm"))], here))(fill)

    return pl.pallas_call(
        kernel,
        out_shape=[
            jax.ShapeDtypeStruct((count, pairs * tokens, width), kind),
            jax.ShapeDtypeStruct((count, pairs * tokens, 2 * width), kind),
            jax.ShapeDtypeStruct((count, 16, HD), kind),
        ],
        in_specs=whole_in_vmem(len(flat)),
        out_specs=whole_in_vmem(3),
        compiler_params=roomy(),
        name="collect",
    )(*flat)


def attend(frames_of_slot, groups, only=None):
    rows, width = groups[0][1].shape[1:]
    scale = 1.0 / math.sqrt(HD)
    operands = [array for group in groups for array in group[1:]]

    def work(*refs):
        out_ref, query_buf, note_buf = refs[len(operands) :]
        here = lax.axis_index("tm")
        frame = pick(frames_of_slot, here)
        columns, key_refs = ([], [])
        for number, group in enumerate(groups):
            query_ref, own_ref, mate_ref, note_ref = refs[4 * number : 4 * number + 4]
            for i, a in enumerate(group[0]):
                columns.append(here ^ a)
                key_refs += [own_ref.at[i], mate_ref.at[i]]

                @pl.when(here ^ a == frame)
                def _(i=i, query_ref=query_ref, note_ref=note_ref):
                    query_buf[...] = query_ref[i]
                    note_buf[...] = note_ref[i].astype(jnp.float32)

        note = note_buf[:1, :]
        lane = lax.broadcasted_iota(jnp.int32, note.shape, 1)
        allowed = [
            jnp.sum(jnp.where(lane == column, note, 0.0), axis=1, keepdims=True) > 0.5
            for column in columns
        ]
        for start in range(0, width, HD):
            channels = slice(start, start + HD)
            keys = jnp.concatenate([ref[:, channels] for ref in key_refs], axis=0)
            scores = (
                lax.dot_general(
                    query_buf[:, channels],
                    keys,
                    (((1,), (1,)), ((), ())),
                    preferred_element_type=jnp.float32,
                )
                * scale
            )
            blocks = [
                jnp.where(hit, scores[:, i * 2 * rows : (i + 1) * 2 * rows], -1e30)
                for i, hit in enumerate(allowed)
            ]
            scores = jnp.concatenate(blocks, axis=1)
            lifted = jnp.exp(scores - jnp.max(scores, axis=1, keepdims=True))
            totals = jnp.sum(lifted, axis=1, keepdims=True)
            values = jnp.concatenate(
                [ref[:, width + start : width + start + HD] for ref in key_refs], axis=0
            )
            mixed = jnp.dot(
                lifted.astype(jnp.bfloat16), values, preferred_element_type=jnp.float32
            )
            out_ref[:, channels] = (mixed / totals).astype(jnp.bfloat16)

    def kernel(*refs):
        if only is None:
            work(*refs)
        else:
            pl.when(lax.axis_index("tm") == only)(lambda: work(*refs))

    return pl.pallas_call(
        kernel,
        out_shape=jax.ShapeDtypeStruct((rows, width), jnp.bfloat16),
        in_specs=whole_in_vmem(len(operands)),
        out_specs=whole_in_vmem(1)[0],
        scratch_shapes=[
            pltpu.VMEM((rows, width), groups[0][1].dtype),
            pltpu.VMEM((16, HD), jnp.float32),
        ],
        compiler_params=roomy(),
        name="attend",
    )(*operands)


def project(pieces, weight, pairs, cuts, only=None):
    rows, width = pieces[0].shape
    tokens = rows // pairs
    depth, columns = weight.shape
    step = math.gcd(columns, 256)
    spans = [slice(first, last) for first, last in zip([0, *cuts], cuts)]

    def work(*refs):
        piece_refs, (weight_ref, out_ref, *short_refs, whole) = (
            refs[: len(pieces)],
            refs[len(pieces) :],
        )
        here = lax.axis_index("head")
        for j, ref in enumerate(piece_refs):
            source = here ^ j
            pair, core = (source // 2, source % 2)
            channels = pl.ds(pl.multiple_of(pair * width, HD), width)
            for b in range(pairs):
                first = ((pair ^ b) * 2 + core) * tokens
                whole[pl.ds(pl.multiple_of(first, 16), tokens), channels] = ref[
                    b * tokens : (b + 1) * tokens, :
                ]
        for start in range(0, columns, step):
            product = jnp.dot(
                whole[...], weight_ref[:, start : start + step], preferred_element_type=jnp.float32
            )
            out_ref[:, start : start + step] = product
            for span, short_ref in zip(spans, short_refs):
                short_ref[:, start : start + step] = product[span, :].astype(jnp.bfloat16)

    def kernel(*refs):
        if only is None:
            work(*refs)
        else:
            pl.when(lax.axis_index("tm") == only)(lambda: work(*refs))

    product, *rounded = pl.pallas_call(
        kernel,
        out_shape=[jax.ShapeDtypeStruct((2 * rows, columns), jnp.float32)]
        + [
            jax.ShapeDtypeStruct((span.stop - span.start, columns), jnp.bfloat16) for span in spans
        ],
        in_specs=whole_in_vmem(len(pieces) + 1),
        out_specs=whole_in_vmem(1 + len(spans)),
        scratch_shapes=[pltpu.VMEM((2 * rows, depth), jnp.bfloat16)],
        compiler_params=roomy(),
        name="project",
    )(*pieces, weight)
    return (product, rounded)


def join(partial, table, arrived, residual=None, gate=None):
    rows, columns = partial[0].shape
    step = math.gcd(columns, 256)
    slots = sorted(set(table))
    extras = [] if residual is None else [residual, gate]
    spans = []
    for parts in arrived:
        ends = np.cumsum([part.shape[0] for part in parts])
        spans += [(int(last) - part.shape[0], int(last)) for part, last in zip(parts, ends)]

    def kernel(*refs):
        own_refs, refs = (refs[: len(slots)], refs[len(slots) :])
        arrived_refs, refs = (refs[: len(spans)], refs[len(spans) :])
        out_ref = refs[-1]
        here = lax.axis_index("tm")
        bounds = sorted({0, rows, *(last for _, last in spans)})
        for slot, own_ref in zip(slots, own_refs):

            @pl.when(pick([entry == slot for entry in table], here))
            def _(own_ref=own_ref):
                for top, bottom in zip(bounds, bounds[1:]):
                    for start in range(0, columns, step):
                        part = (slice(top, bottom), slice(start, start + step))
                        total = own_ref[part]
                        for (first, last), ref in zip(spans, arrived_refs):
                            if first <= top < last:
                                inner = ref[top - first : bottom - first, part[1]]
                                total += inner.astype(jnp.float32)
                        if extras:
                            total = refs[0][part].astype(jnp.float32) + refs[1][:, part[1]] * total
                        out_ref[part] = total.astype(jnp.bfloat16)

    operands = [partial[slot] for slot in slots] + [ref for parts in arrived for ref in parts] + extras
    return pl.pallas_call(
        kernel,
        out_shape=jax.ShapeDtypeStruct((rows, columns), jnp.bfloat16),
        in_specs=whole_in_vmem(len(operands)),
        out_specs=whole_in_vmem(1)[0],
        compiler_params=roomy(),
        name="join",
    )(*operands)


def finish(arrived, partial, below, gate, fresh_frame):
    rows, columns = partial.shape
    step = math.gcd(columns, 256)

    def kernel(arrived_ref, partial_ref, below_ref, gate_ref, fresh_ref, out_ref):
        last = lax.axis_index("tm") == lax.axis_size("tm") - 1

        @pl.when(last)
        def _():
            out_ref[...] = fresh_ref[...]

        @pl.when(jnp.logical_not(last))
        def _():
            for start in range(0, columns, step):
                part = slice(start, start + step)
                total = partial_ref[:, part] + below_ref[:, part].astype(jnp.float32)
                total = arrived_ref[:, part].astype(jnp.float32) + gate_ref[:, part] * total
                out_ref[:, part] = total.astype(jnp.bfloat16)

    return pl.pallas_call(
        kernel,
        out_shape=jax.ShapeDtypeStruct((rows, columns), jnp.bfloat16),
        in_specs=whole_in_vmem(5),
        out_specs=whole_in_vmem(1)[0],
        compiler_params=roomy(),
        name="finish",
    )(arrived, partial, below, gate, fresh_frame)


def line_schedule(frames):
    steps = []
    for step in range(frames - 1):
        down = {z: step + 1 - (frames - 1 - z) for z in range(1, frames)}
        up = {z: frames - 1 - step + z for z in range(frames)}
        down = {z: f for z, f in down.items() if 1 <= f <= z}
        up = {z: f for z, f in up.items() if z + 2 <= f < frames}
        steps.append((down, up))
    order = []
    for z in range(frames):
        sent = [f for down, up in steps for f in (down.get(z), up.get(z)) if f is not None]
        order.append((sent + [z + 1])[: frames - 1])
    return steps, order


def head_plan(
    queries, keys, values, residual, fresh_frame, out_weight, time_weight, noise_steps, frame_mask
):
    frames, across = (lax.axis_size("tm"), lax.axis_size("head"))
    pairs = across // 2
    width = queries.shape[2] // (frames * pairs)
    here = lax.axis_index("tm")
    window = frame_mask.shape[1]
    end = frames - 1
    everywhere = list(range(frames))

    def move(piece, a, j, places):
        links = [
            (z * across + h, (z ^ a) * across + (h ^ j)) for z in places for h in range(across)
        ]
        return lax.ppermute(piece, ("tm", "head"), links)

    moves = [(a, b) for a in reversed(range(frames)) for b in range(pairs)]
    packed = dict(
        zip(moves, pack(queries[0], keys[0], values[0], frame_mask, noise_steps, moves, pairs, width))
    )

    first = {a: (end, end ^ a) for a in (end, end - 1)}
    others = {a: [z for z in everywhere if z not in first.get(a, ())] for a in everywhere}
    near = [a for a in everywhere if a not in first]
    early = {(a, b): move(packed[a, b], a, 2 * b, first[a]) for a in first for b in range(pairs)}
    late, latest = ({(0, 0): packed[0, 0]}, None)
    for a in near:
        for b in range(pairs):
            if (a, b) != (0, 0):
                piece = packed[a, b]
                if latest is not None:
                    piece, late[latest] = lax.optimization_barrier((piece, late[latest]))
                latest = (a, b)
                late[latest] = move(piece, a, 2 * b, everywhere)
    rest = {(a, b): packed[a, b] for a in first for b in range(pairs)}
    rest, early = lax.optimization_barrier((rest, early))
    late.update({(a, b): move(piece, a, 2 * b, others[a]) for (a, b), piece in rest.items()})

    def swap(array, places):
        return move(array, 0, 1, places)

    def gather(part, places):
        pieces = {0: part}
        bit = across // 2
        while bit:
            for j in list(pieces):
                pieces[j ^ bit] = move(pieces[j], 0, bit, places)
            bit //= 2
        return [pieces[j] for j in range(across)]

    early, late = lax.optimization_barrier((early, late))
    query, pair, note = collect(
        [[[(early[a, b], [end])] for b in range(pairs)] for a in first], width
    )
    group = (list(first), query, pair, swap(pair, [end]), note)
    part = attend([1] * frames, [group], end)
    rows = 2 * part.shape[0]
    _, rounded = project(gather(part, [end]), out_weight, pairs, [rows // 4, rows], end)
    late, rounded = lax.optimization_barrier((late, rounded))
    above = [lax.ppermute(part, "tm", [(end, end - 1)]) for part in rounded]

    sources = [[[(late[a, b], None)] for b in range(pairs)] for a in near]
    query, pair, note = collect(sources, width)
    groups = [(near, query, pair, swap(pair, everywhere), note)]
    sources = [
        [
            [(early[a, b], first[a]), (late[a, b], others[a])]
            for b in range(pairs)
        ]
        for a in first
    ]
    query, pair, note = collect(sources, width)
    groups.append((list(first), query, pair, swap(pair, everywhere), note))
    above[0], held = lax.optimization_barrier((above[0], [group[1:] for group in groups]))
    groups = [(group[0], *arrays) for group, arrays in zip(groups, held)]

    notes = jnp.concatenate([groups[0][4], groups[1][4]])[:, 0, window].astype(jnp.float32)
    known = [a for group in groups for a in group[0]]
    slot_of = jnp.array([known.index(z ^ min(z + 1, end)) for z in everywhere])
    noise = jnp.stack([noise_steps[0].astype(jnp.float32), notes[slot_of[here]]])

    steps, order = line_schedule(frames)
    partial, short = ([], [])
    for slot in range(frames - 1):
        part = attend([order[z][slot] for z in everywhere], groups)
        if slot == 1:
            gates = jnp.dot(
                time_features(noise),
                time_weight.astype(jnp.float32),
                precision=lax.Precision.HIGHEST,
            )
            part, gates = lax.optimization_barrier((part, gates))
        product, rounded = project(gather(part, everywhere), out_weight, pairs, [rows])
        partial.append(product)
        short += rounded

    below = lax.ppermute(short[0], "tm", [(z, z + 1) for z in steps[0][1]])
    for number, (down, up) in enumerate(steps[1:], 1):
        sends = {**down, **up}
        table = [order[z].index(sends[z]) if z in sends else 0 for z in everywhere]
        if number < len(steps) - 1:
            payload = join(partial, table, [above, [below]])
            below = lax.ppermute(payload, "tm", [(z, z + 1) for z in up])
        else:
            payload = join(partial, table, [above], residual[0], gates[:1])
        above = [lax.ppermute(payload, "tm", [(z, z - 1) for z in down])]
    return finish(above[0], partial[-1], below, gates[1:], fresh_frame)[None]


def power_of_two(number):
    return number & (number - 1) == 0


def suits_line(frames, window):
    apart = all(not set(down) & set(up) for down, up in line_schedule(frames)[0])
    return 2 < frames <= window and power_of_two(frames) and apart


def on_device(queries, *others):
    frames, across = (lax.axis_size("tm"), lax.axis_size("head"))
    heads = queries.shape[2] // HD
    even = across % 2 == 0 and power_of_two(across)
    if even and suits_line(frames, others[-1].shape[1]) and heads % (frames * across // 2) == 0:
        return head_plan(queries, *others)
    return frame_plan(queries, *others)


def solution(mesh):
    placed = (
        P(("groups", "tm"), "head", None),
        P(("groups", "tm"), "head", None),
        P(("groups", "tm"), "head", None),
        P(("groups", "tm"), None, "head"),
        P("groups", "head"),
        P("tm", "head"),
        P(None, "head"),
        P(("groups", "tm")),
        P(("groups", "tm"), None),
    )
    return jax.shard_map(
        on_device,
        mesh=mesh,
        in_specs=placed,
        out_specs=P(("groups", "tm"), None, "head"),
        check_vma=False,
    )
```

```python
import math

import jax
import jax.numpy as jnp
import numpy as np
from jax import lax
from jax.experimental import pallas as pl
from jax.experimental.pallas import tpu as pltpu
from jax.sharding import PartitionSpec as P

HD = 128
FREQ = 256
STEPS = 50
VMEM_BYTES = 16 * 1024 * 1024
PACK_BYTES = 60 * 1024 * 1024


def shifted(value, axis, steps):
    count = lax.axis_size(axis)
    leading, last = (max(0, -steps), min(count, count - steps))
    return lax.ppermute(value, axis, [(source, source + steps) for source in range(leading, last)])


def time_features(noise_steps):
    timestep = 1000.0 * (noise_steps.astype(jnp.float32) + 1.0) / STEPS
    half = FREQ // 2
    rates = jnp.exp(-math.log(10000.0) * jnp.arange(half).astype(jnp.float32) / half)
    angles = timestep[:, None] * rates[None, :]
    return jnp.concatenate([jnp.cos(angles), jnp.sin(angles)], axis=1)


def frame_plan(
    queries, keys, values, residual, fresh_frame, out_weight, time_weight, noise_steps, frame_mask
):
    query_local, key_local, value_local = (
        lax.all_to_all(queries, "head", split_axis=2, concat_axis=1, tiled=True),
        lax.all_to_all(keys, "head", split_axis=2, concat_axis=1, tiled=True),
        lax.all_to_all(values, "head", split_axis=2, concat_axis=1, tiled=True),
    )
    tokens = query_local.shape[1]
    heads_here = query_local.shape[2] // HD
    scale = 1.0 / math.sqrt(HD)
    query_heads = query_local[0].reshape(tokens, heads_here, HD)
    key_value = jnp.stack([key_local[0], value_local[0]], axis=0)
    frame = lax.axis_index("tm")
    frames_total = lax.axis_size("tm")
    window = min(8, frames_total)
    mask_row = frame_mask[0]
    columns = jnp.arange(mask_row.shape[0], dtype=jnp.int32)

    def allowed_at(offset):
        hits = jnp.sum(jnp.where(columns == frame - offset, mask_row, 0))
        return hits > 0

    def absorb(state, block, allowed):
        running_max, weight_sum, accumulated = state
        key_heads = block[0].reshape(tokens, heads_here, HD)
        value_heads = block[1].reshape(tokens, heads_here, HD)
        scores = (
            jnp.einsum("qhd,khd->hqk", query_heads, key_heads, preferred_element_type=jnp.float32)
            * scale
        )
        new_max = jnp.where(allowed, jnp.maximum(running_max, jnp.max(scores, axis=2)), running_max)
        lifted = jnp.where(allowed, jnp.exp(jnp.minimum(scores - new_max[:, :, None], 0.0)), 0.0)
        factor = jnp.exp(running_max - new_max)
        weight_sum = weight_sum * factor + jnp.sum(lifted, axis=2)
        rounded = lifted.astype(jnp.bfloat16)
        accumulated = accumulated * jnp.transpose(factor)[:, :, None] + jnp.einsum(
            "hqk,khd->qhd", rounded, value_heads, preferred_element_type=jnp.float32
        )
        return (new_max, weight_sum, accumulated)

    state = (
        jnp.full((heads_here, tokens), -1e30, jnp.float32),
        jnp.zeros((heads_here, tokens), jnp.float32),
        jnp.zeros((tokens, heads_here, HD), jnp.float32),
    )
    state = absorb(state, key_value, allowed_at(0))
    moving = key_value
    for offset in range(1, window):
        moving = shifted(moving, "tm", 1)
        state = absorb(state, moving, allowed_at(offset))
    running_max, weight_sum, accumulated = state
    attention = (
        (accumulated / jnp.transpose(weight_sum)[:, :, None])
        .reshape(tokens, heads_here * HD)
        .astype(jnp.bfloat16)
    )
    weight_cols = lax.all_gather(out_weight, "tm", axis=0, tiled=True)
    projected = jnp.dot(
        lax.all_gather(attention, "head", axis=1, tiled=True),
        weight_cols,
        preferred_element_type=jnp.float32,
    )
    gate = jnp.dot(
        time_features(noise_steps), time_weight.astype(jnp.float32), precision=lax.Precision.HIGHEST
    )
    updated = (residual[0].astype(jnp.float32) + gate * projected).astype(jnp.bfloat16)
    moved = shifted(updated, "tm", -1)
    rolled = jnp.where(frame == frames_total - 1, fresh_frame, moved)
    return rolled[None]


def whole_in_vmem(count):
    return [pl.BlockSpec(memory_space=pltpu.VMEM)] * count


def in_hbm(count):
    return [pl.BlockSpec(memory_space=pltpu.HBM)] * count


def roomy():
    return pltpu.CompilerParams(vmem_limit_bytes=VMEM_BYTES)


def pack(queries, keys, values, frames, pairs, width):
    tokens = queries.shape[0]
    half = tokens // 2
    blocks = frames * pairs * 2

    def kernel(query_ref, key_ref, value_ref, query_out, pair_out, loaded, *rest):
        (query_buf, pair_buf, in_sems, out_sems) = rest
        loads = [
            pltpu.make_async_copy(source, loaded.at[place], in_sems.at[place])
            for place, source in enumerate((key_ref, value_ref, query_ref))
        ]
        for load in loads:
            load.start()
        stores = []
        for place, load in enumerate(loads):
            load.wait()
            target, start = ((pair_buf, place * width) if place < 2 else (query_buf, 0))
            for block in range(blocks):
                rows = slice(block % 2 * half, (block % 2 + 1) * half)
                columns = slice(block // 2 * width, (block // 2 + 1) * width)
                target[block * half : (block + 1) * half, start : start + width] = loaded[
                    place, rows, columns
                ]
            if place > 0:
                out = pair_out if place == 1 else query_out
                store = pltpu.make_async_copy(target, out, out_sems.at[place - 1])
                store.start()
                stores.append(store)
        for store in stores:
            store.wait()

    kind = queries.dtype
    query_shape, pair_shape = ((blocks * half, width), (blocks * half, 2 * width))
    return pl.pallas_call(
        kernel,
        out_shape=[
            jax.ShapeDtypeStruct(query_shape, kind),
            jax.ShapeDtypeStruct(pair_shape, kind),
        ],
        in_specs=in_hbm(3),
        out_specs=in_hbm(2),
        scratch_shapes=[
            pltpu.VMEM((3, *queries.shape), kind),
            pltpu.VMEM(query_shape, kind),
            pltpu.VMEM(pair_shape, kind),
            pltpu.SemaphoreType.DMA((3,)),
            pltpu.SemaphoreType.DMA((2,)),
        ],
        compiler_params=pltpu.CompilerParams(vmem_limit_bytes=PACK_BYTES),
        name="pack",
    )(queries, keys, values)


def pick(table, here):
    result = table[0]
    for place, entry in enumerate(table[1:], 1):
        result = jnp.where(here == place, entry, result)
    return result


def attend(frames_of_slot, masks, query, own, mate):
    frames = len(masks)
    rows, width = (query.shape[0] // frames, query.shape[1])
    scale = 1.0 / math.sqrt(HD)

    def kernel(*refs):
        mask_refs, (query_ref, own_ref, mate_ref, out_ref) = (refs[:frames], refs[frames:])
        here = lax.axis_index("tm")
        frame = pick(frames_of_slot, here)
        first = pl.multiple_of(frame * rows, rows)
        allowed = []
        for other in range(frames):
            entry = 0
            for a in range(frames):
                entry = jnp.where(here ^ a == frame, mask_refs[a][0, other], entry)
            allowed.append(entry > 0)
        for start in range(0, width, HD):
            channels = slice(start, start + HD)
            keys = jnp.concatenate([own_ref[:, channels], mate_ref[:, channels]], axis=0)
            scores = (
                lax.dot_general(
                    query_ref[pl.ds(first, rows), channels],
                    keys,
                    (((1,), (1,)), ((), ())),
                    preferred_element_type=jnp.float32,
                )
                * scale
            )
            blocks = [
                jnp.where(allowed[i % frames], scores[:, i * rows : (i + 1) * rows], -1e30)
                for i in range(2 * frames)
            ]
            scores = jnp.concatenate(blocks, axis=1)
            lifted = jnp.exp(scores - jnp.max(scores, axis=1, keepdims=True))
            totals = jnp.sum(lifted, axis=1, keepdims=True)
            channels = slice(width + start, width + start + HD)
            values = jnp.concatenate([own_ref[:, channels], mate_ref[:, channels]], axis=0)
            mixed = jnp.dot(
                lifted.astype(jnp.bfloat16), values, preferred_element_type=jnp.float32
            )
            out_ref[:, start : start + HD] = (mixed / totals).astype(jnp.bfloat16)

    return pl.pallas_call(
        kernel,
        out_shape=jax.ShapeDtypeStruct((rows, width), jnp.bfloat16),
        in_specs=[pl.BlockSpec(memory_space=pltpu.SMEM)] * frames + whole_in_vmem(3),
        out_specs=whole_in_vmem(1)[0],
        compiler_params=roomy(),
        name="attend",
    )(*masks, query, own, mate)


def project(pieces, weight, cuts):
    rows, width = pieces[0].shape
    half = rows // len(pieces)
    depth, columns = weight.shape
    step = math.gcd(columns, 256)
    spans = [slice(first, last) for first, last in zip([0, *cuts], cuts)]

    def kernel(*refs):
        piece_refs, (weight_ref, out_ref, *short_refs, whole) = (
            refs[: len(pieces)],
            refs[len(pieces) :],
        )
        here = lax.axis_index("head")
        for j, ref in enumerate(piece_refs):
            source = here ^ j
            pair, core = (source // 2, source % 2)
            channels = pl.ds(pl.multiple_of(pair * width, HD), width)
            for part in range(len(pieces)):
                first = pl.multiple_of((2 * part + core) * half, half)
                whole[pl.ds(first, half), channels] = ref[part * half : (part + 1) * half, :]
        for start in range(0, columns, step):
            product = jnp.dot(
                whole[...], weight_ref[:, start : start + step], preferred_element_type=jnp.float32
            )
            out_ref[:, start : start + step] = product
            for span, short_ref in zip(spans, short_refs):
                short_ref[:, start : start + step] = product[span, :].astype(jnp.bfloat16)

    product, *rounded = pl.pallas_call(
        kernel,
        out_shape=[jax.ShapeDtypeStruct((2 * rows, columns), jnp.float32)]
        + [
            jax.ShapeDtypeStruct((span.stop - span.start, columns), jnp.bfloat16) for span in spans
        ],
        in_specs=whole_in_vmem(len(pieces) + 1),
        out_specs=whole_in_vmem(1 + len(spans)),
        scratch_shapes=[pltpu.VMEM((2 * rows, depth), jnp.bfloat16)],
        compiler_params=roomy(),
        name="project",
    )(*pieces, weight)
    return (product, rounded)


def join(partial, table, span, arrived, residual=None, gate=None):
    columns = partial[0].shape[1]
    step = math.gcd(columns, 256)
    slots = sorted(set(table))
    extras = [] if residual is None else [residual, gate]

    def kernel(*refs):
        own_refs, refs = (refs[: len(slots)], refs[len(slots) :])
        arrived_refs, refs = (refs[: len(arrived)], refs[len(arrived) :])
        out_ref = refs[-1]
        here = lax.axis_index("tm")
        for slot, own_ref in zip(slots, own_refs):

            @pl.when(pick([entry == slot for entry in table], here))
            def _(own_ref=own_ref):
                for start in range(0, columns, step):
                    part = slice(start, start + step)
                    total = own_ref[span, part]
                    for ref in arrived_refs:
                        total += ref[:, part].astype(jnp.float32)
                    if extras:
                        total = refs[0][span, part].astype(jnp.float32) + refs[1][:, part] * total
                    out_ref[:, part] = total.astype(jnp.bfloat16)

    operands = [partial[slot] for slot in slots] + list(arrived) + extras
    return pl.pallas_call(
        kernel,
        out_shape=jax.ShapeDtypeStruct((span.stop - span.start, columns), jnp.bfloat16),
        in_specs=whole_in_vmem(len(operands)),
        out_specs=whole_in_vmem(1)[0],
        compiler_params=roomy(),
        name="join",
    )(*operands)


def finish(spans, arrived, partial, below, gate, fresh_frame):
    rows, columns = partial.shape
    step = math.gcd(columns, 256)

    def kernel(*refs):
        arrived_refs, below_refs = (refs[: len(spans)], refs[len(spans) : 2 * len(spans)])
        partial_ref, gate_ref, fresh_ref, out_ref = refs[2 * len(spans) :]
        last = lax.axis_index("tm") == lax.axis_size("tm") - 1

        @pl.when(last)
        def _():
            out_ref[...] = fresh_ref[...]

        @pl.when(jnp.logical_not(last))
        def _():
            for span, arrived_ref, below_ref in zip(spans, arrived_refs, below_refs):
                for start in range(0, columns, step):
                    part = slice(start, start + step)
                    total = partial_ref[span, part] + below_ref[:, part].astype(jnp.float32)
                    total = arrived_ref[:, part].astype(jnp.float32) + gate_ref[:, part] * total
                    out_ref[span, part] = total.astype(jnp.bfloat16)

    return pl.pallas_call(
        kernel,
        out_shape=jax.ShapeDtypeStruct((rows, columns), jnp.bfloat16),
        in_specs=whole_in_vmem(2 * len(spans) + 3),
        out_specs=whole_in_vmem(1)[0],
        compiler_params=roomy(),
        name="finish",
    )(*arrived, *below, partial, gate, fresh_frame)


def line_schedule(frames):
    steps = []
    for step in range(frames - 1):
        down = {z: step + 1 - (frames - 1 - z) for z in range(1, frames)}
        up = {z: frames - 1 - step + z for z in range(frames)}
        down = {z: f for z, f in down.items() if 1 <= f <= z}
        up = {z: f for z, f in up.items() if z + 2 <= f < frames}
        steps.append((down, up))
    order = []
    for z in range(frames):
        sent = [f for down, up in steps for f in (down.get(z), up.get(z)) if f is not None]
        order.append((sent + [z + 1])[: frames - 1])
    return steps, order


def head_plan(
    queries, keys, values, residual, fresh_frame, out_weight, time_weight, noise_steps, frame_mask
):
    frames, across = (lax.axis_size("tm"), lax.axis_size("head"))
    pairs = across // 2
    width = queries.shape[2] // (frames * pairs)
    everywhere = range(frames)

    def swap(array, j):
        return lax.ppermute(array, "head", [(h, h ^ j) for h in range(across)])

    def gather(part):
        pieces = {0: part}
        bit = across // 2
        while bit:
            for j in list(pieces):
                pieces[j ^ bit] = swap(pieces[j], bit)
            bit //= 2
        return [pieces[j] for j in range(across)]

    query, own = pack(queries[0], keys[0], values[0], frames, pairs, width)
    query, frame_mask, noise_steps = lax.optimization_barrier((query, frame_mask, noise_steps))
    own = lax.all_to_all(own, ("tm", "head"), split_axis=0, concat_axis=0, tiled=True)
    query = lax.all_to_all(query, ("tm", "head"), split_axis=0, concat_axis=0, tiled=True)
    mate = swap(own, 1)
    masks = [frame_mask] + [
        lax.ppermute(frame_mask, "tm", [(z, z ^ a) for z in everywhere]) for a in everywhere[1:]
    ]
    noise = jnp.concatenate([noise_steps, shifted(noise_steps, "tm", -1)])
    gates = jnp.dot(
        time_features(noise), time_weight.astype(jnp.float32), precision=lax.Precision.HIGHEST
    )
    masks[0], gates = lax.optimization_barrier((masks[0], gates))

    steps, order = line_schedule(frames)
    rows = residual.shape[1]
    cuts = [rows // 2, rows]
    spans = [slice(first, last) for first, last in zip([0, *cuts], cuts)]
    partial, short = ([], [])
    for slot in range(frames - 1):
        part = attend([order[z][slot] for z in everywhere], masks, query, own, mate)
        product, rounded = project(gather(part), out_weight, cuts if slot == 0 else [])
        partial.append(product)
        short.append(rounded)

    above, below, payload = (None, None, short[0])
    for number, (down, up) in enumerate(steps):
        if number > 0:
            sends = {**down, **up}
            table = [order[z].index(sends[z]) if z in sends else 0 for z in everywhere]
            final = number == len(steps) - 1
            extras = (residual[0], gates[:1]) if final else ()
            payload = [
                join(partial, table, span, [above[i]] if final or above is below else [above[i], below[i]], *extras)
                for i, span in enumerate(spans)
            ]
        down_links, up_links = ([(z, z - 1) for z in down], [(z, z + 1) for z in up])
        if number == 0:
            above = [lax.ppermute(part, "tm", down_links + up_links) for part in payload]
            below = above
        else:
            above = [lax.ppermute(part, "tm", down_links) for part in payload]
            if up:
                below = [lax.ppermute(part, "tm", up_links) for part in payload]
    return finish(spans, above, partial[-1], below, gates[1:], fresh_frame)[None]


def power_of_two(number):
    return number & (number - 1) == 0


def suits_line(frames, window):
    apart = all(not set(down) & set(up) for down, up in line_schedule(frames)[0])
    return 2 < frames <= window and power_of_two(frames) and apart


def on_device(queries, *others):
    frames, across = (lax.axis_size("tm"), lax.axis_size("head"))
    heads = queries.shape[2] // HD
    even = across % 2 == 0 and power_of_two(across)
    even = even and queries.shape[1] % 32 == 0
    if even and suits_line(frames, others[-1].shape[1]) and heads % (frames * across // 2) == 0:
        return head_plan(queries, *others)
    return frame_plan(queries, *others)


def solution(mesh):
    placed = (
        P(("groups", "tm"), "head", None),
        P(("groups", "tm"), "head", None),
        P(("groups", "tm"), "head", None),
        P(("groups", "tm"), None, "head"),
        P("groups", "head"),
        P("tm", "head"),
        P(None, "head"),
        P(("groups", "tm")),
        P(("groups", "tm"), None),
    )
    return jax.shard_map(
        on_device,
        mesh=mesh,
        in_specs=placed,
        out_specs=P(("groups", "tm"), None, "head"),
        check_vma=False,
    )
```

```python
import math

import jax
import jax.numpy as jnp
import numpy as np
from jax import lax
from jax.experimental import pallas as pl
from jax.experimental.pallas import tpu as pltpu
from jax.sharding import PartitionSpec as P

HD = 128
FREQ = 256
STEPS = 50
VMEM_BYTES = 16 * 1024 * 1024
PACK_BYTES = 60 * 1024 * 1024


def shifted(value, axis, steps):
    count = lax.axis_size(axis)
    leading, last = (max(0, -steps), min(count, count - steps))
    return lax.ppermute(value, axis, [(source, source + steps) for source in range(leading, last)])


def time_features(noise_steps):
    timestep = 1000.0 * (noise_steps.astype(jnp.float32) + 1.0) / STEPS
    half = FREQ // 2
    rates = jnp.exp(-math.log(10000.0) * jnp.arange(half).astype(jnp.float32) / half)
    angles = timestep[:, None] * rates[None, :]
    return jnp.concatenate([jnp.cos(angles), jnp.sin(angles)], axis=1)


def frame_plan(
    queries, keys, values, residual, fresh_frame, out_weight, time_weight, noise_steps, frame_mask
):
    query_local, key_local, value_local = (
        lax.all_to_all(queries, "head", split_axis=2, concat_axis=1, tiled=True),
        lax.all_to_all(keys, "head", split_axis=2, concat_axis=1, tiled=True),
        lax.all_to_all(values, "head", split_axis=2, concat_axis=1, tiled=True),
    )
    tokens = query_local.shape[1]
    heads_here = query_local.shape[2] // HD
    scale = 1.0 / math.sqrt(HD)
    query_heads = query_local[0].reshape(tokens, heads_here, HD)
    key_value = jnp.stack([key_local[0], value_local[0]], axis=0)
    frame = lax.axis_index("tm")
    frames_total = lax.axis_size("tm")
    window = min(8, frames_total)
    mask_row = frame_mask[0]
    columns = jnp.arange(mask_row.shape[0], dtype=jnp.int32)

    def allowed_at(offset):
        hits = jnp.sum(jnp.where(columns == frame - offset, mask_row, 0))
        return hits > 0

    def absorb(state, block, allowed):
        running_max, weight_sum, accumulated = state
        key_heads = block[0].reshape(tokens, heads_here, HD)
        value_heads = block[1].reshape(tokens, heads_here, HD)
        scores = (
            jnp.einsum("qhd,khd->hqk", query_heads, key_heads, preferred_element_type=jnp.float32)
            * scale
        )
        new_max = jnp.where(allowed, jnp.maximum(running_max, jnp.max(scores, axis=2)), running_max)
        lifted = jnp.where(allowed, jnp.exp(jnp.minimum(scores - new_max[:, :, None], 0.0)), 0.0)
        factor = jnp.exp(running_max - new_max)
        weight_sum = weight_sum * factor + jnp.sum(lifted, axis=2)
        rounded = lifted.astype(jnp.bfloat16)
        accumulated = accumulated * jnp.transpose(factor)[:, :, None] + jnp.einsum(
            "hqk,khd->qhd", rounded, value_heads, preferred_element_type=jnp.float32
        )
        return (new_max, weight_sum, accumulated)

    state = (
        jnp.full((heads_here, tokens), -1e30, jnp.float32),
        jnp.zeros((heads_here, tokens), jnp.float32),
        jnp.zeros((tokens, heads_here, HD), jnp.float32),
    )
    state = absorb(state, key_value, allowed_at(0))
    moving = key_value
    for offset in range(1, window):
        moving = shifted(moving, "tm", 1)
        state = absorb(state, moving, allowed_at(offset))
    running_max, weight_sum, accumulated = state
    attention = (
        (accumulated / jnp.transpose(weight_sum)[:, :, None])
        .reshape(tokens, heads_here * HD)
        .astype(jnp.bfloat16)
    )
    weight_cols = lax.all_gather(out_weight, "tm", axis=0, tiled=True)
    projected = jnp.dot(
        lax.all_gather(attention, "head", axis=1, tiled=True),
        weight_cols,
        preferred_element_type=jnp.float32,
    )
    gate = jnp.dot(
        time_features(noise_steps), time_weight.astype(jnp.float32), precision=lax.Precision.HIGHEST
    )
    updated = (residual[0].astype(jnp.float32) + gate * projected).astype(jnp.bfloat16)
    moved = shifted(updated, "tm", -1)
    rolled = jnp.where(frame == frames_total - 1, fresh_frame, moved)
    return rolled[None]


def whole_in_vmem(count):
    return [pl.BlockSpec(memory_space=pltpu.VMEM)] * count


def in_hbm(count):
    return [pl.BlockSpec(memory_space=pltpu.HBM)] * count


def roomy():
    return pltpu.CompilerParams(vmem_limit_bytes=VMEM_BYTES)


def pack(queries, keys, values, moves, pairs, width):
    tokens = queries.shape[0]
    count = len(moves)

    def kernel(*refs):
        sources, pieces, (loaded, packed, in_sems, out_sems) = (
            refs[:3],
            refs[3 : 3 + count],
            refs[3 + count :],
        )
        frame, pair = (lax.axis_index("tm"), lax.axis_index("head") // 2)
        loads = [
            pltpu.make_async_copy(source, loaded.at[place], in_sems.at[place])
            for place, source in enumerate(sources)
        ]
        for load in loads:
            load.start()
        for load in loads:
            load.wait()
        stores = []
        for number, (a, b) in enumerate(moves):
            block = (frame ^ a) * pairs + (pair ^ b)
            columns = pl.ds(pl.multiple_of(block * width, HD), width)
            for place in range(3):
                packed[number, :, place * width : (place + 1) * width] = loaded[place, :, columns]
            store = pltpu.make_async_copy(packed.at[number], pieces[number], out_sems.at[number])
            store.start()
            stores.append(store)
        for store in stores:
            store.wait()

    return pl.pallas_call(
        kernel,
        out_shape=[jax.ShapeDtypeStruct((tokens, 3 * width), queries.dtype)] * count,
        in_specs=[pl.BlockSpec(memory_space=pltpu.HBM)] * 3,
        out_specs=[pl.BlockSpec(memory_space=pltpu.HBM)] * count,
        scratch_shapes=[
            pltpu.VMEM((3, *queries.shape), queries.dtype),
            pltpu.VMEM((count, tokens, 3 * width), queries.dtype),
            pltpu.SemaphoreType.DMA((3,)),
            pltpu.SemaphoreType.DMA((count,)),
        ],
        compiler_params=pltpu.CompilerParams(vmem_limit_bytes=PACK_BYTES),
        name="pack",
    )(queries, keys, values)


def pick(table, here):
    result = table[0]
    for place, entry in enumerate(table[1:], 1):
        result = jnp.where(here == place, entry, result)
    return result


def attend(notes, frames_of_slot, own, mate, moves, pairs, frames, width):
    lines = notes.shape[0] // frames
    tokens = own[0].shape[0]
    rows, keys_rows = (pairs * tokens, 2 * pairs * tokens)
    scale = 1.0 / math.sqrt(HD)

    def kernel(*refs):
        note_ref, refs = (refs[0], refs[1:])
        own_refs, refs = (refs[: len(moves)], refs[len(moves) :])
        mate_refs, refs = (refs[: len(moves)], refs[len(moves) :])
        out_ref, query_buf, key_buf, value_buf = refs
        here = lax.axis_index("tm")
        for own_ref, mate_ref, (a, b) in zip(own_refs, mate_refs, moves):
            query_buf[here ^ a, b * tokens : (b + 1) * tokens, :] = own_ref[:, :width]
            for side, ref in enumerate((own_ref, mate_ref)):
                span = slice((2 * b + side) * tokens, (2 * b + side + 1) * tokens)
                key_buf[a, span, :] = ref[:, width : 2 * width]
                value_buf[a, span, :] = ref[:, 2 * width :]
        frame = pick(frames_of_slot, here)
        allowed = [note_ref[frame * lines, here ^ a] for a in range(frames)]
        for start in range(0, width, HD):
            channels = slice(start, start + HD)
            query = query_buf[frame, :, channels]
            blocks = []
            for a in range(frames):
                scores = (
                    lax.dot_general(
                        query,
                        key_buf[a, :, channels],
                        (((1,), (1,)), ((), ())),
                        preferred_element_type=jnp.float32,
                    )
                    * scale
                )
                blocks.append(jnp.where(allowed[a] > 0, scores, -1e30))
            scores = jnp.concatenate(blocks, axis=1)
            lifted = jnp.exp(scores - jnp.max(scores, axis=1, keepdims=True))
            totals = jnp.sum(lifted, axis=1, keepdims=True)
            values = value_buf[:, :, channels].reshape(frames * keys_rows, HD)
            mixed = jnp.dot(
                lifted.astype(jnp.bfloat16), values, preferred_element_type=jnp.float32
            )
            out_ref[:, channels] = (mixed / totals).astype(jnp.bfloat16)

    kind = own[0].dtype
    return pl.pallas_call(
        kernel,
        out_shape=jax.ShapeDtypeStruct((rows, width), jnp.bfloat16),
        in_specs=[pl.BlockSpec(memory_space=pltpu.SMEM)] + whole_in_vmem(2 * len(moves)),
        out_specs=whole_in_vmem(1)[0],
        scratch_shapes=[
            pltpu.VMEM((frames, rows, width), kind),
            pltpu.VMEM((frames, keys_rows, width), kind),
            pltpu.VMEM((frames, keys_rows, width), kind),
        ],
        compiler_params=roomy(),
        name="attend",
    )(notes, *own, *mate)


def project(pieces, weight, pairs, cuts):
    rows, width = pieces[0].shape
    tokens = rows // pairs
    depth, columns = weight.shape
    step = math.gcd(columns, 256)
    spans = [slice(first, last) for first, last in zip([0, *cuts], cuts)]

    def kernel(*refs):
        piece_refs, (weight_ref, out_ref, *short_refs, whole) = (
            refs[: len(pieces)],
            refs[len(pieces) :],
        )
        here = lax.axis_index("head")
        for j, ref in enumerate(piece_refs):
            source = here ^ j
            pair, core = (source // 2, source % 2)
            channels = pl.ds(pl.multiple_of(pair * width, HD), width)
            for b in range(pairs):
                first = ((pair ^ b) * 2 + core) * tokens
                whole[pl.ds(pl.multiple_of(first, 16), tokens), channels] = ref[
                    b * tokens : (b + 1) * tokens, :
                ]
        for start in range(0, columns, step):
            product = jnp.dot(
                whole[...], weight_ref[:, start : start + step], preferred_element_type=jnp.float32
            )
            out_ref[:, start : start + step] = product
            for span, short_ref in zip(spans, short_refs):
                short_ref[:, start : start + step] = product[span, :].astype(jnp.bfloat16)

    product, *rounded = pl.pallas_call(
        kernel,
        out_shape=[jax.ShapeDtypeStruct((2 * rows, columns), jnp.float32)]
        + [
            jax.ShapeDtypeStruct((span.stop - span.start, columns), jnp.bfloat16) for span in spans
        ],
        in_specs=whole_in_vmem(len(pieces) + 1),
        out_specs=whole_in_vmem(1 + len(spans)),
        scratch_shapes=[pltpu.VMEM((2 * rows, depth), jnp.bfloat16)],
        compiler_params=roomy(),
        name="project",
    )(*pieces, weight)
    return (product, rounded)


def join(partial, table, span, arrived, residual=None, gate=None):
    columns = partial[0].shape[1]
    step = math.gcd(columns, 256)
    slots = sorted(set(table))
    extras = [] if residual is None else [residual, gate]

    def kernel(*refs):
        own_refs, refs = (refs[: len(slots)], refs[len(slots) :])
        arrived_refs, refs = (refs[: len(arrived)], refs[len(arrived) :])
        out_ref = refs[-1]
        here = lax.axis_index("tm")
        for slot, own_ref in zip(slots, own_refs):

            @pl.when(pick([entry == slot for entry in table], here))
            def _(own_ref=own_ref):
                for start in range(0, columns, step):
                    part = slice(start, start + step)
                    total = own_ref[span, part]
                    for ref in arrived_refs:
                        total += ref[:, part].astype(jnp.float32)
                    if extras:
                        total = refs[0][span, part].astype(jnp.float32) + refs[1][:, part] * total
                    out_ref[:, part] = total.astype(jnp.bfloat16)

    operands = [partial[slot] for slot in slots] + list(arrived) + extras
    return pl.pallas_call(
        kernel,
        out_shape=jax.ShapeDtypeStruct((span.stop - span.start, columns), jnp.bfloat16),
        in_specs=whole_in_vmem(len(operands)),
        out_specs=whole_in_vmem(1)[0],
        compiler_params=roomy(),
        name="join",
    )(*operands)


def finish(spans, arrived, partial, below, gate, fresh_frame):
    rows, columns = partial.shape
    step = math.gcd(columns, 256)

    def kernel(*refs):
        arrived_refs, below_refs = (refs[: len(spans)], refs[len(spans) : 2 * len(spans)])
        partial_ref, gate_ref, fresh_ref, out_ref = refs[2 * len(spans) :]
        last = lax.axis_index("tm") == lax.axis_size("tm") - 1

        @pl.when(last)
        def _():
            out_ref[...] = fresh_ref[...]

        @pl.when(jnp.logical_not(last))
        def _():
            for span, arrived_ref, below_ref in zip(spans, arrived_refs, below_refs):
                for start in range(0, columns, step):
                    part = slice(start, start + step)
                    total = partial_ref[span, part] + below_ref[:, part].astype(jnp.float32)
                    total = arrived_ref[:, part].astype(jnp.float32) + gate_ref[:, part] * total
                    out_ref[span, part] = total.astype(jnp.bfloat16)

    return pl.pallas_call(
        kernel,
        out_shape=jax.ShapeDtypeStruct((rows, columns), jnp.bfloat16),
        in_specs=whole_in_vmem(2 * len(spans) + 3),
        out_specs=whole_in_vmem(1)[0],
        compiler_params=roomy(),
        name="finish",
    )(*arrived, *below, partial, gate, fresh_frame)


def line_schedule(frames):
    steps = []
    for step in range(frames - 1):
        down = {z: step + 1 - (frames - 1 - z) for z in range(1, frames)}
        up = {z: frames - 1 - step + z for z in range(frames)}
        down = {z: f for z, f in down.items() if 1 <= f <= z}
        up = {z: f for z, f in up.items() if z + 2 <= f < frames}
        steps.append((down, up))
    order = []
    for z in range(frames):
        sent = [f for down, up in steps for f in (down.get(z), up.get(z)) if f is not None]
        order.append((sent + [z + 1])[: frames - 1])
    return steps, order


def head_plan(
    queries, keys, values, residual, fresh_frame, out_weight, time_weight, noise_steps, frame_mask
):
    frames, across = (lax.axis_size("tm"), lax.axis_size("head"))
    pairs = across // 2
    width = queries.shape[2] // (frames * pairs)
    everywhere = range(frames)

    def swap(array, j):
        return lax.ppermute(array, "head", [(h, h ^ j) for h in range(across)])

    def gather(part):
        pieces = {0: part}
        bit = across // 2
        while bit:
            for j in list(pieces):
                pieces[j ^ bit] = swap(pieces[j], bit)
            bit //= 2
        return [pieces[j] for j in range(across)]

    far = [(a, b) for b in range(pairs) for a in reversed(everywhere[2:])]
    near = [(0, b) for b in range(pairs)] + [(1, b) for b in range(pairs)]
    moves = near[:-1] + far + near[-1:]
    packed = pack(queries[0], keys[0], values[0], moves, pairs, width)
    own = []
    for piece, (a, b) in zip(packed, moves):
        if (a, b) != (0, 0):
            links = [
                (z * across + h, (z ^ a) * across + (h ^ (2 * b)))
                for z in everywhere
                for h in range(across)
            ]
            piece = lax.ppermute(piece, ("tm", "head"), links)
        own.append(piece)
    mate = [swap(piece, 1) for piece in own]
    note = jnp.concatenate([frame_mask[0], noise_steps])
    note = jnp.pad(note[None], ((0, 7), (0, HD - note.shape[0])))
    notes = lax.all_gather(note, "tm", axis=0, tiled=True)
    here = lax.axis_index("tm")
    following = jnp.minimum(here + 1, frames - 1) * note.shape[0]
    noise = jnp.concatenate([noise_steps, lax.dynamic_slice(notes[:, frame_mask.shape[1]], (following,), (1,))])
    gates = jnp.dot(
        time_features(noise), time_weight.astype(jnp.float32), precision=lax.Precision.HIGHEST
    )
    notes, gates = lax.optimization_barrier((notes, gates))

    steps, order = line_schedule(frames)
    rows = residual.shape[1]
    cuts = [rows // 2, rows]
    spans = [slice(first, last) for first, last in zip([0, *cuts], cuts)]
    partial, short = ([], [])
    for slot in range(frames - 1):
        part = attend(
            notes, [order[z][slot] for z in everywhere], own, mate, moves, pairs, frames, width
        )
        product, rounded = project(gather(part), out_weight, pairs, cuts if slot == 0 else [])
        partial.append(product)
        short.append(rounded)

    above, below, payload = (None, None, short[0])
    for number, (down, up) in enumerate(steps):
        if number > 0:
            sends = {**down, **up}
            table = [order[z].index(sends[z]) if z in sends else 0 for z in everywhere]
            final = number == len(steps) - 1
            extras = (residual[0], gates[:1]) if final else ()
            payload = [
                join(partial, table, span, [above[i]] if final or above is below else [above[i], below[i]], *extras)
                for i, span in enumerate(spans)
            ]
        down_links, up_links = ([(z, z - 1) for z in down], [(z, z + 1) for z in up])
        if number == 0:
            above = [lax.ppermute(part, "tm", down_links + up_links) for part in payload]
            below = above
        else:
            above = [lax.ppermute(part, "tm", down_links) for part in payload]
            if up:
                below = [lax.ppermute(part, "tm", up_links) for part in payload]
    return finish(spans, above, partial[-1], below, gates[1:], fresh_frame)[None]


def power_of_two(number):
    return number & (number - 1) == 0


def suits_line(frames, window):
    apart = all(not set(down) & set(up) for down, up in line_schedule(frames)[0])
    return 2 < frames <= window and power_of_two(frames) and apart


def on_device(queries, *others):
    frames, across = (lax.axis_size("tm"), lax.axis_size("head"))
    heads = queries.shape[2] // HD
    even = across % 2 == 0 and power_of_two(across)
    even = even and queries.shape[1] % 16 == 0
    if even and suits_line(frames, others[-1].shape[1]) and heads % (frames * across // 2) == 0:
        return head_plan(queries, *others)
    return frame_plan(queries, *others)


def solution(mesh):
    placed = (
        P(("groups", "tm"), "head", None),
        P(("groups", "tm"), "head", None),
        P(("groups", "tm"), "head", None),
        P(("groups", "tm"), None, "head"),
        P("groups", "head"),
        P("tm", "head"),
        P(None, "head"),
        P(("groups", "tm")),
        P(("groups", "tm"), None),
    )
    return jax.shard_map(
        on_device,
        mesh=mesh,
        in_specs=placed,
        out_specs=P(("groups", "tm"), None, "head"),
        check_vma=False,
    )
```

```python
import math

import jax
import jax.numpy as jnp
import numpy as np
from jax import lax
from jax.experimental import pallas as pl
from jax.experimental.pallas import tpu as pltpu
from jax.sharding import PartitionSpec as P

HD = 128
FREQ = 256
STEPS = 50
VMEM_BYTES = 16 * 1024 * 1024
PACK_BYTES = 60 * 1024 * 1024


def shifted(value, axis, steps):
    count = lax.axis_size(axis)
    leading, last = (max(0, -steps), min(count, count - steps))
    return lax.ppermute(value, axis, [(source, source + steps) for source in range(leading, last)])


def time_features(noise_steps):
    timestep = 1000.0 * (noise_steps.astype(jnp.float32) + 1.0) / STEPS
    half = FREQ // 2
    rates = jnp.exp(-math.log(10000.0) * jnp.arange(half).astype(jnp.float32) / half)
    angles = timestep[:, None] * rates[None, :]
    return jnp.concatenate([jnp.cos(angles), jnp.sin(angles)], axis=1)


def frame_plan(
    queries, keys, values, residual, fresh_frame, out_weight, time_weight, noise_steps, frame_mask
):
    query_local, key_local, value_local = (
        lax.all_to_all(queries, "head", split_axis=2, concat_axis=1, tiled=True),
        lax.all_to_all(keys, "head", split_axis=2, concat_axis=1, tiled=True),
        lax.all_to_all(values, "head", split_axis=2, concat_axis=1, tiled=True),
    )
    tokens = query_local.shape[1]
    heads_here = query_local.shape[2] // HD
    scale = 1.0 / math.sqrt(HD)
    query_heads = query_local[0].reshape(tokens, heads_here, HD)
    key_value = jnp.stack([key_local[0], value_local[0]], axis=0)
    frame = lax.axis_index("tm")
    frames_total = lax.axis_size("tm")
    window = min(8, frames_total)
    mask_row = frame_mask[0]
    columns = jnp.arange(mask_row.shape[0], dtype=jnp.int32)

    def allowed_at(offset):
        hits = jnp.sum(jnp.where(columns == frame - offset, mask_row, 0))
        return hits > 0

    def absorb(state, block, allowed):
        running_max, weight_sum, accumulated = state
        key_heads = block[0].reshape(tokens, heads_here, HD)
        value_heads = block[1].reshape(tokens, heads_here, HD)
        scores = (
            jnp.einsum("qhd,khd->hqk", query_heads, key_heads, preferred_element_type=jnp.float32)
            * scale
        )
        new_max = jnp.where(allowed, jnp.maximum(running_max, jnp.max(scores, axis=2)), running_max)
        lifted = jnp.where(allowed, jnp.exp(jnp.minimum(scores - new_max[:, :, None], 0.0)), 0.0)
        factor = jnp.exp(running_max - new_max)
        weight_sum = weight_sum * factor + jnp.sum(lifted, axis=2)
        rounded = lifted.astype(jnp.bfloat16)
        accumulated = accumulated * jnp.transpose(factor)[:, :, None] + jnp.einsum(
            "hqk,khd->qhd", rounded, value_heads, preferred_element_type=jnp.float32
        )
        return (new_max, weight_sum, accumulated)

    state = (
        jnp.full((heads_here, tokens), -1e30, jnp.float32),
        jnp.zeros((heads_here, tokens), jnp.float32),
        jnp.zeros((tokens, heads_here, HD), jnp.float32),
    )
    state = absorb(state, key_value, allowed_at(0))
    moving = key_value
    for offset in range(1, window):
        moving = shifted(moving, "tm", 1)
        state = absorb(state, moving, allowed_at(offset))
    running_max, weight_sum, accumulated = state
    attention = (
        (accumulated / jnp.transpose(weight_sum)[:, :, None])
        .reshape(tokens, heads_here * HD)
        .astype(jnp.bfloat16)
    )
    weight_cols = lax.all_gather(out_weight, "tm", axis=0, tiled=True)
    projected = jnp.dot(
        lax.all_gather(attention, "head", axis=1, tiled=True),
        weight_cols,
        preferred_element_type=jnp.float32,
    )
    gate = jnp.dot(
        time_features(noise_steps), time_weight.astype(jnp.float32), precision=lax.Precision.HIGHEST
    )
    updated = (residual[0].astype(jnp.float32) + gate * projected).astype(jnp.bfloat16)
    moved = shifted(updated, "tm", -1)
    rolled = jnp.where(frame == frames_total - 1, fresh_frame, moved)
    return rolled[None]


def whole_in_vmem(count):
    return [pl.BlockSpec(memory_space=pltpu.VMEM)] * count


def in_hbm(count):
    return [pl.BlockSpec(memory_space=pltpu.HBM)] * count


def roomy():
    return pltpu.CompilerParams(vmem_limit_bytes=VMEM_BYTES)


def pack(queries, keys, values, frame_mask, noise_steps, moves, pairs, width):
    tokens = queries.shape[0]
    window = frame_mask.shape[1]
    widths = [3 * width + (HD if b == 0 else 0) for a, b in moves]
    count = len(moves)

    def kernel(*refs):
        sources, small, pieces, scratch = (refs[:3], refs[3:5], refs[5 : 5 + count], refs[5 + count :])
        loaded, packed, mask_ref, noise_ref, in_sems, out_sems = scratch
        frame, pair = (lax.axis_index("tm"), lax.axis_index("head") // 2)
        targets = [loaded.at[place] for place in range(3)] + [mask_ref, noise_ref]
        loads = [
            pltpu.make_async_copy(source, target, in_sems.at[place])
            for place, (source, target) in enumerate(zip((*sources, *small), targets))
        ]
        for load in loads:
            load.start()
        for load in loads:
            load.wait()
        lane = lax.broadcasted_iota(jnp.int32, (tokens, HD), 1)
        note = jnp.where(lane == window, noise_ref[0], 0)
        for column in range(window):
            note = jnp.where(lane == column, mask_ref[0, column], note)
        note = note.astype(jnp.float32).astype(queries.dtype)
        stores = []
        for number, (a, b) in enumerate(moves):
            block = (frame ^ a) * pairs + (pair ^ b)
            columns = pl.ds(pl.multiple_of(block * width, HD), width)
            for place in range(3):
                packed[number, :, place * width : (place + 1) * width] = loaded[place, :, columns]
            if b == 0:
                packed[number, :, 3 * width :] = note
            store = pltpu.make_async_copy(
                packed.at[number, :, : widths[number]], pieces[number], out_sems.at[number]
            )
            store.start()
            stores.append(store)
        for store in stores:
            store.wait()

    return pl.pallas_call(
        kernel,
        out_shape=[jax.ShapeDtypeStruct((tokens, size), queries.dtype) for size in widths],
        in_specs=in_hbm(5),
        out_specs=in_hbm(count),
        scratch_shapes=[
            pltpu.VMEM((3, *queries.shape), queries.dtype),
            pltpu.VMEM((count, tokens, 3 * width + HD), queries.dtype),
            pltpu.SMEM(frame_mask.shape, frame_mask.dtype),
            pltpu.SMEM(noise_steps.shape, noise_steps.dtype),
            pltpu.SemaphoreType.DMA((5,)),
            pltpu.SemaphoreType.DMA((count,)),
        ],
        compiler_params=pltpu.CompilerParams(vmem_limit_bytes=PACK_BYTES),
        name="pack",
    )(queries, keys, values, frame_mask, noise_steps)


def pick(table, here):
    result = table[0]
    for place, entry in enumerate(table[1:], 1):
        result = jnp.where(here == place, entry, result)
    return result


def attend(frames_of_slot, own, mate, moves, pairs, frames, width):
    tokens = own[0].shape[0]
    rows, keys_rows = (pairs * tokens, 2 * pairs * tokens)
    scale = 1.0 / math.sqrt(HD)

    def kernel(*refs):
        own_refs, refs = (refs[: len(moves)], refs[len(moves) :])
        mate_refs, refs = (refs[: len(moves)], refs[len(moves) :])
        out_ref, query_buf, key_buf, value_buf, note_buf = refs
        here = lax.axis_index("tm")
        frame = pick(frames_of_slot, here)
        for own_ref, mate_ref, (a, b) in zip(own_refs, mate_refs, moves):
            query_buf[here ^ a, b * tokens : (b + 1) * tokens, :] = own_ref[:, :width]
            for side, ref in enumerate((own_ref, mate_ref)):
                span = slice((2 * b + side) * tokens, (2 * b + side + 1) * tokens)
                key_buf[a, span, :] = ref[:, width : 2 * width]
                value_buf[a, span, :] = ref[:, 2 * width : 3 * width]
            if b == 0:

                @pl.when(here ^ a == frame)
                def _(own_ref=own_ref):
                    note_buf[...] = own_ref[:16, 3 * width :].astype(jnp.float32)

        note = note_buf[:1, :]
        lane = lax.broadcasted_iota(jnp.int32, note.shape, 1)
        allowed = [
            jnp.sum(jnp.where(lane == here ^ a, note, 0.0), axis=1, keepdims=True) > 0.5
            for a in range(frames)
        ]
        for start in range(0, width, HD):
            channels = slice(start, start + HD)
            query = query_buf[frame, :, channels]
            blocks = []
            for a in range(frames):
                scores = (
                    lax.dot_general(
                        query,
                        key_buf[a, :, channels],
                        (((1,), (1,)), ((), ())),
                        preferred_element_type=jnp.float32,
                    )
                    * scale
                )
                blocks.append(jnp.where(allowed[a], scores, -1e30))
            scores = jnp.concatenate(blocks, axis=1)
            lifted = jnp.exp(scores - jnp.max(scores, axis=1, keepdims=True))
            totals = jnp.sum(lifted, axis=1, keepdims=True)
            values = value_buf[:, :, channels].reshape(frames * keys_rows, HD)
            mixed = jnp.dot(
                lifted.astype(jnp.bfloat16), values, preferred_element_type=jnp.float32
            )
            out_ref[:, channels] = (mixed / totals).astype(jnp.bfloat16)

    kind = own[0].dtype
    return pl.pallas_call(
        kernel,
        out_shape=jax.ShapeDtypeStruct((rows, width), jnp.bfloat16),
        in_specs=whole_in_vmem(2 * len(moves)),
        out_specs=whole_in_vmem(1)[0],
        scratch_shapes=[
            pltpu.VMEM((frames, rows, width), kind),
            pltpu.VMEM((frames, keys_rows, width), kind),
            pltpu.VMEM((frames, keys_rows, width), kind),
            pltpu.VMEM((16, HD), jnp.float32),
        ],
        compiler_params=roomy(),
        name="attend",
    )(*own, *mate)


def project(pieces, weight, pairs, cuts):
    rows, width = pieces[0].shape
    tokens = rows // pairs
    depth, columns = weight.shape
    step = math.gcd(columns, 256)
    spans = [slice(first, last) for first, last in zip([0, *cuts], cuts)]

    def kernel(*refs):
        piece_refs, (weight_ref, out_ref, *short_refs, whole) = (
            refs[: len(pieces)],
            refs[len(pieces) :],
        )
        here = lax.axis_index("head")
        for j, ref in enumerate(piece_refs):
            source = here ^ j
            pair, core = (source // 2, source % 2)
            channels = pl.ds(pl.multiple_of(pair * width, HD), width)
            for b in range(pairs):
                first = ((pair ^ b) * 2 + core) * tokens
                whole[pl.ds(pl.multiple_of(first, 16), tokens), channels] = ref[
                    b * tokens : (b + 1) * tokens, :
                ]
        for start in range(0, columns, step):
            product = jnp.dot(
                whole[...], weight_ref[:, start : start + step], preferred_element_type=jnp.float32
            )
            out_ref[:, start : start + step] = product
            for span, short_ref in zip(spans, short_refs):
                short_ref[:, start : start + step] = product[span, :].astype(jnp.bfloat16)

    product, *rounded = pl.pallas_call(
        kernel,
        out_shape=[jax.ShapeDtypeStruct((2 * rows, columns), jnp.float32)]
        + [
            jax.ShapeDtypeStruct((span.stop - span.start, columns), jnp.bfloat16) for span in spans
        ],
        in_specs=whole_in_vmem(len(pieces) + 1),
        out_specs=whole_in_vmem(1 + len(spans)),
        scratch_shapes=[pltpu.VMEM((2 * rows, depth), jnp.bfloat16)],
        compiler_params=roomy(),
        name="project",
    )(*pieces, weight)
    return (product, rounded)


def join(partial, table, span, arrived, residual=None, gate=None):
    columns = partial[0].shape[1]
    step = math.gcd(columns, 256)
    slots = sorted(set(table))
    extras = [] if residual is None else [residual, gate]

    def kernel(*refs):
        own_refs, refs = (refs[: len(slots)], refs[len(slots) :])
        arrived_refs, refs = (refs[: len(arrived)], refs[len(arrived) :])
        out_ref = refs[-1]
        here = lax.axis_index("tm")
        for slot, own_ref in zip(slots, own_refs):

            @pl.when(pick([entry == slot for entry in table], here))
            def _(own_ref=own_ref):
                for start in range(0, columns, step):
                    part = slice(start, start + step)
                    total = own_ref[span, part]
                    for ref in arrived_refs:
                        total += ref[:, part].astype(jnp.float32)
                    if extras:
                        total = refs[0][span, part].astype(jnp.float32) + refs[1][:, part] * total
                    out_ref[:, part] = total.astype(jnp.bfloat16)

    operands = [partial[slot] for slot in slots] + list(arrived) + extras
    return pl.pallas_call(
        kernel,
        out_shape=jax.ShapeDtypeStruct((span.stop - span.start, columns), jnp.bfloat16),
        in_specs=whole_in_vmem(len(operands)),
        out_specs=whole_in_vmem(1)[0],
        compiler_params=roomy(),
        name="join",
    )(*operands)


def finish(spans, arrived, partial, below, gate, fresh_frame):
    rows, columns = partial.shape
    step = math.gcd(columns, 256)

    def kernel(*refs):
        arrived_refs, below_refs = (refs[: len(spans)], refs[len(spans) : 2 * len(spans)])
        partial_ref, gate_ref, fresh_ref, out_ref = refs[2 * len(spans) :]
        last = lax.axis_index("tm") == lax.axis_size("tm") - 1

        @pl.when(last)
        def _():
            out_ref[...] = fresh_ref[...]

        @pl.when(jnp.logical_not(last))
        def _():
            for span, arrived_ref, below_ref in zip(spans, arrived_refs, below_refs):
                for start in range(0, columns, step):
                    part = slice(start, start + step)
                    total = partial_ref[span, part] + below_ref[:, part].astype(jnp.float32)
                    total = arrived_ref[:, part].astype(jnp.float32) + gate_ref[:, part] * total
                    out_ref[span, part] = total.astype(jnp.bfloat16)

    return pl.pallas_call(
        kernel,
        out_shape=jax.ShapeDtypeStruct((rows, columns), jnp.bfloat16),
        in_specs=whole_in_vmem(2 * len(spans) + 3),
        out_specs=whole_in_vmem(1)[0],
        compiler_params=roomy(),
        name="finish",
    )(*arrived, *below, partial, gate, fresh_frame)


def line_schedule(frames):
    steps = []
    for step in range(frames - 1):
        down = {z: step + 1 - (frames - 1 - z) for z in range(1, frames)}
        up = {z: frames - 1 - step + z for z in range(frames)}
        down = {z: f for z, f in down.items() if 1 <= f <= z}
        up = {z: f for z, f in up.items() if z + 2 <= f < frames}
        steps.append((down, up))
    order = []
    for z in range(frames):
        sent = [f for down, up in steps for f in (down.get(z), up.get(z)) if f is not None]
        order.append((sent + [z + 1])[: frames - 1])
    return steps, order


def head_plan(
    queries, keys, values, residual, fresh_frame, out_weight, time_weight, noise_steps, frame_mask
):
    frames, across = (lax.axis_size("tm"), lax.axis_size("head"))
    pairs = across // 2
    width = queries.shape[2] // (frames * pairs)
    everywhere = range(frames)

    def swap(array, j):
        return lax.ppermute(array, "head", [(h, h ^ j) for h in range(across)])

    def gather(part):
        pieces = {0: part}
        bit = across // 2
        while bit:
            for j in list(pieces):
                pieces[j ^ bit] = swap(pieces[j], bit)
            bit //= 2
        return [pieces[j] for j in range(across)]

    far = [(a, b) for b in range(pairs) for a in reversed(everywhere[2:])]
    near = [(0, b) for b in range(pairs)] + [(1, b) for b in range(pairs)]
    moves = near[:-1] + far + near[-1:]
    packed = pack(
        queries[0], keys[0], values[0], frame_mask, noise_steps, moves, pairs, width
    )
    own = []
    for piece, (a, b) in zip(packed, moves):
        if (a, b) != (0, 0):
            links = [
                (z * across + h, (z ^ a) * across + (h ^ (2 * b)))
                for z in everywhere
                for h in range(across)
            ]
            piece = lax.ppermute(piece, ("tm", "head"), links)
        own.append(piece)
    mate = [swap(piece, 1) for piece in own]
    here = lax.axis_index("tm")
    notes = dict(zip(moves, own))
    notes = jnp.stack([notes[a, 0][0, 3 * width + frame_mask.shape[1]] for a in everywhere])
    across_to = here ^ jnp.minimum(here + 1, frames - 1)
    noise = jnp.concatenate([noise_steps.astype(notes.dtype), lax.dynamic_slice(notes, (across_to,), (1,))])

    steps, order = line_schedule(frames)
    rows = residual.shape[1]
    cuts = [rows // 2, rows]
    spans = [slice(first, last) for first, last in zip([0, *cuts], cuts)]
    partial, short = ([], [])
    for slot in range(frames - 1):
        part = attend(
            [order[z][slot] for z in everywhere], own, mate, moves, pairs, frames, width
        )
        if slot == 1:
            gates = jnp.dot(
                time_features(noise),
                time_weight.astype(jnp.float32),
                precision=lax.Precision.HIGHEST,
            )
            part, gates = lax.optimization_barrier((part, gates))
        product, rounded = project(gather(part), out_weight, pairs, cuts if slot == 0 else [])
        partial.append(product)
        short.append(rounded)

    above, below, payload = (None, None, short[0])
    for number, (down, up) in enumerate(steps):
        if number > 0:
            sends = {**down, **up}
            table = [order[z].index(sends[z]) if z in sends else 0 for z in everywhere]
            final = number == len(steps) - 1
            extras = (residual[0], gates[:1]) if final else ()
            payload = [
                join(partial, table, span, [above[i]] if final or above is below else [above[i], below[i]], *extras)
                for i, span in enumerate(spans)
            ]
        down_links, up_links = ([(z, z - 1) for z in down], [(z, z + 1) for z in up])
        if number == 0:
            above = [lax.ppermute(part, "tm", down_links + up_links) for part in payload]
            below = above
        else:
            above = [lax.ppermute(part, "tm", down_links) for part in payload]
            if up:
                below = [lax.ppermute(part, "tm", up_links) for part in payload]
    return finish(spans, above, partial[-1], below, gates[1:], fresh_frame)[None]


def power_of_two(number):
    return number & (number - 1) == 0


def suits_line(frames, window):
    apart = all(not set(down) & set(up) for down, up in line_schedule(frames)[0])
    return 2 < frames <= window and power_of_two(frames) and apart


def on_device(queries, *others):
    frames, across = (lax.axis_size("tm"), lax.axis_size("head"))
    heads = queries.shape[2] // HD
    even = across % 2 == 0 and power_of_two(across)
    even = even and queries.shape[1] % 16 == 0
    if even and suits_line(frames, others[-1].shape[1]) and heads % (frames * across // 2) == 0:
        return head_plan(queries, *others)
    return frame_plan(queries, *others)


def solution(mesh):
    placed = (
        P(("groups", "tm"), "head", None),
        P(("groups", "tm"), "head", None),
        P(("groups", "tm"), "head", None),
        P(("groups", "tm"), None, "head"),
        P("groups", "head"),
        P("tm", "head"),
        P(None, "head"),
        P(("groups", "tm")),
        P(("groups", "tm"), None),
    )
    return jax.shard_map(
        on_device,
        mesh=mesh,
        in_specs=placed,
        out_specs=P(("groups", "tm"), None, "head"),
        check_vma=False,
    )
```

```python
import math

import jax
import jax.numpy as jnp
import numpy as np
from jax import lax
from jax.experimental import pallas as pl
from jax.experimental.pallas import tpu as pltpu
from jax.sharding import PartitionSpec as P

HD = 128
FREQ = 256
STEPS = 50
VMEM_BYTES = 16 * 1024 * 1024
PACK_BYTES = 60 * 1024 * 1024


def shifted(value, axis, steps):
    count = lax.axis_size(axis)
    leading, last = (max(0, -steps), min(count, count - steps))
    return lax.ppermute(value, axis, [(source, source + steps) for source in range(leading, last)])


def time_features(noise_steps):
    timestep = 1000.0 * (noise_steps.astype(jnp.float32) + 1.0) / STEPS
    half = FREQ // 2
    rates = jnp.exp(-math.log(10000.0) * jnp.arange(half).astype(jnp.float32) / half)
    angles = timestep[:, None] * rates[None, :]
    return jnp.concatenate([jnp.cos(angles), jnp.sin(angles)], axis=1)


def frame_plan(
    queries, keys, values, residual, fresh_frame, out_weight, time_weight, noise_steps, frame_mask
):
    query_local, key_local, value_local = (
        lax.all_to_all(queries, "head", split_axis=2, concat_axis=1, tiled=True),
        lax.all_to_all(keys, "head", split_axis=2, concat_axis=1, tiled=True),
        lax.all_to_all(values, "head", split_axis=2, concat_axis=1, tiled=True),
    )
    tokens = query_local.shape[1]
    heads_here = query_local.shape[2] // HD
    scale = 1.0 / math.sqrt(HD)
    query_heads = query_local[0].reshape(tokens, heads_here, HD)
    key_value = jnp.stack([key_local[0], value_local[0]], axis=0)
    frame = lax.axis_index("tm")
    frames_total = lax.axis_size("tm")
    window = min(8, frames_total)
    mask_row = frame_mask[0]
    columns = jnp.arange(mask_row.shape[0], dtype=jnp.int32)

    def allowed_at(offset):
        hits = jnp.sum(jnp.where(columns == frame - offset, mask_row, 0))
        return hits > 0

    def absorb(state, block, allowed):
        running_max, weight_sum, accumulated = state
        key_heads = block[0].reshape(tokens, heads_here, HD)
        value_heads = block[1].reshape(tokens, heads_here, HD)
        scores = (
            jnp.einsum("qhd,khd->hqk", query_heads, key_heads, preferred_element_type=jnp.float32)
            * scale
        )
        new_max = jnp.where(allowed, jnp.maximum(running_max, jnp.max(scores, axis=2)), running_max)
        lifted = jnp.where(allowed, jnp.exp(jnp.minimum(scores - new_max[:, :, None], 0.0)), 0.0)
        factor = jnp.exp(running_max - new_max)
        weight_sum = weight_sum * factor + jnp.sum(lifted, axis=2)
        rounded = lifted.astype(jnp.bfloat16)
        accumulated = accumulated * jnp.transpose(factor)[:, :, None] + jnp.einsum(
            "hqk,khd->qhd", rounded, value_heads, preferred_element_type=jnp.float32
        )
        return (new_max, weight_sum, accumulated)

    state = (
        jnp.full((heads_here, tokens), -1e30, jnp.float32),
        jnp.zeros((heads_here, tokens), jnp.float32),
        jnp.zeros((tokens, heads_here, HD), jnp.float32),
    )
    state = absorb(state, key_value, allowed_at(0))
    moving = key_value
    for offset in range(1, window):
        moving = shifted(moving, "tm", 1)
        state = absorb(state, moving, allowed_at(offset))
    running_max, weight_sum, accumulated = state
    attention = (
        (accumulated / jnp.transpose(weight_sum)[:, :, None])
        .reshape(tokens, heads_here * HD)
        .astype(jnp.bfloat16)
    )
    weight_cols = lax.all_gather(out_weight, "tm", axis=0, tiled=True)
    projected = jnp.dot(
        lax.all_gather(attention, "head", axis=1, tiled=True),
        weight_cols,
        preferred_element_type=jnp.float32,
    )
    gate = jnp.dot(
        time_features(noise_steps), time_weight.astype(jnp.float32), precision=lax.Precision.HIGHEST
    )
    updated = (residual[0].astype(jnp.float32) + gate * projected).astype(jnp.bfloat16)
    moved = shifted(updated, "tm", -1)
    rolled = jnp.where(frame == frames_total - 1, fresh_frame, moved)
    return rolled[None]


def whole_in_vmem(count):
    return [pl.BlockSpec(memory_space=pltpu.VMEM)] * count


def in_hbm(count):
    return [pl.BlockSpec(memory_space=pltpu.HBM)] * count


def roomy():
    return pltpu.CompilerParams(vmem_limit_bytes=VMEM_BYTES)


def pack(queries, keys, values, frame_mask, noise_steps, moves, pairs, width):
    tokens = queries.shape[0]
    window = frame_mask.shape[1]
    widths = [3 * width + (HD if b == 0 else 0) for a, b in moves]
    count = len(moves)

    def kernel(*refs):
        sources, small, pieces, scratch = (refs[:3], refs[3:5], refs[5 : 5 + count], refs[5 + count :])
        loaded, packed, mask_ref, noise_ref, in_sems, out_sems = scratch
        frame, pair = (lax.axis_index("tm"), lax.axis_index("head") // 2)
        targets = [loaded.at[place] for place in range(3)] + [mask_ref, noise_ref]
        loads = [
            pltpu.make_async_copy(source, target, in_sems.at[place])
            for place, (source, target) in enumerate(zip((*sources, *small), targets))
        ]
        for load in loads:
            load.start()
        for load in loads:
            load.wait()
        lane = lax.broadcasted_iota(jnp.int32, (tokens, HD), 1)
        note = jnp.where(lane == window, noise_ref[0], 0)
        for column in range(window):
            note = jnp.where(lane == column, mask_ref[0, column], note)
        note = note.astype(jnp.float32).astype(queries.dtype)
        stores = []
        for number, (a, b) in enumerate(moves):
            block = (frame ^ a) * pairs + (pair ^ b)
            columns = pl.ds(pl.multiple_of(block * width, HD), width)
            for place in range(3):
                packed[number, :, place * width : (place + 1) * width] = loaded[place, :, columns]
            if b == 0:
                packed[number, :, 3 * width :] = note
            store = pltpu.make_async_copy(
                packed.at[number, :, : widths[number]], pieces[number], out_sems.at[number]
            )
            store.start()
            stores.append(store)
        for store in stores:
            store.wait()

    return pl.pallas_call(
        kernel,
        out_shape=[jax.ShapeDtypeStruct((tokens, size), queries.dtype) for size in widths],
        in_specs=in_hbm(5),
        out_specs=in_hbm(count),
        scratch_shapes=[
            pltpu.VMEM((3, *queries.shape), queries.dtype),
            pltpu.VMEM((count, tokens, 3 * width + HD), queries.dtype),
            pltpu.SMEM(frame_mask.shape, frame_mask.dtype),
            pltpu.SMEM(noise_steps.shape, noise_steps.dtype),
            pltpu.SemaphoreType.DMA((5,)),
            pltpu.SemaphoreType.DMA((count,)),
        ],
        compiler_params=pltpu.CompilerParams(vmem_limit_bytes=PACK_BYTES),
        name="pack",
    )(queries, keys, values, frame_mask, noise_steps)


def pick(table, here):
    result = table[0]
    for place, entry in enumerate(table[1:], 1):
        result = jnp.where(here == place, entry, result)
    return result


def attend(frames_of_slot, own, mate, moves, pairs, frames, width):
    tokens = own[0].shape[0]
    rows, keys_rows = (pairs * tokens, 2 * pairs * tokens)
    scale = math.log2(math.e) / math.sqrt(HD)

    def kernel(*refs):
        own_refs, refs = (refs[: len(moves)], refs[len(moves) :])
        mate_refs, refs = (refs[: len(moves)], refs[len(moves) :])
        out_ref, note_out, query_buf, key_buf, value_buf, note_buf = refs
        here = lax.axis_index("tm")
        frame = pick(frames_of_slot, here)
        for own_ref, mate_ref, (a, b) in zip(own_refs, mate_refs, moves):
            query_buf[here ^ a, b * tokens : (b + 1) * tokens, :] = own_ref[:, :width]
            for side, ref in enumerate((own_ref, mate_ref)):
                span = slice((2 * b + side) * tokens, (2 * b + side + 1) * tokens)
                key_buf[a, span, :] = ref[:, width : 2 * width]
                value_buf[a, span, :] = ref[:, 2 * width : 3 * width]
            if b == 0:
                note_buf[pl.ds(here ^ a, 1), :] = own_ref[:16, 3 * width :].astype(jnp.float32)[:1]

        note = note_buf[pl.ds(frame, 1), :]
        note_out[...] = note_buf[...]
        lane = lax.broadcasted_iota(jnp.int32, note.shape, 1)
        biases = []
        for a in range(frames):
            hit = jnp.sum(jnp.where(lane == here ^ a, note, 0.0), axis=1, keepdims=True)
            biases.append(jnp.broadcast_to((hit - 1.0) * 1e30, (1, keys_rows)))
        bias = jnp.concatenate(biases, axis=1)
        for start in range(0, width, HD):
            channels = slice(start, start + HD)
            query = query_buf[frame, :, channels]
            keys = key_buf[:, :, channels].reshape(frames * keys_rows, HD)
            scores = lax.dot_general(
                query, keys, (((1,), (1,)), ((), ())), preferred_element_type=jnp.float32
            )
            scores = scores * scale + bias
            lifted = jnp.exp2(scores - jnp.max(scores, axis=1, keepdims=True))
            totals = jnp.sum(lifted, axis=1, keepdims=True)
            values = value_buf[:, :, channels].reshape(frames * keys_rows, HD)
            mixed = jnp.dot(
                lifted.astype(jnp.bfloat16), values, preferred_element_type=jnp.float32
            )
            out_ref[:, channels] = (mixed / totals).astype(jnp.bfloat16)

    kind = own[0].dtype
    return pl.pallas_call(
        kernel,
        out_shape=[
            jax.ShapeDtypeStruct((rows, width), jnp.bfloat16),
            jax.ShapeDtypeStruct((16, HD), jnp.float32),
        ],
        in_specs=whole_in_vmem(2 * len(moves)),
        out_specs=whole_in_vmem(2),
        scratch_shapes=[
            pltpu.VMEM((frames, rows, width), kind),
            pltpu.VMEM((frames, keys_rows, width), kind),
            pltpu.VMEM((frames, keys_rows, width), kind),
            pltpu.VMEM((16, HD), jnp.float32),
        ],
        compiler_params=roomy(),
        name="attend",
    )(*own, *mate)


def project(pieces, weight, pairs, cuts):
    rows, width = pieces[0].shape
    tokens = rows // pairs
    depth, columns = weight.shape
    step = math.gcd(columns, 256)
    spans = [slice(first, last) for first, last in zip([0, *cuts], cuts)]

    def kernel(*refs):
        piece_refs, (weight_ref, out_ref, *short_refs, whole) = (
            refs[: len(pieces)],
            refs[len(pieces) :],
        )
        here = lax.axis_index("head")
        for j, ref in enumerate(piece_refs):
            source = here ^ j
            pair, core = (source // 2, source % 2)
            channels = pl.ds(pl.multiple_of(pair * width, HD), width)
            for b in range(pairs):
                first = ((pair ^ b) * 2 + core) * tokens
                whole[pl.ds(pl.multiple_of(first, 16), tokens), channels] = ref[
                    b * tokens : (b + 1) * tokens, :
                ]
        for start in range(0, columns, step):
            product = jnp.dot(
                whole[...], weight_ref[:, start : start + step], preferred_element_type=jnp.float32
            )
            out_ref[:, start : start + step] = product
            for span, short_ref in zip(spans, short_refs):
                short_ref[:, start : start + step] = product[span, :].astype(jnp.bfloat16)

    product, *rounded = pl.pallas_call(
        kernel,
        out_shape=[jax.ShapeDtypeStruct((2 * rows, columns), jnp.float32)]
        + [
            jax.ShapeDtypeStruct((span.stop - span.start, columns), jnp.bfloat16) for span in spans
        ],
        in_specs=whole_in_vmem(len(pieces) + 1),
        out_specs=whole_in_vmem(1 + len(spans)),
        scratch_shapes=[pltpu.VMEM((2 * rows, depth), jnp.bfloat16)],
        compiler_params=roomy(),
        name="project",
    )(*pieces, weight)
    return (product, rounded)


def join(partial, table, span, arrived, residual=None, gate=None):
    columns = partial[0].shape[1]
    step = math.gcd(columns, 256)
    slots = sorted(set(table))
    extras = [] if residual is None else [residual, gate]

    def kernel(*refs):
        own_refs, refs = (refs[: len(slots)], refs[len(slots) :])
        arrived_refs, refs = (refs[: len(arrived)], refs[len(arrived) :])
        out_ref = refs[-1]
        here = lax.axis_index("tm")
        for slot, own_ref in zip(slots, own_refs):

            @pl.when(pick([entry == slot for entry in table], here))
            def _(own_ref=own_ref):
                for start in range(0, columns, step):
                    part = slice(start, start + step)
                    total = own_ref[span, part]
                    for ref in arrived_refs:
                        total += ref[:, part].astype(jnp.float32)
                    if extras:
                        total = refs[0][span, part].astype(jnp.float32) + refs[1][:, part] * total
                    out_ref[:, part] = total.astype(jnp.bfloat16)

    operands = [partial[slot] for slot in slots] + list(arrived) + extras
    return pl.pallas_call(
        kernel,
        out_shape=jax.ShapeDtypeStruct((span.stop - span.start, columns), jnp.bfloat16),
        in_specs=whole_in_vmem(len(operands)),
        out_specs=whole_in_vmem(1)[0],
        compiler_params=roomy(),
        name="join",
    )(*operands)


def finish(spans, arrived, partial, below, gate, fresh_frame):
    rows, columns = partial.shape
    step = math.gcd(columns, 256)

    def kernel(*refs):
        arrived_refs, below_refs = (refs[: len(spans)], refs[len(spans) : 2 * len(spans)])
        partial_ref, gate_ref, fresh_ref, out_ref = refs[2 * len(spans) :]
        last = lax.axis_index("tm") == lax.axis_size("tm") - 1

        @pl.when(last)
        def _():
            out_ref[...] = fresh_ref[...]

        @pl.when(jnp.logical_not(last))
        def _():
            for span, arrived_ref, below_ref in zip(spans, arrived_refs, below_refs):
                for start in range(0, columns, step):
                    part = slice(start, start + step)
                    total = partial_ref[span, part] + below_ref[:, part].astype(jnp.float32)
                    total = arrived_ref[:, part].astype(jnp.float32) + gate_ref[:, part] * total
                    out_ref[span, part] = total.astype(jnp.bfloat16)

    return pl.pallas_call(
        kernel,
        out_shape=jax.ShapeDtypeStruct((rows, columns), jnp.bfloat16),
        in_specs=whole_in_vmem(2 * len(spans) + 3),
        out_specs=whole_in_vmem(1)[0],
        compiler_params=roomy(),
        name="finish",
    )(*arrived, *below, partial, gate, fresh_frame)


def line_schedule(frames):
    steps = []
    for step in range(frames - 1):
        down = {z: step + 1 - (frames - 1 - z) for z in range(1, frames)}
        up = {z: frames - 1 - step + z for z in range(frames)}
        down = {z: f for z, f in down.items() if 1 <= f <= z}
        up = {z: f for z, f in up.items() if z + 2 <= f < frames}
        steps.append((down, up))
    order = []
    for z in range(frames):
        sent = [f for down, up in steps for f in (down.get(z), up.get(z)) if f is not None]
        order.append((sent + [z + 1])[: frames - 1])
    return steps, order


def head_plan(
    queries, keys, values, residual, fresh_frame, out_weight, time_weight, noise_steps, frame_mask
):
    frames, across = (lax.axis_size("tm"), lax.axis_size("head"))
    pairs = across // 2
    width = queries.shape[2] // (frames * pairs)
    everywhere = range(frames)

    def swap(array, j):
        return lax.ppermute(array, "head", [(h, h ^ j) for h in range(across)])

    def gather(part, meanwhile=None):
        pieces = {0: part}
        bit = across // 2
        while bit:
            for j in list(pieces):
                pieces[j ^ bit] = swap(pieces[j], bit)
            if meanwhile is not None and bit == across // 2:
                pieces[bit], meanwhile = lax.optimization_barrier((pieces[bit], meanwhile))
            bit //= 2
        return ([pieces[j] for j in range(across)], meanwhile)

    far = [(a, b) for b in range(pairs) for a in reversed(everywhere[2:])]
    near = [(0, b) for b in range(pairs)] + [(1, b) for b in range(pairs)]
    moves = near[:-1] + far + near[-1:]
    packed = pack(
        queries[0], keys[0], values[0], frame_mask, noise_steps, moves, pairs, width
    )
    own = []
    for piece, (a, b) in zip(packed, moves):
        if (a, b) != (0, 0):
            links = [
                (z * across + h, (z ^ a) * across + (h ^ (2 * b)))
                for z in everywhere
                for h in range(across)
            ]
            piece = lax.ppermute(piece, ("tm", "head"), links)
        own.append(piece)
    mate = [swap(piece, 1) for piece in own]
    steps, order = line_schedule(frames)
    rows = residual.shape[1]
    cuts = [rows // 2, rows]
    spans = [slice(first, last) for first, last in zip([0, *cuts], cuts)]
    def attend_slot(slot):
        frames_of_slot = [order[z][slot] for z in everywhere]
        return attend(frames_of_slot, own, mate, moves, pairs, frames, width)

    part, _ = attend_slot(0)
    following, notes = attend_slot(1)
    pieces, following = gather(part, following)
    product, payload = project(pieces, out_weight, pairs, cuts)
    partial = [product]
    down, up = steps[0]
    links = [(z, z - 1) for z in down] + [(z, z + 1) for z in up]
    above = [lax.ppermute(part, "tm", links) for part in payload]
    below = above
    own[0], above[0] = lax.optimization_barrier((own[0], above[0]))
    for slot in range(1, frames - 1):
        part = following if slot == 1 else attend_slot(slot)[0]
        partial.append(project(gather(part)[0], out_weight, pairs, [])[0])
    noise = lax.dynamic_slice(notes[:, frame_mask.shape[1]], (lax.axis_index("tm"),), (2,))
    gates = jnp.dot(
        time_features(noise), time_weight.astype(jnp.float32), precision=lax.Precision.HIGHEST
    )

    for number, (down, up) in enumerate(steps[1:], 1):
        sends = {**down, **up}
        table = [order[z].index(sends[z]) if z in sends else 0 for z in everywhere]
        final = number == len(steps) - 1
        extras = (residual[0], gates[:1]) if final else ()
        payload = [
            join(
                partial,
                table,
                span,
                [above[i]] if final or above is below else [above[i], below[i]],
                *extras,
            )
            for i, span in enumerate(spans)
        ]
        above = [lax.ppermute(part, "tm", [(z, z - 1) for z in down]) for part in payload]
        if up:
            below = [lax.ppermute(part, "tm", [(z, z + 1) for z in up]) for part in payload]
    return finish(spans, above, partial[-1], below, gates[1:], fresh_frame)[None]


def power_of_two(number):
    return number & (number - 1) == 0


def suits_line(frames, window):
    apart = all(not set(down) & set(up) for down, up in line_schedule(frames)[0])
    return 2 < frames <= window and power_of_two(frames) and apart


def on_device(queries, *others):
    frames, across = (lax.axis_size("tm"), lax.axis_size("head"))
    heads = queries.shape[2] // HD
    even = across % 2 == 0 and power_of_two(across)
    even = even and queries.shape[1] % 16 == 0
    if even and suits_line(frames, others[-1].shape[1]) and heads % (frames * across // 2) == 0:
        return head_plan(queries, *others)
    return frame_plan(queries, *others)


def solution(mesh):
    placed = (
        P(("groups", "tm"), "head", None),
        P(("groups", "tm"), "head", None),
        P(("groups", "tm"), "head", None),
        P(("groups", "tm"), None, "head"),
        P("groups", "head"),
        P("tm", "head"),
        P(None, "head"),
        P(("groups", "tm")),
        P(("groups", "tm"), None),
    )
    return jax.shard_map(
        on_device,
        mesh=mesh,
        in_specs=placed,
        out_specs=P(("groups", "tm"), None, "head"),
        check_vma=False,
    )
```

```python
import math

import jax
import jax.numpy as jnp
import numpy as np
from jax import lax
from jax.experimental import pallas as pl
from jax.experimental.pallas import tpu as pltpu
from jax.sharding import PartitionSpec as P

HD = 128
FREQ = 256
STEPS = 50
VMEM_BYTES = 16 * 1024 * 1024
PACK_BYTES = 60 * 1024 * 1024


def shifted(value, axis, steps):
    count = lax.axis_size(axis)
    leading, last = (max(0, -steps), min(count, count - steps))
    return lax.ppermute(value, axis, [(source, source + steps) for source in range(leading, last)])


def time_features(noise_steps):
    timestep = 1000.0 * (noise_steps.astype(jnp.float32) + 1.0) / STEPS
    half = FREQ // 2
    rates = jnp.exp(-math.log(10000.0) * jnp.arange(half).astype(jnp.float32) / half)
    angles = timestep[:, None] * rates[None, :]
    return jnp.concatenate([jnp.cos(angles), jnp.sin(angles)], axis=1)


def frame_plan(
    queries, keys, values, residual, fresh_frame, out_weight, time_weight, noise_steps, frame_mask
):
    query_local, key_local, value_local = (
        lax.all_to_all(queries, "head", split_axis=2, concat_axis=1, tiled=True),
        lax.all_to_all(keys, "head", split_axis=2, concat_axis=1, tiled=True),
        lax.all_to_all(values, "head", split_axis=2, concat_axis=1, tiled=True),
    )
    tokens = query_local.shape[1]
    heads_here = query_local.shape[2] // HD
    scale = 1.0 / math.sqrt(HD)
    query_heads = query_local[0].reshape(tokens, heads_here, HD)
    key_value = jnp.stack([key_local[0], value_local[0]], axis=0)
    frame = lax.axis_index("tm")
    frames_total = lax.axis_size("tm")
    window = min(8, frames_total)
    mask_row = frame_mask[0]
    columns = jnp.arange(mask_row.shape[0], dtype=jnp.int32)

    def allowed_at(offset):
        hits = jnp.sum(jnp.where(columns == frame - offset, mask_row, 0))
        return hits > 0

    def absorb(state, block, allowed):
        running_max, weight_sum, accumulated = state
        key_heads = block[0].reshape(tokens, heads_here, HD)
        value_heads = block[1].reshape(tokens, heads_here, HD)
        scores = (
            jnp.einsum("qhd,khd->hqk", query_heads, key_heads, preferred_element_type=jnp.float32)
            * scale
        )
        new_max = jnp.where(allowed, jnp.maximum(running_max, jnp.max(scores, axis=2)), running_max)
        lifted = jnp.where(allowed, jnp.exp(jnp.minimum(scores - new_max[:, :, None], 0.0)), 0.0)
        factor = jnp.exp(running_max - new_max)
        weight_sum = weight_sum * factor + jnp.sum(lifted, axis=2)
        rounded = lifted.astype(jnp.bfloat16)
        accumulated = accumulated * jnp.transpose(factor)[:, :, None] + jnp.einsum(
            "hqk,khd->qhd", rounded, value_heads, preferred_element_type=jnp.float32
        )
        return (new_max, weight_sum, accumulated)

    state = (
        jnp.full((heads_here, tokens), -1e30, jnp.float32),
        jnp.zeros((heads_here, tokens), jnp.float32),
        jnp.zeros((tokens, heads_here, HD), jnp.float32),
    )
    state = absorb(state, key_value, allowed_at(0))
    moving = key_value
    for offset in range(1, window):
        moving = shifted(moving, "tm", 1)
        state = absorb(state, moving, allowed_at(offset))
    running_max, weight_sum, accumulated = state
    attention = (
        (accumulated / jnp.transpose(weight_sum)[:, :, None])
        .reshape(tokens, heads_here * HD)
        .astype(jnp.bfloat16)
    )
    weight_cols = lax.all_gather(out_weight, "tm", axis=0, tiled=True)
    projected = jnp.dot(
        lax.all_gather(attention, "head", axis=1, tiled=True),
        weight_cols,
        preferred_element_type=jnp.float32,
    )
    gate = jnp.dot(
        time_features(noise_steps), time_weight.astype(jnp.float32), precision=lax.Precision.HIGHEST
    )
    updated = (residual[0].astype(jnp.float32) + gate * projected).astype(jnp.bfloat16)
    moved = shifted(updated, "tm", -1)
    rolled = jnp.where(frame == frames_total - 1, fresh_frame, moved)
    return rolled[None]


def whole_in_vmem(count):
    return [pl.BlockSpec(memory_space=pltpu.VMEM)] * count


def in_hbm(count):
    return [pl.BlockSpec(memory_space=pltpu.HBM)] * count


def roomy():
    return pltpu.CompilerParams(vmem_limit_bytes=VMEM_BYTES)


def pack(queries, keys, values, frame_mask, noise_steps, moves, pairs, width):
    tokens = queries.shape[0]
    window = frame_mask.shape[1]
    widths = [3 * width + (HD if b == 0 else 0) for a, b in moves]
    count = len(moves)

    def kernel(*refs):
        sources, small, pieces, scratch = (refs[:3], refs[3:5], refs[5 : 5 + count], refs[5 + count :])
        loaded, packed, mask_ref, noise_ref, in_sems, out_sems = scratch
        frame, pair = (lax.axis_index("tm"), lax.axis_index("head") // 2)
        targets = [loaded.at[place] for place in range(3)] + [mask_ref, noise_ref]
        loads = [
            pltpu.make_async_copy(source, target, in_sems.at[place])
            for place, (source, target) in enumerate(zip((*sources, *small), targets))
        ]
        for load in loads:
            load.start()
        for load in loads:
            load.wait()
        lane = lax.broadcasted_iota(jnp.int32, (tokens, HD), 1)
        note = jnp.where(lane == window, noise_ref[0], 0)
        for column in range(window):
            note = jnp.where(lane == column, mask_ref[0, column], note)
        note = note.astype(jnp.float32).astype(queries.dtype)
        stores = []
        for number, (a, b) in enumerate(moves):
            block = (frame ^ a) * pairs + (pair ^ b)
            columns = pl.ds(pl.multiple_of(block * width, HD), width)
            for place in range(3):
                packed[number, :, place * width : (place + 1) * width] = loaded[place, :, columns]
            if b == 0:
                packed[number, :, 3 * width :] = note
            store = pltpu.make_async_copy(
                packed.at[number, :, : widths[number]], pieces[number], out_sems.at[number]
            )
            store.start()
            stores.append(store)
        for store in stores:
            store.wait()

    return pl.pallas_call(
        kernel,
        out_shape=[jax.ShapeDtypeStruct((tokens, size), queries.dtype) for size in widths],
        in_specs=in_hbm(5),
        out_specs=in_hbm(count),
        scratch_shapes=[
            pltpu.VMEM((3, *queries.shape), queries.dtype),
            pltpu.VMEM((count, tokens, 3 * width + HD), queries.dtype),
            pltpu.SMEM(frame_mask.shape, frame_mask.dtype),
            pltpu.SMEM(noise_steps.shape, noise_steps.dtype),
            pltpu.SemaphoreType.DMA((5,)),
            pltpu.SemaphoreType.DMA((count,)),
        ],
        compiler_params=pltpu.CompilerParams(vmem_limit_bytes=PACK_BYTES),
        name="pack",
    )(queries, keys, values, frame_mask, noise_steps)


def bring(*arrays):
    def kernel(*refs):
        for source, target in zip(refs[: len(arrays)], refs[len(arrays) :]):
            target[...] = source[...]

    return pl.pallas_call(
        kernel,
        out_shape=[jax.ShapeDtypeStruct(array.shape, array.dtype) for array in arrays],
        in_specs=whole_in_vmem(len(arrays)),
        out_specs=whole_in_vmem(len(arrays)),
        compiler_params=roomy(),
        name="bring",
    )(*arrays)


def pick(table, here):
    result = table[0]
    for place, entry in enumerate(table[1:], 1):
        result = jnp.where(here == place, entry, result)
    return result


def attend(frames_of_slot, own, mate, moves, pairs, frames, width):
    tokens = own[0].shape[0]
    rows, keys_rows = (pairs * tokens, 2 * pairs * tokens)
    scale = math.log2(math.e) / math.sqrt(HD)

    def kernel(*refs):
        own_refs, refs = (refs[: len(moves)], refs[len(moves) :])
        mate_refs, refs = (refs[: len(moves)], refs[len(moves) :])
        out_ref, note_out, query_buf, key_buf, value_buf, note_buf = refs
        here = lax.axis_index("tm")
        frame = pick(frames_of_slot, here)
        for own_ref, mate_ref, (a, b) in zip(own_refs, mate_refs, moves):
            query_buf[here ^ a, b * tokens : (b + 1) * tokens, :] = own_ref[:, :width]
            for side, ref in enumerate((own_ref, mate_ref)):
                span = slice((2 * b + side) * tokens, (2 * b + side + 1) * tokens)
                key_buf[a, span, :] = ref[:, width : 2 * width]
                value_buf[a, span, :] = ref[:, 2 * width : 3 * width]
            if b == 0:
                note_buf[pl.ds(here ^ a, 1), :] = own_ref[:16, 3 * width :].astype(jnp.float32)[:1]

        note = note_buf[pl.ds(frame, 1), :]
        note_out[...] = note_buf[...]
        lane = lax.broadcasted_iota(jnp.int32, note.shape, 1)
        biases = []
        for a in range(frames):
            hit = jnp.sum(jnp.where(lane == here ^ a, note, 0.0), axis=1, keepdims=True)
            biases.append(jnp.broadcast_to((hit - 1.0) * 1e30, (1, keys_rows)))
        bias = jnp.concatenate(biases, axis=1)
        for start in range(0, width, HD):
            channels = slice(start, start + HD)
            query = query_buf[frame, :, channels]
            keys = key_buf[:, :, channels].reshape(frames * keys_rows, HD)
            scores = lax.dot_general(
                query, keys, (((1,), (1,)), ((), ())), preferred_element_type=jnp.float32
            )
            scores = scores * scale + bias
            lifted = jnp.exp2(scores - jnp.max(scores, axis=1, keepdims=True))
            totals = jnp.sum(lifted, axis=1, keepdims=True)
            values = value_buf[:, :, channels].reshape(frames * keys_rows, HD)
            mixed = jnp.dot(
                lifted.astype(jnp.bfloat16), values, preferred_element_type=jnp.float32
            )
            out_ref[:, channels] = (mixed / totals).astype(jnp.bfloat16)

    kind = own[0].dtype
    return pl.pallas_call(
        kernel,
        out_shape=[
            jax.ShapeDtypeStruct((rows, width), jnp.bfloat16),
            jax.ShapeDtypeStruct((16, HD), jnp.float32),
        ],
        in_specs=whole_in_vmem(2 * len(moves)),
        out_specs=whole_in_vmem(2),
        scratch_shapes=[
            pltpu.VMEM((frames, rows, width), kind),
            pltpu.VMEM((frames, keys_rows, width), kind),
            pltpu.VMEM((frames, keys_rows, width), kind),
            pltpu.VMEM((16, HD), jnp.float32),
        ],
        compiler_params=roomy(),
        name="attend",
    )(*own, *mate)


def put_together(piece_refs, whole):
    rows, width = piece_refs[0].shape
    pairs = len(piece_refs) // 2
    tokens = rows // pairs
    here = lax.axis_index("head")
    for j, ref in enumerate(piece_refs):
        source = here ^ j
        pair, core = (source // 2, source % 2)
        channels = pl.ds(pl.multiple_of(pair * width, HD), width)
        for b in range(pairs):
            first = ((pair ^ b) * 2 + core) * tokens
            whole[pl.ds(pl.multiple_of(first, 16), tokens), channels] = ref[
                b * tokens : (b + 1) * tokens, :
            ]


def project(pieces, weight, parts, beyond=None):
    rows, depth = (2 * pieces[0].shape[0], weight.shape[0])
    count = len(pieces)
    operands = [*pieces, weight]
    if beyond is not None:
        operands += [*beyond[0], beyond[1], beyond[2]]

    def kernel(*refs):
        out_refs = refs[len(operands) : len(operands) + 2 * len(parts)]
        whole = refs[len(operands) + 2 * len(parts)]
        put_together(refs[:count], whole)
        weight_ref = refs[count]
        for part, out_ref, short_ref in zip(parts, out_refs[::2], out_refs[1::2]):
            out_ref[...] = jnp.dot(
                whole[...], weight_ref[:, part], preferred_element_type=jnp.float32
            )
            if beyond is None:
                short_ref[...] = out_ref[...].astype(jnp.bfloat16)
        if beyond is not None:
            own_ref, other_ref = refs[2 * count + 1 : 2 * count + 3]
            share = depth // 2
            out_ref, short_ref = out_refs

            @pl.when(lax.axis_index("tm") == lax.axis_size("tm") - 2)
            def _():
                put_together(refs[count + 1 : 2 * count + 1], whole)
                group = lax.axis_index("groups")
                for place, ref in ((group, own_ref), (1 - group, other_ref)):
                    channels = pl.ds(pl.multiple_of(place * share, HD), share)
                    out_ref[...] += jnp.dot(
                        whole[:, channels], ref[...], preferred_element_type=jnp.float32
                    )

            short_ref[...] = out_ref[...].astype(jnp.bfloat16)

    outs = []
    for part in parts:
        for kind in (jnp.float32, jnp.bfloat16):
            outs.append(jax.ShapeDtypeStruct((rows, part.stop - part.start), kind))
    outs = pl.pallas_call(
        kernel,
        out_shape=outs,
        in_specs=whole_in_vmem(len(operands)),
        out_specs=whole_in_vmem(len(outs)),
        scratch_shapes=[pltpu.VMEM((rows, depth), jnp.bfloat16)],
        compiler_params=roomy(),
        name="project",
    )(*operands)
    return (list(outs[::2]), list(outs[1::2]))


def join(partial, table, arrived, part, residual=None, gate=None):
    rows, columns = partial[0].shape
    slots = sorted(set(table))
    extras = [] if residual is None else [residual, gate]
    step = math.gcd(columns, 256)

    def kernel(*refs):
        own_refs, refs = (refs[: len(slots)], refs[len(slots) :])
        arrived_refs, refs = (refs[: len(arrived)], refs[len(arrived) :])
        out_ref = refs[-1]
        here = lax.axis_index("tm")
        for slot, own_ref in zip(slots, own_refs):

            @pl.when(pick([entry == slot for entry in table], here))
            def _(own_ref=own_ref):
                for start in range(0, columns, step):
                    inner = slice(start, start + step)
                    outer = slice(part.start + start, part.start + start + step)
                    total = own_ref[:, inner]
                    for ref in arrived_refs:
                        total += ref[:, inner].astype(jnp.float32)
                    if extras:
                        total = refs[0][:, outer].astype(jnp.float32) + refs[1][:, outer] * total
                    out_ref[:, inner] = total.astype(jnp.bfloat16)

    operands = [partial[slot] for slot in slots] + list(arrived) + extras
    return pl.pallas_call(
        kernel,
        out_shape=jax.ShapeDtypeStruct((rows, columns), jnp.bfloat16),
        in_specs=whole_in_vmem(len(operands)),
        out_specs=whole_in_vmem(1)[0],
        compiler_params=roomy(),
        name="join",
    )(*operands)


def finish(parts, arrived, partial, below, gate, fresh_frame):
    rows, columns = fresh_frame.shape
    flat = [array for arrays in arrived for array in arrays]

    def kernel(*refs):
        arrived_refs, refs = (iter(refs[: len(flat)]), refs[len(flat) :])
        partial_refs, below_refs = (refs[: len(parts)], refs[len(parts) : 2 * len(parts)])
        gate_ref, fresh_ref, out_ref = refs[2 * len(parts) :]
        last = lax.axis_index("tm") == lax.axis_size("tm") - 1

        @pl.when(last)
        def _():
            out_ref[...] = fresh_ref[...]

        @pl.when(jnp.logical_not(last))
        def _():
            for number, part in enumerate(parts):
                mine = [next(arrived_refs) for _ in arrived[number]]
                step = math.gcd(part.stop - part.start, 256)
                for start in range(0, part.stop - part.start, step):
                    inner = slice(start, start + step)
                    outer = slice(part.start + start, part.start + start + step)
                    total = partial_refs[number][:, inner]
                    total += below_refs[number][:, inner].astype(jnp.float32)
                    total = gate_ref[:, outer] * total
                    for ref in mine:
                        total += ref[:, inner].astype(jnp.float32)
                    out_ref[:, outer] = total.astype(jnp.bfloat16)

    return pl.pallas_call(
        kernel,
        out_shape=jax.ShapeDtypeStruct((rows, columns), jnp.bfloat16),
        in_specs=whole_in_vmem(len(flat) + 2 * len(parts) + 2),
        out_specs=whole_in_vmem(1)[0],
        compiler_params=roomy(),
        name="finish",
    )(*flat, *partial, *below, gate, fresh_frame)


def line_schedule(frames):
    steps = []
    for step in range(frames - 1):
        down = {z: step + 1 - (frames - 1 - z) for z in range(1, frames)}
        up = {z: frames - 1 - step + z for z in range(frames)}
        down = {z: f for z, f in down.items() if 1 <= f <= z}
        up = {z: f for z, f in up.items() if z + 2 <= f < frames}
        steps.append((down, up))
    order = []
    for z in range(frames):
        sent = [f for down, up in steps for f in (down.get(z), up.get(z)) if f is not None]
        order.append((sent + [z + 1])[: frames - 1])
    return steps, order


def head_plan(
    queries, keys, values, residual, fresh_frame, out_weight, time_weight, noise_steps, frame_mask
):
    frames, across = (lax.axis_size("tm"), lax.axis_size("head"))
    pairs = across // 2
    width = queries.shape[2] // (frames * pairs)
    everywhere = range(frames)
    here = lax.axis_index("tm")

    def swap(array, j):
        return lax.ppermute(array, "head", [(h, h ^ j) for h in range(across)])

    def gather(part, meanwhile=None):
        pieces = {0: part}
        bit = across // 2
        while bit:
            for j in list(pieces):
                pieces[j ^ bit] = swap(pieces[j], bit)
            if meanwhile is not None and bit == across // 2:
                pieces[bit], meanwhile = lax.optimization_barrier((pieces[bit], meanwhile))
            bit //= 2
        return ([pieces[j] for j in range(across)], meanwhile)

    far = [(a, b) for b in range(pairs) for a in reversed(everywhere[2:])]
    near = [(0, b) for b in range(pairs)] + [(1, b) for b in range(pairs)]
    moves = near[:-1] + far + near[-1:]
    packed = pack(
        queries[0], keys[0], values[0], frame_mask, noise_steps, moves, pairs, width
    )
    own = []
    for piece, (a, b) in zip(packed, moves):
        if (a, b) != (0, 0):
            links = [
                (z * across + h, (z ^ a) * across + (h ^ (2 * b)))
                for z in everywhere
                for h in range(across)
            ]
            piece = lax.ppermute(piece, ("tm", "head"), links)
        own.append(piece)
    mine = moves.index((0, 0))
    own[mine], weight = bring(own[mine], out_weight)
    mate = [swap(piece, 1) for piece in own]

    steps, order = line_schedule(frames)
    half = out_weight.shape[1] // 2
    near_part, far_part = (slice(0, half), slice(half, 2 * half))
    end = frames - 1

    share = out_weight.shape[0] // 2
    sent = lax.dynamic_slice(out_weight, (lax.axis_index("groups") * share, 0), (share, half))
    brought = lax.ppermute(sent, "tm", [(end, end - 1)])
    exchange = [(g * frames + end - 1, (1 - g) * frames + end - 1) for g in range(2)]

    def attend_slot(slot, own):
        frames_of_slot = [order[z][slot] for z in everywhere]
        return attend(frames_of_slot, own, mate, moves, pairs, frames, width)

    def hand_on(part):
        pieces = {}
        for j in range(0, across, 2):
            links = [(end * across + h, (end - 1) * across + (h ^ j)) for h in range(across)]
            pieces[j] = lax.ppermute(part, ("tm", "head"), links)
        links = [((end - 1) * across + h, (end - 1) * across + (h ^ 1)) for h in range(across)]
        for j in range(0, across, 2):
            pieces[j + 1] = lax.ppermute(pieces[j], ("tm", "head"), links)
        return [pieces[j] for j in range(across)]

    def down_from(places):
        return [(z, z - 1) for z in places]

    def up_from(places):
        return [(z, z + 1) for z in places]

    part, _ = attend_slot(0, own)
    brought, own[mine] = lax.optimization_barrier((brought, own[mine]))
    other = lax.ppermute(brought, ("groups", "tm"), exchange)
    following, notes = attend_slot(1, own)
    pieces, following = gather(part, following)
    far_partial, far_short = project(pieces, weight, [far_part])
    far_above = lax.ppermute(far_short[0], "tm", down_from(steps[0][0]) + up_from(steps[0][1]))
    near_partial, near_short = project(pieces, weight, [near_part], (hand_on(part), brought, other))
    near_above = lax.ppermute(near_short[0], "tm", down_from([end - 1]))
    near_below = lax.ppermute(near_short[0], "tm", up_from(steps[0][1]))

    pieces, _ = gather(following)
    next_near, _ = project(pieces, weight, [near_part], (hand_on(following), brought, other))
    next_far, _ = project(pieces, weight, [far_part])
    near_partial += next_near
    far_partial += next_far
    own[mine], near_above = lax.optimization_barrier((own[mine], near_above))
    part, _ = attend_slot(2, own)
    last_partial, _ = project(gather(part)[0], weight, [near_part, far_part])
    near_partial.append(last_partial[0])
    far_partial.append(last_partial[1])

    noise = lax.dynamic_slice(notes[:, frame_mask.shape[1]], (here,), (2,))
    gates = jnp.dot(
        time_features(noise), time_weight.astype(jnp.float32), precision=lax.Precision.HIGHEST
    )
    tables = []
    for down, up in steps:
        sends = {**down, **up}
        tables.append([order[z].index(sends[z]) if z in sends else 0 for z in everywhere])
    extras = (residual[0], gates[:1])

    payload = join(near_partial, tables[2], [near_above], near_part, *extras)
    near_arrived = lax.ppermute(payload, "tm", down_from(range(1, end)))
    payload = join(near_partial, tables[1], [near_below], near_part)
    near_below = lax.ppermute(payload, "tm", up_from(steps[1][1]))
    payload = join(far_partial, tables[1], [far_above], far_part)
    far_above = lax.ppermute(payload, "tm", down_from(steps[1][0]))
    far_below = lax.ppermute(payload, "tm", up_from(steps[1][1]))
    payload = join(near_partial, [2] * frames, [], near_part, *extras)
    near_last = lax.ppermute(payload, "tm", down_from([end]))
    payload = join(far_partial, tables[2], [far_above], far_part, *extras)
    far_arrived = lax.ppermute(payload, "tm", down_from(steps[2][0]))
    return finish(
        [near_part, far_part],
        [[near_arrived, near_last], [far_arrived]],
        [near_partial[2], far_partial[2]],
        [near_below, far_below],
        gates[1:],
        fresh_frame,
    )[None]


def power_of_two(number):
    return number & (number - 1) == 0


def suits_line(frames, window):
    apart = all(not set(down) & set(up) for down, up in line_schedule(frames)[0])
    return 3 < frames <= window and power_of_two(frames) and apart


def on_device(queries, *others):
    frames, across = (lax.axis_size("tm"), lax.axis_size("head"))
    heads = queries.shape[2] // HD
    even = across % 2 == 0 and power_of_two(across)
    even = even and queries.shape[1] % 16 == 0 and lax.axis_size("groups") == 2
    even = even and others[4].shape[0] % (2 * HD) == 0 and others[4].shape[1] % (2 * HD) == 0
    if even and suits_line(frames, others[-1].shape[1]) and heads % (frames * across // 2) == 0:
        return head_plan(queries, *others)
    return frame_plan(queries, *others)


def solution(mesh):
    placed = (
        P(("groups", "tm"), "head", None),
        P(("groups", "tm"), "head", None),
        P(("groups", "tm"), "head", None),
        P(("groups", "tm"), None, "head"),
        P("groups", "head"),
        P("tm", "head"),
        P(None, "head"),
        P(("groups", "tm")),
        P(("groups", "tm"), None),
    )
    return jax.shard_map(
        on_device,
        mesh=mesh,
        in_specs=placed,
        out_specs=P(("groups", "tm"), None, "head"),
        check_vma=False,
    )
```

```python
import math

import jax
import jax.numpy as jnp
import numpy as np
from jax import lax
from jax.experimental import pallas as pl
from jax.experimental.pallas import tpu as pltpu
from jax.sharding import PartitionSpec as P

HD = 128
FREQ = 256
STEPS = 50
VMEM_BYTES = 16 * 1024 * 1024
PACK_BYTES = 60 * 1024 * 1024


def shifted(value, axis, steps):
    count = lax.axis_size(axis)
    leading, last = (max(0, -steps), min(count, count - steps))
    return lax.ppermute(value, axis, [(source, source + steps) for source in range(leading, last)])


def time_features(noise_steps):
    timestep = 1000.0 * (noise_steps.astype(jnp.float32) + 1.0) / STEPS
    half = FREQ // 2
    rates = jnp.exp(-math.log(10000.0) * jnp.arange(half).astype(jnp.float32) / half)
    angles = timestep[:, None] * rates[None, :]
    return jnp.concatenate([jnp.cos(angles), jnp.sin(angles)], axis=1)


def frame_plan(
    queries, keys, values, residual, fresh_frame, out_weight, time_weight, noise_steps, frame_mask
):
    query_local, key_local, value_local = (
        lax.all_to_all(queries, "head", split_axis=2, concat_axis=1, tiled=True),
        lax.all_to_all(keys, "head", split_axis=2, concat_axis=1, tiled=True),
        lax.all_to_all(values, "head", split_axis=2, concat_axis=1, tiled=True),
    )
    tokens = query_local.shape[1]
    heads_here = query_local.shape[2] // HD
    scale = 1.0 / math.sqrt(HD)
    query_heads = query_local[0].reshape(tokens, heads_here, HD)
    key_value = jnp.stack([key_local[0], value_local[0]], axis=0)
    frame = lax.axis_index("tm")
    frames_total = lax.axis_size("tm")
    window = min(8, frames_total)
    mask_row = frame_mask[0]
    columns = jnp.arange(mask_row.shape[0], dtype=jnp.int32)

    def allowed_at(offset):
        hits = jnp.sum(jnp.where(columns == frame - offset, mask_row, 0))
        return hits > 0

    def absorb(state, block, allowed):
        running_max, weight_sum, accumulated = state
        key_heads = block[0].reshape(tokens, heads_here, HD)
        value_heads = block[1].reshape(tokens, heads_here, HD)
        scores = (
            jnp.einsum("qhd,khd->hqk", query_heads, key_heads, preferred_element_type=jnp.float32)
            * scale
        )
        new_max = jnp.where(allowed, jnp.maximum(running_max, jnp.max(scores, axis=2)), running_max)
        lifted = jnp.where(allowed, jnp.exp(jnp.minimum(scores - new_max[:, :, None], 0.0)), 0.0)
        factor = jnp.exp(running_max - new_max)
        weight_sum = weight_sum * factor + jnp.sum(lifted, axis=2)
        rounded = lifted.astype(jnp.bfloat16)
        accumulated = accumulated * jnp.transpose(factor)[:, :, None] + jnp.einsum(
            "hqk,khd->qhd", rounded, value_heads, preferred_element_type=jnp.float32
        )
        return (new_max, weight_sum, accumulated)

    state = (
        jnp.full((heads_here, tokens), -1e30, jnp.float32),
        jnp.zeros((heads_here, tokens), jnp.float32),
        jnp.zeros((tokens, heads_here, HD), jnp.float32),
    )
    state = absorb(state, key_value, allowed_at(0))
    moving = key_value
    for offset in range(1, window):
        moving = shifted(moving, "tm", 1)
        state = absorb(state, moving, allowed_at(offset))
    running_max, weight_sum, accumulated = state
    attention = (
        (accumulated / jnp.transpose(weight_sum)[:, :, None])
        .reshape(tokens, heads_here * HD)
        .astype(jnp.bfloat16)
    )
    weight_cols = lax.all_gather(out_weight, "tm", axis=0, tiled=True)
    projected = jnp.dot(
        lax.all_gather(attention, "head", axis=1, tiled=True),
        weight_cols,
        preferred_element_type=jnp.float32,
    )
    gate = jnp.dot(
        time_features(noise_steps), time_weight.astype(jnp.float32), precision=lax.Precision.HIGHEST
    )
    updated = (residual[0].astype(jnp.float32) + gate * projected).astype(jnp.bfloat16)
    moved = shifted(updated, "tm", -1)
    rolled = jnp.where(frame == frames_total - 1, fresh_frame, moved)
    return rolled[None]


def whole_in_vmem(count):
    return [pl.BlockSpec(memory_space=pltpu.VMEM)] * count


def in_hbm(count):
    return [pl.BlockSpec(memory_space=pltpu.HBM)] * count


def roomy():
    return pltpu.CompilerParams(vmem_limit_bytes=VMEM_BYTES)


def pack(queries, keys, values, frame_mask, noise_steps, moves, pairs, width):
    tokens = queries.shape[0]
    window = frame_mask.shape[1]
    widths = [3 * width + (HD if b == 0 else 0) for a, b in moves]
    count = len(moves)

    def kernel(*refs):
        sources, small, pieces, scratch = (refs[:3], refs[3:5], refs[5 : 5 + count], refs[5 + count :])
        loaded, packed, mask_ref, noise_ref, in_sems, out_sems = scratch
        frame, pair = (lax.axis_index("tm"), lax.axis_index("head") // 2)
        targets = [loaded.at[place] for place in range(3)] + [mask_ref, noise_ref]
        loads = [
            pltpu.make_async_copy(source, target, in_sems.at[place])
            for place, (source, target) in enumerate(zip((*sources, *small), targets))
        ]
        for load in loads:
            load.start()
        for load in loads:
            load.wait()
        lane = lax.broadcasted_iota(jnp.int32, (tokens, HD), 1)
        note = jnp.where(lane == window, noise_ref[0], 0)
        for column in range(window):
            note = jnp.where(lane == column, mask_ref[0, column], note)
        note = note.astype(jnp.float32).astype(queries.dtype)
        stores = []
        for number, (a, b) in enumerate(moves):
            block = (frame ^ a) * pairs + (pair ^ b)
            columns = pl.ds(pl.multiple_of(block * width, HD), width)
            for place in range(3):
                packed[number, :, place * width : (place + 1) * width] = loaded[place, :, columns]
            if b == 0:
                packed[number, :, 3 * width :] = note
            store = pltpu.make_async_copy(
                packed.at[number, :, : widths[number]], pieces[number], out_sems.at[number]
            )
            store.start()
            stores.append(store)
        for store in stores:
            store.wait()

    return pl.pallas_call(
        kernel,
        out_shape=[jax.ShapeDtypeStruct((tokens, size), queries.dtype) for size in widths],
        in_specs=in_hbm(5),
        out_specs=in_hbm(count),
        scratch_shapes=[
            pltpu.VMEM((3, *queries.shape), queries.dtype),
            pltpu.VMEM((count, tokens, 3 * width + HD), queries.dtype),
            pltpu.SMEM(frame_mask.shape, frame_mask.dtype),
            pltpu.SMEM(noise_steps.shape, noise_steps.dtype),
            pltpu.SemaphoreType.DMA((5,)),
            pltpu.SemaphoreType.DMA((count,)),
        ],
        compiler_params=pltpu.CompilerParams(vmem_limit_bytes=PACK_BYTES),
        name="pack",
    )(queries, keys, values, frame_mask, noise_steps)


def bring(*arrays):
    def kernel(*refs):
        for source, target in zip(refs[: len(arrays)], refs[len(arrays) :]):
            target[...] = source[...]

    return pl.pallas_call(
        kernel,
        out_shape=[jax.ShapeDtypeStruct(array.shape, array.dtype) for array in arrays],
        in_specs=whole_in_vmem(len(arrays)),
        out_specs=whole_in_vmem(len(arrays)),
        compiler_params=roomy(),
        name="bring",
    )(*arrays)


def pick(table, here):
    result = table[0]
    for place, entry in enumerate(table[1:], 1):
        result = jnp.where(here == place, entry, result)
    return result


def attend(frames_of_slot, own, mate, moves, pairs, frames, width):
    tokens = own[0].shape[0]
    rows, keys_rows = (pairs * tokens, 2 * pairs * tokens)
    scale = math.log2(math.e) / math.sqrt(HD)

    def kernel(*refs):
        own_refs, refs = (refs[: len(moves)], refs[len(moves) :])
        mate_refs, refs = (refs[: len(moves)], refs[len(moves) :])
        out_ref, note_out, query_buf, key_buf, value_buf, note_buf = refs
        here = lax.axis_index("tm")
        frame = pick(frames_of_slot, here)
        for own_ref, mate_ref, (a, b) in zip(own_refs, mate_refs, moves):
            query_buf[here ^ a, b * tokens : (b + 1) * tokens, :] = own_ref[:, :width]
            for side, ref in enumerate((own_ref, mate_ref)):
                span = slice((2 * b + side) * tokens, (2 * b + side + 1) * tokens)
                key_buf[a, span, :] = ref[:, width : 2 * width]
                value_buf[a, span, :] = ref[:, 2 * width : 3 * width]
            if b == 0:
                note_buf[pl.ds(here ^ a, 1), :] = own_ref[:16, 3 * width :].astype(jnp.float32)[:1]

        note = note_buf[pl.ds(frame, 1), :]
        note_out[...] = note_buf[...]
        lane = lax.broadcasted_iota(jnp.int32, note.shape, 1)
        biases = []
        for a in range(frames):
            hit = jnp.sum(jnp.where(lane == here ^ a, note, 0.0), axis=1, keepdims=True)
            biases.append(jnp.broadcast_to((hit - 1.0) * 1e30, (1, keys_rows)))
        bias = jnp.concatenate(biases, axis=1)
        for start in range(0, width, HD):
            channels = slice(start, start + HD)
            query = query_buf[frame, :, channels]
            keys = key_buf[:, :, channels].reshape(frames * keys_rows, HD)
            scores = lax.dot_general(
                query, keys, (((1,), (1,)), ((), ())), preferred_element_type=jnp.float32
            )
            scores = scores * scale + bias
            lifted = jnp.exp2(scores - jnp.max(scores, axis=1, keepdims=True))
            totals = jnp.sum(lifted, axis=1, keepdims=True)
            values = value_buf[:, :, channels].reshape(frames * keys_rows, HD)
            mixed = jnp.dot(
                lifted.astype(jnp.bfloat16), values, preferred_element_type=jnp.float32
            )
            out_ref[:, channels] = (mixed / totals).astype(jnp.bfloat16)

    kind = own[0].dtype
    return pl.pallas_call(
        kernel,
        out_shape=[
            jax.ShapeDtypeStruct((rows, width), jnp.bfloat16),
            jax.ShapeDtypeStruct((16, HD), jnp.float32),
        ],
        in_specs=whole_in_vmem(2 * len(moves)),
        out_specs=whole_in_vmem(2),
        scratch_shapes=[
            pltpu.VMEM((frames, rows, width), kind),
            pltpu.VMEM((frames, keys_rows, width), kind),
            pltpu.VMEM((frames, keys_rows, width), kind),
            pltpu.VMEM((16, HD), jnp.float32),
        ],
        compiler_params=roomy(),
        name="attend",
    )(*own, *mate)


def project(pieces, weight):
    flat = [piece for part in pieces for piece in part]
    rows, width = flat[0].shape
    pairs = len(pieces[0])
    tokens = rows // pairs
    depth, columns = weight.shape
    step = math.gcd(columns, 256)

    def kernel(*refs):
        sources = iter(refs[: len(flat)])
        weight_ref, refs = (refs[len(flat)], refs[len(flat) + 1 :])
        whole = refs[-1]
        here = lax.axis_index("head") // 2
        for k, part in enumerate(pieces):
            for move in range(pairs):
                source = next(sources)
                pair = here ^ move
                channels = pl.ds(pl.multiple_of(pair * width, HD), width)
                for b in range(pairs):
                    first = k * rows + (pair ^ b) * tokens
                    whole[pl.ds(pl.multiple_of(first, 16), tokens), channels] = source[
                        b * tokens : (b + 1) * tokens, :
                    ]
        for start in range(0, columns, step):
            inner = slice(start, start + step)
            product = jnp.dot(
                whole[...], weight_ref[:, inner], preferred_element_type=jnp.float32
            )
            for k in range(len(pieces)):
                share = product[k * rows : (k + 1) * rows, :]
                refs[2 * k][:, inner] = share
                refs[2 * k + 1][:, inner] = share.astype(jnp.bfloat16)

    outs = pl.pallas_call(
        kernel,
        out_shape=[
            jax.ShapeDtypeStruct((rows, columns), kind)
            for _ in pieces
            for kind in (jnp.float32, jnp.bfloat16)
        ],
        in_specs=whole_in_vmem(len(flat) + 1),
        out_specs=whole_in_vmem(2 * len(pieces)),
        scratch_shapes=[pltpu.VMEM((len(pieces) * rows, depth), jnp.bfloat16)],
        compiler_params=roomy(),
        name="project",
    )(*flat, weight)
    return (list(outs[::2]), list(outs[1::2]))


def frame_rows(k, pairs, tokens):
    core = (lax.axis_index("head") % 2) ^ k
    return [pl.ds(pl.multiple_of((2 * p + core) * tokens, 16), tokens) for p in range(pairs)]


def join(partial, table, arrived, k, pairs, residual=None, gate=None):
    rows, columns = partial[0].shape
    tokens = rows // pairs
    step = math.gcd(columns, 256)
    slots = sorted(set(table))
    extras = [] if residual is None else [residual, gate]

    def kernel(*refs):
        own_refs, refs = (refs[: len(slots)], refs[len(slots) :])
        arrived_refs, refs = (refs[: len(arrived)], refs[len(arrived) :])
        out_ref = refs[-1]
        here = lax.axis_index("tm")
        places = frame_rows(k, pairs, tokens)
        for slot, own_ref in zip(slots, own_refs):

            @pl.when(pick([entry == slot for entry in table], here))
            def _(own_ref=own_ref):
                for p, place in enumerate(places):
                    inner = slice(p * tokens, (p + 1) * tokens)
                    for start in range(0, columns, step):
                        part = slice(start, start + step)
                        total = own_ref[inner, part]
                        for ref in arrived_refs:
                            total += ref[inner, part].astype(jnp.float32)
                        if extras:
                            kept = refs[0][place, part].astype(jnp.float32)
                            total = kept + refs[1][:, part] * total
                        out_ref[inner, part] = total.astype(jnp.bfloat16)

    operands = [partial[slot] for slot in slots] + list(arrived) + extras
    return pl.pallas_call(
        kernel,
        out_shape=jax.ShapeDtypeStruct((rows, columns), jnp.bfloat16),
        in_specs=whole_in_vmem(len(operands)),
        out_specs=whole_in_vmem(1)[0],
        compiler_params=roomy(),
        name="join",
    )(*operands)


def finish(arrived, partial, below, gate, fresh_frame, pairs):
    rows, columns = partial[0].shape
    tokens = rows // pairs
    step = math.gcd(columns, 256)
    sets = len(partial)

    def kernel(*refs):
        arrived_refs, partial_refs, below_refs = (
            refs[:sets],
            refs[sets : 2 * sets],
            refs[2 * sets : 3 * sets],
        )
        gate_ref, fresh_ref, out_ref = refs[3 * sets :]
        last = lax.axis_index("tm") == lax.axis_size("tm") - 1

        @pl.when(last)
        def _():
            out_ref[...] = fresh_ref[...]

        @pl.when(jnp.logical_not(last))
        def _():
            for k in range(sets):
                for p, place in enumerate(frame_rows(k, pairs, tokens)):
                    inner = slice(p * tokens, (p + 1) * tokens)
                    for start in range(0, columns, step):
                        part = slice(start, start + step)
                        total = partial_refs[k][inner, part]
                        total += below_refs[k][inner, part].astype(jnp.float32)
                        total = gate_ref[:, part] * total
                        total += arrived_refs[k][inner, part].astype(jnp.float32)
                        out_ref[place, part] = total.astype(jnp.bfloat16)

    return pl.pallas_call(
        kernel,
        out_shape=jax.ShapeDtypeStruct(fresh_frame.shape, jnp.bfloat16),
        in_specs=whole_in_vmem(3 * sets + 2),
        out_specs=whole_in_vmem(1)[0],
        compiler_params=roomy(),
        name="finish",
    )(*arrived, *partial, *below, gate, fresh_frame)


def line_schedule(frames):
    steps = []
    for step in range(frames - 1):
        down = {z: step + 1 - (frames - 1 - z) for z in range(1, frames)}
        up = {z: frames - 1 - step + z for z in range(frames)}
        down = {z: f for z, f in down.items() if 1 <= f <= z}
        up = {z: f for z, f in up.items() if z + 2 <= f < frames}
        steps.append((down, up))
    order = []
    for z in range(frames):
        sent = [f for down, up in steps for f in (down.get(z), up.get(z)) if f is not None]
        order.append((sent + [z + 1])[: frames - 1])
    return steps, order


def head_plan(
    queries, keys, values, residual, fresh_frame, out_weight, time_weight, noise_steps, frame_mask
):
    frames, across = (lax.axis_size("tm"), lax.axis_size("head"))
    pairs = across // 2
    width = queries.shape[2] // (frames * pairs)
    everywhere = range(frames)

    def swap(array, j):
        return lax.ppermute(array, "head", [(h, h ^ j) for h in range(across)])

    def gather(part, meanwhile=None):
        near = [part]
        for move in range(1, pairs):
            piece = swap(part, 2 * move)
            if meanwhile is not None:
                piece, meanwhile = lax.optimization_barrier((piece, meanwhile))
            near.append(piece)
        return ([near, [swap(piece, 1) for piece in near]], meanwhile)

    far = [(a, b) for b in range(pairs) for a in reversed(everywhere[2:])]
    near = [(0, b) for b in range(pairs)] + [(1, b) for b in range(pairs)]
    moves = near[:-1] + far + near[-1:]
    packed = pack(
        queries[0], keys[0], values[0], frame_mask, noise_steps, moves, pairs, width
    )
    own = []
    for piece, (a, b) in zip(packed, moves):
        if (a, b) != (0, 0):
            links = [
                (z * across + h, (z ^ a) * across + (h ^ (2 * b)))
                for z in everywhere
                for h in range(across)
            ]
            piece = lax.ppermute(piece, ("tm", "head"), links)
        own.append(piece)
    mine = moves.index((0, 0))
    own[mine], weight = bring(own[mine], out_weight)
    mate = [swap(piece, 1) for piece in own]

    steps, order = line_schedule(frames)

    def attend_slot(slot):
        frames_of_slot = [order[z][slot] for z in everywhere]
        return attend(frames_of_slot, own, mate, moves, pairs, frames, width)

    part, _ = attend_slot(0)
    following, notes = attend_slot(1)
    pieces, following = gather(part, following)
    partial, payload = ([[]], [])
    for rows in pieces:
        product, rounded = project([rows], weight)
        partial[0] += product
        payload += rounded
    down, up = steps[0]
    links = [(z, z - 1) for z in down] + [(z, z + 1) for z in up]
    above = [lax.ppermute(part, "tm", links) for part in payload]
    below = above
    own[mine], above[0] = lax.optimization_barrier((own[mine], above[0]))
    for slot in range(1, frames - 1):
        part = following if slot == 1 else attend_slot(slot)[0]
        partial.append(project(gather(part)[0], weight)[0])
    noise = lax.dynamic_slice(notes[:, frame_mask.shape[1]], (lax.axis_index("tm"),), (2,))
    gates = jnp.dot(
        time_features(noise), time_weight.astype(jnp.float32), precision=lax.Precision.HIGHEST
    )

    for number, (down, up) in enumerate(steps[1:], 1):
        sends = {**down, **up}
        table = [order[z].index(sends[z]) if z in sends else 0 for z in everywhere]
        final = number == len(steps) - 1
        extras = (residual[0], gates[:1]) if final else ()
        payload = [
            join(
                [products[k] for products in partial],
                table,
                [above[k]] if final or above is below else [above[k], below[k]],
                k,
                pairs,
                *extras,
            )
            for k in range(2)
        ]
        above = [lax.ppermute(part, "tm", [(z, z - 1) for z in down]) for part in payload]
        if up:
            below = [lax.ppermute(part, "tm", [(z, z + 1) for z in up]) for part in payload]
    return finish(above, partial[-1], below, gates[1:], fresh_frame, pairs)[None]


def power_of_two(number):
    return number & (number - 1) == 0


def suits_line(frames, window):
    apart = all(not set(down) & set(up) for down, up in line_schedule(frames)[0])
    return 2 < frames <= window and power_of_two(frames) and apart


def on_device(queries, *others):
    frames, across = (lax.axis_size("tm"), lax.axis_size("head"))
    heads = queries.shape[2] // HD
    even = across % 2 == 0 and power_of_two(across)
    even = even and queries.shape[1] % 16 == 0
    if even and suits_line(frames, others[-1].shape[1]) and heads % (frames * across // 2) == 0:
        return head_plan(queries, *others)
    return frame_plan(queries, *others)


def solution(mesh):
    placed = (
        P(("groups", "tm"), "head", None),
        P(("groups", "tm"), "head", None),
        P(("groups", "tm"), "head", None),
        P(("groups", "tm"), None, "head"),
        P("groups", "head"),
        P("tm", "head"),
        P(None, "head"),
        P(("groups", "tm")),
        P(("groups", "tm"), None),
    )
    return jax.shard_map(
        on_device,
        mesh=mesh,
        in_specs=placed,
        out_specs=P(("groups", "tm"), None, "head"),
        check_vma=False,
    )
```

```python
import math

import jax
import jax.numpy as jnp
import numpy as np
from jax import lax
from jax.experimental import pallas as pl
from jax.experimental.pallas import tpu as pltpu
from jax.sharding import PartitionSpec as P

HD = 128
FREQ = 256
STEPS = 50
VMEM_BYTES = 16 * 1024 * 1024
PACK_BYTES = 60 * 1024 * 1024


def shifted(value, axis, steps):
    count = lax.axis_size(axis)
    leading, last = (max(0, -steps), min(count, count - steps))
    return lax.ppermute(value, axis, [(source, source + steps) for source in range(leading, last)])


def time_features(noise_steps):
    timestep = 1000.0 * (noise_steps.astype(jnp.float32) + 1.0) / STEPS
    half = FREQ // 2
    rates = jnp.exp(-math.log(10000.0) * jnp.arange(half).astype(jnp.float32) / half)
    angles = timestep[:, None] * rates[None, :]
    return jnp.concatenate([jnp.cos(angles), jnp.sin(angles)], axis=1)


def frame_plan(
    queries, keys, values, residual, fresh_frame, out_weight, time_weight, noise_steps, frame_mask
):
    query_local, key_local, value_local = (
        lax.all_to_all(queries, "head", split_axis=2, concat_axis=1, tiled=True),
        lax.all_to_all(keys, "head", split_axis=2, concat_axis=1, tiled=True),
        lax.all_to_all(values, "head", split_axis=2, concat_axis=1, tiled=True),
    )
    tokens = query_local.shape[1]
    heads_here = query_local.shape[2] // HD
    scale = 1.0 / math.sqrt(HD)
    query_heads = query_local[0].reshape(tokens, heads_here, HD)
    key_value = jnp.stack([key_local[0], value_local[0]], axis=0)
    frame = lax.axis_index("tm")
    frames_total = lax.axis_size("tm")
    window = min(8, frames_total)
    mask_row = frame_mask[0]
    columns = jnp.arange(mask_row.shape[0], dtype=jnp.int32)

    def allowed_at(offset):
        hits = jnp.sum(jnp.where(columns == frame - offset, mask_row, 0))
        return hits > 0

    def absorb(state, block, allowed):
        running_max, weight_sum, accumulated = state
        key_heads = block[0].reshape(tokens, heads_here, HD)
        value_heads = block[1].reshape(tokens, heads_here, HD)
        scores = (
            jnp.einsum("qhd,khd->hqk", query_heads, key_heads, preferred_element_type=jnp.float32)
            * scale
        )
        new_max = jnp.where(allowed, jnp.maximum(running_max, jnp.max(scores, axis=2)), running_max)
        lifted = jnp.where(allowed, jnp.exp(jnp.minimum(scores - new_max[:, :, None], 0.0)), 0.0)
        factor = jnp.exp(running_max - new_max)
        weight_sum = weight_sum * factor + jnp.sum(lifted, axis=2)
        rounded = lifted.astype(jnp.bfloat16)
        accumulated = accumulated * jnp.transpose(factor)[:, :, None] + jnp.einsum(
            "hqk,khd->qhd", rounded, value_heads, preferred_element_type=jnp.float32
        )
        return (new_max, weight_sum, accumulated)

    state = (
        jnp.full((heads_here, tokens), -1e30, jnp.float32),
        jnp.zeros((heads_here, tokens), jnp.float32),
        jnp.zeros((tokens, heads_here, HD), jnp.float32),
    )
    state = absorb(state, key_value, allowed_at(0))
    moving = key_value
    for offset in range(1, window):
        moving = shifted(moving, "tm", 1)
        state = absorb(state, moving, allowed_at(offset))
    running_max, weight_sum, accumulated = state
    attention = (
        (accumulated / jnp.transpose(weight_sum)[:, :, None])
        .reshape(tokens, heads_here * HD)
        .astype(jnp.bfloat16)
    )
    weight_cols = lax.all_gather(out_weight, "tm", axis=0, tiled=True)
    projected = jnp.dot(
        lax.all_gather(attention, "head", axis=1, tiled=True),
        weight_cols,
        preferred_element_type=jnp.float32,
    )
    gate = jnp.dot(
        time_features(noise_steps), time_weight.astype(jnp.float32), precision=lax.Precision.HIGHEST
    )
    updated = (residual[0].astype(jnp.float32) + gate * projected).astype(jnp.bfloat16)
    moved = shifted(updated, "tm", -1)
    rolled = jnp.where(frame == frames_total - 1, fresh_frame, moved)
    return rolled[None]


def whole_in_vmem(count):
    return [pl.BlockSpec(memory_space=pltpu.VMEM)] * count


def in_hbm(count):
    return [pl.BlockSpec(memory_space=pltpu.HBM)] * count


def roomy():
    return pltpu.CompilerParams(vmem_limit_bytes=VMEM_BYTES)


def pack(queries, keys, values, frame_mask, noise_steps, moves, pairs, width):
    tokens = queries.shape[0]
    window = frame_mask.shape[1]
    widths = [3 * width + (HD if b == 0 else 0) for a, b in moves]
    count = len(moves)

    def kernel(*refs):
        sources, small, pieces, scratch = (refs[:3], refs[3:5], refs[5 : 5 + count], refs[5 + count :])
        loaded, packed, mask_ref, noise_ref, in_sems, out_sems = scratch
        frame, pair = (lax.axis_index("tm"), lax.axis_index("head") // 2)
        targets = [loaded.at[place] for place in range(3)] + [mask_ref, noise_ref]
        loads = [
            pltpu.make_async_copy(source, target, in_sems.at[place])
            for place, (source, target) in enumerate(zip((*sources, *small), targets))
        ]
        for load in loads:
            load.start()
        for load in loads:
            load.wait()
        lane = lax.broadcasted_iota(jnp.int32, (tokens, HD), 1)
        note = jnp.where(lane == window, noise_ref[0], 0)
        for column in range(window):
            note = jnp.where(lane == column, mask_ref[0, column], note)
        note = note.astype(jnp.float32).astype(queries.dtype)
        stores = []
        for number, (a, b) in enumerate(moves):
            block = (frame ^ a) * pairs + (pair ^ b)
            columns = pl.ds(pl.multiple_of(block * width, HD), width)
            for place in range(3):
                packed[number, :, place * width : (place + 1) * width] = loaded[place, :, columns]
            if b == 0:
                packed[number, :, 3 * width :] = note
            store = pltpu.make_async_copy(
                packed.at[number, :, : widths[number]], pieces[number], out_sems.at[number]
            )
            store.start()
            stores.append(store)
        for store in stores:
            store.wait()

    return pl.pallas_call(
        kernel,
        out_shape=[jax.ShapeDtypeStruct((tokens, size), queries.dtype) for size in widths],
        in_specs=in_hbm(5),
        out_specs=in_hbm(count),
        scratch_shapes=[
            pltpu.VMEM((3, *queries.shape), queries.dtype),
            pltpu.VMEM((count, tokens, 3 * width + HD), queries.dtype),
            pltpu.SMEM(frame_mask.shape, frame_mask.dtype),
            pltpu.SMEM(noise_steps.shape, noise_steps.dtype),
            pltpu.SemaphoreType.DMA((5,)),
            pltpu.SemaphoreType.DMA((count,)),
        ],
        compiler_params=pltpu.CompilerParams(vmem_limit_bytes=PACK_BYTES),
        name="pack",
    )(queries, keys, values, frame_mask, noise_steps)


def bring(*arrays):
    def kernel(*refs):
        for source, target in zip(refs[: len(arrays)], refs[len(arrays) :]):
            target[...] = source[...]

    return pl.pallas_call(
        kernel,
        out_shape=[jax.ShapeDtypeStruct(array.shape, array.dtype) for array in arrays],
        in_specs=whole_in_vmem(len(arrays)),
        out_specs=whole_in_vmem(len(arrays)),
        compiler_params=roomy(),
        name="bring",
    )(*arrays)


def pick(table, here):
    result = table[0]
    for place, entry in enumerate(table[1:], 1):
        result = jnp.where(here == place, entry, result)
    return result


def attend_frames(slots, out_refs, query_buf, key_buf, value_buf, note_ref):
    frames, keys_rows, width = key_buf.shape
    scale = math.log2(math.e) / math.sqrt(HD)
    here = lax.axis_index("tm")
    for frames_of_slot, out_ref in zip(slots, out_refs):
        frame = pick(frames_of_slot, here)
        note = note_ref[pl.ds(frame, 1), :]
        lane = lax.broadcasted_iota(jnp.int32, note.shape, 1)
        biases = []
        for a in range(frames):
            hit = jnp.sum(jnp.where(lane == here ^ a, note, 0.0), axis=1, keepdims=True)
            biases.append(jnp.broadcast_to((hit - 1.0) * 1e30, (1, keys_rows)))
        bias = jnp.concatenate(biases, axis=1)
        for start in range(0, width, HD):
            channels = slice(start, start + HD)
            query = query_buf[frame, :, channels]
            keys = key_buf[:, :, channels].reshape(frames * keys_rows, HD)
            scores = lax.dot_general(
                query, keys, (((1,), (1,)), ((), ())), preferred_element_type=jnp.float32
            )
            scores = scores * scale + bias
            lifted = jnp.exp2(scores - jnp.max(scores, axis=1, keepdims=True))
            totals = jnp.sum(lifted, axis=1, keepdims=True)
            values = value_buf[:, :, channels].reshape(frames * keys_rows, HD)
            mixed = jnp.dot(
                lifted.astype(jnp.bfloat16), values, preferred_element_type=jnp.float32
            )
            out_ref[:, channels] = (mixed / totals).astype(jnp.bfloat16)


def attend(slots, own, mate, moves, pairs, frames, width):
    tokens = own[0].shape[0]
    rows, keys_rows = (pairs * tokens, 2 * pairs * tokens)

    def kernel(*refs):
        own_refs, refs = (refs[: len(moves)], refs[len(moves) :])
        mate_refs, refs = (refs[: len(moves)], refs[len(moves) :])
        out_refs, (query_buf, key_buf, value_buf, note_out) = (refs[: len(slots)], refs[len(slots) :])
        here = lax.axis_index("tm")
        for own_ref, mate_ref, (a, b) in zip(own_refs, mate_refs, moves):
            query_buf[here ^ a, b * tokens : (b + 1) * tokens, :] = own_ref[:, :width]
            for side, ref in enumerate((own_ref, mate_ref)):
                span = slice((2 * b + side) * tokens, (2 * b + side + 1) * tokens)
                key_buf[a, span, :] = ref[:, width : 2 * width]
                value_buf[a, span, :] = ref[:, 2 * width : 3 * width]
            if b == 0:
                note_out[pl.ds(here ^ a, 1), :] = own_ref[:16, 3 * width :].astype(jnp.float32)[:1]
        attend_frames(slots, out_refs, query_buf, key_buf, value_buf, note_out)

    kind = own[0].dtype
    outs = pl.pallas_call(
        kernel,
        out_shape=[jax.ShapeDtypeStruct((rows, width), jnp.bfloat16)] * len(slots)
        + [
            jax.ShapeDtypeStruct((frames, rows, width), kind),
            jax.ShapeDtypeStruct((frames, keys_rows, width), kind),
            jax.ShapeDtypeStruct((frames, keys_rows, width), kind),
            jax.ShapeDtypeStruct((16, HD), jnp.float32),
        ],
        in_specs=whole_in_vmem(2 * len(moves)),
        out_specs=whole_in_vmem(len(slots) + 4),
        compiler_params=roomy(),
        name="attend",
    )(*own, *mate)
    return (outs[: len(slots)], outs[len(slots) :])


def attend_again(slots, held):
    rows, width = held[0].shape[1:]

    def kernel(*refs):
        attend_frames(slots, refs[len(held) :], *refs[: len(held)])

    return pl.pallas_call(
        kernel,
        out_shape=[jax.ShapeDtypeStruct((rows, width), jnp.bfloat16)] * len(slots),
        in_specs=whole_in_vmem(len(held)),
        out_specs=whole_in_vmem(len(slots)),
        compiler_params=roomy(),
        name="attend_again",
    )(*held)


def project(pieces, weight, kinds):
    flat = [piece for part in pieces for piece in part]
    rows, width = flat[0].shape
    pairs = len(pieces[0])
    tokens = rows // pairs
    depth, columns = weight.shape
    step = math.gcd(columns, 256)

    def kernel(*refs):
        sources = iter(refs[: len(flat)])
        weight_ref, refs = (refs[len(flat)], refs[len(flat) + 1 :])
        whole = refs[-1]
        here = lax.axis_index("head") // 2
        for k, part in enumerate(pieces):
            for move in range(pairs):
                source = next(sources)
                pair = here ^ move
                channels = pl.ds(pl.multiple_of(pair * width, HD), width)
                for b in range(pairs):
                    first = k * rows + (pair ^ b) * tokens
                    whole[pl.ds(pl.multiple_of(first, 16), tokens), channels] = source[
                        b * tokens : (b + 1) * tokens, :
                    ]

        @pl.loop(0, columns // step)
        def _(number):
            inner = pl.ds(pl.multiple_of(number * step, HD), step)
            product = jnp.dot(
                whole[...], weight_ref[:, inner], preferred_element_type=jnp.float32
            )
            for k in range(len(pieces)):
                share = product[k * rows : (k + 1) * rows, :]
                for out_ref in refs[k * len(kinds) : (k + 1) * len(kinds)]:
                    out_ref[:, inner] = share.astype(out_ref.dtype)

    outs = pl.pallas_call(
        kernel,
        out_shape=[
            jax.ShapeDtypeStruct((rows, columns), kind)
            for _ in pieces
            for kind in kinds
        ],
        in_specs=whole_in_vmem(len(flat) + 1),
        out_specs=whole_in_vmem(len(kinds) * len(pieces)),
        scratch_shapes=[pltpu.VMEM((len(pieces) * rows, depth), jnp.bfloat16)],
        compiler_params=roomy(),
        name="project",
    )(*flat, weight)
    return [list(outs[number :: len(kinds)]) for number in range(len(kinds))]


def frame_rows(k, pairs, tokens):
    core = (lax.axis_index("head") % 2) ^ k
    return [pl.ds(pl.multiple_of((2 * p + core) * tokens, 16), tokens) for p in range(pairs)]


def join(partial, table, arrived, k, pairs, residual=None, gate=None):
    rows, columns = partial[0].shape
    tokens = rows // pairs
    step = math.gcd(columns, 256)
    slots = sorted(set(table))
    extras = [] if residual is None else [residual, gate]

    def kernel(*refs):
        own_refs, refs = (refs[: len(slots)], refs[len(slots) :])
        arrived_refs, refs = (refs[: len(arrived)], refs[len(arrived) :])
        out_ref = refs[-1]
        here = lax.axis_index("tm")
        places = frame_rows(k, pairs, tokens)
        for slot, own_ref in zip(slots, own_refs):

            @pl.when(pick([entry == slot for entry in table], here))
            def _(own_ref=own_ref):
                for p, place in enumerate(places):
                    inner = slice(p * tokens, (p + 1) * tokens)
                    for start in range(0, columns, step):
                        part = slice(start, start + step)
                        total = own_ref[inner, part]
                        for ref in arrived_refs:
                            total += ref[inner, part].astype(jnp.float32)
                        if extras:
                            kept = refs[0][place, part].astype(jnp.float32)
                            total = kept + refs[1][:, part] * total
                        out_ref[inner, part] = total.astype(jnp.bfloat16)

    operands = [partial[slot] for slot in slots] + list(arrived) + extras
    return pl.pallas_call(
        kernel,
        out_shape=jax.ShapeDtypeStruct((rows, columns), jnp.bfloat16),
        in_specs=whole_in_vmem(len(operands)),
        out_specs=whole_in_vmem(1)[0],
        compiler_params=roomy(),
        name="join",
    )(*operands)


def finish(arrived, partial, below, gate, fresh_frame, pairs):
    rows, columns = partial[0].shape
    tokens = rows // pairs
    step = math.gcd(columns, 256)
    sets = len(partial)

    def kernel(*refs):
        arrived_refs, partial_refs, below_refs = (
            refs[:sets],
            refs[sets : 2 * sets],
            refs[2 * sets : 3 * sets],
        )
        gate_ref, fresh_ref, out_ref = refs[3 * sets :]
        last = lax.axis_index("tm") == lax.axis_size("tm") - 1

        @pl.when(last)
        def _():
            out_ref[...] = fresh_ref[...]

        @pl.when(jnp.logical_not(last))
        def _():
            for k in range(sets):
                for p, place in enumerate(frame_rows(k, pairs, tokens)):
                    inner = slice(p * tokens, (p + 1) * tokens)
                    for start in range(0, columns, step):
                        part = slice(start, start + step)
                        total = partial_refs[k][inner, part]
                        total += below_refs[k][inner, part].astype(jnp.float32)
                        total = gate_ref[:, part] * total
                        total += arrived_refs[k][inner, part].astype(jnp.float32)
                        out_ref[place, part] = total.astype(jnp.bfloat16)

    return pl.pallas_call(
        kernel,
        out_shape=jax.ShapeDtypeStruct(fresh_frame.shape, jnp.bfloat16),
        in_specs=whole_in_vmem(3 * sets + 2),
        out_specs=whole_in_vmem(1)[0],
        compiler_params=roomy(),
        name="finish",
    )(*arrived, *partial, *below, gate, fresh_frame)


def line_schedule(frames):
    steps = []
    for step in range(frames - 1):
        down = {z: step + 1 - (frames - 1 - z) for z in range(1, frames)}
        up = {z: frames - 1 - step + z for z in range(frames)}
        down = {z: f for z, f in down.items() if 1 <= f <= z}
        up = {z: f for z, f in up.items() if z + 2 <= f < frames}
        steps.append((down, up))
    order = []
    for z in range(frames):
        sent = [f for down, up in steps for f in (down.get(z), up.get(z)) if f is not None]
        order.append((sent + [z + 1])[: frames - 1])
    return steps, order


def head_plan(
    queries, keys, values, residual, fresh_frame, out_weight, time_weight, noise_steps, frame_mask
):
    frames, across = (lax.axis_size("tm"), lax.axis_size("head"))
    pairs = across // 2
    width = queries.shape[2] // (frames * pairs)
    everywhere = range(frames)

    def swap(array, j):
        return lax.ppermute(array, "head", [(h, h ^ j) for h in range(across)])

    def gather(part, meanwhile=None):
        near = [part]
        for move in range(1, pairs):
            piece = swap(part, 2 * move)
            if meanwhile is not None:
                piece, meanwhile = lax.optimization_barrier((piece, meanwhile))
            near.append(piece)
        return ([near, [swap(piece, 1) for piece in near]], meanwhile)

    far = [(a, b) for b in range(pairs) for a in reversed(everywhere[2:])]
    near = [(0, b) for b in range(pairs)] + [(1, b) for b in range(pairs)]
    moves = near[:-1] + far + near[-1:]
    packed = pack(
        queries[0], keys[0], values[0], frame_mask, noise_steps, moves, pairs, width
    )
    own = []
    for piece, (a, b) in zip(packed, moves):
        if (a, b) != (0, 0):
            links = [
                (z * across + h, (z ^ a) * across + (h ^ (2 * b)))
                for z in everywhere
                for h in range(across)
            ]
            piece = lax.ppermute(piece, ("tm", "head"), links)
        own.append(piece)
    mine = moves.index((0, 0))
    (own[mine],), weight = (bring(own[mine]), out_weight)
    mate = [swap(piece, 1) for piece in own]

    steps, order = line_schedule(frames)

    named = [[order[z][slot] for z in everywhere] for slot in range(frames - 1)]
    (part,), held = attend(named[:1], own, mate, moves, pairs, frames, width)
    following = attend_again(named[1:], held)
    notes = held[-1]
    pieces, following = gather(part, following)
    partial, payload = ([[]], [])
    for rows in pieces:
        product, rounded = project([rows], weight, (jnp.float32, jnp.bfloat16))
        partial[0] += product
        payload += rounded
    down, up = steps[0]
    links = [(z, z - 1) for z in down] + [(z, z + 1) for z in up]
    above = [lax.ppermute(part, "tm", links) for part in payload]
    below = above
    for part in following:
        partial.append(project(gather(part)[0], weight, (jnp.float32,))[0])
    noise = lax.dynamic_slice(notes[:, frame_mask.shape[1]], (lax.axis_index("tm"),), (2,))
    gates = jnp.dot(
        time_features(noise), time_weight.astype(jnp.float32), precision=lax.Precision.HIGHEST
    )

    for number, (down, up) in enumerate(steps[1:], 1):
        sends = {**down, **up}
        table = [order[z].index(sends[z]) if z in sends else 0 for z in everywhere]
        final = number == len(steps) - 1
        extras = (residual[0], gates[:1]) if final else ()
        payload = [
            join(
                [products[k] for products in partial],
                table,
                [above[k]] if final or above is below else [above[k], below[k]],
                k,
                pairs,
                *extras,
            )
            for k in range(2)
        ]
        above = [lax.ppermute(part, "tm", [(z, z - 1) for z in down]) for part in payload]
        if up:
            below = [lax.ppermute(part, "tm", [(z, z + 1) for z in up]) for part in payload]
    return finish(above, partial[-1], below, gates[1:], fresh_frame, pairs)[None]


def power_of_two(number):
    return number & (number - 1) == 0


def suits_line(frames, window):
    apart = all(not set(down) & set(up) for down, up in line_schedule(frames)[0])
    return 2 < frames <= window and power_of_two(frames) and apart


def on_device(queries, *others):
    frames, across = (lax.axis_size("tm"), lax.axis_size("head"))
    heads = queries.shape[2] // HD
    even = across % 2 == 0 and power_of_two(across)
    even = even and queries.shape[1] % 16 == 0
    if even and suits_line(frames, others[-1].shape[1]) and heads % (frames * across // 2) == 0:
        return head_plan(queries, *others)
    return frame_plan(queries, *others)


def solution(mesh):
    placed = (
        P(("groups", "tm"), "head", None),
        P(("groups", "tm"), "head", None),
        P(("groups", "tm"), "head", None),
        P(("groups", "tm"), None, "head"),
        P("groups", "head"),
        P("tm", "head"),
        P(None, "head"),
        P(("groups", "tm")),
        P(("groups", "tm"), None),
    )
    return jax.shard_map(
        on_device,
        mesh=mesh,
        in_specs=placed,
        out_specs=P(("groups", "tm"), None, "head"),
        check_vma=False,
    )
```

```python
import math

import jax
import jax.numpy as jnp
import numpy as np
from jax import lax
from jax.experimental import pallas as pl
from jax.experimental.pallas import tpu as pltpu
from jax.sharding import PartitionSpec as P

HD = 128
FREQ = 256
STEPS = 50
VMEM_BYTES = 16 * 1024 * 1024
PACK_BYTES = 60 * 1024 * 1024


def shifted(value, axis, steps):
    count = lax.axis_size(axis)
    leading, last = (max(0, -steps), min(count, count - steps))
    return lax.ppermute(value, axis, [(source, source + steps) for source in range(leading, last)])


def time_features(noise_steps):
    timestep = 1000.0 * (noise_steps.astype(jnp.float32) + 1.0) / STEPS
    half = FREQ // 2
    rates = jnp.exp(-math.log(10000.0) * jnp.arange(half).astype(jnp.float32) / half)
    angles = timestep[:, None] * rates[None, :]
    return jnp.concatenate([jnp.cos(angles), jnp.sin(angles)], axis=1)


def frame_plan(
    queries, keys, values, residual, fresh_frame, out_weight, time_weight, noise_steps, frame_mask
):
    query_local, key_local, value_local = (
        lax.all_to_all(queries, "head", split_axis=2, concat_axis=1, tiled=True),
        lax.all_to_all(keys, "head", split_axis=2, concat_axis=1, tiled=True),
        lax.all_to_all(values, "head", split_axis=2, concat_axis=1, tiled=True),
    )
    tokens = query_local.shape[1]
    heads_here = query_local.shape[2] // HD
    scale = 1.0 / math.sqrt(HD)
    query_heads = query_local[0].reshape(tokens, heads_here, HD)
    key_value = jnp.stack([key_local[0], value_local[0]], axis=0)
    frame = lax.axis_index("tm")
    frames_total = lax.axis_size("tm")
    window = min(8, frames_total)
    mask_row = frame_mask[0]
    columns = jnp.arange(mask_row.shape[0], dtype=jnp.int32)

    def allowed_at(offset):
        hits = jnp.sum(jnp.where(columns == frame - offset, mask_row, 0))
        return hits > 0

    def absorb(state, block, allowed):
        running_max, weight_sum, accumulated = state
        key_heads = block[0].reshape(tokens, heads_here, HD)
        value_heads = block[1].reshape(tokens, heads_here, HD)
        scores = (
            jnp.einsum("qhd,khd->hqk", query_heads, key_heads, preferred_element_type=jnp.float32)
            * scale
        )
        new_max = jnp.where(allowed, jnp.maximum(running_max, jnp.max(scores, axis=2)), running_max)
        lifted = jnp.where(allowed, jnp.exp(jnp.minimum(scores - new_max[:, :, None], 0.0)), 0.0)
        factor = jnp.exp(running_max - new_max)
        weight_sum = weight_sum * factor + jnp.sum(lifted, axis=2)
        rounded = lifted.astype(jnp.bfloat16)
        accumulated = accumulated * jnp.transpose(factor)[:, :, None] + jnp.einsum(
            "hqk,khd->qhd", rounded, value_heads, preferred_element_type=jnp.float32
        )
        return (new_max, weight_sum, accumulated)

    state = (
        jnp.full((heads_here, tokens), -1e30, jnp.float32),
        jnp.zeros((heads_here, tokens), jnp.float32),
        jnp.zeros((tokens, heads_here, HD), jnp.float32),
    )
    state = absorb(state, key_value, allowed_at(0))
    moving = key_value
    for offset in range(1, window):
        moving = shifted(moving, "tm", 1)
        state = absorb(state, moving, allowed_at(offset))
    running_max, weight_sum, accumulated = state
    attention = (
        (accumulated / jnp.transpose(weight_sum)[:, :, None])
        .reshape(tokens, heads_here * HD)
        .astype(jnp.bfloat16)
    )
    weight_cols = lax.all_gather(out_weight, "tm", axis=0, tiled=True)
    projected = jnp.dot(
        lax.all_gather(attention, "head", axis=1, tiled=True),
        weight_cols,
        preferred_element_type=jnp.float32,
    )
    gate = jnp.dot(
        time_features(noise_steps), time_weight.astype(jnp.float32), precision=lax.Precision.HIGHEST
    )
    updated = (residual[0].astype(jnp.float32) + gate * projected).astype(jnp.bfloat16)
    moved = shifted(updated, "tm", -1)
    rolled = jnp.where(frame == frames_total - 1, fresh_frame, moved)
    return rolled[None]


def whole_in_vmem(count):
    return [pl.BlockSpec(memory_space=pltpu.VMEM)] * count


def in_hbm(count):
    return [pl.BlockSpec(memory_space=pltpu.HBM)] * count


def roomy():
    return pltpu.CompilerParams(vmem_limit_bytes=VMEM_BYTES)


def pack(queries, keys, values, frame_mask, noise_steps, moves, pairs, width):
    tokens = queries.shape[0]
    window = frame_mask.shape[1]
    widths = [3 * width + (HD if b == 0 else 0) for a, b in moves]
    count = len(moves)

    def kernel(*refs):
        sources, small, pieces, scratch = (refs[:3], refs[3:5], refs[5 : 5 + count], refs[5 + count :])
        loaded, packed, mask_ref, noise_ref, in_sems, out_sems = scratch
        frame, pair = (lax.axis_index("tm"), lax.axis_index("head") // 2)
        targets = [loaded.at[place] for place in range(3)] + [mask_ref, noise_ref]
        loads = [
            pltpu.make_async_copy(source, target, in_sems.at[place])
            for place, (source, target) in enumerate(zip((*sources, *small), targets))
        ]
        for load in loads:
            load.start()
        for load in loads:
            load.wait()
        lane = lax.broadcasted_iota(jnp.int32, (tokens, HD), 1)
        note = jnp.where(lane == window, noise_ref[0], 0)
        for column in range(window):
            note = jnp.where(lane == column, mask_ref[0, column], note)
        note = note.astype(jnp.float32).astype(queries.dtype)
        stores = []
        for number, (a, b) in enumerate(moves):
            block = (frame ^ a) * pairs + (pair ^ b)
            columns = pl.ds(pl.multiple_of(block * width, HD), width)
            for place in range(3):
                packed[number, :, place * width : (place + 1) * width] = loaded[place, :, columns]
            if b == 0:
                packed[number, :, 3 * width :] = note
            store = pltpu.make_async_copy(
                packed.at[number, :, : widths[number]], pieces[number], out_sems.at[number]
            )
            store.start()
            stores.append(store)
        for store in stores:
            store.wait()

    return pl.pallas_call(
        kernel,
        out_shape=[jax.ShapeDtypeStruct((tokens, size), queries.dtype) for size in widths],
        in_specs=in_hbm(5),
        out_specs=in_hbm(count),
        scratch_shapes=[
            pltpu.VMEM((3, *queries.shape), queries.dtype),
            pltpu.VMEM((count, tokens, 3 * width + HD), queries.dtype),
            pltpu.SMEM(frame_mask.shape, frame_mask.dtype),
            pltpu.SMEM(noise_steps.shape, noise_steps.dtype),
            pltpu.SemaphoreType.DMA((5,)),
            pltpu.SemaphoreType.DMA((count,)),
        ],
        compiler_params=pltpu.CompilerParams(vmem_limit_bytes=PACK_BYTES),
        name="pack",
    )(queries, keys, values, frame_mask, noise_steps)


def bring(*arrays):
    def kernel(*refs):
        for source, target in zip(refs[: len(arrays)], refs[len(arrays) :]):
            target[...] = source[...]

    return pl.pallas_call(
        kernel,
        out_shape=[jax.ShapeDtypeStruct(array.shape, array.dtype) for array in arrays],
        in_specs=whole_in_vmem(len(arrays)),
        out_specs=whole_in_vmem(len(arrays)),
        compiler_params=roomy(),
        name="bring",
    )(*arrays)


def pick(table, here):
    result = table[0]
    for place, entry in enumerate(table[1:], 1):
        result = jnp.where(here == place, entry, result)
    return result


def attend_frames(slots, out_refs, query_buf, key_buf, value_buf, note_ref):
    frames, keys_rows, width = key_buf.shape
    scale = math.log2(math.e) / math.sqrt(HD)
    here = lax.axis_index("tm")
    for frames_of_slot, out_ref in zip(slots, out_refs):
        frame = pick(frames_of_slot, here)
        note = note_ref[pl.ds(frame, 1), :]
        lane = lax.broadcasted_iota(jnp.int32, note.shape, 1)
        biases = []
        for a in range(frames):
            hit = jnp.sum(jnp.where(lane == here ^ a, note, 0.0), axis=1, keepdims=True)
            biases.append(jnp.broadcast_to((hit - 1.0) * 1e30, (1, keys_rows)))
        bias = jnp.concatenate(biases, axis=1)
        for start in range(0, width, HD):
            channels = slice(start, start + HD)
            query = query_buf[frame, :, channels]
            keys = key_buf[:, :, channels].reshape(frames * keys_rows, HD)
            scores = lax.dot_general(
                query, keys, (((1,), (1,)), ((), ())), preferred_element_type=jnp.float32
            )
            scores = scores * scale + bias
            lifted = jnp.exp2(scores - jnp.max(scores, axis=1, keepdims=True))
            totals = jnp.sum(lifted, axis=1, keepdims=True)
            values = value_buf[:, :, channels].reshape(frames * keys_rows, HD)
            mixed = jnp.dot(
                lifted.astype(jnp.bfloat16), values, preferred_element_type=jnp.float32
            )
            out_ref[:, channels] = (mixed / totals).astype(jnp.bfloat16)


def attend(slots, own, mate, moves, pairs, frames, width):
    tokens = own[0].shape[0]
    rows, keys_rows = (pairs * tokens, 2 * pairs * tokens)

    def kernel(*refs):
        own_refs, refs = (refs[: len(moves)], refs[len(moves) :])
        mate_refs, refs = (refs[: len(moves)], refs[len(moves) :])
        out_refs, (query_buf, key_buf, value_buf, note_out) = (refs[: len(slots)], refs[len(slots) :])
        here = lax.axis_index("tm")
        for own_ref, mate_ref, (a, b) in zip(own_refs, mate_refs, moves):
            query_buf[here ^ a, b * tokens : (b + 1) * tokens, :] = own_ref[:, :width]
            for side, ref in enumerate((own_ref, mate_ref)):
                span = slice((2 * b + side) * tokens, (2 * b + side + 1) * tokens)
                key_buf[a, span, :] = ref[:, width : 2 * width]
                value_buf[a, span, :] = ref[:, 2 * width : 3 * width]
            if b == 0:
                note_out[pl.ds(here ^ a, 1), :] = own_ref[:16, 3 * width :].astype(jnp.float32)[:1]
        attend_frames(slots, out_refs, query_buf, key_buf, value_buf, note_out)

    kind = own[0].dtype
    outs = pl.pallas_call(
        kernel,
        out_shape=[jax.ShapeDtypeStruct((rows, width), jnp.bfloat16)] * len(slots)
        + [
            jax.ShapeDtypeStruct((frames, rows, width), kind),
            jax.ShapeDtypeStruct((frames, keys_rows, width), kind),
            jax.ShapeDtypeStruct((frames, keys_rows, width), kind),
            jax.ShapeDtypeStruct((16, HD), jnp.float32),
        ],
        in_specs=whole_in_vmem(2 * len(moves)),
        out_specs=whole_in_vmem(len(slots) + 4),
        compiler_params=roomy(),
        name="attend",
    )(*own, *mate)
    return (outs[: len(slots)], outs[len(slots) :])


def attend_again(slots, held):
    rows, width = held[0].shape[1:]

    def kernel(*refs):
        attend_frames(slots, refs[len(held) :], *refs[: len(held)])

    return pl.pallas_call(
        kernel,
        out_shape=[jax.ShapeDtypeStruct((rows, width), jnp.bfloat16)] * len(slots),
        in_specs=whole_in_vmem(len(held)),
        out_specs=whole_in_vmem(len(slots)),
        compiler_params=roomy(),
        name="attend_again",
    )(*held)


def project(pieces, weight, kinds):
    flat = [piece for part in pieces for piece in part]
    rows, width = flat[0].shape
    pairs = len(pieces[0])
    tokens = rows // pairs
    depth, columns = weight.shape
    step = math.gcd(columns, 256)

    def kernel(*refs):
        sources = iter(refs[: len(flat)])
        weight_ref, refs = (refs[len(flat)], refs[len(flat) + 1 :])
        whole = refs[-1]
        here = lax.axis_index("head") // 2
        for k, part in enumerate(pieces):
            for move in range(pairs):
                source = next(sources)
                pair = here ^ move
                channels = pl.ds(pl.multiple_of(pair * width, HD), width)
                for b in range(pairs):
                    first = k * rows + (pair ^ b) * tokens
                    whole[pl.ds(pl.multiple_of(first, 16), tokens), channels] = source[
                        b * tokens : (b + 1) * tokens, :
                    ]
        for start in range(0, columns, step):
            inner = slice(start, start + step)
            product = jnp.dot(
                whole[...], weight_ref[:, inner], preferred_element_type=jnp.float32
            )
            for k in range(len(pieces)):
                share = product[k * rows : (k + 1) * rows, :]
                for out_ref in refs[k * len(kinds) : (k + 1) * len(kinds)]:
                    out_ref[:, inner] = share.astype(out_ref.dtype)

    outs = pl.pallas_call(
        kernel,
        out_shape=[
            jax.ShapeDtypeStruct((rows, columns), kind)
            for _ in pieces
            for kind in kinds
        ],
        in_specs=whole_in_vmem(len(flat) + 1),
        out_specs=whole_in_vmem(len(kinds) * len(pieces)),
        scratch_shapes=[pltpu.VMEM((len(pieces) * rows, depth), jnp.bfloat16)],
        compiler_params=roomy(),
        name="project",
    )(*flat, weight)
    return [list(outs[number :: len(kinds)]) for number in range(len(kinds))]


def gates_of(notes, time_weight, column, frames):
    depth, columns = time_weight.shape
    half = depth // 2

    def kernel(note_ref, weight_ref, here_ref, next_ref):
        here = lax.axis_index("tm")
        following = jnp.minimum(here + 1, frames - 1)
        rows = jnp.concatenate([note_ref[pl.ds(here, 1), :], note_ref[pl.ds(following, 1), :]], axis=0)
        lane = lax.broadcasted_iota(jnp.int32, rows.shape, 1)
        noise = jnp.sum(jnp.where(lane == column, rows, 0.0), axis=1, keepdims=True)
        timestep = 1000.0 * (noise + 1.0) / STEPS
        place = lax.broadcasted_iota(jnp.int32, (2, half), 1).astype(jnp.float32)
        angles = timestep * jnp.exp(-math.log(10000.0) * place / half)
        features = jnp.concatenate([jnp.cos(angles), jnp.sin(angles)], axis=1)
        gates = jnp.dot(
            features,
            weight_ref[...].astype(jnp.float32),
            precision=lax.Precision.HIGHEST,
            preferred_element_type=jnp.float32,
        )
        here_ref[...] = gates[:1]
        next_ref[...] = gates[1:]

    return pl.pallas_call(
        kernel,
        out_shape=[jax.ShapeDtypeStruct((1, columns), jnp.float32)] * 2,
        in_specs=whole_in_vmem(2),
        out_specs=whole_in_vmem(2),
        compiler_params=roomy(),
        name="gates_of",
    )(notes, time_weight)


def frame_rows(k, pairs, tokens):
    core = (lax.axis_index("head") % 2) ^ k
    return [pl.ds(pl.multiple_of((2 * p + core) * tokens, 16), tokens) for p in range(pairs)]


def join(partial, table, arrived, k, pairs, residual=None, gate=None):
    rows, columns = partial[0].shape
    tokens = rows // pairs
    step = math.gcd(columns, 256)
    slots = sorted(set(table))
    extras = [] if residual is None else [residual, gate]

    def kernel(*refs):
        own_refs, refs = (refs[: len(slots)], refs[len(slots) :])
        arrived_refs, refs = (refs[: len(arrived)], refs[len(arrived) :])
        out_ref = refs[-1]
        here = lax.axis_index("tm")
        places = frame_rows(k, pairs, tokens)
        for slot, own_ref in zip(slots, own_refs):

            @pl.when(pick([entry == slot for entry in table], here))
            def _(own_ref=own_ref):
                for p, place in enumerate(places):
                    inner = slice(p * tokens, (p + 1) * tokens)
                    for start in range(0, columns, step):
                        part = slice(start, start + step)
                        total = own_ref[inner, part]
                        for ref in arrived_refs:
                            total += ref[inner, part].astype(jnp.float32)
                        if extras:
                            kept = refs[0][place, part].astype(jnp.float32)
                            total = kept + refs[1][:, part] * total
                        out_ref[inner, part] = total.astype(jnp.bfloat16)

    operands = [partial[slot] for slot in slots] + list(arrived) + extras
    return pl.pallas_call(
        kernel,
        out_shape=jax.ShapeDtypeStruct((rows, columns), jnp.bfloat16),
        in_specs=whole_in_vmem(len(operands)),
        out_specs=whole_in_vmem(1)[0],
        compiler_params=roomy(),
        name="join",
    )(*operands)


def finish(arrived, partial, below, gate, fresh_frame, pairs):
    rows, columns = partial[0].shape
    tokens = rows // pairs
    step = math.gcd(columns, 256)
    sets = len(partial)

    def kernel(*refs):
        arrived_refs, partial_refs, below_refs = (
            refs[:sets],
            refs[sets : 2 * sets],
            refs[2 * sets : 3 * sets],
        )
        gate_ref, fresh_ref, out_ref = refs[3 * sets :]
        last = lax.axis_index("tm") == lax.axis_size("tm") - 1

        @pl.when(last)
        def _():
            out_ref[...] = fresh_ref[...]

        @pl.when(jnp.logical_not(last))
        def _():
            for k in range(sets):
                for p, place in enumerate(frame_rows(k, pairs, tokens)):
                    inner = slice(p * tokens, (p + 1) * tokens)
                    for start in range(0, columns, step):
                        part = slice(start, start + step)
                        total = partial_refs[k][inner, part]
                        total += below_refs[k][inner, part].astype(jnp.float32)
                        total = gate_ref[:, part] * total
                        total += arrived_refs[k][inner, part].astype(jnp.float32)
                        out_ref[place, part] = total.astype(jnp.bfloat16)

    return pl.pallas_call(
        kernel,
        out_shape=jax.ShapeDtypeStruct(fresh_frame.shape, jnp.bfloat16),
        in_specs=whole_in_vmem(3 * sets + 2),
        out_specs=whole_in_vmem(1)[0],
        compiler_params=roomy(),
        name="finish",
    )(*arrived, *partial, *below, gate, fresh_frame)


def line_schedule(frames):
    steps = []
    for step in range(frames - 1):
        down = {z: step + 1 - (frames - 1 - z) for z in range(1, frames)}
        up = {z: frames - 1 - step + z for z in range(frames)}
        down = {z: f for z, f in down.items() if 1 <= f <= z}
        up = {z: f for z, f in up.items() if z + 2 <= f < frames}
        steps.append((down, up))
    order = []
    for z in range(frames):
        sent = [f for down, up in steps for f in (down.get(z), up.get(z)) if f is not None]
        order.append((sent + [z + 1])[: frames - 1])
    return steps, order


def head_plan(
    queries, keys, values, residual, fresh_frame, out_weight, time_weight, noise_steps, frame_mask
):
    frames, across = (lax.axis_size("tm"), lax.axis_size("head"))
    pairs = across // 2
    width = queries.shape[2] // (frames * pairs)
    everywhere = range(frames)

    def swap(array, j):
        return lax.ppermute(array, "head", [(h, h ^ j) for h in range(across)])

    def gather(part, meanwhile=None):
        near = [part]
        for move in range(1, pairs):
            piece = swap(part, 2 * move)
            if meanwhile is not None:
                piece, meanwhile = lax.optimization_barrier((piece, meanwhile))
            near.append(piece)
        return ([near, [swap(piece, 1) for piece in near]], meanwhile)

    far = [(a, b) for b in range(pairs) for a in reversed(everywhere[2:])]
    near = [(0, b) for b in range(pairs)] + [(1, b) for b in range(pairs)]
    moves = near[:-1] + far + near[-1:]
    packed = pack(
        queries[0], keys[0], values[0], frame_mask, noise_steps, moves, pairs, width
    )
    own = []
    for piece, (a, b) in zip(packed, moves):
        if (a, b) == near[-1]:
            piece, own[1] = lax.optimization_barrier((piece, own[1]))
        if (a, b) != (0, 0):
            links = [
                (z * across + h, (z ^ a) * across + (h ^ (2 * b)))
                for z in everywhere
                for h in range(across)
            ]
            piece = lax.ppermute(piece, ("tm", "head"), links)
        own.append(piece)
    mine = moves.index((0, 0))
    (own[mine],), weight = (bring(own[mine]), out_weight)
    mate = [swap(piece, 1) for piece in own]

    steps, order = line_schedule(frames)

    named = [[order[z][slot] for z in everywhere] for slot in range(frames - 1)]
    (part,), held = attend(named[:1], own, mate, moves, pairs, frames, width)
    following = attend_again(named[1:], held)
    pieces, following = gather(part, following)
    partial, payload = ([[]], [])
    for rows in pieces:
        product, rounded = project([rows], weight, (jnp.float32, jnp.bfloat16))
        partial[0] += product
        payload += rounded
    down, up = steps[0]
    links = [(z, z - 1) for z in down] + [(z, z + 1) for z in up]
    above = [lax.ppermute(part, "tm", links) for part in payload]
    below = above
    for part in following:
        partial.append(project(gather(part)[0], weight, (jnp.float32,))[0])
    gates = gates_of(held[-1], time_weight, frame_mask.shape[1], frames)

    for number, (down, up) in enumerate(steps[1:], 1):
        sends = {**down, **up}
        table = [order[z].index(sends[z]) if z in sends else 0 for z in everywhere]
        final = number == len(steps) - 1
        extras = (residual[0], gates[0]) if final else ()
        payload = [
            join(
                [products[k] for products in partial],
                table,
                [above[k]] if final or above is below else [above[k], below[k]],
                k,
                pairs,
                *extras,
            )
            for k in range(2)
        ]
        above = [lax.ppermute(part, "tm", [(z, z - 1) for z in down]) for part in payload]
        if up:
            below = [lax.ppermute(part, "tm", [(z, z + 1) for z in up]) for part in payload]
    return finish(above, partial[-1], below, gates[1], fresh_frame, pairs)[None]


def power_of_two(number):
    return number & (number - 1) == 0


def suits_line(frames, window):
    apart = all(not set(down) & set(up) for down, up in line_schedule(frames)[0])
    return 2 < frames <= window and power_of_two(frames) and apart


def on_device(queries, *others):
    frames, across = (lax.axis_size("tm"), lax.axis_size("head"))
    heads = queries.shape[2] // HD
    even = across % 2 == 0 and power_of_two(across)
    even = even and queries.shape[1] % 16 == 0
    if even and suits_line(frames, others[-1].shape[1]) and heads % (frames * across // 2) == 0:
        return head_plan(queries, *others)
    return frame_plan(queries, *others)


def solution(mesh):
    placed = (
        P(("groups", "tm"), "head", None),
        P(("groups", "tm"), "head", None),
        P(("groups", "tm"), "head", None),
        P(("groups", "tm"), None, "head"),
        P("groups", "head"),
        P("tm", "head"),
        P(None, "head"),
        P(("groups", "tm")),
        P(("groups", "tm"), None),
    )
    return jax.shard_map(
        on_device,
        mesh=mesh,
        in_specs=placed,
        out_specs=P(("groups", "tm"), None, "head"),
        check_vma=False,
    )
```

```python
import math

import jax
import jax.numpy as jnp
import numpy as np
from jax import lax
from jax.experimental import pallas as pl
from jax.experimental.pallas import tpu as pltpu
from jax.sharding import PartitionSpec as P

HD = 128
FREQ = 256
STEPS = 50
VMEM_BYTES = 16 * 1024 * 1024
PACK_BYTES = 60 * 1024 * 1024


def shifted(value, axis, steps):
    count = lax.axis_size(axis)
    leading, last = (max(0, -steps), min(count, count - steps))
    return lax.ppermute(value, axis, [(source, source + steps) for source in range(leading, last)])


def time_features(noise_steps):
    timestep = 1000.0 * (noise_steps.astype(jnp.float32) + 1.0) / STEPS
    half = FREQ // 2
    rates = jnp.exp(-math.log(10000.0) * jnp.arange(half).astype(jnp.float32) / half)
    angles = timestep[:, None] * rates[None, :]
    return jnp.concatenate([jnp.cos(angles), jnp.sin(angles)], axis=1)


def frame_plan(
    queries, keys, values, residual, fresh_frame, out_weight, time_weight, noise_steps, frame_mask
):
    query_local, key_local, value_local = (
        lax.all_to_all(queries, "head", split_axis=2, concat_axis=1, tiled=True),
        lax.all_to_all(keys, "head", split_axis=2, concat_axis=1, tiled=True),
        lax.all_to_all(values, "head", split_axis=2, concat_axis=1, tiled=True),
    )
    tokens = query_local.shape[1]
    heads_here = query_local.shape[2] // HD
    scale = 1.0 / math.sqrt(HD)
    query_heads = query_local[0].reshape(tokens, heads_here, HD)
    key_value = jnp.stack([key_local[0], value_local[0]], axis=0)
    frame = lax.axis_index("tm")
    frames_total = lax.axis_size("tm")
    window = min(8, frames_total)
    mask_row = frame_mask[0]
    columns = jnp.arange(mask_row.shape[0], dtype=jnp.int32)

    def allowed_at(offset):
        hits = jnp.sum(jnp.where(columns == frame - offset, mask_row, 0))
        return hits > 0

    def absorb(state, block, allowed):
        running_max, weight_sum, accumulated = state
        key_heads = block[0].reshape(tokens, heads_here, HD)
        value_heads = block[1].reshape(tokens, heads_here, HD)
        scores = (
            jnp.einsum("qhd,khd->hqk", query_heads, key_heads, preferred_element_type=jnp.float32)
            * scale
        )
        new_max = jnp.where(allowed, jnp.maximum(running_max, jnp.max(scores, axis=2)), running_max)
        lifted = jnp.where(allowed, jnp.exp(jnp.minimum(scores - new_max[:, :, None], 0.0)), 0.0)
        factor = jnp.exp(running_max - new_max)
        weight_sum = weight_sum * factor + jnp.sum(lifted, axis=2)
        rounded = lifted.astype(jnp.bfloat16)
        accumulated = accumulated * jnp.transpose(factor)[:, :, None] + jnp.einsum(
            "hqk,khd->qhd", rounded, value_heads, preferred_element_type=jnp.float32
        )
        return (new_max, weight_sum, accumulated)

    state = (
        jnp.full((heads_here, tokens), -1e30, jnp.float32),
        jnp.zeros((heads_here, tokens), jnp.float32),
        jnp.zeros((tokens, heads_here, HD), jnp.float32),
    )
    state = absorb(state, key_value, allowed_at(0))
    moving = key_value
    for offset in range(1, window):
        moving = shifted(moving, "tm", 1)
        state = absorb(state, moving, allowed_at(offset))
    running_max, weight_sum, accumulated = state
    attention = (
        (accumulated / jnp.transpose(weight_sum)[:, :, None])
        .reshape(tokens, heads_here * HD)
        .astype(jnp.bfloat16)
    )
    weight_cols = lax.all_gather(out_weight, "tm", axis=0, tiled=True)
    projected = jnp.dot(
        lax.all_gather(attention, "head", axis=1, tiled=True),
        weight_cols,
        preferred_element_type=jnp.float32,
    )
    gate = jnp.dot(
        time_features(noise_steps), time_weight.astype(jnp.float32), precision=lax.Precision.HIGHEST
    )
    updated = (residual[0].astype(jnp.float32) + gate * projected).astype(jnp.bfloat16)
    moved = shifted(updated, "tm", -1)
    rolled = jnp.where(frame == frames_total - 1, fresh_frame, moved)
    return rolled[None]


def whole_in_vmem(count):
    return [pl.BlockSpec(memory_space=pltpu.VMEM)] * count


def in_hbm(count):
    return [pl.BlockSpec(memory_space=pltpu.HBM)] * count


def roomy():
    return pltpu.CompilerParams(vmem_limit_bytes=VMEM_BYTES)


def pack(queries, keys, values, frame_mask, noise_steps, moves, pairs, width):
    tokens = queries.shape[0]
    window = frame_mask.shape[1]
    widths = [3 * width + (HD if b == 0 else 0) for a, b in moves]
    count = len(moves)

    def kernel(*refs):
        sources, small, pieces, scratch = (refs[:3], refs[3:5], refs[5 : 5 + count], refs[5 + count :])
        loaded, packed, mask_ref, noise_ref, in_sems, out_sems = scratch
        frame, pair = (lax.axis_index("tm"), lax.axis_index("head") // 2)
        targets = [loaded.at[place] for place in range(3)] + [mask_ref, noise_ref]
        loads = [
            pltpu.make_async_copy(source, target, in_sems.at[place])
            for place, (source, target) in enumerate(zip((*sources, *small), targets))
        ]
        for load in loads:
            load.start()
        for load in loads:
            load.wait()
        lane = lax.broadcasted_iota(jnp.int32, (tokens, HD), 1)
        note = jnp.where(lane == window, noise_ref[0], 0)
        for column in range(window):
            note = jnp.where(lane == column, mask_ref[0, column], note)
        note = note.astype(jnp.float32).astype(queries.dtype)
        stores = []
        for number, (a, b) in enumerate(moves):
            block = (frame ^ a) * pairs + (pair ^ b)
            columns = pl.ds(pl.multiple_of(block * width, HD), width)
            for place in range(3):
                packed[number, :, place * width : (place + 1) * width] = loaded[place, :, columns]
            if b == 0:
                packed[number, :, 3 * width :] = note
            store = pltpu.make_async_copy(
                packed.at[number, :, : widths[number]], pieces[number], out_sems.at[number]
            )
            store.start()
            stores.append(store)
        for store in stores:
            store.wait()

    return pl.pallas_call(
        kernel,
        out_shape=[jax.ShapeDtypeStruct((tokens, size), queries.dtype) for size in widths],
        in_specs=in_hbm(5),
        out_specs=in_hbm(count),
        scratch_shapes=[
            pltpu.VMEM((3, *queries.shape), queries.dtype),
            pltpu.VMEM((count, tokens, 3 * width + HD), queries.dtype),
            pltpu.SMEM(frame_mask.shape, frame_mask.dtype),
            pltpu.SMEM(noise_steps.shape, noise_steps.dtype),
            pltpu.SemaphoreType.DMA((5,)),
            pltpu.SemaphoreType.DMA((count,)),
        ],
        compiler_params=pltpu.CompilerParams(vmem_limit_bytes=PACK_BYTES),
        name="pack",
    )(queries, keys, values, frame_mask, noise_steps)


def bring(*arrays):
    def kernel(*refs):
        for source, target in zip(refs[: len(arrays)], refs[len(arrays) :]):
            target[...] = source[...]

    return pl.pallas_call(
        kernel,
        out_shape=[jax.ShapeDtypeStruct(array.shape, array.dtype) for array in arrays],
        in_specs=whole_in_vmem(len(arrays)),
        out_specs=whole_in_vmem(len(arrays)),
        compiler_params=roomy(),
        name="bring",
    )(*arrays)


def pick(table, here):
    result = table[0]
    for place, entry in enumerate(table[1:], 1):
        result = jnp.where(here == place, entry, result)
    return result


def attend_frames(slots, out_refs, query_buf, key_buf, value_buf, note_ref):
    frames, keys_rows, width = key_buf.shape
    scale = math.log2(math.e) / math.sqrt(HD)
    here = lax.axis_index("tm")
    for frames_of_slot, out_ref in zip(slots, out_refs):
        frame = pick(frames_of_slot, here)
        note = note_ref[pl.ds(frame, 1), :]
        lane = lax.broadcasted_iota(jnp.int32, note.shape, 1)
        biases = []
        for a in range(frames):
            hit = jnp.sum(jnp.where(lane == here ^ a, note, 0.0), axis=1, keepdims=True)
            biases.append(jnp.broadcast_to((hit - 1.0) * 1e30, (1, keys_rows)))
        bias = jnp.concatenate(biases, axis=1)
        for start in range(0, width, HD):
            channels = slice(start, start + HD)
            query = query_buf[frame, :, channels]
            keys = key_buf[:, :, channels].reshape(frames * keys_rows, HD)
            scores = lax.dot_general(
                query, keys, (((1,), (1,)), ((), ())), preferred_element_type=jnp.float32
            )
            scores = scores * scale + bias
            lifted = jnp.exp2(scores - jnp.max(scores, axis=1, keepdims=True))
            totals = jnp.sum(lifted, axis=1, keepdims=True)
            values = value_buf[:, :, channels].reshape(frames * keys_rows, HD)
            mixed = jnp.dot(
                lifted.astype(jnp.bfloat16), values, preferred_element_type=jnp.float32
            )
            out_ref[:, channels] = (mixed / totals).astype(jnp.bfloat16)


def attend(slots, own, mate, moves, pairs, frames, width):
    tokens = own[0].shape[0]
    rows, keys_rows = (pairs * tokens, 2 * pairs * tokens)

    def kernel(*refs):
        own_refs, refs = (refs[: len(moves)], refs[len(moves) :])
        mate_refs, refs = (refs[: len(moves)], refs[len(moves) :])
        out_refs, (query_buf, key_buf, value_buf, note_out) = (refs[: len(slots)], refs[len(slots) :])
        here = lax.axis_index("tm")
        for own_ref, mate_ref, (a, b) in zip(own_refs, mate_refs, moves):
            query_buf[here ^ a, b * tokens : (b + 1) * tokens, :] = own_ref[:, :width]
            for side, ref in enumerate((own_ref, mate_ref)):
                span = slice((2 * b + side) * tokens, (2 * b + side + 1) * tokens)
                key_buf[a, span, :] = ref[:, width : 2 * width]
                value_buf[a, span, :] = ref[:, 2 * width : 3 * width]
            if b == 0:
                note_out[pl.ds(here ^ a, 1), :] = own_ref[:16, 3 * width :].astype(jnp.float32)[:1]
        attend_frames(slots, out_refs, query_buf, key_buf, value_buf, note_out)

    kind = own[0].dtype
    outs = pl.pallas_call(
        kernel,
        out_shape=[jax.ShapeDtypeStruct((rows, width), jnp.bfloat16)] * len(slots)
        + [
            jax.ShapeDtypeStruct((frames, rows, width), kind),
            jax.ShapeDtypeStruct((frames, keys_rows, width), kind),
            jax.ShapeDtypeStruct((frames, keys_rows, width), kind),
            jax.ShapeDtypeStruct((16, HD), jnp.float32),
        ],
        in_specs=whole_in_vmem(2 * len(moves)),
        out_specs=whole_in_vmem(len(slots) + 4),
        compiler_params=roomy(),
        name="attend",
    )(*own, *mate)
    return (outs[: len(slots)], outs[len(slots) :])


def attend_again(slots, held):
    rows, width = held[0].shape[1:]

    def kernel(*refs):
        out_ref = refs[len(held)]
        parts = [out_ref.at[slot * rows : (slot + 1) * rows] for slot in range(len(slots))]
        attend_frames(slots, parts, *refs[: len(held)])

    return pl.pallas_call(
        kernel,
        out_shape=jax.ShapeDtypeStruct((len(slots) * rows, width), jnp.bfloat16),
        in_specs=whole_in_vmem(len(held)),
        out_specs=whole_in_vmem(1)[0],
        compiler_params=roomy(),
        name="attend_again",
    )(*held)


def project(pieces, weight, kinds, slots=1):
    flat = [piece for part in pieces for piece in part]
    rows, width = (flat[0].shape[0] // slots, flat[0].shape[1])
    pairs, sets = (len(pieces[0]), len(pieces))
    tokens = rows // pairs
    depth, columns = weight.shape
    step = math.gcd(columns, 256)

    def kernel(*refs):
        sources = iter(refs[: len(flat)])
        weight_ref, refs = (refs[len(flat)], refs[len(flat) + 1 :])
        whole = refs[-1]
        here = lax.axis_index("head") // 2
        for k in range(sets):
            for move in range(pairs):
                source = next(sources)
                pair = here ^ move
                channels = pl.ds(pl.multiple_of(pair * width, HD), width)
                for slot in range(slots):
                    for b in range(pairs):
                        first = (slot * sets + k) * rows + (pair ^ b) * tokens
                        start = slot * rows + b * tokens
                        whole[pl.ds(pl.multiple_of(first, 16), tokens), channels] = source[
                            start : start + tokens, :
                        ]
        for start in range(0, columns, step):
            inner = slice(start, start + step)
            product = jnp.dot(
                whole[...], weight_ref[:, inner], preferred_element_type=jnp.float32
            )
            for number in range(slots * sets):
                share = product[number * rows : (number + 1) * rows, :]
                for out_ref in refs[number * len(kinds) : (number + 1) * len(kinds)]:
                    out_ref[:, inner] = share.astype(out_ref.dtype)

    outs = pl.pallas_call(
        kernel,
        out_shape=[
            jax.ShapeDtypeStruct((rows, columns), kind)
            for _ in range(slots * sets)
            for kind in kinds
        ],
        in_specs=whole_in_vmem(len(flat) + 1),
        out_specs=whole_in_vmem(len(kinds) * slots * sets),
        scratch_shapes=[pltpu.VMEM((slots * sets * rows, depth), jnp.bfloat16)],
        compiler_params=roomy(),
        name="project",
    )(*flat, weight)
    return [list(outs[number :: len(kinds)]) for number in range(len(kinds))]


def gates_of(notes, time_weight, column, frames):
    depth, columns = time_weight.shape
    half = depth // 2

    def kernel(note_ref, weight_ref, here_ref, next_ref):
        here = lax.axis_index("tm")
        following = jnp.minimum(here + 1, frames - 1)
        rows = jnp.concatenate([note_ref[pl.ds(here, 1), :], note_ref[pl.ds(following, 1), :]], axis=0)
        lane = lax.broadcasted_iota(jnp.int32, rows.shape, 1)
        noise = jnp.sum(jnp.where(lane == column, rows, 0.0), axis=1, keepdims=True)
        timestep = 1000.0 * (noise + 1.0) / STEPS
        place = lax.broadcasted_iota(jnp.int32, (2, half), 1).astype(jnp.float32)
        angles = timestep * jnp.exp(-math.log(10000.0) * place / half)
        features = jnp.concatenate([jnp.cos(angles), jnp.sin(angles)], axis=1)
        gates = jnp.dot(
            features,
            weight_ref[...].astype(jnp.float32),
            precision=lax.Precision.HIGHEST,
            preferred_element_type=jnp.float32,
        )
        here_ref[...] = gates[:1]
        next_ref[...] = gates[1:]

    return pl.pallas_call(
        kernel,
        out_shape=[jax.ShapeDtypeStruct((1, columns), jnp.float32)] * 2,
        in_specs=whole_in_vmem(2),
        out_specs=whole_in_vmem(2),
        compiler_params=roomy(),
        name="gates_of",
    )(notes, time_weight)


def frame_rows(k, pairs, tokens):
    core = (lax.axis_index("head") % 2) ^ k
    return [pl.ds(pl.multiple_of((2 * p + core) * tokens, 16), tokens) for p in range(pairs)]


def join(partial, table, arrived, k, pairs, residual=None, gate=None):
    rows, columns = partial[0].shape
    tokens = rows // pairs
    step = math.gcd(columns, 256)
    slots = sorted(set(table))
    extras = [] if residual is None else [residual, gate]

    def kernel(*refs):
        own_refs, refs = (refs[: len(slots)], refs[len(slots) :])
        arrived_refs, refs = (refs[: len(arrived)], refs[len(arrived) :])
        out_ref = refs[-1]
        here = lax.axis_index("tm")
        places = frame_rows(k, pairs, tokens)
        for slot, own_ref in zip(slots, own_refs):

            @pl.when(pick([entry == slot for entry in table], here))
            def _(own_ref=own_ref):
                for p, place in enumerate(places):
                    inner = slice(p * tokens, (p + 1) * tokens)
                    for start in range(0, columns, step):
                        part = slice(start, start + step)
                        total = own_ref[inner, part]
                        for ref in arrived_refs:
                            total += ref[inner, part].astype(jnp.float32)
                        if extras:
                            kept = refs[0][place, part].astype(jnp.float32)
                            total = kept + refs[1][:, part] * total
                        out_ref[inner, part] = total.astype(jnp.bfloat16)

    operands = [partial[slot] for slot in slots] + list(arrived) + extras
    return pl.pallas_call(
        kernel,
        out_shape=jax.ShapeDtypeStruct((rows, columns), jnp.bfloat16),
        in_specs=whole_in_vmem(len(operands)),
        out_specs=whole_in_vmem(1)[0],
        compiler_params=roomy(),
        name="join",
    )(*operands)


def finish(arrived, partial, below, gate, fresh_frame, pairs):
    rows, columns = partial[0].shape
    tokens = rows // pairs
    step = math.gcd(columns, 256)
    sets = len(partial)

    def kernel(*refs):
        arrived_refs, partial_refs, below_refs = (
            refs[:sets],
            refs[sets : 2 * sets],
            refs[2 * sets : 3 * sets],
        )
        gate_ref, fresh_ref, out_ref = refs[3 * sets :]
        last = lax.axis_index("tm") == lax.axis_size("tm") - 1

        @pl.when(last)
        def _():
            out_ref[...] = fresh_ref[...]

        @pl.when(jnp.logical_not(last))
        def _():
            for k in range(sets):
                for p, place in enumerate(frame_rows(k, pairs, tokens)):
                    inner = slice(p * tokens, (p + 1) * tokens)
                    for start in range(0, columns, step):
                        part = slice(start, start + step)
                        total = partial_refs[k][inner, part]
                        total += below_refs[k][inner, part].astype(jnp.float32)
                        total = gate_ref[:, part] * total
                        total += arrived_refs[k][inner, part].astype(jnp.float32)
                        out_ref[place, part] = total.astype(jnp.bfloat16)

    return pl.pallas_call(
        kernel,
        out_shape=jax.ShapeDtypeStruct(fresh_frame.shape, jnp.bfloat16),
        in_specs=whole_in_vmem(3 * sets + 2),
        out_specs=whole_in_vmem(1)[0],
        compiler_params=roomy(),
        name="finish",
    )(*arrived, *partial, *below, gate, fresh_frame)


def line_schedule(frames):
    steps = []
    for step in range(frames - 1):
        down = {z: step + 1 - (frames - 1 - z) for z in range(1, frames)}
        up = {z: frames - 1 - step + z for z in range(frames)}
        down = {z: f for z, f in down.items() if 1 <= f <= z}
        up = {z: f for z, f in up.items() if z + 2 <= f < frames}
        steps.append((down, up))
    order = []
    for z in range(frames):
        sent = [f for down, up in steps for f in (down.get(z), up.get(z)) if f is not None]
        order.append((sent + [z + 1])[: frames - 1])
    return steps, order


def head_plan(
    queries, keys, values, residual, fresh_frame, out_weight, time_weight, noise_steps, frame_mask
):
    frames, across = (lax.axis_size("tm"), lax.axis_size("head"))
    pairs = across // 2
    width = queries.shape[2] // (frames * pairs)
    everywhere = range(frames)

    def swap(array, j):
        return lax.ppermute(array, "head", [(h, h ^ j) for h in range(across)])

    def gather(part, meanwhile=None):
        near = [part]
        for move in range(1, pairs):
            piece = swap(part, 2 * move)
            if meanwhile is not None:
                piece, meanwhile = lax.optimization_barrier((piece, meanwhile))
            near.append(piece)
        return ([near, [swap(piece, 1) for piece in near]], meanwhile)

    far = [(a, b) for b in range(pairs) for a in reversed(everywhere[2:])]
    near = [(0, b) for b in range(1, pairs)] + [(1, b) for b in range(pairs)]
    moves = near + far + [(0, 0)]
    packed = pack(
        queries[0], keys[0], values[0], frame_mask, noise_steps, moves, pairs, width
    )
    own = []
    for number, (piece, (a, b)) in enumerate(zip(packed, moves)):
        if (a, b) != (0, 0):
            if a == 1:
                piece, own[0] = lax.optimization_barrier((piece, own[0]))
            links = [
                (z * across + h, (z ^ a) * across + (h ^ (2 * b)))
                for z in everywhere
                for h in range(across)
            ]
            piece = lax.ppermute(piece, ("tm", "head"), links)
        own.append(piece)
    for number, move in enumerate(moves):
        if move in far:
            for other in range(pairs - 1, len(near)):
                own[number], own[other] = lax.optimization_barrier((own[number], own[other]))
    mine = moves.index((0, 0))
    (own[mine],), weight = (bring(own[mine]), out_weight)
    mate = [swap(piece, 1) for piece in own]

    steps, order = line_schedule(frames)

    named = [[order[z][slot] for z in everywhere] for slot in range(frames - 1)]
    (part,), held = attend(named[:1], own, mate, moves, pairs, frames, width)
    following = attend_again(named[1:], held)
    pieces, following = gather(part, following)
    partial, payload = ([[]], [])
    for rows in pieces:
        product, rounded = project([rows], weight, (jnp.float32, jnp.bfloat16))
        partial[0] += product
        payload += rounded
    following, payload[1] = lax.optimization_barrier((following, payload[1]))
    down, up = steps[0]
    links = [(z, z - 1) for z in down] + [(z, z + 1) for z in up]
    above = [lax.ppermute(part, "tm", links) for part in payload]
    below = above
    pieces, _ = gather(following)
    later = project(pieces, weight, (jnp.float32,), frames - 2)[0]
    partial += [later[2 * slot : 2 * slot + 2] for slot in range(frames - 2)]
    gates = gates_of(held[-1], time_weight, frame_mask.shape[1], frames)

    for number, (down, up) in enumerate(steps[1:], 1):
        sends = {**down, **up}
        table = [order[z].index(sends[z]) if z in sends else 0 for z in everywhere]
        final = number == len(steps) - 1
        extras = (residual[0], gates[0]) if final else ()
        payload = [
            join(
                [products[k] for products in partial],
                table,
                [above[k]] if final or above is below else [above[k], below[k]],
                k,
                pairs,
                *extras,
            )
            for k in range(2)
        ]
        above = [lax.ppermute(part, "tm", [(z, z - 1) for z in down]) for part in payload]
        if up:
            below = [lax.ppermute(part, "tm", [(z, z + 1) for z in up]) for part in payload]
    return finish(above, partial[-1], below, gates[1], fresh_frame, pairs)[None]


def power_of_two(number):
    return number & (number - 1) == 0


def suits_line(frames, window):
    apart = all(not set(down) & set(up) for down, up in line_schedule(frames)[0])
    return 2 < frames <= window and power_of_two(frames) and apart


def on_device(queries, *others):
    frames, across = (lax.axis_size("tm"), lax.axis_size("head"))
    heads = queries.shape[2] // HD
    even = across % 2 == 0 and power_of_two(across)
    even = even and queries.shape[1] % 16 == 0
    if even and suits_line(frames, others[-1].shape[1]) and heads % (frames * across // 2) == 0:
        return head_plan(queries, *others)
    return frame_plan(queries, *others)


def solution(mesh):
    placed = (
        P(("groups", "tm"), "head", None),
        P(("groups", "tm"), "head", None),
        P(("groups", "tm"), "head", None),
        P(("groups", "tm"), None, "head"),
        P("groups", "head"),
        P("tm", "head"),
        P(None, "head"),
        P(("groups", "tm")),
        P(("groups", "tm"), None),
    )
    return jax.shard_map(
        on_device,
        mesh=mesh,
        in_specs=placed,
        out_specs=P(("groups", "tm"), None, "head"),
        check_vma=False,
    )
```

```python
import math

import jax
import jax.numpy as jnp
import numpy as np
from jax import lax
from jax.experimental import pallas as pl
from jax.experimental.pallas import tpu as pltpu
from jax.sharding import PartitionSpec as P

HD = 128
FREQ = 256
STEPS = 50
VMEM_BYTES = 16 * 1024 * 1024
PACK_BYTES = 60 * 1024 * 1024


def shifted(value, axis, steps):
    count = lax.axis_size(axis)
    leading, last = (max(0, -steps), min(count, count - steps))
    return lax.ppermute(value, axis, [(source, source + steps) for source in range(leading, last)])


def time_features(noise_steps):
    timestep = 1000.0 * (noise_steps.astype(jnp.float32) + 1.0) / STEPS
    half = FREQ // 2
    rates = jnp.exp(-math.log(10000.0) * jnp.arange(half).astype(jnp.float32) / half)
    angles = timestep[:, None] * rates[None, :]
    return jnp.concatenate([jnp.cos(angles), jnp.sin(angles)], axis=1)


def frame_plan(
    queries, keys, values, residual, fresh_frame, out_weight, time_weight, noise_steps, frame_mask
):
    query_local, key_local, value_local = (
        lax.all_to_all(queries, "head", split_axis=2, concat_axis=1, tiled=True),
        lax.all_to_all(keys, "head", split_axis=2, concat_axis=1, tiled=True),
        lax.all_to_all(values, "head", split_axis=2, concat_axis=1, tiled=True),
    )
    tokens = query_local.shape[1]
    heads_here = query_local.shape[2] // HD
    scale = 1.0 / math.sqrt(HD)
    query_heads = query_local[0].reshape(tokens, heads_here, HD)
    key_value = jnp.stack([key_local[0], value_local[0]], axis=0)
    frame = lax.axis_index("tm")
    frames_total = lax.axis_size("tm")
    window = min(8, frames_total)
    mask_row = frame_mask[0]
    columns = jnp.arange(mask_row.shape[0], dtype=jnp.int32)

    def allowed_at(offset):
        hits = jnp.sum(jnp.where(columns == frame - offset, mask_row, 0))
        return hits > 0

    def absorb(state, block, allowed):
        running_max, weight_sum, accumulated = state
        key_heads = block[0].reshape(tokens, heads_here, HD)
        value_heads = block[1].reshape(tokens, heads_here, HD)
        scores = (
            jnp.einsum("qhd,khd->hqk", query_heads, key_heads, preferred_element_type=jnp.float32)
            * scale
        )
        new_max = jnp.where(allowed, jnp.maximum(running_max, jnp.max(scores, axis=2)), running_max)
        lifted = jnp.where(allowed, jnp.exp(jnp.minimum(scores - new_max[:, :, None], 0.0)), 0.0)
        factor = jnp.exp(running_max - new_max)
        weight_sum = weight_sum * factor + jnp.sum(lifted, axis=2)
        rounded = lifted.astype(jnp.bfloat16)
        accumulated = accumulated * jnp.transpose(factor)[:, :, None] + jnp.einsum(
            "hqk,khd->qhd", rounded, value_heads, preferred_element_type=jnp.float32
        )
        return (new_max, weight_sum, accumulated)

    state = (
        jnp.full((heads_here, tokens), -1e30, jnp.float32),
        jnp.zeros((heads_here, tokens), jnp.float32),
        jnp.zeros((tokens, heads_here, HD), jnp.float32),
    )
    state = absorb(state, key_value, allowed_at(0))
    moving = key_value
    for offset in range(1, window):
        moving = shifted(moving, "tm", 1)
        state = absorb(state, moving, allowed_at(offset))
    running_max, weight_sum, accumulated = state
    attention = (
        (accumulated / jnp.transpose(weight_sum)[:, :, None])
        .reshape(tokens, heads_here * HD)
        .astype(jnp.bfloat16)
    )
    weight_cols = lax.all_gather(out_weight, "tm", axis=0, tiled=True)
    projected = jnp.dot(
        lax.all_gather(attention, "head", axis=1, tiled=True),
        weight_cols,
        preferred_element_type=jnp.float32,
    )
    gate = jnp.dot(
        time_features(noise_steps), time_weight.astype(jnp.float32), precision=lax.Precision.HIGHEST
    )
    updated = (residual[0].astype(jnp.float32) + gate * projected).astype(jnp.bfloat16)
    moved = shifted(updated, "tm", -1)
    rolled = jnp.where(frame == frames_total - 1, fresh_frame, moved)
    return rolled[None]


def whole_in_vmem(count):
    return [pl.BlockSpec(memory_space=pltpu.VMEM)] * count


def in_hbm(count):
    return [pl.BlockSpec(memory_space=pltpu.HBM)] * count


def roomy():
    return pltpu.CompilerParams(vmem_limit_bytes=VMEM_BYTES)


def pack(queries, keys, values, frame_mask, noise_steps, moves, pairs, width):
    tokens = queries.shape[0]
    window = frame_mask.shape[1]
    widths = [3 * width + (HD if b == 0 else 0) for a, b in moves]
    count = len(moves)

    def kernel(*refs):
        sources, small, pieces, scratch = (refs[:3], refs[3:5], refs[5 : 5 + count], refs[5 + count :])
        loaded, packed, mask_ref, noise_ref, in_sems, out_sems = scratch
        frame, pair = (lax.axis_index("tm"), lax.axis_index("head") // 2)
        targets = [loaded.at[place] for place in range(3)] + [mask_ref, noise_ref]
        loads = [
            pltpu.make_async_copy(source, target, in_sems.at[place])
            for place, (source, target) in enumerate(zip((*sources, *small), targets))
        ]
        for load in loads:
            load.start()
        for load in loads:
            load.wait()
        lane = lax.broadcasted_iota(jnp.int32, (tokens, HD), 1)
        note = jnp.where(lane == window, noise_ref[0], 0)
        for column in range(window):
            note = jnp.where(lane == column, mask_ref[0, column], note)
        note = note.astype(jnp.float32).astype(queries.dtype)
        stores = []
        for number, (a, b) in enumerate(moves):
            block = (frame ^ a) * pairs + (pair ^ b)
            columns = pl.ds(pl.multiple_of(block * width, HD), width)
            for place in range(3):
                packed[number, :, place * width : (place + 1) * width] = loaded[place, :, columns]
            if b == 0:
                packed[number, :, 3 * width :] = note
            store = pltpu.make_async_copy(
                packed.at[number, :, : widths[number]], pieces[number], out_sems.at[number]
            )
            store.start()
            stores.append(store)
        for store in stores:
            store.wait()

    return pl.pallas_call(
        kernel,
        out_shape=[jax.ShapeDtypeStruct((tokens, size), queries.dtype) for size in widths],
        in_specs=in_hbm(5),
        out_specs=in_hbm(count),
        scratch_shapes=[
            pltpu.VMEM((3, *queries.shape), queries.dtype),
            pltpu.VMEM((count, tokens, 3 * width + HD), queries.dtype),
            pltpu.SMEM(frame_mask.shape, frame_mask.dtype),
            pltpu.SMEM(noise_steps.shape, noise_steps.dtype),
            pltpu.SemaphoreType.DMA((5,)),
            pltpu.SemaphoreType.DMA((count,)),
        ],
        compiler_params=pltpu.CompilerParams(vmem_limit_bytes=PACK_BYTES),
        name="pack",
    )(queries, keys, values, frame_mask, noise_steps)


def bring(*arrays):
    def kernel(*refs):
        for source, target in zip(refs[: len(arrays)], refs[len(arrays) :]):
            target[...] = source[...]

    return pl.pallas_call(
        kernel,
        out_shape=[jax.ShapeDtypeStruct(array.shape, array.dtype) for array in arrays],
        in_specs=whole_in_vmem(len(arrays)),
        out_specs=whole_in_vmem(len(arrays)),
        compiler_params=roomy(),
        name="bring",
    )(*arrays)


def pick(table, here):
    result = table[0]
    for place, entry in enumerate(table[1:], 1):
        result = jnp.where(here == place, entry, result)
    return result


def attend_frames(slots, out_refs, query_buf, key_buf, value_buf, note_ref):
    frames, keys_rows, width = key_buf.shape
    scale = math.log2(math.e) / math.sqrt(HD)
    here = lax.axis_index("tm")
    for frames_of_slot, out_ref in zip(slots, out_refs):
        frame = pick(frames_of_slot, here)
        note = note_ref[pl.ds(frame, 1), :]
        lane = lax.broadcasted_iota(jnp.int32, note.shape, 1)
        biases = []
        for a in range(frames):
            hit = jnp.sum(jnp.where(lane == here ^ a, note, 0.0), axis=1, keepdims=True)
            biases.append(jnp.broadcast_to((hit - 1.0) * 1e30, (1, keys_rows)))
        bias = jnp.concatenate(biases, axis=1)
        for start in range(0, width, HD):
            channels = slice(start, start + HD)
            query = query_buf[frame, :, channels]
            keys = key_buf[:, :, channels].reshape(frames * keys_rows, HD)
            scores = lax.dot_general(
                query, keys, (((1,), (1,)), ((), ())), preferred_element_type=jnp.float32
            )
            scores = scores * scale + bias
            lifted = jnp.exp2(scores - jnp.max(scores, axis=1, keepdims=True))
            totals = jnp.sum(lifted, axis=1, keepdims=True)
            values = value_buf[:, :, channels].reshape(frames * keys_rows, HD)
            mixed = jnp.dot(
                lifted.astype(jnp.bfloat16), values, preferred_element_type=jnp.float32
            )
            out_ref[:, channels] = (mixed / totals).astype(jnp.bfloat16)


def attend(slots, own, mate, moves, pairs, frames, width):
    tokens = own[0].shape[0]
    rows, keys_rows = (pairs * tokens, 2 * pairs * tokens)

    def kernel(*refs):
        own_refs, refs = (refs[: len(moves)], refs[len(moves) :])
        mate_refs, refs = (refs[: len(moves)], refs[len(moves) :])
        out_refs, (query_buf, key_buf, value_buf, note_out) = (refs[: len(slots)], refs[len(slots) :])
        here = lax.axis_index("tm")
        for own_ref, mate_ref, (a, b) in zip(own_refs, mate_refs, moves):
            query_buf[here ^ a, b * tokens : (b + 1) * tokens, :] = own_ref[:, :width]
            for side, ref in enumerate((own_ref, mate_ref)):
                span = slice((2 * b + side) * tokens, (2 * b + side + 1) * tokens)
                key_buf[a, span, :] = ref[:, width : 2 * width]
                value_buf[a, span, :] = ref[:, 2 * width : 3 * width]
            if b == 0:
                note_out[pl.ds(here ^ a, 1), :] = own_ref[:16, 3 * width :].astype(jnp.float32)[:1]
        attend_frames(slots, out_refs, query_buf, key_buf, value_buf, note_out)

    kind = own[0].dtype
    outs = pl.pallas_call(
        kernel,
        out_shape=[jax.ShapeDtypeStruct((rows, width), jnp.bfloat16)] * len(slots)
        + [
            jax.ShapeDtypeStruct((frames, rows, width), kind),
            jax.ShapeDtypeStruct((frames, keys_rows, width), kind),
            jax.ShapeDtypeStruct((frames, keys_rows, width), kind),
            jax.ShapeDtypeStruct((16, HD), jnp.float32),
        ],
        in_specs=whole_in_vmem(2 * len(moves)),
        out_specs=whole_in_vmem(len(slots) + 4),
        compiler_params=roomy(),
        name="attend",
    )(*own, *mate)
    return (outs[: len(slots)], outs[len(slots) :])


def attend_again(slots, held):
    rows, width = held[0].shape[1:]

    def kernel(*refs):
        out_ref = refs[len(held)]
        parts = [out_ref.at[slot * rows : (slot + 1) * rows] for slot in range(len(slots))]
        attend_frames(slots, parts, *refs[: len(held)])

    return pl.pallas_call(
        kernel,
        out_shape=jax.ShapeDtypeStruct((len(slots) * rows, width), jnp.bfloat16),
        in_specs=whole_in_vmem(len(held)),
        out_specs=whole_in_vmem(1)[0],
        compiler_params=roomy(),
        name="attend_again",
    )(*held)


def project(pieces, weight, kinds, slots=1):
    flat = [piece for part in pieces for piece in part]
    rows, width = (flat[0].shape[0] // slots, flat[0].shape[1])
    pairs, sets = (len(pieces[0]), len(pieces))
    tokens = rows // pairs
    depth, columns = weight.shape
    step = math.gcd(columns, 256)

    def kernel(*refs):
        sources = iter(refs[: len(flat)])
        weight_ref, refs = (refs[len(flat)], refs[len(flat) + 1 :])
        whole = refs[-1]
        here = lax.axis_index("head") // 2
        for k in range(sets):
            for move in range(pairs):
                source = next(sources)
                pair = here ^ move
                channels = pl.ds(pl.multiple_of(pair * width, HD), width)
                for slot in range(slots):
                    for b in range(pairs):
                        first = (slot * sets + k) * rows + (pair ^ b) * tokens
                        start = slot * rows + b * tokens
                        whole[pl.ds(pl.multiple_of(first, 16), tokens), channels] = source[
                            start : start + tokens, :
                        ]
        for start in range(0, columns, step):
            inner = slice(start, start + step)
            product = jnp.dot(
                whole[...], weight_ref[:, inner], preferred_element_type=jnp.float32
            )
            for number in range(slots * sets):
                share = product[number * rows : (number + 1) * rows, :]
                for out_ref in refs[number * len(kinds) : (number + 1) * len(kinds)]:
                    out_ref[:, inner] = share.astype(out_ref.dtype)

    outs = pl.pallas_call(
        kernel,
        out_shape=[
            jax.ShapeDtypeStruct((rows, columns), kind)
            for _ in range(slots * sets)
            for kind in kinds
        ],
        in_specs=whole_in_vmem(len(flat) + 1),
        out_specs=whole_in_vmem(len(kinds) * slots * sets),
        scratch_shapes=[pltpu.VMEM((slots * sets * rows, depth), jnp.bfloat16)],
        compiler_params=roomy(),
        name="project",
    )(*flat, weight)
    return [list(outs[number :: len(kinds)]) for number in range(len(kinds))]


def gates_of(notes, time_weight, column, frames):
    depth, columns = time_weight.shape
    half = depth // 2

    def kernel(note_ref, weight_ref, here_ref, next_ref):
        here = lax.axis_index("tm")
        following = jnp.minimum(here + 1, frames - 1)
        rows = jnp.concatenate([note_ref[pl.ds(here, 1), :], note_ref[pl.ds(following, 1), :]], axis=0)
        lane = lax.broadcasted_iota(jnp.int32, rows.shape, 1)
        noise = jnp.sum(jnp.where(lane == column, rows, 0.0), axis=1, keepdims=True)
        timestep = 1000.0 * (noise + 1.0) / STEPS
        place = lax.broadcasted_iota(jnp.int32, (2, half), 1).astype(jnp.float32)
        angles = timestep * jnp.exp(-math.log(10000.0) * place / half)
        features = jnp.concatenate([jnp.cos(angles), jnp.sin(angles)], axis=1)
        gates = jnp.dot(
            features,
            weight_ref[...].astype(jnp.float32),
            precision=lax.Precision.HIGHEST,
            preferred_element_type=jnp.float32,
        )
        here_ref[...] = gates[:1]
        next_ref[...] = gates[1:]

    return pl.pallas_call(
        kernel,
        out_shape=[jax.ShapeDtypeStruct((1, columns), jnp.float32)] * 2,
        in_specs=whole_in_vmem(2),
        out_specs=whole_in_vmem(2),
        compiler_params=roomy(),
        name="gates_of",
    )(notes, time_weight)


def frame_rows(k, pairs, tokens):
    core = (lax.axis_index("head") % 2) ^ k
    return [pl.ds(pl.multiple_of((2 * p + core) * tokens, 16), tokens) for p in range(pairs)]


def join(partial, table, arrived, k, pairs, residual=None, gate=None):
    rows, columns = partial[0].shape
    tokens = rows // pairs
    step = math.gcd(columns, 256)
    slots = sorted(set(table))
    extras = [] if residual is None else [residual, gate]

    def kernel(*refs):
        own_refs, refs = (refs[: len(slots)], refs[len(slots) :])
        arrived_refs, refs = (refs[: len(arrived)], refs[len(arrived) :])
        out_ref = refs[-1]
        here = lax.axis_index("tm")
        places = frame_rows(k, pairs, tokens)
        for slot, own_ref in zip(slots, own_refs):

            @pl.when(pick([entry == slot for entry in table], here))
            def _(own_ref=own_ref):
                for p, place in enumerate(places):
                    inner = slice(p * tokens, (p + 1) * tokens)
                    for start in range(0, columns, step):
                        part = slice(start, start + step)
                        total = own_ref[inner, part]
                        for ref in arrived_refs:
                            total += ref[inner, part].astype(jnp.float32)
                        if extras:
                            kept = refs[0][place, part].astype(jnp.float32)
                            total = kept + refs[1][:, part] * total
                        out_ref[inner, part] = total.astype(jnp.bfloat16)

    operands = [partial[slot] for slot in slots] + list(arrived) + extras
    return pl.pallas_call(
        kernel,
        out_shape=jax.ShapeDtypeStruct((rows, columns), jnp.bfloat16),
        in_specs=whole_in_vmem(len(operands)),
        out_specs=whole_in_vmem(1)[0],
        compiler_params=roomy(),
        name="join",
    )(*operands)


def finish(arrived, partial, below, gate, fresh_frame, pairs):
    rows, columns = partial[0].shape
    tokens = rows // pairs
    step = math.gcd(columns, 256)
    sets = len(partial)

    def kernel(*refs):
        arrived_refs, partial_refs, below_refs = (
            refs[:sets],
            refs[sets : 2 * sets],
            refs[2 * sets : 3 * sets],
        )
        gate_ref, fresh_ref, out_ref = refs[3 * sets :]
        last = lax.axis_index("tm") == lax.axis_size("tm") - 1

        @pl.when(last)
        def _():
            out_ref[...] = fresh_ref[...]

        @pl.when(jnp.logical_not(last))
        def _():
            for k in range(sets):
                for p, place in enumerate(frame_rows(k, pairs, tokens)):
                    inner = slice(p * tokens, (p + 1) * tokens)
                    for start in range(0, columns, step):
                        part = slice(start, start + step)
                        total = partial_refs[k][inner, part]
                        total += below_refs[k][inner, part].astype(jnp.float32)
                        total = gate_ref[:, part] * total
                        total += arrived_refs[k][inner, part].astype(jnp.float32)
                        out_ref[place, part] = total.astype(jnp.bfloat16)

    return pl.pallas_call(
        kernel,
        out_shape=jax.ShapeDtypeStruct(fresh_frame.shape, jnp.bfloat16),
        in_specs=whole_in_vmem(3 * sets + 2),
        out_specs=whole_in_vmem(1)[0],
        compiler_params=roomy(),
        name="finish",
    )(*arrived, *partial, *below, gate, fresh_frame)


def line_schedule(frames):
    steps = []
    for step in range(frames - 1):
        down = {z: step + 1 - (frames - 1 - z) for z in range(1, frames)}
        up = {z: frames - 1 - step + z for z in range(frames)}
        down = {z: f for z, f in down.items() if 1 <= f <= z}
        up = {z: f for z, f in up.items() if z + 2 <= f < frames}
        steps.append((down, up))
    order = []
    for z in range(frames):
        sent = [f for down, up in steps for f in (down.get(z), up.get(z)) if f is not None]
        order.append((sent + [z + 1])[: frames - 1])
    return steps, order


def head_plan(
    queries, keys, values, residual, fresh_frame, out_weight, time_weight, noise_steps, frame_mask
):
    frames, across = (lax.axis_size("tm"), lax.axis_size("head"))
    pairs = across // 2
    width = queries.shape[2] // (frames * pairs)
    everywhere = range(frames)

    def swap(array, j):
        return lax.ppermute(array, "head", [(h, h ^ j) for h in range(across)])

    def gather(part, meanwhile=None):
        near = [part]
        for move in range(1, pairs):
            piece = swap(part, 2 * move)
            if meanwhile is not None:
                piece, meanwhile = lax.optimization_barrier((piece, meanwhile))
            near.append(piece)
        return ([near, [swap(piece, 1) for piece in near]], meanwhile)

    far = [(a, b) for b in range(pairs) for a in reversed(everywhere[2:])]
    near = [(0, b) for b in range(1, pairs)] + [(1, b) for b in range(pairs)]
    moves = far + near + [(0, 0)]
    packed = pack(
        queries[0], keys[0], values[0], frame_mask, noise_steps, moves, pairs, width
    )
    own = []
    for piece, (a, b) in zip(packed, moves):
        if (a, b) != (0, 0):
            links = [
                (z * across + h, (z ^ a) * across + (h ^ (2 * b)))
                for z in everywhere
                for h in range(across)
            ]
            piece = lax.ppermute(piece, ("tm", "head"), links)
        own.append(piece)
    first = len(far)
    for number in range(first):
        own[number], own[first] = lax.optimization_barrier((own[number], own[first]))
    mine = moves.index((0, 0))
    (own[mine],), weight = (bring(own[mine]), out_weight)
    mate = [swap(piece, 1) for piece in own]

    steps, order = line_schedule(frames)

    named = [[order[z][slot] for z in everywhere] for slot in range(frames - 1)]
    (part,), held = attend(named[:1], own, mate, moves, pairs, frames, width)
    following = attend_again(named[1:], held)
    pieces, following = gather(part, following)
    partial, payload = ([[]], [])
    for rows in pieces:
        product, rounded = project([rows], weight, (jnp.float32, jnp.bfloat16))
        partial[0] += product
        payload += rounded
    following, payload[0] = lax.optimization_barrier((following, payload[0]))
    down, up = steps[0]
    links = [(z, z - 1) for z in down] + [(z, z + 1) for z in up]
    above = [lax.ppermute(part, "tm", links) for part in payload]
    below = above
    pieces, _ = gather(following)
    later = project(pieces, weight, (jnp.float32,), frames - 2)[0]
    partial += [later[2 * slot : 2 * slot + 2] for slot in range(frames - 2)]
    gates = gates_of(held[-1], time_weight, frame_mask.shape[1], frames)

    for number, (down, up) in enumerate(steps[1:], 1):
        sends = {**down, **up}
        table = [order[z].index(sends[z]) if z in sends else 0 for z in everywhere]
        final = number == len(steps) - 1
        extras = (residual[0], gates[0]) if final else ()
        payload = [
            join(
                [products[k] for products in partial],
                table,
                [above[k]] if final or above is below else [above[k], below[k]],
                k,
                pairs,
                *extras,
            )
            for k in range(2)
        ]
        above = [lax.ppermute(part, "tm", [(z, z - 1) for z in down]) for part in payload]
        if up:
            below = [lax.ppermute(part, "tm", [(z, z + 1) for z in up]) for part in payload]
    return finish(above, partial[-1], below, gates[1], fresh_frame, pairs)[None]


def power_of_two(number):
    return number & (number - 1) == 0


def suits_line(frames, window):
    apart = all(not set(down) & set(up) for down, up in line_schedule(frames)[0])
    return 2 < frames <= window and power_of_two(frames) and apart


def on_device(queries, *others):
    frames, across = (lax.axis_size("tm"), lax.axis_size("head"))
    heads = queries.shape[2] // HD
    even = across % 2 == 0 and power_of_two(across)
    even = even and queries.shape[1] % 16 == 0
    if even and suits_line(frames, others[-1].shape[1]) and heads % (frames * across // 2) == 0:
        return head_plan(queries, *others)
    return frame_plan(queries, *others)


def solution(mesh):
    placed = (
        P(("groups", "tm"), "head", None),
        P(("groups", "tm"), "head", None),
        P(("groups", "tm"), "head", None),
        P(("groups", "tm"), None, "head"),
        P("groups", "head"),
        P("tm", "head"),
        P(None, "head"),
        P(("groups", "tm")),
        P(("groups", "tm"), None),
    )
    return jax.shard_map(
        on_device,
        mesh=mesh,
        in_specs=placed,
        out_specs=P(("groups", "tm"), None, "head"),
        check_vma=False,
    )
```

```python
import math

import jax
import jax.numpy as jnp
import numpy as np
from jax import lax
from jax.experimental import pallas as pl
from jax.experimental.pallas import tpu as pltpu
from jax.sharding import PartitionSpec as P

HD = 128
FREQ = 256
STEPS = 50
NOTE_ROWS = 16
VMEM_BYTES = 16 * 1024 * 1024
PACK_BYTES = 60 * 1024 * 1024


def shifted(value, axis, steps):
    count = lax.axis_size(axis)
    leading, last = (max(0, -steps), min(count, count - steps))
    return lax.ppermute(value, axis, [(source, source + steps) for source in range(leading, last)])


def time_features(noise_steps):
    timestep = 1000.0 * (noise_steps.astype(jnp.float32) + 1.0) / STEPS
    half = FREQ // 2
    rates = jnp.exp(-math.log(10000.0) * jnp.arange(half).astype(jnp.float32) / half)
    angles = timestep[:, None] * rates[None, :]
    return jnp.concatenate([jnp.cos(angles), jnp.sin(angles)], axis=1)


def frame_plan(
    queries, keys, values, residual, fresh_frame, out_weight, time_weight, noise_steps, frame_mask
):
    query_local, key_local, value_local = (
        lax.all_to_all(queries, "head", split_axis=2, concat_axis=1, tiled=True),
        lax.all_to_all(keys, "head", split_axis=2, concat_axis=1, tiled=True),
        lax.all_to_all(values, "head", split_axis=2, concat_axis=1, tiled=True),
    )
    tokens = query_local.shape[1]
    heads_here = query_local.shape[2] // HD
    scale = 1.0 / math.sqrt(HD)
    query_heads = query_local[0].reshape(tokens, heads_here, HD)
    key_value = jnp.stack([key_local[0], value_local[0]], axis=0)
    frame = lax.axis_index("tm")
    frames_total = lax.axis_size("tm")
    window = min(8, frames_total)
    mask_row = frame_mask[0]
    columns = jnp.arange(mask_row.shape[0], dtype=jnp.int32)

    def allowed_at(offset):
        hits = jnp.sum(jnp.where(columns == frame - offset, mask_row, 0))
        return hits > 0

    def absorb(state, block, allowed):
        running_max, weight_sum, accumulated = state
        key_heads = block[0].reshape(tokens, heads_here, HD)
        value_heads = block[1].reshape(tokens, heads_here, HD)
        scores = (
            jnp.einsum("qhd,khd->hqk", query_heads, key_heads, preferred_element_type=jnp.float32)
            * scale
        )
        new_max = jnp.where(allowed, jnp.maximum(running_max, jnp.max(scores, axis=2)), running_max)
        lifted = jnp.where(allowed, jnp.exp(jnp.minimum(scores - new_max[:, :, None], 0.0)), 0.0)
        factor = jnp.exp(running_max - new_max)
        weight_sum = weight_sum * factor + jnp.sum(lifted, axis=2)
        rounded = lifted.astype(jnp.bfloat16)
        accumulated = accumulated * jnp.transpose(factor)[:, :, None] + jnp.einsum(
            "hqk,khd->qhd", rounded, value_heads, preferred_element_type=jnp.float32
        )
        return (new_max, weight_sum, accumulated)

    state = (
        jnp.full((heads_here, tokens), -1e30, jnp.float32),
        jnp.zeros((heads_here, tokens), jnp.float32),
        jnp.zeros((tokens, heads_here, HD), jnp.float32),
    )
    state = absorb(state, key_value, allowed_at(0))
    moving = key_value
    for offset in range(1, window):
        moving = shifted(moving, "tm", 1)
        state = absorb(state, moving, allowed_at(offset))
    running_max, weight_sum, accumulated = state
    attention = (
        (accumulated / jnp.transpose(weight_sum)[:, :, None])
        .reshape(tokens, heads_here * HD)
        .astype(jnp.bfloat16)
    )
    weight_cols = lax.all_gather(out_weight, "tm", axis=0, tiled=True)
    projected = jnp.dot(
        lax.all_gather(attention, "head", axis=1, tiled=True),
        weight_cols,
        preferred_element_type=jnp.float32,
    )
    gate = jnp.dot(
        time_features(noise_steps), time_weight.astype(jnp.float32), precision=lax.Precision.HIGHEST
    )
    updated = (residual[0].astype(jnp.float32) + gate * projected).astype(jnp.bfloat16)
    moved = shifted(updated, "tm", -1)
    rolled = jnp.where(frame == frames_total - 1, fresh_frame, moved)
    return rolled[None]


def whole_in_vmem(count):
    return [pl.BlockSpec(memory_space=pltpu.VMEM)] * count


def in_hbm(count):
    return [pl.BlockSpec(memory_space=pltpu.HBM)] * count


def roomy():
    return pltpu.CompilerParams(vmem_limit_bytes=VMEM_BYTES)


def pack(queries, keys, values, frame_mask, noise_steps, moves, pairs, width):
    tokens, kind = (queries.shape[0], queries.dtype)
    window = frame_mask.shape[1]
    heads = width // HD
    body = 3 * heads * tokens
    heights = [body + (NOTE_ROWS if b == 0 else 0) for a, b in moves]
    count = len(moves)

    def kernel(*refs):
        sources, small, pieces, scratch = (refs[:3], refs[3:5], refs[5 : 5 + count], refs[5 + count :])
        loaded, packed, mask_ref, noise_ref, in_sems, out_sems = scratch
        frame, pair = (lax.axis_index("tm"), lax.axis_index("head") // 2)
        targets = [loaded.at[place] for place in range(3)] + [mask_ref, noise_ref]
        loads = [
            pltpu.make_async_copy(source, target, in_sems.at[place])
            for place, (source, target) in enumerate(zip((*sources, *small), targets))
        ]
        for load in loads:
            load.start()
        for load in loads:
            load.wait()
        lane = lax.broadcasted_iota(jnp.int32, (NOTE_ROWS, HD), 1)
        note = jnp.where(lane == window, noise_ref[0], 0)
        for column in range(window):
            note = jnp.where(lane == column, mask_ref[0, column], note)
        note = note.astype(jnp.float32).astype(kind)
        stores = []
        for number, (a, b) in enumerate(moves):
            block = (frame ^ a) * pairs + (pair ^ b)
            for place in range(3):
                for head in range(heads):
                    columns = pl.ds(pl.multiple_of((block * heads + head) * HD, HD), HD)
                    first = (place * heads + head) * tokens
                    packed[number, first : first + tokens, :] = loaded[place, :, columns]
            if b == 0:
                packed[number, body:, :] = note
            store = pltpu.make_async_copy(
                packed.at[number, : heights[number]], pieces[number], out_sems.at[number]
            )
            store.start()
            stores.append(store)
        for store in stores:
            store.wait()

    return pl.pallas_call(
        kernel,
        out_shape=[jax.ShapeDtypeStruct((height, HD), kind) for height in heights],
        in_specs=in_hbm(5),
        out_specs=in_hbm(count),
        scratch_shapes=[
            pltpu.VMEM((3, *queries.shape), kind),
            pltpu.VMEM((count, body + NOTE_ROWS, HD), kind),
            pltpu.SMEM(frame_mask.shape, frame_mask.dtype),
            pltpu.SMEM(noise_steps.shape, noise_steps.dtype),
            pltpu.SemaphoreType.DMA((5,)),
            pltpu.SemaphoreType.DMA((count,)),
        ],
        compiler_params=pltpu.CompilerParams(vmem_limit_bytes=PACK_BYTES),
        name="pack",
    )(queries, keys, values, frame_mask, noise_steps)


def bring(*arrays):
    def kernel(*refs):
        for source, target in zip(refs[: len(arrays)], refs[len(arrays) :]):
            target[...] = source[...]

    return pl.pallas_call(
        kernel,
        out_shape=[jax.ShapeDtypeStruct(array.shape, array.dtype) for array in arrays],
        in_specs=whole_in_vmem(len(arrays)),
        out_specs=whole_in_vmem(len(arrays)),
        compiler_params=roomy(),
        name="bring",
    )(*arrays)


def pick(table, here):
    result = table[0]
    for place, entry in enumerate(table[1:], 1):
        result = jnp.where(here == place, entry, result)
    return result


def attend_frames(slots, out_refs, query_buf, key_buf, value_buf, note_ref):
    frames, keys_rows, width = key_buf.shape
    scale = math.log2(math.e) / math.sqrt(HD)
    here = lax.axis_index("tm")
    for frames_of_slot, out_ref in zip(slots, out_refs):
        frame = pick(frames_of_slot, here)
        note = note_ref[pl.ds(frame, 1), :]
        lane = lax.broadcasted_iota(jnp.int32, note.shape, 1)
        biases = []
        for a in range(frames):
            hit = jnp.sum(jnp.where(lane == here ^ a, note, 0.0), axis=1, keepdims=True)
            biases.append(jnp.broadcast_to((hit - 1.0) * 1e30, (1, keys_rows)))
        bias = jnp.concatenate(biases, axis=1)
        for start in range(0, width, HD):
            channels = slice(start, start + HD)
            query = query_buf[frame, :, channels]
            keys = key_buf[:, :, channels].reshape(frames * keys_rows, HD)
            scores = lax.dot_general(
                query, keys, (((1,), (1,)), ((), ())), preferred_element_type=jnp.float32
            )
            scores = scores * scale + bias
            lifted = jnp.exp2(scores - jnp.max(scores, axis=1, keepdims=True))
            totals = jnp.sum(lifted, axis=1, keepdims=True)
            values = value_buf[:, :, channels].reshape(frames * keys_rows, HD)
            mixed = jnp.dot(
                lifted.astype(jnp.bfloat16), values, preferred_element_type=jnp.float32
            )
            out_ref[:, channels] = (mixed / totals).astype(jnp.bfloat16)


def attend(slots, own, mate, moves, pairs, frames, width):
    heads = width // HD
    tokens = (own[moves.index((0, 0))].shape[0] - NOTE_ROWS) // (3 * heads)
    rows, keys_rows = (pairs * tokens, 2 * pairs * tokens)

    def kernel(*refs):
        own_refs, refs = (refs[: len(moves)], refs[len(moves) :])
        mate_refs, refs = (refs[: len(moves)], refs[len(moves) :])
        out_refs, (query_buf, key_buf, value_buf, note_out) = (refs[: len(slots)], refs[len(slots) :])
        here = lax.axis_index("tm")
        for own_ref, mate_ref, (a, b) in zip(own_refs, mate_refs, moves):
            for head in range(heads):
                channels = slice(head * HD, (head + 1) * HD)
                query, key, value = [
                    slice((place * heads + head) * tokens, (place * heads + head + 1) * tokens)
                    for place in range(3)
                ]
                query_buf[here ^ a, b * tokens : (b + 1) * tokens, channels] = own_ref[query, :]
                for side, ref in enumerate((own_ref, mate_ref)):
                    span = slice((2 * b + side) * tokens, (2 * b + side + 1) * tokens)
                    key_buf[a, span, channels] = ref[key, :]
                    value_buf[a, span, channels] = ref[value, :]
            if b == 0:
                note_out[pl.ds(here ^ a, 1), :] = own_ref[3 * heads * tokens :, :].astype(jnp.float32)[:1]
        attend_frames(slots, out_refs, query_buf, key_buf, value_buf, note_out)

    kind = own[0].dtype
    outs = pl.pallas_call(
        kernel,
        out_shape=[jax.ShapeDtypeStruct((rows, width), jnp.bfloat16)] * len(slots)
        + [
            jax.ShapeDtypeStruct((frames, rows, width), kind),
            jax.ShapeDtypeStruct((frames, keys_rows, width), kind),
            jax.ShapeDtypeStruct((frames, keys_rows, width), kind),
            jax.ShapeDtypeStruct((16, HD), jnp.float32),
        ],
        in_specs=whole_in_vmem(2 * len(moves)),
        out_specs=whole_in_vmem(len(slots) + 4),
        compiler_params=roomy(),
        name="attend",
    )(*own, *mate)
    return (outs[: len(slots)], outs[len(slots) :])


def attend_again(slots, held):
    rows, width = held[0].shape[1:]

    def kernel(*refs):
        out_ref = refs[len(held)]
        parts = [out_ref.at[slot * rows : (slot + 1) * rows] for slot in range(len(slots))]
        attend_frames(slots, parts, *refs[: len(held)])

    return pl.pallas_call(
        kernel,
        out_shape=jax.ShapeDtypeStruct((len(slots) * rows, width), jnp.bfloat16),
        in_specs=whole_in_vmem(len(held)),
        out_specs=whole_in_vmem(1)[0],
        compiler_params=roomy(),
        name="attend_again",
    )(*held)


def project(pieces, weight, kinds, slots=1):
    flat = [piece for part in pieces for piece in part]
    rows, width = (flat[0].shape[0] // slots, flat[0].shape[1])
    pairs, sets = (len(pieces[0]), len(pieces))
    tokens = rows // pairs
    depth, columns = weight.shape
    step = math.gcd(columns, 256)

    def kernel(*refs):
        sources = iter(refs[: len(flat)])
        weight_ref, refs = (refs[len(flat)], refs[len(flat) + 1 :])
        whole = refs[-1]
        here = lax.axis_index("head") // 2
        for k in range(sets):
            for move in range(pairs):
                source = next(sources)
                pair = here ^ move
                channels = pl.ds(pl.multiple_of(pair * width, HD), width)
                for slot in range(slots):
                    for b in range(pairs):
                        first = (slot * sets + k) * rows + (pair ^ b) * tokens
                        start = slot * rows + b * tokens
                        whole[pl.ds(pl.multiple_of(first, 16), tokens), channels] = source[
                            start : start + tokens, :
                        ]
        for start in range(0, columns, step):
            inner = slice(start, start + step)
            product = jnp.dot(
                whole[...], weight_ref[:, inner], preferred_element_type=jnp.float32
            )
            for number in range(slots * sets):
                share = product[number * rows : (number + 1) * rows, :]
                for out_ref in refs[number * len(kinds) : (number + 1) * len(kinds)]:
                    out_ref[:, inner] = share.astype(out_ref.dtype)

    outs = pl.pallas_call(
        kernel,
        out_shape=[
            jax.ShapeDtypeStruct((rows, columns), kind)
            for _ in range(slots * sets)
            for kind in kinds
        ],
        in_specs=whole_in_vmem(len(flat) + 1),
        out_specs=whole_in_vmem(len(kinds) * slots * sets),
        scratch_shapes=[pltpu.VMEM((slots * sets * rows, depth), jnp.bfloat16)],
        compiler_params=roomy(),
        name="project",
    )(*flat, weight)
    return [list(outs[number :: len(kinds)]) for number in range(len(kinds))]


def gates_of(notes, time_weight, column, frames):
    depth, columns = time_weight.shape
    half = depth // 2

    def kernel(note_ref, weight_ref, here_ref, next_ref):
        here = lax.axis_index("tm")
        following = jnp.minimum(here + 1, frames - 1)
        rows = jnp.concatenate([note_ref[pl.ds(here, 1), :], note_ref[pl.ds(following, 1), :]], axis=0)
        lane = lax.broadcasted_iota(jnp.int32, rows.shape, 1)
        noise = jnp.sum(jnp.where(lane == column, rows, 0.0), axis=1, keepdims=True)
        timestep = 1000.0 * (noise + 1.0) / STEPS
        place = lax.broadcasted_iota(jnp.int32, (2, half), 1).astype(jnp.float32)
        angles = timestep * jnp.exp(-math.log(10000.0) * place / half)
        features = jnp.concatenate([jnp.cos(angles), jnp.sin(angles)], axis=1)
        gates = jnp.dot(
            features,
            weight_ref[...].astype(jnp.float32),
            precision=lax.Precision.HIGHEST,
            preferred_element_type=jnp.float32,
        )
        here_ref[...] = gates[:1]
        next_ref[...] = gates[1:]

    return pl.pallas_call(
        kernel,
        out_shape=[jax.ShapeDtypeStruct((1, columns), jnp.float32)] * 2,
        in_specs=whole_in_vmem(2),
        out_specs=whole_in_vmem(2),
        compiler_params=roomy(),
        name="gates_of",
    )(notes, time_weight)


def frame_rows(k, pairs, tokens):
    core = (lax.axis_index("head") % 2) ^ k
    return [pl.ds(pl.multiple_of((2 * p + core) * tokens, 16), tokens) for p in range(pairs)]


def join(partial, table, arrived, k, pairs, residual=None, gate=None):
    rows, columns = partial[0].shape
    tokens = rows // pairs
    step = math.gcd(columns, 256)
    slots = sorted(set(table))
    extras = [] if residual is None else [residual, gate]

    def kernel(*refs):
        own_refs, refs = (refs[: len(slots)], refs[len(slots) :])
        arrived_refs, refs = (refs[: len(arrived)], refs[len(arrived) :])
        out_ref = refs[-1]
        here = lax.axis_index("tm")
        places = frame_rows(k, pairs, tokens)
        for slot, own_ref in zip(slots, own_refs):

            @pl.when(pick([entry == slot for entry in table], here))
            def _(own_ref=own_ref):
                for p, place in enumerate(places):
                    inner = slice(p * tokens, (p + 1) * tokens)
                    for start in range(0, columns, step):
                        part = slice(start, start + step)
                        total = own_ref[inner, part]
                        for ref in arrived_refs:
                            total += ref[inner, part].astype(jnp.float32)
                        if extras:
                            kept = refs[0][place, part].astype(jnp.float32)
                            total = kept + refs[1][:, part] * total
                        out_ref[inner, part] = total.astype(jnp.bfloat16)

    operands = [partial[slot] for slot in slots] + list(arrived) + extras
    return pl.pallas_call(
        kernel,
        out_shape=jax.ShapeDtypeStruct((rows, columns), jnp.bfloat16),
        in_specs=whole_in_vmem(len(operands)),
        out_specs=whole_in_vmem(1)[0],
        compiler_params=roomy(),
        name="join",
    )(*operands)


def finish(arrived, partial, below, gate, fresh_frame, pairs):
    rows, columns = partial[0].shape
    tokens = rows // pairs
    step = math.gcd(columns, 256)
    sets = len(partial)

    def kernel(*refs):
        arrived_refs, partial_refs, below_refs = (
            refs[:sets],
            refs[sets : 2 * sets],
            refs[2 * sets : 3 * sets],
        )
        gate_ref, fresh_ref, out_ref = refs[3 * sets :]
        last = lax.axis_index("tm") == lax.axis_size("tm") - 1

        @pl.when(last)
        def _():
            out_ref[...] = fresh_ref[...]

        @pl.when(jnp.logical_not(last))
        def _():
            for k in range(sets):
                for p, place in enumerate(frame_rows(k, pairs, tokens)):
                    inner = slice(p * tokens, (p + 1) * tokens)
                    for start in range(0, columns, step):
                        part = slice(start, start + step)
                        total = partial_refs[k][inner, part]
                        total += below_refs[k][inner, part].astype(jnp.float32)
                        total = gate_ref[:, part] * total
                        total += arrived_refs[k][inner, part].astype(jnp.float32)
                        out_ref[place, part] = total.astype(jnp.bfloat16)

    return pl.pallas_call(
        kernel,
        out_shape=jax.ShapeDtypeStruct(fresh_frame.shape, jnp.bfloat16),
        in_specs=whole_in_vmem(3 * sets + 2),
        out_specs=whole_in_vmem(1)[0],
        compiler_params=roomy(),
        name="finish",
    )(*arrived, *partial, *below, gate, fresh_frame)


def line_schedule(frames):
    steps = []
    for step in range(frames - 1):
        down = {z: step + 1 - (frames - 1 - z) for z in range(1, frames)}
        up = {z: frames - 1 - step + z for z in range(frames)}
        down = {z: f for z, f in down.items() if 1 <= f <= z}
        up = {z: f for z, f in up.items() if z + 2 <= f < frames}
        steps.append((down, up))
    order = []
    for z in range(frames):
        sent = [f for down, up in steps for f in (down.get(z), up.get(z)) if f is not None]
        order.append((sent + [z + 1])[: frames - 1])
    return steps, order


def head_plan(
    queries, keys, values, residual, fresh_frame, out_weight, time_weight, noise_steps, frame_mask
):
    frames, across = (lax.axis_size("tm"), lax.axis_size("head"))
    pairs = across // 2
    width = queries.shape[2] // (frames * pairs)
    everywhere = range(frames)

    def swap(array, j):
        return lax.ppermute(array, "head", [(h, h ^ j) for h in range(across)])

    def gather(part, meanwhile=None):
        near = [part]
        for move in range(1, pairs):
            piece = swap(part, 2 * move)
            if meanwhile is not None:
                piece, meanwhile = lax.optimization_barrier((piece, meanwhile))
            near.append(piece)
        return ([near, [swap(piece, 1) for piece in near]], meanwhile)

    far = [(a, b) for b in range(pairs) for a in reversed(everywhere[2:])]
    near = [(0, b) for b in range(1, pairs)] + [(1, b) for b in range(pairs - 1)]
    moves = [(1, pairs - 1)] + far + near + [(0, 0)]
    packed = pack(
        queries[0], keys[0], values[0], frame_mask, noise_steps, moves, pairs, width
    )
    own = []
    for piece, (a, b) in zip(packed, moves):
        if (a, b) != (0, 0):
            links = [
                (z * across + h, (z ^ a) * across + (h ^ (2 * b)))
                for z in everywhere
                for h in range(across)
            ]
            piece = lax.ppermute(piece, ("tm", "head"), links)
        own.append(piece)
    for number in range(1, 1 + len(far)):
        own[number], own[0] = lax.optimization_barrier((own[number], own[0]))
    mine = moves.index((0, 0))
    (own[mine],), weight = (bring(own[mine]), out_weight)
    mate = [swap(piece, 1) for piece in own]

    steps, order = line_schedule(frames)

    named = [[order[z][slot] for z in everywhere] for slot in range(frames - 1)]
    (part,), held = attend(named[:1], own, mate, moves, pairs, frames, width)
    following = attend_again(named[1:], held)
    pieces, following = gather(part, following)
    partial, payload = ([[]], [])
    for rows in pieces:
        product, rounded = project([rows], weight, (jnp.float32, jnp.bfloat16))
        partial[0] += product
        payload += rounded
    following, payload[0] = lax.optimization_barrier((following, payload[0]))
    down, up = steps[0]
    links = [(z, z - 1) for z in down] + [(z, z + 1) for z in up]
    above = [lax.ppermute(part, "tm", links) for part in payload]
    below = above
    pieces, _ = gather(following)
    later = project(pieces, weight, (jnp.float32,), frames - 2)[0]
    partial += [later[2 * slot : 2 * slot + 2] for slot in range(frames - 2)]
    gates = gates_of(held[-1], time_weight, frame_mask.shape[1], frames)

    for number, (down, up) in enumerate(steps[1:], 1):
        sends = {**down, **up}
        table = [order[z].index(sends[z]) if z in sends else 0 for z in everywhere]
        final = number == len(steps) - 1
        extras = (residual[0], gates[0]) if final else ()
        payload = [
            join(
                [products[k] for products in partial],
                table,
                [above[k]] if final or above is below else [above[k], below[k]],
                k,
                pairs,
                *extras,
            )
            for k in range(2)
        ]
        above = [lax.ppermute(part, "tm", [(z, z - 1) for z in down]) for part in payload]
        if up:
            below = [lax.ppermute(part, "tm", [(z, z + 1) for z in up]) for part in payload]
    return finish(above, partial[-1], below, gates[1], fresh_frame, pairs)[None]


def power_of_two(number):
    return number & (number - 1) == 0


def suits_line(frames, window):
    apart = all(not set(down) & set(up) for down, up in line_schedule(frames)[0])
    return 2 < frames <= window and power_of_two(frames) and apart


def on_device(queries, *others):
    frames, across = (lax.axis_size("tm"), lax.axis_size("head"))
    heads = queries.shape[2] // HD
    even = across % 2 == 0 and power_of_two(across)
    even = even and queries.shape[1] % 16 == 0
    if even and suits_line(frames, others[-1].shape[1]) and heads % (frames * across // 2) == 0:
        return head_plan(queries, *others)
    return frame_plan(queries, *others)


def solution(mesh):
    placed = (
        P(("groups", "tm"), "head", None),
        P(("groups", "tm"), "head", None),
        P(("groups", "tm"), "head", None),
        P(("groups", "tm"), None, "head"),
        P("groups", "head"),
        P("tm", "head"),
        P(None, "head"),
        P(("groups", "tm")),
        P(("groups", "tm"), None),
    )
    return jax.shard_map(
        on_device,
        mesh=mesh,
        in_specs=placed,
        out_specs=P(("groups", "tm"), None, "head"),
        check_vma=False,
    )
```

```python
import math

import jax
import jax.numpy as jnp
import numpy as np
from jax import lax
from jax.experimental import pallas as pl
from jax.experimental.pallas import tpu as pltpu
from jax.sharding import PartitionSpec as P

HD = 128
FREQ = 256
STEPS = 50
NOTE_ROWS = 16
VMEM_BYTES = 16 * 1024 * 1024
PACK_BYTES = 60 * 1024 * 1024


def shifted(value, axis, steps):
    count = lax.axis_size(axis)
    leading, last = (max(0, -steps), min(count, count - steps))
    return lax.ppermute(value, axis, [(source, source + steps) for source in range(leading, last)])


def time_features(noise_steps):
    timestep = 1000.0 * (noise_steps.astype(jnp.float32) + 1.0) / STEPS
    half = FREQ // 2
    rates = jnp.exp(-math.log(10000.0) * jnp.arange(half).astype(jnp.float32) / half)
    angles = timestep[:, None] * rates[None, :]
    return jnp.concatenate([jnp.cos(angles), jnp.sin(angles)], axis=1)


def frame_plan(
    queries, keys, values, residual, fresh_frame, out_weight, time_weight, noise_steps, frame_mask
):
    query_local, key_local, value_local = (
        lax.all_to_all(queries, "head", split_axis=2, concat_axis=1, tiled=True),
        lax.all_to_all(keys, "head", split_axis=2, concat_axis=1, tiled=True),
        lax.all_to_all(values, "head", split_axis=2, concat_axis=1, tiled=True),
    )
    tokens = query_local.shape[1]
    heads_here = query_local.shape[2] // HD
    scale = 1.0 / math.sqrt(HD)
    query_heads = query_local[0].reshape(tokens, heads_here, HD)
    key_value = jnp.stack([key_local[0], value_local[0]], axis=0)
    frame = lax.axis_index("tm")
    frames_total = lax.axis_size("tm")
    window = min(8, frames_total)
    mask_row = frame_mask[0]
    columns = jnp.arange(mask_row.shape[0], dtype=jnp.int32)

    def allowed_at(offset):
        hits = jnp.sum(jnp.where(columns == frame - offset, mask_row, 0))
        return hits > 0

    def absorb(state, block, allowed):
        running_max, weight_sum, accumulated = state
        key_heads = block[0].reshape(tokens, heads_here, HD)
        value_heads = block[1].reshape(tokens, heads_here, HD)
        scores = (
            jnp.einsum("qhd,khd->hqk", query_heads, key_heads, preferred_element_type=jnp.float32)
            * scale
        )
        new_max = jnp.where(allowed, jnp.maximum(running_max, jnp.max(scores, axis=2)), running_max)
        lifted = jnp.where(allowed, jnp.exp(jnp.minimum(scores - new_max[:, :, None], 0.0)), 0.0)
        factor = jnp.exp(running_max - new_max)
        weight_sum = weight_sum * factor + jnp.sum(lifted, axis=2)
        rounded = lifted.astype(jnp.bfloat16)
        accumulated = accumulated * jnp.transpose(factor)[:, :, None] + jnp.einsum(
            "hqk,khd->qhd", rounded, value_heads, preferred_element_type=jnp.float32
        )
        return (new_max, weight_sum, accumulated)

    state = (
        jnp.full((heads_here, tokens), -1e30, jnp.float32),
        jnp.zeros((heads_here, tokens), jnp.float32),
        jnp.zeros((tokens, heads_here, HD), jnp.float32),
    )
    state = absorb(state, key_value, allowed_at(0))
    moving = key_value
    for offset in range(1, window):
        moving = shifted(moving, "tm", 1)
        state = absorb(state, moving, allowed_at(offset))
    running_max, weight_sum, accumulated = state
    attention = (
        (accumulated / jnp.transpose(weight_sum)[:, :, None])
        .reshape(tokens, heads_here * HD)
        .astype(jnp.bfloat16)
    )
    weight_cols = lax.all_gather(out_weight, "tm", axis=0, tiled=True)
    projected = jnp.dot(
        lax.all_gather(attention, "head", axis=1, tiled=True),
        weight_cols,
        preferred_element_type=jnp.float32,
    )
    gate = jnp.dot(
        time_features(noise_steps), time_weight.astype(jnp.float32), precision=lax.Precision.HIGHEST
    )
    updated = (residual[0].astype(jnp.float32) + gate * projected).astype(jnp.bfloat16)
    moved = shifted(updated, "tm", -1)
    rolled = jnp.where(frame == frames_total - 1, fresh_frame, moved)
    return rolled[None]


def whole_in_vmem(count):
    return [pl.BlockSpec(memory_space=pltpu.VMEM)] * count


def in_hbm(count):
    return [pl.BlockSpec(memory_space=pltpu.HBM)] * count


def roomy():
    return pltpu.CompilerParams(vmem_limit_bytes=VMEM_BYTES)


def pack(queries, keys, values, frame_mask, noise_steps, moves, pairs, width):
    tokens, kind = (queries.shape[0], queries.dtype)
    window = frame_mask.shape[1]
    heads = width // HD
    body = 3 * heads * tokens
    heights = [body + (NOTE_ROWS if b == 0 else 0) for _, _, b in moves]
    count = len(moves)

    def kernel(*refs):
        sources, small, pieces, scratch = (refs[:3], refs[3:5], refs[5 : 5 + count], refs[5 + count :])
        loaded, packed, mask_ref, noise_ref, in_sems, out_sems = scratch
        frame, pair = (lax.axis_index("tm"), lax.axis_index("head") // 2)
        targets = [loaded.at[place] for place in range(3)] + [mask_ref, noise_ref]
        loads = [
            pltpu.make_async_copy(source, target, in_sems.at[place])
            for place, (source, target) in enumerate(zip((*sources, *small), targets))
        ]
        for load in loads:
            load.start()
        for load in loads:
            load.wait()
        lane = lax.broadcasted_iota(jnp.int32, (NOTE_ROWS, HD), 1)
        note = jnp.where(lane == window, noise_ref[0], 0)
        for column in range(window):
            note = jnp.where(lane == column, mask_ref[0, column], note)
        note = note.astype(jnp.float32).astype(kind)
        stores = []
        for number, (targets, _, b) in enumerate(moves):
            block = pick(targets, frame) * pairs + (pair ^ b)
            for place in range(3):
                for head in range(heads):
                    columns = pl.ds(pl.multiple_of((block * heads + head) * HD, HD), HD)
                    first = (place * heads + head) * tokens
                    packed[number, first : first + tokens, :] = loaded[place, :, columns]
            if b == 0:
                packed[number, body:, :] = note
            store = pltpu.make_async_copy(
                packed.at[number, : heights[number]], pieces[number], out_sems.at[number]
            )
            store.start()
            stores.append(store)
        for store in stores:
            store.wait()

    return pl.pallas_call(
        kernel,
        out_shape=[jax.ShapeDtypeStruct((height, HD), kind) for height in heights],
        in_specs=in_hbm(5),
        out_specs=in_hbm(count),
        scratch_shapes=[
            pltpu.VMEM((3, *queries.shape), kind),
            pltpu.VMEM((count, body + NOTE_ROWS, HD), kind),
            pltpu.SMEM(frame_mask.shape, frame_mask.dtype),
            pltpu.SMEM(noise_steps.shape, noise_steps.dtype),
            pltpu.SemaphoreType.DMA((5,)),
            pltpu.SemaphoreType.DMA((count,)),
        ],
        compiler_params=pltpu.CompilerParams(vmem_limit_bytes=PACK_BYTES),
        name="pack",
    )(queries, keys, values, frame_mask, noise_steps)


def bring(*arrays):
    def kernel(*refs):
        for source, target in zip(refs[: len(arrays)], refs[len(arrays) :]):
            target[...] = source[...]

    return pl.pallas_call(
        kernel,
        out_shape=[jax.ShapeDtypeStruct(array.shape, array.dtype) for array in arrays],
        in_specs=whole_in_vmem(len(arrays)),
        out_specs=whole_in_vmem(len(arrays)),
        compiler_params=roomy(),
        name="bring",
    )(*arrays)


def pick(table, here):
    result = table[0]
    for place, entry in enumerate(table[1:], 1):
        result = jnp.where(here == place, entry, result)
    return result


def attend_frames(slots, out_refs, query_buf, key_buf, value_buf, note_ref):
    frames, keys_rows, width = key_buf.shape
    scale = math.log2(math.e) / math.sqrt(HD)
    here = lax.axis_index("tm")
    for frames_of_slot, out_ref in zip(slots, out_refs):
        frame = pick(frames_of_slot, here)
        note = note_ref[pl.ds(frame, 1), :]
        lane = lax.broadcasted_iota(jnp.int32, note.shape, 1)
        biases = []
        for other in range(frames):
            hit = jnp.sum(jnp.where(lane == other, note, 0.0), axis=1, keepdims=True)
            biases.append(jnp.broadcast_to((hit - 1.0) * 1e30, (1, keys_rows)))
        bias = jnp.concatenate(biases, axis=1)
        for start in range(0, width, HD):
            channels = slice(start, start + HD)
            query = query_buf[frame, :, channels]
            keys = key_buf[:, :, channels].reshape(frames * keys_rows, HD)
            scores = lax.dot_general(
                query, keys, (((1,), (1,)), ((), ())), preferred_element_type=jnp.float32
            )
            scores = scores * scale + bias
            lifted = jnp.exp2(scores - jnp.max(scores, axis=1, keepdims=True))
            totals = jnp.sum(lifted, axis=1, keepdims=True)
            values = value_buf[:, :, channels].reshape(frames * keys_rows, HD)
            mixed = jnp.dot(
                lifted.astype(jnp.bfloat16), values, preferred_element_type=jnp.float32
            )
            out_ref[:, channels] = (mixed / totals).astype(jnp.bfloat16)


def attend(slots, own, mate, moves, pairs, frames, width, only=None):
    heads = width // HD
    height = min(piece.shape[0] for piece in own)
    tokens = height // (3 * heads)
    rows, keys_rows = (pairs * tokens, 2 * pairs * tokens)

    def work(*refs):
        own_refs, refs = (refs[: len(moves)], refs[len(moves) :])
        mate_refs, refs = (refs[: len(moves)], refs[len(moves) :])
        out_ref, query_buf, key_buf, value_buf, note_out = refs
        here = lax.axis_index("tm")
        for own_ref, mate_ref, (_, sources, b) in zip(own_refs, mate_refs, moves):

            def take(own_ref=own_ref, mate_ref=mate_ref, sources=sources, b=b):
                frame = pick([0 if source is None else source for source in sources], here)
                for head in range(heads):
                    channels = slice(head * HD, (head + 1) * HD)
                    query, key, value = [
                        slice((place * heads + head) * tokens, (place * heads + head + 1) * tokens)
                        for place in range(3)
                    ]
                    query_buf[frame, b * tokens : (b + 1) * tokens, channels] = own_ref[query, :]
                    for side, ref in enumerate((own_ref, mate_ref)):
                        span = slice((2 * b + side) * tokens, (2 * b + side + 1) * tokens)
                        key_buf[frame, span, channels] = ref[key, :]
                        value_buf[frame, span, channels] = ref[value, :]
                if b == 0:
                    note_out[pl.ds(frame, 1), :] = own_ref[3 * heads * tokens :, :].astype(
                        jnp.float32
                    )[:1]

            if only is None and None in sources:
                pl.when(pick([source is not None for source in sources], here))(take)
            else:
                take()
        parts = [out_ref.at[slot * rows : (slot + 1) * rows] for slot in range(len(slots))]
        attend_frames(slots, parts, query_buf, key_buf, value_buf, note_out)

    def kernel(*refs):
        if only is None:
            work(*refs)
        else:
            pl.when(lax.axis_index("tm") == only)(lambda: work(*refs))

    kind = own[0].dtype
    out, *held = pl.pallas_call(
        kernel,
        out_shape=[
            jax.ShapeDtypeStruct((len(slots) * rows, width), jnp.bfloat16),
            jax.ShapeDtypeStruct((frames, rows, width), kind),
            jax.ShapeDtypeStruct((frames, keys_rows, width), kind),
            jax.ShapeDtypeStruct((frames, keys_rows, width), kind),
            jax.ShapeDtypeStruct((16, HD), jnp.float32),
        ],
        in_specs=whole_in_vmem(2 * len(moves)),
        out_specs=whole_in_vmem(5),
        compiler_params=roomy(),
        name="attend",
    )(*own, *mate)
    return (out, held)


def attend_again(slots, held):
    rows, width = held[0].shape[1:]

    def kernel(*refs):
        out_ref = refs[len(held)]
        parts = [out_ref.at[slot * rows : (slot + 1) * rows] for slot in range(len(slots))]
        attend_frames(slots, parts, *refs[: len(held)])

    return pl.pallas_call(
        kernel,
        out_shape=jax.ShapeDtypeStruct((len(slots) * rows, width), jnp.bfloat16),
        in_specs=whole_in_vmem(len(held)),
        out_specs=whole_in_vmem(1)[0],
        compiler_params=roomy(),
        name="attend_again",
    )(*held)


def project(pieces, weight, kinds, slots=1, cuts=None, only=None):
    flat = [piece for part in pieces for piece in part]
    rows, width = (flat[0].shape[0] // slots, flat[0].shape[1])
    pairs, sets = (len(pieces[0]), len(pieces))
    tokens = rows // pairs
    depth, columns = weight.shape
    step = math.gcd(columns, 256)
    ends = cuts or [(number + 1) * rows for number in range(slots * sets)]
    spans = list(zip([0, *ends], ends))

    def work(*refs):
        sources = iter(refs[: len(flat)])
        weight_ref, refs = (refs[len(flat)], refs[len(flat) + 1 :])
        whole = refs[-1]
        here = lax.axis_index("head") // 2
        for k in range(sets):
            for move in range(pairs):
                source = next(sources)
                pair = here ^ move
                channels = pl.ds(pl.multiple_of(pair * width, HD), width)
                for slot in range(slots):
                    for b in range(pairs):
                        first = (slot * sets + k) * rows + (pair ^ b) * tokens
                        start = slot * rows + b * tokens
                        whole[pl.ds(pl.multiple_of(first, 16), tokens), channels] = source[
                            start : start + tokens, :
                        ]
        for start in range(0, columns, step):
            inner = slice(start, start + step)
            product = jnp.dot(
                whole[...], weight_ref[:, inner], preferred_element_type=jnp.float32
            )
            for number, (top, bottom) in enumerate(spans):
                share = product[top:bottom, :]
                for out_ref in refs[number * len(kinds) : (number + 1) * len(kinds)]:
                    out_ref[:, inner] = share.astype(out_ref.dtype)

    def kernel(*refs):
        if only is None:
            work(*refs)
        else:
            pl.when(lax.axis_index("tm") == only)(lambda: work(*refs))

    outs = pl.pallas_call(
        kernel,
        out_shape=[
            jax.ShapeDtypeStruct((bottom - top, columns), kind)
            for top, bottom in spans
            for kind in kinds
        ],
        in_specs=whole_in_vmem(len(flat) + 1),
        out_specs=whole_in_vmem(len(kinds) * len(spans)),
        scratch_shapes=[pltpu.VMEM((slots * sets * rows, depth), jnp.bfloat16)],
        compiler_params=roomy(),
        name="project",
    )(*flat, weight)
    return [list(outs[number :: len(kinds)]) for number in range(len(kinds))]


def gates_of(notes, time_weight, column, frames):
    depth, columns = time_weight.shape
    half = depth // 2

    def kernel(note_ref, weight_ref, here_ref, next_ref):
        here = lax.axis_index("tm")
        following = jnp.minimum(here + 1, frames - 1)
        rows = jnp.concatenate([note_ref[pl.ds(here, 1), :], note_ref[pl.ds(following, 1), :]], axis=0)
        lane = lax.broadcasted_iota(jnp.int32, rows.shape, 1)
        noise = jnp.sum(jnp.where(lane == column, rows, 0.0), axis=1, keepdims=True)
        timestep = 1000.0 * (noise + 1.0) / STEPS
        place = lax.broadcasted_iota(jnp.int32, (2, half), 1).astype(jnp.float32)
        angles = timestep * jnp.exp(-math.log(10000.0) * place / half)
        features = jnp.concatenate([jnp.cos(angles), jnp.sin(angles)], axis=1)
        gates = jnp.dot(
            features,
            weight_ref[...].astype(jnp.float32),
            precision=lax.Precision.HIGHEST,
            preferred_element_type=jnp.float32,
        )
        here_ref[...] = gates[:1]
        next_ref[...] = gates[1:]

    return pl.pallas_call(
        kernel,
        out_shape=[jax.ShapeDtypeStruct((1, columns), jnp.float32)] * 2,
        in_specs=whole_in_vmem(2),
        out_specs=whole_in_vmem(2),
        compiler_params=roomy(),
        name="gates_of",
    )(notes, time_weight)


def frame_rows(k, pairs, tokens):
    core = (lax.axis_index("head") % 2) ^ k
    return [pl.ds(pl.multiple_of((2 * p + core) * tokens, 16), tokens) for p in range(pairs)]


def join(partial, table, arrived, k, pairs, residual=None, gate=None):
    rows, columns = partial[0].shape
    tokens = rows // pairs
    step = math.gcd(columns, 256)
    slots = sorted(set(table))
    extras = [] if residual is None else [residual, gate]
    starts = [0]
    if len(arrived) > 1:
        starts = [sum(part.shape[0] for part in arrived[:n]) - k * rows for n in range(len(arrived))]

    def kernel(*refs):
        own_refs, refs = (refs[: len(slots)], refs[len(slots) :])
        arrived_refs, refs = (refs[: len(arrived)], refs[len(arrived) :])
        out_ref = refs[-1]
        here = lax.axis_index("tm")
        places = frame_rows(k, pairs, tokens)
        for slot, own_ref in zip(slots, own_refs):

            @pl.when(pick([entry == slot for entry in table], here))
            def _(own_ref=own_ref):
                for p, place in enumerate(places):
                    inner = slice(p * tokens, (p + 1) * tokens)
                    for start in range(0, columns, step):
                        part = slice(start, start + step)
                        total = own_ref[inner, part]
                        for first, ref in zip(starts, arrived_refs):
                            if first <= inner.start and inner.stop <= first + ref.shape[0]:
                                rising = ref[inner.start - first : inner.stop - first, part]
                                total += rising.astype(jnp.float32)
                        if extras:
                            kept = refs[0][place, part].astype(jnp.float32)
                            total = kept + refs[1][:, part] * total
                        out_ref[inner, part] = total.astype(jnp.bfloat16)

    operands = [partial[slot] for slot in slots] + list(arrived) + extras
    return pl.pallas_call(
        kernel,
        out_shape=jax.ShapeDtypeStruct((rows, columns), jnp.bfloat16),
        in_specs=whole_in_vmem(len(operands)),
        out_specs=whole_in_vmem(1)[0],
        compiler_params=roomy(),
        name="join",
    )(*operands)


def finish(arrived, partial, below, gate, fresh_frame, pairs):
    rows, columns = partial[0].shape
    tokens = rows // pairs
    step = math.gcd(columns, 256)
    sets = len(partial)

    def kernel(*refs):
        arrived_refs, partial_refs, below_refs = (
            refs[:sets],
            refs[sets : 2 * sets],
            refs[2 * sets : 3 * sets],
        )
        gate_ref, fresh_ref, out_ref = refs[3 * sets :]
        last = lax.axis_index("tm") == lax.axis_size("tm") - 1

        @pl.when(last)
        def _():
            out_ref[...] = fresh_ref[...]

        @pl.when(jnp.logical_not(last))
        def _():
            for k in range(sets):
                for p, place in enumerate(frame_rows(k, pairs, tokens)):
                    inner = slice(p * tokens, (p + 1) * tokens)
                    for start in range(0, columns, step):
                        part = slice(start, start + step)
                        total = partial_refs[k][inner, part]
                        total += below_refs[k][inner, part].astype(jnp.float32)
                        total = gate_ref[:, part] * total
                        total += arrived_refs[k][inner, part].astype(jnp.float32)
                        out_ref[place, part] = total.astype(jnp.bfloat16)

    return pl.pallas_call(
        kernel,
        out_shape=jax.ShapeDtypeStruct(fresh_frame.shape, jnp.bfloat16),
        in_specs=whole_in_vmem(3 * sets + 2),
        out_specs=whole_in_vmem(1)[0],
        compiler_params=roomy(),
        name="finish",
    )(*arrived, *partial, *below, gate, fresh_frame)


def line_schedule(frames):
    steps = []
    for step in range(frames - 1):
        down = {z: step + 1 - (frames - 1 - z) for z in range(1, frames)}
        up = {z: frames - 1 - step + z for z in range(frames)}
        down = {z: f for z, f in down.items() if 1 <= f <= z}
        up = {z: f for z, f in up.items() if z + 2 <= f < frames}
        steps.append((down, up))
    order = []
    for z in range(frames):
        sent = [f for down, up in steps for f in (down.get(z), up.get(z)) if f is not None]
        order.append((sent + [z + 1])[: frames - 1])
    return steps, order


def line_rounds(frames):
    half = frames // 2
    rounds = [{source: target} for target in reversed(range(half, frames)) for source in range(half)]
    rest = [(z, z - 1) for z in reversed(range(1, frames))]
    rest += [(z, y) for y in reversed(range(frames)) for z in reversed(range(frames)) if y < z - 1]
    rest += [(z, y) for z in reversed(range(frames)) for y in range(z + 1, frames)]
    for source, target in rest:
        if any(pairs.get(source) == target for pairs in rounds):
            continue
        for pairs in rounds:
            if source not in pairs and target not in pairs.values():
                pairs[source] = target
                break
        else:
            rounds.append({source: target})
    return rounds


def head_plan(
    queries, keys, values, residual, fresh_frame, out_weight, time_weight, noise_steps, frame_mask
):
    frames, across = (lax.axis_size("tm"), lax.axis_size("head"))
    pairs = across // 2
    width = queries.shape[2] // (frames * pairs)
    everywhere = range(frames)

    end = frames - 1

    def swap(array, j, places=everywhere):
        links = [(z * across + h, z * across + (h ^ j)) for z in places for h in range(across)]
        return lax.ppermute(array, ("tm", "head"), links)

    def gather(part, places=everywhere, after=None):
        near = [part] + [swap(part, 2 * move, places) for move in range(1, pairs)]
        if after is not None:
            near, after[0] = lax.optimization_barrier((near, after[0]))
        return [near, [swap(piece, 1, places) for piece in near]]

    rounds = line_rounds(frames)
    moves = []
    for number in (0, 1, 2, 3):
        for b in range(pairs):
            targets = [rounds[number].get(z, z) for z in everywhere]
            sources = [None] * frames
            for source, target in rounds[number].items():
                sources[target] = source
            moves.append((targets, sources, b))
    moves += [(list(everywhere), list(everywhere), b) for b in reversed(range(pairs))]
    packed = pack(
        queries[0], keys[0], values[0], frame_mask, noise_steps, moves, pairs, width
    )
    own = []
    for piece, (targets, sources, b) in zip(packed, moves):
        links = [
            (z * across + h, targets[z] * across + (h ^ (2 * b)))
            for z in everywhere
            if targets[z] != z or b > 0 and sources[z] == z
            for h in range(across)
        ]
        if links:
            piece = lax.ppermute(piece, ("tm", "head"), links)
        own.append(piece)
    first = 2 * pairs
    (own[-1],) = bring(own[-1])

    mate = [swap(piece, 1) for piece in own[:first]]
    mate[0], own[first] = lax.optimization_barrier((mate[0], own[first]))
    part, _ = attend(
        [[1] * frames], own[:first], mate, moves[:first], pairs, 2, width, end
    )
    pieces = gather(part, [end])
    pieces[0][1], own[first + 1], own[first + 2] = lax.optimization_barrier(
        (pieces[0][1], own[first + 1], own[first + 2])
    )
    rows = 2 * part.shape[0]
    (above,) = project(pieces, out_weight, (jnp.bfloat16,), cuts=[rows // 4, rows], only=end)
    above = [lax.ppermute(rounded, "tm", [(end, end - 1)]) for rounded in above]
    own[first + 4], above[0] = lax.optimization_barrier((own[first + 4], above[0]))
    mate += [swap(piece, 1) for piece in own[first:]]

    steps, order = line_schedule(frames)
    named = [[order[z][slot] for z in everywhere] for slot in range(frames - 1)]
    part, held = attend(named[:2], own, mate, moves, pairs, frames, width)
    following = attend_again(named[2:], held)
    kinds = (jnp.float32, jnp.bfloat16)
    after = [above]
    pieces = gather(part, after=after)
    above = after[0]
    product, rounded = project(pieces, out_weight, kinds, 2)
    partial = [product[:2], product[2:]]
    below = [lax.ppermute(rounded[k], "tm", [(z, z + 1) for z in steps[0][1]]) for k in range(2)]
    partial.append(project(gather(following), out_weight, (jnp.float32,))[0])
    gates = gates_of(held[-1], time_weight, frame_mask.shape[1], frames)

    for number, (down, up) in enumerate(steps[1:], 1):
        sends = {**down, **up}
        table = [order[z].index(sends[z]) if z in sends else 0 for z in everywhere]
        final = number == len(steps) - 1
        extras = (residual[0], gates[0]) if final else ()
        sets = [[products[k] for products in partial] for k in range(2)]
        if up:
            rising = [join(sets[k], table, [below[k]], k, pairs) for k in range(2)]
            below = [lax.ppermute(part, "tm", [(z, z + 1) for z in up]) for part in rising]
        falls = [above, above] if number == 1 else [[above[0]], [above[1]]]
        falling = [join(sets[k], table, falls[k], k, pairs, *extras) for k in range(2)]
        above = [lax.ppermute(part, "tm", [(z, z - 1) for z in down]) for part in falling]
    return finish(above, partial[-1], below, gates[1], fresh_frame, pairs)[None]


def power_of_two(number):
    return number & (number - 1) == 0


def suits_line(frames, window):
    apart = all(not set(down) & set(up) for down, up in line_schedule(frames)[0])
    return 2 < frames <= window and power_of_two(frames) and apart and len(line_rounds(frames)) == 4


def on_device(queries, *others):
    frames, across = (lax.axis_size("tm"), lax.axis_size("head"))
    heads = queries.shape[2] // HD
    even = across % 2 == 0 and power_of_two(across)
    even = even and queries.shape[1] % 16 == 0
    if even and suits_line(frames, others[-1].shape[1]) and heads % (frames * across // 2) == 0:
        return head_plan(queries, *others)
    return frame_plan(queries, *others)


def solution(mesh):
    placed = (
        P(("groups", "tm"), "head", None),
        P(("groups", "tm"), "head", None),
        P(("groups", "tm"), "head", None),
        P(("groups", "tm"), None, "head"),
        P("groups", "head"),
        P("tm", "head"),
        P(None, "head"),
        P(("groups", "tm")),
        P(("groups", "tm"), None),
    )
    return jax.shard_map(
        on_device,
        mesh=mesh,
        in_specs=placed,
        out_specs=P(("groups", "tm"), None, "head"),
        check_vma=False,
    )
```

```python
import math

import jax
import jax.numpy as jnp
import numpy as np
from jax import lax
from jax.experimental import pallas as pl
from jax.experimental.pallas import tpu as pltpu
from jax.sharding import PartitionSpec as P

HD = 128
FREQ = 256
STEPS = 50
NOTE_ROWS = 16
VMEM_BYTES = 16 * 1024 * 1024
PACK_BYTES = 60 * 1024 * 1024


def shifted(value, axis, steps):
    count = lax.axis_size(axis)
    leading, last = (max(0, -steps), min(count, count - steps))
    return lax.ppermute(value, axis, [(source, source + steps) for source in range(leading, last)])


def time_features(noise_steps):
    timestep = 1000.0 * (noise_steps.astype(jnp.float32) + 1.0) / STEPS
    half = FREQ // 2
    rates = jnp.exp(-math.log(10000.0) * jnp.arange(half).astype(jnp.float32) / half)
    angles = timestep[:, None] * rates[None, :]
    return jnp.concatenate([jnp.cos(angles), jnp.sin(angles)], axis=1)


def frame_plan(
    queries, keys, values, residual, fresh_frame, out_weight, time_weight, noise_steps, frame_mask
):
    query_local, key_local, value_local = (
        lax.all_to_all(queries, "head", split_axis=2, concat_axis=1, tiled=True),
        lax.all_to_all(keys, "head", split_axis=2, concat_axis=1, tiled=True),
        lax.all_to_all(values, "head", split_axis=2, concat_axis=1, tiled=True),
    )
    tokens = query_local.shape[1]
    heads_here = query_local.shape[2] // HD
    scale = 1.0 / math.sqrt(HD)
    query_heads = query_local[0].reshape(tokens, heads_here, HD)
    key_value = jnp.stack([key_local[0], value_local[0]], axis=0)
    frame = lax.axis_index("tm")
    frames_total = lax.axis_size("tm")
    window = min(8, frames_total)
    mask_row = frame_mask[0]
    columns = jnp.arange(mask_row.shape[0], dtype=jnp.int32)

    def allowed_at(offset):
        hits = jnp.sum(jnp.where(columns == frame - offset, mask_row, 0))
        return hits > 0

    def absorb(state, block, allowed):
        running_max, weight_sum, accumulated = state
        key_heads = block[0].reshape(tokens, heads_here, HD)
        value_heads = block[1].reshape(tokens, heads_here, HD)
        scores = (
            jnp.einsum("qhd,khd->hqk", query_heads, key_heads, preferred_element_type=jnp.float32)
            * scale
        )
        new_max = jnp.where(allowed, jnp.maximum(running_max, jnp.max(scores, axis=2)), running_max)
        lifted = jnp.where(allowed, jnp.exp(jnp.minimum(scores - new_max[:, :, None], 0.0)), 0.0)
        factor = jnp.exp(running_max - new_max)
        weight_sum = weight_sum * factor + jnp.sum(lifted, axis=2)
        rounded = lifted.astype(jnp.bfloat16)
        accumulated = accumulated * jnp.transpose(factor)[:, :, None] + jnp.einsum(
            "hqk,khd->qhd", rounded, value_heads, preferred_element_type=jnp.float32
        )
        return (new_max, weight_sum, accumulated)

    state = (
        jnp.full((heads_here, tokens), -1e30, jnp.float32),
        jnp.zeros((heads_here, tokens), jnp.float32),
        jnp.zeros((tokens, heads_here, HD), jnp.float32),
    )
    state = absorb(state, key_value, allowed_at(0))
    moving = key_value
    for offset in range(1, window):
        moving = shifted(moving, "tm", 1)
        state = absorb(state, moving, allowed_at(offset))
    running_max, weight_sum, accumulated = state
    attention = (
        (accumulated / jnp.transpose(weight_sum)[:, :, None])
        .reshape(tokens, heads_here * HD)
        .astype(jnp.bfloat16)
    )
    weight_cols = lax.all_gather(out_weight, "tm", axis=0, tiled=True)
    projected = jnp.dot(
        lax.all_gather(attention, "head", axis=1, tiled=True),
        weight_cols,
        preferred_element_type=jnp.float32,
    )
    gate = jnp.dot(
        time_features(noise_steps), time_weight.astype(jnp.float32), precision=lax.Precision.HIGHEST
    )
    updated = (residual[0].astype(jnp.float32) + gate * projected).astype(jnp.bfloat16)
    moved = shifted(updated, "tm", -1)
    rolled = jnp.where(frame == frames_total - 1, fresh_frame, moved)
    return rolled[None]


def whole_in_vmem(count):
    return [pl.BlockSpec(memory_space=pltpu.VMEM)] * count


def in_hbm(count):
    return [pl.BlockSpec(memory_space=pltpu.HBM)] * count


def roomy():
    return pltpu.CompilerParams(vmem_limit_bytes=VMEM_BYTES)


def pack(queries, keys, values, frame_mask, noise_steps, moves, pairs, width):
    tokens, kind = (queries.shape[0], queries.dtype)
    window = frame_mask.shape[1]
    heads = width // HD
    body = 3 * heads * tokens
    heights = [body + (NOTE_ROWS if b == 0 else 0) for a, b in moves]
    count = len(moves)

    def kernel(*refs):
        sources, small, pieces, scratch = (refs[:3], refs[3:5], refs[5 : 5 + count], refs[5 + count :])
        loaded, packed, mask_ref, noise_ref, in_sems, out_sems = scratch
        frame, pair = (lax.axis_index("tm"), lax.axis_index("head") // 2)
        targets = [loaded.at[place] for place in range(3)] + [mask_ref, noise_ref]
        loads = [
            pltpu.make_async_copy(source, target, in_sems.at[place])
            for place, (source, target) in enumerate(zip((*sources, *small), targets))
        ]
        for load in loads:
            load.start()
        for load in loads:
            load.wait()
        lane = lax.broadcasted_iota(jnp.int32, (NOTE_ROWS, HD), 1)
        note = jnp.where(lane == window, noise_ref[0], 0)
        for column in range(window):
            note = jnp.where(lane == column, mask_ref[0, column], note)
        note = note.astype(jnp.float32).astype(kind)
        stores = []
        for number, (a, b) in enumerate(moves):
            block = (frame ^ a) * pairs + (pair ^ b)
            for place in range(3):
                for head in range(heads):
                    columns = pl.ds(pl.multiple_of((block * heads + head) * HD, HD), HD)
                    first = (place * heads + head) * tokens
                    packed[number, first : first + tokens, :] = loaded[place, :, columns]
            if b == 0:
                packed[number, body:, :] = note
            store = pltpu.make_async_copy(
                packed.at[number, : heights[number]], pieces[number], out_sems.at[number]
            )
            store.start()
            stores.append(store)
        for store in stores:
            store.wait()

    return pl.pallas_call(
        kernel,
        out_shape=[jax.ShapeDtypeStruct((height, HD), kind) for height in heights],
        in_specs=in_hbm(5),
        out_specs=in_hbm(count),
        scratch_shapes=[
            pltpu.VMEM((3, *queries.shape), kind),
            pltpu.VMEM((count, body + NOTE_ROWS, HD), kind),
            pltpu.SMEM(frame_mask.shape, frame_mask.dtype),
            pltpu.SMEM(noise_steps.shape, noise_steps.dtype),
            pltpu.SemaphoreType.DMA((5,)),
            pltpu.SemaphoreType.DMA((count,)),
        ],
        compiler_params=pltpu.CompilerParams(vmem_limit_bytes=PACK_BYTES),
        name="pack",
    )(queries, keys, values, frame_mask, noise_steps)


def bring(*arrays):
    def kernel(*refs):
        for source, target in zip(refs[: len(arrays)], refs[len(arrays) :]):
            target[...] = source[...]

    return pl.pallas_call(
        kernel,
        out_shape=[jax.ShapeDtypeStruct(array.shape, array.dtype) for array in arrays],
        in_specs=whole_in_vmem(len(arrays)),
        out_specs=whole_in_vmem(len(arrays)),
        compiler_params=roomy(),
        name="bring",
    )(*arrays)


def pick(table, here):
    result = table[0]
    for place, entry in enumerate(table[1:], 1):
        result = jnp.where(here == place, entry, result)
    return result


def attend_frames(slots, out_refs, query_buf, key_buf, value_buf, note_ref):
    frames, keys_rows, width = key_buf.shape
    scale = math.log2(math.e) / math.sqrt(HD)
    here = lax.axis_index("tm")
    for frames_of_slot, out_ref in zip(slots, out_refs):
        frame = pick(frames_of_slot, here)
        note = note_ref[pl.ds(frame, 1), :]
        lane = lax.broadcasted_iota(jnp.int32, note.shape, 1)
        biases = []
        for a in range(frames):
            hit = jnp.sum(jnp.where(lane == here ^ a, note, 0.0), axis=1, keepdims=True)
            biases.append(jnp.broadcast_to((hit - 1.0) * 1e30, (1, keys_rows)))
        bias = jnp.concatenate(biases, axis=1)
        for start in range(0, width, HD):
            channels = slice(start, start + HD)
            query = query_buf[frame, :, channels]
            keys = key_buf[:, :, channels].reshape(frames * keys_rows, HD)
            scores = lax.dot_general(
                query, keys, (((1,), (1,)), ((), ())), preferred_element_type=jnp.float32
            )
            scores = scores * scale + bias
            lifted = jnp.exp2(scores - jnp.max(scores, axis=1, keepdims=True))
            totals = jnp.sum(lifted, axis=1, keepdims=True)
            values = value_buf[:, :, channels].reshape(frames * keys_rows, HD)
            mixed = jnp.dot(
                lifted.astype(jnp.bfloat16), values, preferred_element_type=jnp.float32
            )
            out_ref[:, channels] = (mixed / totals).astype(jnp.bfloat16)


def attend(slots, own, mate, moves, pairs, frames, width):
    heads = width // HD
    tokens = (own[moves.index((0, 0))].shape[0] - NOTE_ROWS) // (3 * heads)
    rows, keys_rows = (pairs * tokens, 2 * pairs * tokens)

    def kernel(*refs):
        own_refs, refs = (refs[: len(moves)], refs[len(moves) :])
        mate_refs, refs = (refs[: len(moves)], refs[len(moves) :])
        out_refs, (query_buf, key_buf, value_buf, note_out) = (refs[: len(slots)], refs[len(slots) :])
        here = lax.axis_index("tm")
        for own_ref, mate_ref, (a, b) in zip(own_refs, mate_refs, moves):
            for head in range(heads):
                channels = slice(head * HD, (head + 1) * HD)
                query, key, value = [
                    slice((place * heads + head) * tokens, (place * heads + head + 1) * tokens)
                    for place in range(3)
                ]
                query_buf[here ^ a, b * tokens : (b + 1) * tokens, channels] = own_ref[query, :]
                for side, ref in enumerate((own_ref, mate_ref)):
                    span = slice((2 * b + side) * tokens, (2 * b + side + 1) * tokens)
                    key_buf[a, span, channels] = ref[key, :]
                    value_buf[a, span, channels] = ref[value, :]
            if b == 0:
                note_out[pl.ds(here ^ a, 1), :] = own_ref[3 * heads * tokens :, :].astype(jnp.float32)[:1]
        attend_frames(slots, out_refs, query_buf, key_buf, value_buf, note_out)

    kind = own[0].dtype
    outs = pl.pallas_call(
        kernel,
        out_shape=[jax.ShapeDtypeStruct((rows, width), jnp.bfloat16)] * len(slots)
        + [
            jax.ShapeDtypeStruct((frames, rows, width), kind),
            jax.ShapeDtypeStruct((frames, keys_rows, width), kind),
            jax.ShapeDtypeStruct((frames, keys_rows, width), kind),
            jax.ShapeDtypeStruct((16, HD), jnp.float32),
        ],
        in_specs=whole_in_vmem(2 * len(moves)),
        out_specs=whole_in_vmem(len(slots) + 4),
        compiler_params=roomy(),
        name="attend",
    )(*own, *mate)
    return (outs[: len(slots)], outs[len(slots) :])


def attend_again(slots, held):
    rows, width = held[0].shape[1:]

    def kernel(*refs):
        out_ref = refs[len(held)]
        parts = [out_ref.at[slot * rows : (slot + 1) * rows] for slot in range(len(slots))]
        attend_frames(slots, parts, *refs[: len(held)])

    return pl.pallas_call(
        kernel,
        out_shape=jax.ShapeDtypeStruct((len(slots) * rows, width), jnp.bfloat16),
        in_specs=whole_in_vmem(len(held)),
        out_specs=whole_in_vmem(1)[0],
        compiler_params=roomy(),
        name="attend_again",
    )(*held)


def project(pieces, weight, kinds, slots=1):
    flat = [piece for part in pieces for piece in part]
    rows, width = (flat[0].shape[0] // slots, flat[0].shape[1])
    pairs, sets = (len(pieces[0]), len(pieces))
    tokens = rows // pairs
    depth, columns = weight.shape
    step = math.gcd(columns, 256)

    def kernel(*refs):
        sources = iter(refs[: len(flat)])
        weight_ref, refs = (refs[len(flat)], refs[len(flat) + 1 :])
        whole = refs[-1]
        here = lax.axis_index("head") // 2
        for k in range(sets):
            for move in range(pairs):
                source = next(sources)
                pair = here ^ move
                channels = pl.ds(pl.multiple_of(pair * width, HD), width)
                for slot in range(slots):
                    for b in range(pairs):
                        first = (slot * sets + k) * rows + (pair ^ b) * tokens
                        start = slot * rows + b * tokens
                        whole[pl.ds(pl.multiple_of(first, 16), tokens), channels] = source[
                            start : start + tokens, :
                        ]
        for start in range(0, columns, step):
            inner = slice(start, start + step)
            product = jnp.dot(
                whole[...], weight_ref[:, inner], preferred_element_type=jnp.float32
            )
            for number in range(slots * sets):
                share = product[number * rows : (number + 1) * rows, :]
                for out_ref in refs[number * len(kinds) : (number + 1) * len(kinds)]:
                    out_ref[:, inner] = share.astype(out_ref.dtype)

    outs = pl.pallas_call(
        kernel,
        out_shape=[
            jax.ShapeDtypeStruct((rows, columns), kind)
            for _ in range(slots * sets)
            for kind in kinds
        ],
        in_specs=whole_in_vmem(len(flat) + 1),
        out_specs=whole_in_vmem(len(kinds) * slots * sets),
        scratch_shapes=[pltpu.VMEM((slots * sets * rows, depth), jnp.bfloat16)],
        compiler_params=roomy(),
        name="project",
    )(*flat, weight)
    return [list(outs[number :: len(kinds)]) for number in range(len(kinds))]


def gates_of(notes, time_weight, column, frames):
    depth, columns = time_weight.shape
    half = depth // 2

    def kernel(note_ref, weight_ref, here_ref, next_ref):
        here = lax.axis_index("tm")
        following = jnp.minimum(here + 1, frames - 1)
        rows = jnp.concatenate([note_ref[pl.ds(here, 1), :], note_ref[pl.ds(following, 1), :]], axis=0)
        lane = lax.broadcasted_iota(jnp.int32, rows.shape, 1)
        noise = jnp.sum(jnp.where(lane == column, rows, 0.0), axis=1, keepdims=True)
        timestep = 1000.0 * (noise + 1.0) / STEPS
        place = lax.broadcasted_iota(jnp.int32, (2, half), 1).astype(jnp.float32)
        angles = timestep * jnp.exp(-math.log(10000.0) * place / half)
        features = jnp.concatenate([jnp.cos(angles), jnp.sin(angles)], axis=1)
        gates = jnp.dot(
            features,
            weight_ref[...].astype(jnp.float32),
            precision=lax.Precision.HIGHEST,
            preferred_element_type=jnp.float32,
        )
        here_ref[...] = gates[:1]
        next_ref[...] = gates[1:]

    return pl.pallas_call(
        kernel,
        out_shape=[jax.ShapeDtypeStruct((1, columns), jnp.float32)] * 2,
        in_specs=whole_in_vmem(2),
        out_specs=whole_in_vmem(2),
        compiler_params=roomy(),
        name="gates_of",
    )(notes, time_weight)


def frame_rows(k, pairs, tokens):
    core = (lax.axis_index("head") % 2) ^ k
    return [pl.ds(pl.multiple_of((2 * p + core) * tokens, 16), tokens) for p in range(pairs)]


def join(partial, table, arrived, k, pairs, residual=None, gate=None):
    rows, columns = partial[0].shape
    tokens = rows // pairs
    step = math.gcd(columns, 256)
    slots = sorted(set(table))
    extras = [] if residual is None else [residual, gate]

    def kernel(*refs):
        own_refs, refs = (refs[: len(slots)], refs[len(slots) :])
        arrived_refs, refs = (refs[: len(arrived)], refs[len(arrived) :])
        out_ref = refs[-1]
        here = lax.axis_index("tm")
        places = frame_rows(k, pairs, tokens)
        for slot, own_ref in zip(slots, own_refs):

            @pl.when(pick([entry == slot for entry in table], here))
            def _(own_ref=own_ref):
                for p, place in enumerate(places):
                    inner = slice(p * tokens, (p + 1) * tokens)
                    for start in range(0, columns, step):
                        part = slice(start, start + step)
                        total = own_ref[inner, part]
                        for ref in arrived_refs:
                            total += ref[inner, part].astype(jnp.float32)
                        if extras:
                            kept = refs[0][place, part].astype(jnp.float32)
                            total = kept + refs[1][:, part] * total
                        out_ref[inner, part] = total.astype(jnp.bfloat16)

    operands = [partial[slot] for slot in slots] + list(arrived) + extras
    return pl.pallas_call(
        kernel,
        out_shape=jax.ShapeDtypeStruct((rows, columns), jnp.bfloat16),
        in_specs=whole_in_vmem(len(operands)),
        out_specs=whole_in_vmem(1)[0],
        compiler_params=roomy(),
        name="join",
    )(*operands)


def finish(k, arrived, partial, below, gate, fresh_frame, pairs, started=None):
    rows, columns = partial.shape
    tokens = rows // pairs
    step = math.gcd(columns, 256)

    def kernel(*refs):
        arrived_ref, partial_ref, below_ref, gate_ref, fresh_ref = refs[:5]
        out_ref, done, sems = refs[-3:]
        last = lax.axis_index("tm") == lax.axis_size("tm") - 1
        places = frame_rows(k, pairs, tokens)

        @pl.when(last)
        def _():
            for p, place in enumerate(places):
                done[p * tokens : (p + 1) * tokens, :] = fresh_ref[place, :]

        @pl.when(jnp.logical_not(last))
        def _():
            for p in range(pairs):
                inner = slice(p * tokens, (p + 1) * tokens)
                for start in range(0, columns, step):
                    part = slice(start, start + step)
                    total = partial_ref[inner, part] + below_ref[inner, part].astype(jnp.float32)
                    total = gate_ref[:, part] * total
                    total += arrived_ref[inner, part].astype(jnp.float32)
                    done[inner, part] = total.astype(jnp.bfloat16)

        copies = [
            pltpu.make_async_copy(
                done.at[p * tokens : (p + 1) * tokens, :], out_ref.at[place, :], sems.at[p]
            )
            for p, place in enumerate(places)
        ]
        for copy in copies:
            copy.start()
        for copy in copies:
            copy.wait()

    operands = [arrived, partial, below, gate, fresh_frame]
    specs = whole_in_vmem(5)
    aliases = {}
    if started is not None:
        operands.append(started)
        specs = specs + in_hbm(1)
        aliases = {5: 0}
    return pl.pallas_call(
        kernel,
        out_shape=jax.ShapeDtypeStruct(fresh_frame.shape, jnp.bfloat16),
        in_specs=specs,
        out_specs=in_hbm(1)[0],
        scratch_shapes=[
            pltpu.VMEM((rows, columns), jnp.bfloat16),
            pltpu.SemaphoreType.DMA((pairs,)),
        ],
        input_output_aliases=aliases,
        compiler_params=roomy(),
        name="finish",
    )(*operands)


def line_schedule(frames):
    steps = []
    for step in range(frames - 1):
        down = {z: step + 1 - (frames - 1 - z) for z in range(1, frames)}
        up = {z: frames - 1 - step + z for z in range(frames)}
        down = {z: f for z, f in down.items() if 1 <= f <= z}
        up = {z: f for z, f in up.items() if z + 2 <= f < frames}
        steps.append((down, up))
    order = []
    for z in range(frames):
        sent = [f for down, up in steps for f in (down.get(z), up.get(z)) if f is not None]
        order.append((sent + [z + 1])[: frames - 1])
    return steps, order


def head_plan(
    queries, keys, values, residual, fresh_frame, out_weight, time_weight, noise_steps, frame_mask
):
    frames, across = (lax.axis_size("tm"), lax.axis_size("head"))
    pairs = across // 2
    width = queries.shape[2] // (frames * pairs)
    everywhere = range(frames)

    def swap(array, j):
        return lax.ppermute(array, "head", [(h, h ^ j) for h in range(across)])

    def gather(part, meanwhile=None):
        near = [part]
        for move in range(1, pairs):
            piece = swap(part, 2 * move)
            if meanwhile is not None:
                piece, meanwhile = lax.optimization_barrier((piece, meanwhile))
            near.append(piece)
        return ([near, [swap(piece, 1) for piece in near]], meanwhile)

    far = [(a, b) for b in range(pairs) for a in reversed(everywhere[2:])]
    near = [(0, b) for b in range(1, pairs)] + [(1, b) for b in reversed(range(pairs))]
    moves = near[:1] + far + near[1:] + [(0, 0)]
    packed = pack(
        queries[0], keys[0], values[0], frame_mask, noise_steps, moves, pairs, width
    )
    own = []
    for piece, (a, b) in zip(packed, moves):
        if (a, b) != (0, 0):
            links = [
                (z * across + h, (z ^ a) * across + (h ^ (2 * b)))
                for z in everywhere
                for h in range(across)
            ]
            piece = lax.ppermute(piece, ("tm", "head"), links)
        own.append(piece)
    for number in range(1, 1 + len(far)):
        own[number], own[0] = lax.optimization_barrier((own[number], own[0]))
    mine = moves.index((0, 0))
    (own[mine],), weight = (bring(own[mine]), out_weight)
    mate = [swap(piece, 1) for piece in own]

    steps, order = line_schedule(frames)

    named = [[order[z][slot] for z in everywhere] for slot in range(frames - 1)]
    (part,), held = attend(named[:1], own, mate, moves, pairs, frames, width)
    following = attend_again(named[1:], held)
    pieces, following = gather(part, following)
    partial, payload = ([[]], [])
    for rows in pieces:
        product, rounded = project([rows], weight, (jnp.float32, jnp.bfloat16))
        partial[0] += product
        payload += rounded
    following, payload[0] = lax.optimization_barrier((following, payload[0]))
    down, up = steps[0]
    links = [(z, z - 1) for z in down] + [(z, z + 1) for z in up]
    above = [lax.ppermute(part, "tm", links) for part in payload]
    below = above
    pieces, _ = gather(following)
    later = project(pieces, weight, (jnp.float32,), frames - 2)[0]
    partial += [later[2 * slot : 2 * slot + 2] for slot in range(frames - 2)]
    gates = gates_of(held[-1], time_weight, frame_mask.shape[1], frames)

    for number, (down, up) in enumerate(steps[1:], 1):
        sends = {**down, **up}
        table = [order[z].index(sends[z]) if z in sends else 0 for z in everywhere]
        final = number == len(steps) - 1
        extras = (residual[0], gates[0]) if final else ()
        payload = [
            join(
                [products[k] for products in partial],
                table,
                [above[k]] if final or above is below else [above[k], below[k]],
                k,
                pairs,
                *extras,
            )
            for k in range(2)
        ]
        above = [lax.ppermute(part, "tm", [(z, z - 1) for z in down]) for part in payload]
        if up:
            below = [lax.ppermute(part, "tm", [(z, z + 1) for z in up]) for part in payload]
    result = None
    for k in range(2):
        result = finish(
            k, above[k], partial[-1][k], below[k], gates[1], fresh_frame, pairs, result
        )
    return result[None]


def power_of_two(number):
    return number & (number - 1) == 0


def suits_line(frames, window):
    apart = all(not set(down) & set(up) for down, up in line_schedule(frames)[0])
    return 2 < frames <= window and power_of_two(frames) and apart


def on_device(queries, *others):
    frames, across = (lax.axis_size("tm"), lax.axis_size("head"))
    heads = queries.shape[2] // HD
    even = across % 2 == 0 and power_of_two(across)
    even = even and queries.shape[1] % 16 == 0
    if even and suits_line(frames, others[-1].shape[1]) and heads % (frames * across // 2) == 0:
        return head_plan(queries, *others)
    return frame_plan(queries, *others)


def solution(mesh):
    placed = (
        P(("groups", "tm"), "head", None),
        P(("groups", "tm"), "head", None),
        P(("groups", "tm"), "head", None),
        P(("groups", "tm"), None, "head"),
        P("groups", "head"),
        P("tm", "head"),
        P(None, "head"),
        P(("groups", "tm")),
        P(("groups", "tm"), None),
    )
    return jax.shard_map(
        on_device,
        mesh=mesh,
        in_specs=placed,
        out_specs=P(("groups", "tm"), None, "head"),
        check_vma=False,
    )
```

```python
import math

import jax
import jax.numpy as jnp
import numpy as np
from jax import lax
from jax.experimental import pallas as pl
from jax.experimental.pallas import tpu as pltpu
from jax.sharding import PartitionSpec as P

HD = 128
FREQ = 256
STEPS = 50
NOTE_ROWS = 16
VMEM_BYTES = 16 * 1024 * 1024
PACK_BYTES = 60 * 1024 * 1024


def shifted(value, axis, steps):
    count = lax.axis_size(axis)
    leading, last = (max(0, -steps), min(count, count - steps))
    return lax.ppermute(value, axis, [(source, source + steps) for source in range(leading, last)])


def time_features(noise_steps):
    timestep = 1000.0 * (noise_steps.astype(jnp.float32) + 1.0) / STEPS
    half = FREQ // 2
    rates = jnp.exp(-math.log(10000.0) * jnp.arange(half).astype(jnp.float32) / half)
    angles = timestep[:, None] * rates[None, :]
    return jnp.concatenate([jnp.cos(angles), jnp.sin(angles)], axis=1)


def frame_plan(
    queries, keys, values, residual, fresh_frame, out_weight, time_weight, noise_steps, frame_mask
):
    query_local, key_local, value_local = (
        lax.all_to_all(queries, "head", split_axis=2, concat_axis=1, tiled=True),
        lax.all_to_all(keys, "head", split_axis=2, concat_axis=1, tiled=True),
        lax.all_to_all(values, "head", split_axis=2, concat_axis=1, tiled=True),
    )
    tokens = query_local.shape[1]
    heads_here = query_local.shape[2] // HD
    scale = 1.0 / math.sqrt(HD)
    query_heads = query_local[0].reshape(tokens, heads_here, HD)
    key_value = jnp.stack([key_local[0], value_local[0]], axis=0)
    frame = lax.axis_index("tm")
    frames_total = lax.axis_size("tm")
    window = min(8, frames_total)
    mask_row = frame_mask[0]
    columns = jnp.arange(mask_row.shape[0], dtype=jnp.int32)

    def allowed_at(offset):
        hits = jnp.sum(jnp.where(columns == frame - offset, mask_row, 0))
        return hits > 0

    def absorb(state, block, allowed):
        running_max, weight_sum, accumulated = state
        key_heads = block[0].reshape(tokens, heads_here, HD)
        value_heads = block[1].reshape(tokens, heads_here, HD)
        scores = (
            jnp.einsum("qhd,khd->hqk", query_heads, key_heads, preferred_element_type=jnp.float32)
            * scale
        )
        new_max = jnp.where(allowed, jnp.maximum(running_max, jnp.max(scores, axis=2)), running_max)
        lifted = jnp.where(allowed, jnp.exp(jnp.minimum(scores - new_max[:, :, None], 0.0)), 0.0)
        factor = jnp.exp(running_max - new_max)
        weight_sum = weight_sum * factor + jnp.sum(lifted, axis=2)
        rounded = lifted.astype(jnp.bfloat16)
        accumulated = accumulated * jnp.transpose(factor)[:, :, None] + jnp.einsum(
            "hqk,khd->qhd", rounded, value_heads, preferred_element_type=jnp.float32
        )
        return (new_max, weight_sum, accumulated)

    state = (
        jnp.full((heads_here, tokens), -1e30, jnp.float32),
        jnp.zeros((heads_here, tokens), jnp.float32),
        jnp.zeros((tokens, heads_here, HD), jnp.float32),
    )
    state = absorb(state, key_value, allowed_at(0))
    moving = key_value
    for offset in range(1, window):
        moving = shifted(moving, "tm", 1)
        state = absorb(state, moving, allowed_at(offset))
    running_max, weight_sum, accumulated = state
    attention = (
        (accumulated / jnp.transpose(weight_sum)[:, :, None])
        .reshape(tokens, heads_here * HD)
        .astype(jnp.bfloat16)
    )
    weight_cols = lax.all_gather(out_weight, "tm", axis=0, tiled=True)
    projected = jnp.dot(
        lax.all_gather(attention, "head", axis=1, tiled=True),
        weight_cols,
        preferred_element_type=jnp.float32,
    )
    gate = jnp.dot(
        time_features(noise_steps), time_weight.astype(jnp.float32), precision=lax.Precision.HIGHEST
    )
    updated = (residual[0].astype(jnp.float32) + gate * projected).astype(jnp.bfloat16)
    moved = shifted(updated, "tm", -1)
    rolled = jnp.where(frame == frames_total - 1, fresh_frame, moved)
    return rolled[None]


def whole_in_vmem(count):
    return [pl.BlockSpec(memory_space=pltpu.VMEM)] * count


def in_hbm(count):
    return [pl.BlockSpec(memory_space=pltpu.HBM)] * count


def roomy():
    return pltpu.CompilerParams(vmem_limit_bytes=VMEM_BYTES)


def pack(queries, keys, values, frame_mask, noise_steps, moves, pairs, width):
    tokens, kind = (queries.shape[0], queries.dtype)
    window = frame_mask.shape[1]
    heads = width // HD
    body = 3 * heads * tokens
    heights = [body + (NOTE_ROWS if b == 0 else 0) for a, b in moves]
    count = len(moves)

    def kernel(*refs):
        sources, small, pieces, scratch = (refs[:3], refs[3:5], refs[5 : 5 + count], refs[5 + count :])
        loaded, packed, mask_ref, noise_ref, in_sems, out_sems = scratch
        frame, pair = (lax.axis_index("tm"), lax.axis_index("head") // 2)
        targets = [loaded.at[place] for place in range(3)] + [mask_ref, noise_ref]
        loads = [
            pltpu.make_async_copy(source, target, in_sems.at[place])
            for place, (source, target) in enumerate(zip((*sources, *small), targets))
        ]
        for load in loads:
            load.start()
        for load in loads:
            load.wait()
        lane = lax.broadcasted_iota(jnp.int32, (NOTE_ROWS, HD), 1)
        note = jnp.where(lane == window, noise_ref[0], 0)
        for column in range(window):
            note = jnp.where(lane == column, mask_ref[0, column], note)
        note = note.astype(jnp.float32).astype(kind)
        stores = []
        for number, (a, b) in enumerate(moves):
            block = (frame ^ a) * pairs + (pair ^ b)
            for place in range(3):
                for head in range(heads):
                    columns = pl.ds(pl.multiple_of((block * heads + head) * HD, HD), HD)
                    first = (place * heads + head) * tokens
                    packed[number, first : first + tokens, :] = loaded[place, :, columns]
            if b == 0:
                packed[number, body:, :] = note
            store = pltpu.make_async_copy(
                packed.at[number, : heights[number]], pieces[number], out_sems.at[number]
            )
            store.start()
            stores.append(store)
        for store in stores:
            store.wait()

    return pl.pallas_call(
        kernel,
        out_shape=[jax.ShapeDtypeStruct((height, HD), kind) for height in heights],
        in_specs=in_hbm(5),
        out_specs=in_hbm(count),
        scratch_shapes=[
            pltpu.VMEM((3, *queries.shape), kind),
            pltpu.VMEM((count, body + NOTE_ROWS, HD), kind),
            pltpu.SMEM(frame_mask.shape, frame_mask.dtype),
            pltpu.SMEM(noise_steps.shape, noise_steps.dtype),
            pltpu.SemaphoreType.DMA((5,)),
            pltpu.SemaphoreType.DMA((count,)),
        ],
        compiler_params=pltpu.CompilerParams(vmem_limit_bytes=PACK_BYTES),
        name="pack",
    )(queries, keys, values, frame_mask, noise_steps)


def bring(*arrays):
    def kernel(*refs):
        for source, target in zip(refs[: len(arrays)], refs[len(arrays) :]):
            target[...] = source[...]

    return pl.pallas_call(
        kernel,
        out_shape=[jax.ShapeDtypeStruct(array.shape, array.dtype) for array in arrays],
        in_specs=whole_in_vmem(len(arrays)),
        out_specs=whole_in_vmem(len(arrays)),
        compiler_params=roomy(),
        name="bring",
    )(*arrays)


def pick(table, here):
    result = table[0]
    for place, entry in enumerate(table[1:], 1):
        result = jnp.where(here == place, entry, result)
    return result


def attend_frames(slots, out_refs, query_buf, key_buf, value_buf, note_ref):
    frames, keys_rows, width = key_buf.shape
    scale = math.log2(math.e) / math.sqrt(HD)
    here = lax.axis_index("tm")
    for frames_of_slot, out_ref in zip(slots, out_refs):
        frame = pick(frames_of_slot, here)
        note = note_ref[pl.ds(frame, 1), :]
        lane = lax.broadcasted_iota(jnp.int32, note.shape, 1)
        biases = []
        for a in range(frames):
            hit = jnp.sum(jnp.where(lane == here ^ a, note, 0.0), axis=1, keepdims=True)
            biases.append(jnp.broadcast_to((hit - 1.0) * 1e30, (1, keys_rows)))
        bias = jnp.concatenate(biases, axis=1)
        for start in range(0, width, HD):
            channels = slice(start, start + HD)
            query = query_buf[frame, :, channels]
            keys = key_buf[:, :, channels].reshape(frames * keys_rows, HD)
            scores = lax.dot_general(
                query, keys, (((1,), (1,)), ((), ())), preferred_element_type=jnp.float32
            )
            scores = scores * scale + bias
            lifted = jnp.exp2(scores - jnp.max(scores, axis=1, keepdims=True))
            totals = jnp.sum(lifted, axis=1, keepdims=True)
            values = value_buf[:, :, channels].reshape(frames * keys_rows, HD)
            mixed = jnp.dot(
                lifted.astype(jnp.bfloat16), values, preferred_element_type=jnp.float32
            )
            out_ref[:, channels] = (mixed / totals).astype(jnp.bfloat16)


def attend(slots, own, mate, moves, pairs, frames, width):
    heads = width // HD
    tokens = (own[moves.index((0, 0))].shape[0] - NOTE_ROWS) // (3 * heads)
    rows, keys_rows = (pairs * tokens, 2 * pairs * tokens)

    def kernel(*refs):
        own_refs, refs = (refs[: len(moves)], refs[len(moves) :])
        mate_refs, refs = (refs[: len(moves)], refs[len(moves) :])
        out_refs, (query_buf, key_buf, value_buf, note_out) = (refs[: len(slots)], refs[len(slots) :])
        here = lax.axis_index("tm")
        for own_ref, mate_ref, (a, b) in zip(own_refs, mate_refs, moves):
            for head in range(heads):
                channels = slice(head * HD, (head + 1) * HD)
                query, key, value = [
                    slice((place * heads + head) * tokens, (place * heads + head + 1) * tokens)
                    for place in range(3)
                ]
                query_buf[here ^ a, b * tokens : (b + 1) * tokens, channels] = own_ref[query, :]
                for side, ref in enumerate((own_ref, mate_ref)):
                    span = slice((2 * b + side) * tokens, (2 * b + side + 1) * tokens)
                    key_buf[a, span, channels] = ref[key, :]
                    value_buf[a, span, channels] = ref[value, :]
            if b == 0:
                note_out[pl.ds(here ^ a, 1), :] = own_ref[3 * heads * tokens :, :].astype(jnp.float32)[:1]
        attend_frames(slots, out_refs, query_buf, key_buf, value_buf, note_out)

    kind = own[0].dtype
    outs = pl.pallas_call(
        kernel,
        out_shape=[jax.ShapeDtypeStruct((rows, width), jnp.bfloat16)] * len(slots)
        + [
            jax.ShapeDtypeStruct((frames, rows, width), kind),
            jax.ShapeDtypeStruct((frames, keys_rows, width), kind),
            jax.ShapeDtypeStruct((frames, keys_rows, width), kind),
            jax.ShapeDtypeStruct((16, HD), jnp.float32),
        ],
        in_specs=whole_in_vmem(2 * len(moves)),
        out_specs=whole_in_vmem(len(slots) + 4),
        compiler_params=roomy(),
        name="attend",
    )(*own, *mate)
    return (outs[: len(slots)], outs[len(slots) :])


def attend_again(slots, held):
    rows, width = held[0].shape[1:]

    def kernel(*refs):
        out_ref = refs[len(held)]
        parts = [out_ref.at[slot * rows : (slot + 1) * rows] for slot in range(len(slots))]
        attend_frames(slots, parts, *refs[: len(held)])

    return pl.pallas_call(
        kernel,
        out_shape=jax.ShapeDtypeStruct((len(slots) * rows, width), jnp.bfloat16),
        in_specs=whole_in_vmem(len(held)),
        out_specs=whole_in_vmem(1)[0],
        compiler_params=roomy(),
        name="attend_again",
    )(*held)


def project(pieces, weight, kinds, slots=1):
    flat = [piece for part in pieces for piece in part]
    rows, width = (flat[0].shape[0] // slots, flat[0].shape[1])
    pairs, sets = (len(pieces[0]), len(pieces))
    tokens = rows // pairs
    depth, columns = weight.shape
    step = math.gcd(columns, 256)

    def kernel(*refs):
        sources = iter(refs[: len(flat)])
        weight_ref, refs = (refs[len(flat)], refs[len(flat) + 1 :])
        whole = refs[-1]
        here = lax.axis_index("head") // 2
        for k in range(sets):
            for move in range(pairs):
                source = next(sources)
                pair = here ^ move
                channels = pl.ds(pl.multiple_of(pair * width, HD), width)
                for slot in range(slots):
                    for b in range(pairs):
                        first = (slot * sets + k) * rows + (pair ^ b) * tokens
                        start = slot * rows + b * tokens
                        whole[pl.ds(pl.multiple_of(first, 16), tokens), channels] = source[
                            start : start + tokens, :
                        ]
        for start in range(0, columns, step):
            inner = slice(start, start + step)
            product = jnp.dot(
                whole[...], weight_ref[:, inner], preferred_element_type=jnp.float32
            )
            for number in range(slots * sets):
                share = product[number * rows : (number + 1) * rows, :]
                for out_ref in refs[number * len(kinds) : (number + 1) * len(kinds)]:
                    out_ref[:, inner] = share.astype(out_ref.dtype)

    outs = pl.pallas_call(
        kernel,
        out_shape=[
            jax.ShapeDtypeStruct((rows, columns), kind)
            for _ in range(slots * sets)
            for kind in kinds
        ],
        in_specs=whole_in_vmem(len(flat) + 1),
        out_specs=whole_in_vmem(len(kinds) * slots * sets),
        scratch_shapes=[pltpu.VMEM((slots * sets * rows, depth), jnp.bfloat16)],
        compiler_params=roomy(),
        name="project",
    )(*flat, weight)
    return [list(outs[number :: len(kinds)]) for number in range(len(kinds))]


def gates_of(notes, time_weight, column, frames):
    depth, columns = time_weight.shape
    half = depth // 2

    def kernel(note_ref, weight_ref, here_ref, next_ref):
        here = lax.axis_index("tm")
        following = jnp.minimum(here + 1, frames - 1)
        rows = jnp.concatenate([note_ref[pl.ds(here, 1), :], note_ref[pl.ds(following, 1), :]], axis=0)
        lane = lax.broadcasted_iota(jnp.int32, rows.shape, 1)
        noise = jnp.sum(jnp.where(lane == column, rows, 0.0), axis=1, keepdims=True)
        timestep = 1000.0 * (noise + 1.0) / STEPS
        place = lax.broadcasted_iota(jnp.int32, (2, half), 1).astype(jnp.float32)
        angles = timestep * jnp.exp(-math.log(10000.0) * place / half)
        features = jnp.concatenate([jnp.cos(angles), jnp.sin(angles)], axis=1)
        gates = jnp.dot(
            features,
            weight_ref[...].astype(jnp.float32),
            precision=lax.Precision.HIGHEST,
            preferred_element_type=jnp.float32,
        )
        here_ref[...] = gates[:1]
        next_ref[...] = gates[1:]

    return pl.pallas_call(
        kernel,
        out_shape=[jax.ShapeDtypeStruct((1, columns), jnp.float32)] * 2,
        in_specs=whole_in_vmem(2),
        out_specs=whole_in_vmem(2),
        compiler_params=roomy(),
        name="gates_of",
    )(notes, time_weight)


def frame_rows(k, pairs, tokens):
    core = (lax.axis_index("head") % 2) ^ k
    return [pl.ds(pl.multiple_of((2 * p + core) * tokens, 16), tokens) for p in range(pairs)]


def join(partial, table, arrived, k, pairs, residual=None, gate=None):
    rows, columns = partial[0].shape
    tokens = rows // pairs
    step = math.gcd(columns, 256)
    slots = sorted(set(table))
    extras = [] if residual is None else [residual, gate]

    def kernel(*refs):
        own_refs, refs = (refs[: len(slots)], refs[len(slots) :])
        arrived_refs, refs = (refs[: len(arrived)], refs[len(arrived) :])
        out_ref = refs[-1]
        here = lax.axis_index("tm")
        places = frame_rows(k, pairs, tokens)
        for slot, own_ref in zip(slots, own_refs):

            @pl.when(pick([entry == slot for entry in table], here))
            def _(own_ref=own_ref):
                for p, place in enumerate(places):
                    inner = slice(p * tokens, (p + 1) * tokens)
                    for start in range(0, columns, step):
                        part = slice(start, start + step)
                        total = own_ref[inner, part]
                        for ref in arrived_refs:
                            total += ref[inner, part].astype(jnp.float32)
                        if extras:
                            kept = refs[0][place, part].astype(jnp.float32)
                            total = kept + refs[1][:, part] * total
                        out_ref[inner, part] = total.astype(jnp.bfloat16)

    operands = [partial[slot] for slot in slots] + list(arrived) + extras
    return pl.pallas_call(
        kernel,
        out_shape=jax.ShapeDtypeStruct((rows, columns), jnp.bfloat16),
        in_specs=whole_in_vmem(len(operands)),
        out_specs=whole_in_vmem(1)[0],
        compiler_params=roomy(),
        name="join",
    )(*operands)


def finish(k, arrived, partial, below, gate, fresh_frame, pairs, started=None):
    rows, columns = partial.shape
    tokens = rows // pairs
    step = math.gcd(columns, 256)

    def kernel(*refs):
        arrived_ref, partial_ref, below_ref, gate_ref, fresh_ref = refs[:5]
        out_ref, done, sems = refs[-3:]
        last = lax.axis_index("tm") == lax.axis_size("tm") - 1
        places = frame_rows(k, pairs, tokens)

        @pl.when(last)
        def _():
            for p, place in enumerate(places):
                done[p * tokens : (p + 1) * tokens, :] = fresh_ref[place, :]

        @pl.when(jnp.logical_not(last))
        def _():
            for p in range(pairs):
                inner = slice(p * tokens, (p + 1) * tokens)
                for start in range(0, columns, step):
                    part = slice(start, start + step)
                    total = partial_ref[inner, part] + below_ref[inner, part].astype(jnp.float32)
                    total = gate_ref[:, part] * total
                    total += arrived_ref[inner, part].astype(jnp.float32)
                    done[inner, part] = total.astype(jnp.bfloat16)

        copies = [
            pltpu.make_async_copy(
                done.at[p * tokens : (p + 1) * tokens, :], out_ref.at[place, :], sems.at[p]
            )
            for p, place in enumerate(places)
        ]
        for copy in copies:
            copy.start()
        for copy in copies:
            copy.wait()

    operands = [arrived, partial, below, gate, fresh_frame]
    specs = whole_in_vmem(5)
    aliases = {}
    if started is not None:
        operands.append(started)
        specs = specs + in_hbm(1)
        aliases = {5: 0}
    return pl.pallas_call(
        kernel,
        out_shape=jax.ShapeDtypeStruct(fresh_frame.shape, jnp.bfloat16),
        in_specs=specs,
        out_specs=in_hbm(1)[0],
        scratch_shapes=[
            pltpu.VMEM((rows, columns), jnp.bfloat16),
            pltpu.SemaphoreType.DMA((pairs,)),
        ],
        input_output_aliases=aliases,
        compiler_params=roomy(),
        name="finish",
    )(*operands)


def line_schedule(frames):
    steps = []
    for step in range(frames - 1):
        down = {z: step + 1 - (frames - 1 - z) for z in range(1, frames)}
        up = {z: frames - 1 - step + z for z in range(frames)}
        down = {z: f for z, f in down.items() if 1 <= f <= z}
        up = {z: f for z, f in up.items() if z + 2 <= f < frames}
        steps.append((down, up))
    order = []
    for z in range(frames):
        sent = [f for down, up in steps for f in (down.get(z), up.get(z)) if f is not None]
        order.append((sent + [z + 1])[: frames - 1])
    return steps, order


def head_plan(
    queries, keys, values, residual, fresh_frame, out_weight, time_weight, noise_steps, frame_mask
):
    frames, across = (lax.axis_size("tm"), lax.axis_size("head"))
    pairs = across // 2
    width = queries.shape[2] // (frames * pairs)
    everywhere = range(frames)

    def swap(array, j):
        return lax.ppermute(array, "head", [(h, h ^ j) for h in range(across)])

    def gather(part, meanwhile=None):
        near = [part]
        for move in range(1, pairs):
            piece = swap(part, 2 * move)
            if meanwhile is not None:
                piece, meanwhile = lax.optimization_barrier((piece, meanwhile))
            near.append(piece)
        return ([near, [swap(piece, 1) for piece in near]], meanwhile)

    far = [(a, b) for b in range(pairs) for a in reversed(everywhere[2:])]
    near = [(1, pairs - 1)] + [(0, b) for b in range(1, pairs)] + [(1, b) for b in range(pairs - 1)]
    moves = far + near + [(0, 0)]
    packed = pack(
        queries[0], keys[0], values[0], frame_mask, noise_steps, moves, pairs, width
    )
    first = len(far)
    own = []
    for piece, (a, b) in zip(packed, moves):
        if (a, b) != (0, 0):
            if a == 0:
                piece, own[first] = lax.optimization_barrier((piece, own[first]))
            links = [
                (z * across + h, (z ^ a) * across + (h ^ (2 * b)))
                for z in everywhere
                for h in range(across)
            ]
            piece = lax.ppermute(piece, ("tm", "head"), links)
        own.append(piece)
    for number in range(first):
        own[number], own[first] = lax.optimization_barrier((own[number], own[first]))
    mine = moves.index((0, 0))
    (own[mine],), weight = (bring(own[mine]), out_weight)
    mate = [swap(piece, 1) for piece in own]

    steps, order = line_schedule(frames)

    named = [[order[z][slot] for z in everywhere] for slot in range(frames - 1)]
    (part,), held = attend(named[:1], own, mate, moves, pairs, frames, width)
    following = attend_again(named[1:], held)
    pieces, following = gather(part, following)
    partial, payload = ([[]], [])
    for rows in pieces:
        product, rounded = project([rows], weight, (jnp.float32, jnp.bfloat16))
        partial[0] += product
        payload += rounded
    following, payload[0] = lax.optimization_barrier((following, payload[0]))
    down, up = steps[0]
    links = [(z, z - 1) for z in down] + [(z, z + 1) for z in up]
    above = [lax.ppermute(part, "tm", links) for part in payload]
    below = above
    pieces, _ = gather(following)
    later = project(pieces, weight, (jnp.float32,), frames - 2)[0]
    partial += [later[2 * slot : 2 * slot + 2] for slot in range(frames - 2)]
    gates = gates_of(held[-1], time_weight, frame_mask.shape[1], frames)

    for number, (down, up) in enumerate(steps[1:], 1):
        sends = {**down, **up}
        table = [order[z].index(sends[z]) if z in sends else 0 for z in everywhere]
        final = number == len(steps) - 1
        extras = (residual[0], gates[0]) if final else ()
        payload = [
            join(
                [products[k] for products in partial],
                table,
                [above[k]] if final or above is below else [above[k], below[k]],
                k,
                pairs,
                *extras,
            )
            for k in range(2)
        ]
        above = [lax.ppermute(part, "tm", [(z, z - 1) for z in down]) for part in payload]
        if up:
            below = [lax.ppermute(part, "tm", [(z, z + 1) for z in up]) for part in payload]
    result = None
    for k in range(2):
        result = finish(
            k, above[k], partial[-1][k], below[k], gates[1], fresh_frame, pairs, result
        )
    return result[None]


def power_of_two(number):
    return number & (number - 1) == 0


def suits_line(frames, window):
    apart = all(not set(down) & set(up) for down, up in line_schedule(frames)[0])
    return 2 < frames <= window and power_of_two(frames) and apart


def on_device(queries, *others):
    frames, across = (lax.axis_size("tm"), lax.axis_size("head"))
    heads = queries.shape[2] // HD
    even = across % 2 == 0 and power_of_two(across)
    even = even and queries.shape[1] % 16 == 0
    if even and suits_line(frames, others[-1].shape[1]) and heads % (frames * across // 2) == 0:
        return head_plan(queries, *others)
    return frame_plan(queries, *others)


def solution(mesh):
    placed = (
        P(("groups", "tm"), "head", None),
        P(("groups", "tm"), "head", None),
        P(("groups", "tm"), "head", None),
        P(("groups", "tm"), None, "head"),
        P("groups", "head"),
        P("tm", "head"),
        P(None, "head"),
        P(("groups", "tm")),
        P(("groups", "tm"), None),
    )
    return jax.shard_map(
        on_device,
        mesh=mesh,
        in_specs=placed,
        out_specs=P(("groups", "tm"), None, "head"),
        check_vma=False,
    )
```

```python
import math

import jax
import jax.numpy as jnp
import numpy as np
from jax import lax
from jax.experimental import pallas as pl
from jax.experimental.pallas import tpu as pltpu
from jax.sharding import PartitionSpec as P

HD = 128
FREQ = 256
STEPS = 50
NOTE_ROWS = 16
VMEM_BYTES = 16 * 1024 * 1024
PACK_BYTES = 60 * 1024 * 1024


def shifted(value, axis, steps):
    count = lax.axis_size(axis)
    leading, last = (max(0, -steps), min(count, count - steps))
    return lax.ppermute(value, axis, [(source, source + steps) for source in range(leading, last)])


def time_features(noise_steps):
    timestep = 1000.0 * (noise_steps.astype(jnp.float32) + 1.0) / STEPS
    half = FREQ // 2
    rates = jnp.exp(-math.log(10000.0) * jnp.arange(half).astype(jnp.float32) / half)
    angles = timestep[:, None] * rates[None, :]
    return jnp.concatenate([jnp.cos(angles), jnp.sin(angles)], axis=1)


def frame_plan(
    queries, keys, values, residual, fresh_frame, out_weight, time_weight, noise_steps, frame_mask
):
    query_local, key_local, value_local = (
        lax.all_to_all(queries, "head", split_axis=2, concat_axis=1, tiled=True),
        lax.all_to_all(keys, "head", split_axis=2, concat_axis=1, tiled=True),
        lax.all_to_all(values, "head", split_axis=2, concat_axis=1, tiled=True),
    )
    tokens = query_local.shape[1]
    heads_here = query_local.shape[2] // HD
    scale = 1.0 / math.sqrt(HD)
    query_heads = query_local[0].reshape(tokens, heads_here, HD)
    key_value = jnp.stack([key_local[0], value_local[0]], axis=0)
    frame = lax.axis_index("tm")
    frames_total = lax.axis_size("tm")
    window = min(8, frames_total)
    mask_row = frame_mask[0]
    columns = jnp.arange(mask_row.shape[0], dtype=jnp.int32)

    def allowed_at(offset):
        hits = jnp.sum(jnp.where(columns == frame - offset, mask_row, 0))
        return hits > 0

    def absorb(state, block, allowed):
        running_max, weight_sum, accumulated = state
        key_heads = block[0].reshape(tokens, heads_here, HD)
        value_heads = block[1].reshape(tokens, heads_here, HD)
        scores = (
            jnp.einsum("qhd,khd->hqk", query_heads, key_heads, preferred_element_type=jnp.float32)
            * scale
        )
        new_max = jnp.where(allowed, jnp.maximum(running_max, jnp.max(scores, axis=2)), running_max)
        lifted = jnp.where(allowed, jnp.exp(jnp.minimum(scores - new_max[:, :, None], 0.0)), 0.0)
        factor = jnp.exp(running_max - new_max)
        weight_sum = weight_sum * factor + jnp.sum(lifted, axis=2)
        rounded = lifted.astype(jnp.bfloat16)
        accumulated = accumulated * jnp.transpose(factor)[:, :, None] + jnp.einsum(
            "hqk,khd->qhd", rounded, value_heads, preferred_element_type=jnp.float32
        )
        return (new_max, weight_sum, accumulated)

    state = (
        jnp.full((heads_here, tokens), -1e30, jnp.float32),
        jnp.zeros((heads_here, tokens), jnp.float32),
        jnp.zeros((tokens, heads_here, HD), jnp.float32),
    )
    state = absorb(state, key_value, allowed_at(0))
    moving = key_value
    for offset in range(1, window):
        moving = shifted(moving, "tm", 1)
        state = absorb(state, moving, allowed_at(offset))
    running_max, weight_sum, accumulated = state
    attention = (
        (accumulated / jnp.transpose(weight_sum)[:, :, None])
        .reshape(tokens, heads_here * HD)
        .astype(jnp.bfloat16)
    )
    weight_cols = lax.all_gather(out_weight, "tm", axis=0, tiled=True)
    projected = jnp.dot(
        lax.all_gather(attention, "head", axis=1, tiled=True),
        weight_cols,
        preferred_element_type=jnp.float32,
    )
    gate = jnp.dot(
        time_features(noise_steps), time_weight.astype(jnp.float32), precision=lax.Precision.HIGHEST
    )
    updated = (residual[0].astype(jnp.float32) + gate * projected).astype(jnp.bfloat16)
    moved = shifted(updated, "tm", -1)
    rolled = jnp.where(frame == frames_total - 1, fresh_frame, moved)
    return rolled[None]


def whole_in_vmem(count):
    return [pl.BlockSpec(memory_space=pltpu.VMEM)] * count


def in_hbm(count):
    return [pl.BlockSpec(memory_space=pltpu.HBM)] * count


def roomy():
    return pltpu.CompilerParams(vmem_limit_bytes=VMEM_BYTES)


def pack(queries, keys, values, frame_mask, noise_steps, moves, pairs, width):
    tokens, kind = (queries.shape[0], queries.dtype)
    window = frame_mask.shape[1]
    heads = width // HD
    body = 3 * heads * tokens
    heights = [body + (NOTE_ROWS if b == 0 else 0) for a, b in moves]
    count = len(moves)

    def kernel(*refs):
        sources, small, pieces, scratch = (refs[:3], refs[3:5], refs[5 : 5 + count], refs[5 + count :])
        loaded, packed, mask_ref, noise_ref, in_sems, out_sems = scratch
        frame, pair = (lax.axis_index("tm"), lax.axis_index("head") // 2)
        targets = [loaded.at[place] for place in range(3)] + [mask_ref, noise_ref]
        loads = [
            pltpu.make_async_copy(source, target, in_sems.at[place])
            for place, (source, target) in enumerate(zip((*sources, *small), targets))
        ]
        for load in loads:
            load.start()
        for load in loads:
            load.wait()
        lane = lax.broadcasted_iota(jnp.int32, (NOTE_ROWS, HD), 1)
        note = jnp.where(lane == window, noise_ref[0], 0)
        for column in range(window):
            note = jnp.where(lane == column, mask_ref[0, column], note)
        note = note.astype(jnp.float32).astype(kind)
        stores = []
        for number, (a, b) in enumerate(moves):
            block = (frame ^ a) * pairs + (pair ^ b)
            for place in range(3):
                for head in range(heads):
                    columns = pl.ds(pl.multiple_of((block * heads + head) * HD, HD), HD)
                    first = (place * heads + head) * tokens
                    packed[number, first : first + tokens, :] = loaded[place, :, columns]
            if b == 0:
                packed[number, body:, :] = note
            store = pltpu.make_async_copy(
                packed.at[number, : heights[number]], pieces[number], out_sems.at[number]
            )
            store.start()
            stores.append(store)
        for store in stores:
            store.wait()

    return pl.pallas_call(
        kernel,
        out_shape=[jax.ShapeDtypeStruct((height, HD), kind) for height in heights],
        in_specs=in_hbm(5),
        out_specs=in_hbm(count),
        scratch_shapes=[
            pltpu.VMEM((3, *queries.shape), kind),
            pltpu.VMEM((count, body + NOTE_ROWS, HD), kind),
            pltpu.SMEM(frame_mask.shape, frame_mask.dtype),
            pltpu.SMEM(noise_steps.shape, noise_steps.dtype),
            pltpu.SemaphoreType.DMA((5,)),
            pltpu.SemaphoreType.DMA((count,)),
        ],
        compiler_params=pltpu.CompilerParams(vmem_limit_bytes=PACK_BYTES),
        name="pack",
    )(queries, keys, values, frame_mask, noise_steps)


def bring(*arrays):
    def kernel(*refs):
        for source, target in zip(refs[: len(arrays)], refs[len(arrays) :]):
            target[...] = source[...]

    return pl.pallas_call(
        kernel,
        out_shape=[jax.ShapeDtypeStruct(array.shape, array.dtype) for array in arrays],
        in_specs=whole_in_vmem(len(arrays)),
        out_specs=whole_in_vmem(len(arrays)),
        compiler_params=roomy(),
        name="bring",
    )(*arrays)


def pick(table, here):
    result = table[0]
    for place, entry in enumerate(table[1:], 1):
        result = jnp.where(here == place, entry, result)
    return result


def attend_frames(slots, out_refs, query_buf, key_buf, value_buf, note_ref):
    frames, keys_rows, width = key_buf.shape
    scale = math.log2(math.e) / math.sqrt(HD)
    here = lax.axis_index("tm")
    for frames_of_slot, out_ref in zip(slots, out_refs):
        frame = pick(frames_of_slot, here)
        note = note_ref[pl.ds(frame, 1), :]
        lane = lax.broadcasted_iota(jnp.int32, note.shape, 1)
        biases = []
        for a in range(frames):
            hit = jnp.sum(jnp.where(lane == here ^ a, note, 0.0), axis=1, keepdims=True)
            biases.append(jnp.broadcast_to((hit - 1.0) * 1e30, (1, keys_rows)))
        bias = jnp.concatenate(biases, axis=1)
        for start in range(0, width, HD):
            channels = slice(start, start + HD)
            query = query_buf[frame, :, channels]
            keys = key_buf[:, :, channels].reshape(frames * keys_rows, HD)
            scores = lax.dot_general(
                query, keys, (((1,), (1,)), ((), ())), preferred_element_type=jnp.float32
            )
            scores = scores * scale + bias
            lifted = jnp.exp2(scores - jnp.max(scores, axis=1, keepdims=True))
            totals = jnp.sum(lifted, axis=1, keepdims=True)
            values = value_buf[:, :, channels].reshape(frames * keys_rows, HD)
            mixed = jnp.dot(
                lifted.astype(jnp.bfloat16), values, preferred_element_type=jnp.float32
            )
            out_ref[:, channels] = (mixed / totals).astype(jnp.bfloat16)


def attend(slots, own, mate, moves, pairs, frames, width):
    heads = width // HD
    tokens = (own[moves.index((0, 0))].shape[0] - NOTE_ROWS) // (3 * heads)
    rows, keys_rows = (pairs * tokens, 2 * pairs * tokens)

    def kernel(*refs):
        own_refs, refs = (refs[: len(moves)], refs[len(moves) :])
        mate_refs, refs = (refs[: len(moves)], refs[len(moves) :])
        out_refs, (query_buf, key_buf, value_buf, note_out) = (refs[: len(slots)], refs[len(slots) :])
        here = lax.axis_index("tm")
        for own_ref, mate_ref, (a, b) in zip(own_refs, mate_refs, moves):
            for head in range(heads):
                channels = slice(head * HD, (head + 1) * HD)
                query, key, value = [
                    slice((place * heads + head) * tokens, (place * heads + head + 1) * tokens)
                    for place in range(3)
                ]
                query_buf[here ^ a, b * tokens : (b + 1) * tokens, channels] = own_ref[query, :]
                for side, ref in enumerate((own_ref, mate_ref)):
                    span = slice((2 * b + side) * tokens, (2 * b + side + 1) * tokens)
                    key_buf[a, span, channels] = ref[key, :]
                    value_buf[a, span, channels] = ref[value, :]
            if b == 0:
                note_out[pl.ds(here ^ a, 1), :] = own_ref[3 * heads * tokens :, :].astype(jnp.float32)[:1]
        attend_frames(slots, out_refs, query_buf, key_buf, value_buf, note_out)

    kind = own[0].dtype
    outs = pl.pallas_call(
        kernel,
        out_shape=[jax.ShapeDtypeStruct((rows, width), jnp.bfloat16)] * len(slots)
        + [
            jax.ShapeDtypeStruct((frames, rows, width), kind),
            jax.ShapeDtypeStruct((frames, keys_rows, width), kind),
            jax.ShapeDtypeStruct((frames, keys_rows, width), kind),
            jax.ShapeDtypeStruct((16, HD), jnp.float32),
        ],
        in_specs=whole_in_vmem(2 * len(moves)),
        out_specs=whole_in_vmem(len(slots) + 4),
        compiler_params=roomy(),
        name="attend",
    )(*own, *mate)
    return (outs[: len(slots)], outs[len(slots) :])


def attend_again(slots, held):
    rows, width = held[0].shape[1:]

    def kernel(*refs):
        out_ref = refs[len(held)]
        parts = [out_ref.at[slot * rows : (slot + 1) * rows] for slot in range(len(slots))]
        attend_frames(slots, parts, *refs[: len(held)])

    return pl.pallas_call(
        kernel,
        out_shape=jax.ShapeDtypeStruct((len(slots) * rows, width), jnp.bfloat16),
        in_specs=whole_in_vmem(len(held)),
        out_specs=whole_in_vmem(1)[0],
        compiler_params=roomy(),
        name="attend_again",
    )(*held)


def project(pieces, weight, kinds, slots=1):
    flat = [piece for part in pieces for piece in part]
    rows, width = (flat[0].shape[0] // slots, flat[0].shape[1])
    pairs, sets = (len(pieces[0]), len(pieces))
    tokens = rows // pairs
    depth, columns = weight.shape
    step = math.gcd(columns, 256)

    def kernel(*refs):
        sources = iter(refs[: len(flat)])
        weight_ref, refs = (refs[len(flat)], refs[len(flat) + 1 :])
        whole = refs[-1]
        here = lax.axis_index("head") // 2
        for k in range(sets):
            for move in range(pairs):
                source = next(sources)
                pair = here ^ move
                channels = pl.ds(pl.multiple_of(pair * width, HD), width)
                for slot in range(slots):
                    for b in range(pairs):
                        first = (slot * sets + k) * rows + (pair ^ b) * tokens
                        start = slot * rows + b * tokens
                        whole[pl.ds(pl.multiple_of(first, 16), tokens), channels] = source[
                            start : start + tokens, :
                        ]
        for start in range(0, columns, step):
            inner = slice(start, start + step)
            product = jnp.dot(
                whole[...], weight_ref[:, inner], preferred_element_type=jnp.float32
            )
            for number in range(slots * sets):
                share = product[number * rows : (number + 1) * rows, :]
                for out_ref in refs[number * len(kinds) : (number + 1) * len(kinds)]:
                    out_ref[:, inner] = share.astype(out_ref.dtype)

    outs = pl.pallas_call(
        kernel,
        out_shape=[
            jax.ShapeDtypeStruct((rows, columns), kind)
            for _ in range(slots * sets)
            for kind in kinds
        ],
        in_specs=whole_in_vmem(len(flat) + 1),
        out_specs=whole_in_vmem(len(kinds) * slots * sets),
        scratch_shapes=[pltpu.VMEM((slots * sets * rows, depth), jnp.bfloat16)],
        compiler_params=roomy(),
        name="project",
    )(*flat, weight)
    return [list(outs[number :: len(kinds)]) for number in range(len(kinds))]


def gates_of(notes, time_weight, column, frames):
    depth, columns = time_weight.shape
    half = depth // 2

    def kernel(note_ref, weight_ref, here_ref, next_ref):
        here = lax.axis_index("tm")
        following = jnp.minimum(here + 1, frames - 1)
        rows = jnp.concatenate([note_ref[pl.ds(here, 1), :], note_ref[pl.ds(following, 1), :]], axis=0)
        lane = lax.broadcasted_iota(jnp.int32, rows.shape, 1)
        noise = jnp.sum(jnp.where(lane == column, rows, 0.0), axis=1, keepdims=True)
        timestep = 1000.0 * (noise + 1.0) / STEPS
        place = lax.broadcasted_iota(jnp.int32, (2, half), 1).astype(jnp.float32)
        angles = timestep * jnp.exp(-math.log(10000.0) * place / half)
        features = jnp.concatenate([jnp.cos(angles), jnp.sin(angles)], axis=1)
        gates = jnp.dot(
            features,
            weight_ref[...].astype(jnp.float32),
            precision=lax.Precision.HIGHEST,
            preferred_element_type=jnp.float32,
        )
        here_ref[...] = gates[:1]
        next_ref[...] = gates[1:]

    return pl.pallas_call(
        kernel,
        out_shape=[jax.ShapeDtypeStruct((1, columns), jnp.float32)] * 2,
        in_specs=whole_in_vmem(2),
        out_specs=whole_in_vmem(2),
        compiler_params=roomy(),
        name="gates_of",
    )(notes, time_weight)


def frame_rows(k, pairs, tokens):
    core = (lax.axis_index("head") % 2) ^ k
    return [pl.ds(pl.multiple_of((2 * p + core) * tokens, 16), tokens) for p in range(pairs)]


def join(partial, table, arrived, k, pairs, residual=None, gate=None):
    rows, columns = partial[0].shape
    tokens = rows // pairs
    step = math.gcd(columns, 256)
    slots = sorted(set(table))
    extras = [] if residual is None else [residual, gate]

    def kernel(*refs):
        own_refs, refs = (refs[: len(slots)], refs[len(slots) :])
        arrived_refs, refs = (refs[: len(arrived)], refs[len(arrived) :])
        out_ref = refs[-1]
        here = lax.axis_index("tm")
        places = frame_rows(k, pairs, tokens)
        for slot, own_ref in zip(slots, own_refs):

            @pl.when(pick([entry == slot for entry in table], here))
            def _(own_ref=own_ref):
                for p, place in enumerate(places):
                    inner = slice(p * tokens, (p + 1) * tokens)
                    for start in range(0, columns, step):
                        part = slice(start, start + step)
                        total = own_ref[inner, part]
                        for ref in arrived_refs:
                            total += ref[inner, part].astype(jnp.float32)
                        if extras:
                            kept = refs[0][place, part].astype(jnp.float32)
                            total = kept + refs[1][:, part] * total
                        out_ref[inner, part] = total.astype(jnp.bfloat16)

    operands = [partial[slot] for slot in slots] + list(arrived) + extras
    return pl.pallas_call(
        kernel,
        out_shape=jax.ShapeDtypeStruct((rows, columns), jnp.bfloat16),
        in_specs=whole_in_vmem(len(operands)),
        out_specs=whole_in_vmem(1)[0],
        compiler_params=roomy(),
        name="join",
    )(*operands)


def finish(k, arrived, partial, below, gate, fresh_frame, pairs, started=None):
    rows, columns = partial.shape
    tokens = rows // pairs
    step = math.gcd(columns, 256)

    def kernel(*refs):
        arrived_ref, partial_ref, below_ref, gate_ref, fresh_ref = refs[:5]
        out_ref, done, sems = refs[-3:]
        last = lax.axis_index("tm") == lax.axis_size("tm") - 1
        places = frame_rows(k, pairs, tokens)

        @pl.when(last)
        def _():
            for p, place in enumerate(places):
                done[p * tokens : (p + 1) * tokens, :] = fresh_ref[place, :]

        @pl.when(jnp.logical_not(last))
        def _():
            for p in range(pairs):
                inner = slice(p * tokens, (p + 1) * tokens)
                for start in range(0, columns, step):
                    part = slice(start, start + step)
                    total = partial_ref[inner, part] + below_ref[inner, part].astype(jnp.float32)
                    total = gate_ref[:, part] * total
                    total += arrived_ref[inner, part].astype(jnp.float32)
                    done[inner, part] = total.astype(jnp.bfloat16)

        copies = [
            pltpu.make_async_copy(
                done.at[p * tokens : (p + 1) * tokens, :], out_ref.at[place, :], sems.at[p]
            )
            for p, place in enumerate(places)
        ]
        for copy in copies:
            copy.start()
        for copy in copies:
            copy.wait()

    operands = [arrived, partial, below, gate, fresh_frame]
    specs = whole_in_vmem(5)
    aliases = {}
    if started is not None:
        operands.append(started)
        specs = specs + in_hbm(1)
        aliases = {5: 0}
    return pl.pallas_call(
        kernel,
        out_shape=jax.ShapeDtypeStruct(fresh_frame.shape, jnp.bfloat16),
        in_specs=specs,
        out_specs=in_hbm(1)[0],
        scratch_shapes=[
            pltpu.VMEM((rows, columns), jnp.bfloat16),
            pltpu.SemaphoreType.DMA((pairs,)),
        ],
        input_output_aliases=aliases,
        compiler_params=roomy(),
        name="finish",
    )(*operands)


def line_schedule(frames):
    steps = []
    for step in range(frames - 1):
        down = {z: step + 1 - (frames - 1 - z) for z in range(1, frames)}
        up = {z: frames - 1 - step + z for z in range(frames)}
        down = {z: f for z, f in down.items() if 1 <= f <= z}
        up = {z: f for z, f in up.items() if z + 2 <= f < frames}
        steps.append((down, up))
    order = []
    for z in range(frames):
        sent = [f for down, up in steps for f in (down.get(z), up.get(z)) if f is not None]
        order.append((sent + [z + 1])[: frames - 1])
    return steps, order


def head_plan(
    queries, keys, values, residual, fresh_frame, out_weight, time_weight, noise_steps, frame_mask
):
    frames, across = (lax.axis_size("tm"), lax.axis_size("head"))
    pairs = across // 2
    width = queries.shape[2] // (frames * pairs)
    everywhere = range(frames)

    def swap(array, j):
        return lax.ppermute(array, "head", [(h, h ^ j) for h in range(across)])

    def gather(part, meanwhile=None):
        near = [part]
        for move in range(1, pairs):
            piece = swap(part, 2 * move)
            if meanwhile is not None:
                piece, meanwhile = lax.optimization_barrier((piece, meanwhile))
            near.append(piece)
        return ([near, [swap(piece, 1) for piece in near]], meanwhile)

    far = [(a, b) for b in range(pairs) for a in reversed(everywhere[2:])]
    near = [(1, pairs - 1)] + [(0, b) for b in range(1, pairs)] + [(1, b) for b in range(pairs - 1)]
    moves = far + near + [(0, 0)]
    packed = []
    for some in (moves[: len(far) + 1], moves[len(far) + 1 :]):
        packed += pack(
            queries[0], keys[0], values[0], frame_mask, noise_steps, some, pairs, width
        )
    first = len(far)
    own = []
    for piece, (a, b) in zip(packed, moves):
        if (a, b) != (0, 0):
            if a == 0:
                piece, own[first] = lax.optimization_barrier((piece, own[first]))
            links = [
                (z * across + h, (z ^ a) * across + (h ^ (2 * b)))
                for z in everywhere
                for h in range(across)
            ]
            piece = lax.ppermute(piece, ("tm", "head"), links)
        own.append(piece)
    for number in range(first):
        own[number], own[first] = lax.optimization_barrier((own[number], own[first]))
    mine = moves.index((0, 0))
    (own[mine],), weight = (bring(own[mine]), out_weight)
    mate = [swap(piece, 1) for piece in own]

    steps, order = line_schedule(frames)

    named = [[order[z][slot] for z in everywhere] for slot in range(frames - 1)]
    (part,), held = attend(named[:1], own, mate, moves, pairs, frames, width)
    following = attend_again(named[1:], held)
    pieces, following = gather(part, following)
    partial, payload = ([[]], [])
    for rows in pieces:
        product, rounded = project([rows], weight, (jnp.float32, jnp.bfloat16))
        partial[0] += product
        payload += rounded
    following, payload[0] = lax.optimization_barrier((following, payload[0]))
    down, up = steps[0]
    links = [(z, z - 1) for z in down] + [(z, z + 1) for z in up]
    above = [lax.ppermute(part, "tm", links) for part in payload]
    below = above
    pieces, _ = gather(following)
    later = project(pieces, weight, (jnp.float32,), frames - 2)[0]
    partial += [later[2 * slot : 2 * slot + 2] for slot in range(frames - 2)]
    gates = gates_of(held[-1], time_weight, frame_mask.shape[1], frames)

    for number, (down, up) in enumerate(steps[1:], 1):
        sends = {**down, **up}
        table = [order[z].index(sends[z]) if z in sends else 0 for z in everywhere]
        final = number == len(steps) - 1
        extras = (residual[0], gates[0]) if final else ()
        payload = [
            join(
                [products[k] for products in partial],
                table,
                [above[k]] if final or above is below else [above[k], below[k]],
                k,
                pairs,
                *extras,
            )
            for k in range(2)
        ]
        above = [lax.ppermute(part, "tm", [(z, z - 1) for z in down]) for part in payload]
        if up:
            below = [lax.ppermute(part, "tm", [(z, z + 1) for z in up]) for part in payload]
    result = None
    for k in range(2):
        result = finish(
            k, above[k], partial[-1][k], below[k], gates[1], fresh_frame, pairs, result
        )
    return result[None]


def power_of_two(number):
    return number & (number - 1) == 0


def suits_line(frames, window):
    apart = all(not set(down) & set(up) for down, up in line_schedule(frames)[0])
    return 2 < frames <= window and power_of_two(frames) and apart


def on_device(queries, *others):
    frames, across = (lax.axis_size("tm"), lax.axis_size("head"))
    heads = queries.shape[2] // HD
    even = across % 2 == 0 and power_of_two(across)
    even = even and queries.shape[1] % 16 == 0
    if even and suits_line(frames, others[-1].shape[1]) and heads % (frames * across // 2) == 0:
        return head_plan(queries, *others)
    return frame_plan(queries, *others)


def solution(mesh):
    placed = (
        P(("groups", "tm"), "head", None),
        P(("groups", "tm"), "head", None),
        P(("groups", "tm"), "head", None),
        P(("groups", "tm"), None, "head"),
        P("groups", "head"),
        P("tm", "head"),
        P(None, "head"),
        P(("groups", "tm")),
        P(("groups", "tm"), None),
    )
    return jax.shard_map(
        on_device,
        mesh=mesh,
        in_specs=placed,
        out_specs=P(("groups", "tm"), None, "head"),
        check_vma=False,
    )
```

```python
import math

import jax
import jax.numpy as jnp
import numpy as np
from jax import lax
from jax.experimental import pallas as pl
from jax.experimental.pallas import tpu as pltpu
from jax.sharding import PartitionSpec as P

HD = 128
FREQ = 256
STEPS = 50
NOTE_ROWS = 16
VMEM_BYTES = 16 * 1024 * 1024
PACK_BYTES = 60 * 1024 * 1024


def shifted(value, axis, steps):
    count = lax.axis_size(axis)
    leading, last = (max(0, -steps), min(count, count - steps))
    return lax.ppermute(value, axis, [(source, source + steps) for source in range(leading, last)])


def time_features(noise_steps):
    timestep = 1000.0 * (noise_steps.astype(jnp.float32) + 1.0) / STEPS
    half = FREQ // 2
    rates = jnp.exp(-math.log(10000.0) * jnp.arange(half).astype(jnp.float32) / half)
    angles = timestep[:, None] * rates[None, :]
    return jnp.concatenate([jnp.cos(angles), jnp.sin(angles)], axis=1)


def frame_plan(
    queries, keys, values, residual, fresh_frame, out_weight, time_weight, noise_steps, frame_mask
):
    query_local, key_local, value_local = (
        lax.all_to_all(queries, "head", split_axis=2, concat_axis=1, tiled=True),
        lax.all_to_all(keys, "head", split_axis=2, concat_axis=1, tiled=True),
        lax.all_to_all(values, "head", split_axis=2, concat_axis=1, tiled=True),
    )
    tokens = query_local.shape[1]
    heads_here = query_local.shape[2] // HD
    scale = 1.0 / math.sqrt(HD)
    query_heads = query_local[0].reshape(tokens, heads_here, HD)
    key_value = jnp.stack([key_local[0], value_local[0]], axis=0)
    frame = lax.axis_index("tm")
    frames_total = lax.axis_size("tm")
    window = min(8, frames_total)
    mask_row = frame_mask[0]
    columns = jnp.arange(mask_row.shape[0], dtype=jnp.int32)

    def allowed_at(offset):
        hits = jnp.sum(jnp.where(columns == frame - offset, mask_row, 0))
        return hits > 0

    def absorb(state, block, allowed):
        running_max, weight_sum, accumulated = state
        key_heads = block[0].reshape(tokens, heads_here, HD)
        value_heads = block[1].reshape(tokens, heads_here, HD)
        scores = (
            jnp.einsum("qhd,khd->hqk", query_heads, key_heads, preferred_element_type=jnp.float32)
            * scale
        )
        new_max = jnp.where(allowed, jnp.maximum(running_max, jnp.max(scores, axis=2)), running_max)
        lifted = jnp.where(allowed, jnp.exp(jnp.minimum(scores - new_max[:, :, None], 0.0)), 0.0)
        factor = jnp.exp(running_max - new_max)
        weight_sum = weight_sum * factor + jnp.sum(lifted, axis=2)
        rounded = lifted.astype(jnp.bfloat16)
        accumulated = accumulated * jnp.transpose(factor)[:, :, None] + jnp.einsum(
            "hqk,khd->qhd", rounded, value_heads, preferred_element_type=jnp.float32
        )
        return (new_max, weight_sum, accumulated)

    state = (
        jnp.full((heads_here, tokens), -1e30, jnp.float32),
        jnp.zeros((heads_here, tokens), jnp.float32),
        jnp.zeros((tokens, heads_here, HD), jnp.float32),
    )
    state = absorb(state, key_value, allowed_at(0))
    moving = key_value
    for offset in range(1, window):
        moving = shifted(moving, "tm", 1)
        state = absorb(state, moving, allowed_at(offset))
    running_max, weight_sum, accumulated = state
    attention = (
        (accumulated / jnp.transpose(weight_sum)[:, :, None])
        .reshape(tokens, heads_here * HD)
        .astype(jnp.bfloat16)
    )
    weight_cols = lax.all_gather(out_weight, "tm", axis=0, tiled=True)
    projected = jnp.dot(
        lax.all_gather(attention, "head", axis=1, tiled=True),
        weight_cols,
        preferred_element_type=jnp.float32,
    )
    gate = jnp.dot(
        time_features(noise_steps), time_weight.astype(jnp.float32), precision=lax.Precision.HIGHEST
    )
    updated = (residual[0].astype(jnp.float32) + gate * projected).astype(jnp.bfloat16)
    moved = shifted(updated, "tm", -1)
    rolled = jnp.where(frame == frames_total - 1, fresh_frame, moved)
    return rolled[None]


def whole_in_vmem(count):
    return [pl.BlockSpec(memory_space=pltpu.VMEM)] * count


def in_hbm(count):
    return [pl.BlockSpec(memory_space=pltpu.HBM)] * count


def roomy():
    return pltpu.CompilerParams(vmem_limit_bytes=VMEM_BYTES)


def pack(queries, keys, values, frame_mask, noise_steps, moves, pairs, width):
    tokens, kind = (queries.shape[0], queries.dtype)
    window = frame_mask.shape[1]
    heads = width // HD
    body = 3 * heads * tokens
    heights = [body + (NOTE_ROWS if b == 0 else 0) for a, b in moves]
    count = len(moves)

    def kernel(*refs):
        sources, small, pieces, scratch = (refs[:3], refs[3:5], refs[5 : 5 + count], refs[5 + count :])
        loaded, packed, mask_ref, noise_ref, in_sems, out_sems = scratch
        frame, pair = (lax.axis_index("tm"), lax.axis_index("head") // 2)
        targets = [loaded.at[place] for place in range(3)] + [mask_ref, noise_ref]
        loads = [
            pltpu.make_async_copy(source, target, in_sems.at[place])
            for place, (source, target) in enumerate(zip((*sources, *small), targets))
        ]
        for load in loads:
            load.start()
        for load in loads[:3]:
            load.wait()
        stores = []

        def fill(number, a, b):
            block = (frame ^ a) * pairs + (pair ^ b)
            for place in range(3):
                for head in range(heads):
                    columns = pl.ds(pl.multiple_of((block * heads + head) * HD, HD), HD)
                    first = (place * heads + head) * tokens
                    packed[number, first : first + tokens, :] = loaded[place, :, columns]

        def send(number):
            store = pltpu.make_async_copy(
                packed.at[number, : heights[number]], pieces[number], out_sems.at[number]
            )
            store.start()
            stores.append(store)

        for number, (a, b) in enumerate(moves):
            fill(number, a, b)
            if b > 0:
                send(number)
        for load in loads[3:]:
            load.wait()
        lane = lax.broadcasted_iota(jnp.int32, (NOTE_ROWS, HD), 1)
        note = jnp.where(lane == window, noise_ref[0], 0)
        for column in range(window):
            note = jnp.where(lane == column, mask_ref[0, column], note)
        note = note.astype(jnp.float32).astype(kind)
        for number, (a, b) in enumerate(moves):
            if b == 0:
                packed[number, body:, :] = note
                send(number)
        for store in stores:
            store.wait()

    return pl.pallas_call(
        kernel,
        out_shape=[jax.ShapeDtypeStruct((height, HD), kind) for height in heights],
        in_specs=in_hbm(5),
        out_specs=in_hbm(count),
        scratch_shapes=[
            pltpu.VMEM((3, *queries.shape), kind),
            pltpu.VMEM((count, body + NOTE_ROWS, HD), kind),
            pltpu.SMEM(frame_mask.shape, frame_mask.dtype),
            pltpu.SMEM(noise_steps.shape, noise_steps.dtype),
            pltpu.SemaphoreType.DMA((5,)),
            pltpu.SemaphoreType.DMA((count,)),
        ],
        compiler_params=pltpu.CompilerParams(vmem_limit_bytes=PACK_BYTES),
        name="pack",
    )(queries, keys, values, frame_mask, noise_steps)


def bring(*arrays):
    def kernel(*refs):
        for source, target in zip(refs[: len(arrays)], refs[len(arrays) :]):
            target[...] = source[...]

    return pl.pallas_call(
        kernel,
        out_shape=[jax.ShapeDtypeStruct(array.shape, array.dtype) for array in arrays],
        in_specs=whole_in_vmem(len(arrays)),
        out_specs=whole_in_vmem(len(arrays)),
        compiler_params=roomy(),
        name="bring",
    )(*arrays)


def pick(table, here):
    result = table[0]
    for place, entry in enumerate(table[1:], 1):
        result = jnp.where(here == place, entry, result)
    return result


def attend_frames(slots, out_refs, query_buf, key_buf, value_buf, note_ref):
    frames, keys_rows, width = key_buf.shape
    scale = math.log2(math.e) / math.sqrt(HD)
    here = lax.axis_index("tm")
    for frames_of_slot, out_ref in zip(slots, out_refs):
        frame = pick(frames_of_slot, here)
        note = note_ref[pl.ds(frame, 1), :]
        lane = lax.broadcasted_iota(jnp.int32, note.shape, 1)
        biases = []
        for a in range(frames):
            hit = jnp.sum(jnp.where(lane == here ^ a, note, 0.0), axis=1, keepdims=True)
            biases.append(jnp.broadcast_to((hit - 1.0) * 1e30, (1, keys_rows)))
        bias = jnp.concatenate(biases, axis=1)
        for start in range(0, width, HD):
            channels = slice(start, start + HD)
            query = query_buf[frame, :, channels]
            keys = key_buf[:, :, channels].reshape(frames * keys_rows, HD)
            scores = lax.dot_general(
                query, keys, (((1,), (1,)), ((), ())), preferred_element_type=jnp.float32
            )
            scores = scores * scale + bias
            lifted = jnp.exp2(scores - jnp.max(scores, axis=1, keepdims=True))
            totals = jnp.sum(lifted, axis=1, keepdims=True)
            values = value_buf[:, :, channels].reshape(frames * keys_rows, HD)
            mixed = jnp.dot(
                lifted.astype(jnp.bfloat16), values, preferred_element_type=jnp.float32
            )
            out_ref[:, channels] = (mixed / totals).astype(jnp.bfloat16)


def attend(slots, own, mate, moves, pairs, frames, width):
    heads = width // HD
    tokens = (own[moves.index((0, 0))].shape[0] - NOTE_ROWS) // (3 * heads)
    rows, keys_rows = (pairs * tokens, 2 * pairs * tokens)

    def kernel(*refs):
        own_refs, refs = (refs[: len(moves)], refs[len(moves) :])
        mate_refs, refs = (refs[: len(moves)], refs[len(moves) :])
        out_refs, (query_buf, key_buf, value_buf, note_out) = (refs[: len(slots)], refs[len(slots) :])
        here = lax.axis_index("tm")
        for own_ref, mate_ref, (a, b) in zip(own_refs, mate_refs, moves):
            for head in range(heads):
                channels = slice(head * HD, (head + 1) * HD)
                query, key, value = [
                    slice((place * heads + head) * tokens, (place * heads + head + 1) * tokens)
                    for place in range(3)
                ]
                query_buf[here ^ a, b * tokens : (b + 1) * tokens, channels] = own_ref[query, :]
                for side, ref in enumerate((own_ref, mate_ref)):
                    span = slice((2 * b + side) * tokens, (2 * b + side + 1) * tokens)
                    key_buf[a, span, channels] = ref[key, :]
                    value_buf[a, span, channels] = ref[value, :]
            if b == 0:
                note_out[pl.ds(here ^ a, 1), :] = own_ref[3 * heads * tokens :, :].astype(jnp.float32)[:1]
        attend_frames(slots, out_refs, query_buf, key_buf, value_buf, note_out)

    kind = own[0].dtype
    outs = pl.pallas_call(
        kernel,
        out_shape=[jax.ShapeDtypeStruct((rows, width), jnp.bfloat16)] * len(slots)
        + [
            jax.ShapeDtypeStruct((frames, rows, width), kind),
            jax.ShapeDtypeStruct((frames, keys_rows, width), kind),
            jax.ShapeDtypeStruct((frames, keys_rows, width), kind),
            jax.ShapeDtypeStruct((16, HD), jnp.float32),
        ],
        in_specs=whole_in_vmem(2 * len(moves)),
        out_specs=whole_in_vmem(len(slots) + 4),
        compiler_params=roomy(),
        name="attend",
    )(*own, *mate)
    return (outs[: len(slots)], outs[len(slots) :])


def attend_again(slots, held):
    rows, width = held[0].shape[1:]

    def kernel(*refs):
        out_ref = refs[len(held)]
        parts = [out_ref.at[slot * rows : (slot + 1) * rows] for slot in range(len(slots))]
        attend_frames(slots, parts, *refs[: len(held)])

    return pl.pallas_call(
        kernel,
        out_shape=jax.ShapeDtypeStruct((len(slots) * rows, width), jnp.bfloat16),
        in_specs=whole_in_vmem(len(held)),
        out_specs=whole_in_vmem(1)[0],
        compiler_params=roomy(),
        name="attend_again",
    )(*held)


def project(pieces, weight, kinds, slots=1):
    flat = [piece for part in pieces for piece in part]
    rows, width = (flat[0].shape[0] // slots, flat[0].shape[1])
    pairs, sets = (len(pieces[0]), len(pieces))
    tokens = rows // pairs
    depth, columns = weight.shape
    step = math.gcd(columns, 256)

    def kernel(*refs):
        sources = iter(refs[: len(flat)])
        weight_ref, refs = (refs[len(flat)], refs[len(flat) + 1 :])
        whole = refs[-1]
        here = lax.axis_index("head") // 2
        for k in range(sets):
            for move in range(pairs):
                source = next(sources)
                pair = here ^ move
                channels = pl.ds(pl.multiple_of(pair * width, HD), width)
                for slot in range(slots):
                    for b in range(pairs):
                        first = (slot * sets + k) * rows + (pair ^ b) * tokens
                        start = slot * rows + b * tokens
                        whole[pl.ds(pl.multiple_of(first, 16), tokens), channels] = source[
                            start : start + tokens, :
                        ]
        for start in range(0, columns, step):
            inner = slice(start, start + step)
            product = jnp.dot(
                whole[...], weight_ref[:, inner], preferred_element_type=jnp.float32
            )
            for number in range(slots * sets):
                share = product[number * rows : (number + 1) * rows, :]
                for out_ref in refs[number * len(kinds) : (number + 1) * len(kinds)]:
                    out_ref[:, inner] = share.astype(out_ref.dtype)

    outs = pl.pallas_call(
        kernel,
        out_shape=[
            jax.ShapeDtypeStruct((rows, columns), kind)
            for _ in range(slots * sets)
            for kind in kinds
        ],
        in_specs=whole_in_vmem(len(flat) + 1),
        out_specs=whole_in_vmem(len(kinds) * slots * sets),
        scratch_shapes=[pltpu.VMEM((slots * sets * rows, depth), jnp.bfloat16)],
        compiler_params=roomy(),
        name="project",
    )(*flat, weight)
    return [list(outs[number :: len(kinds)]) for number in range(len(kinds))]


def gates_of(notes, time_weight, column, frames):
    depth, columns = time_weight.shape
    half = depth // 2

    def kernel(note_ref, weight_ref, here_ref, next_ref):
        here = lax.axis_index("tm")
        following = jnp.minimum(here + 1, frames - 1)
        rows = jnp.concatenate([note_ref[pl.ds(here, 1), :], note_ref[pl.ds(following, 1), :]], axis=0)
        lane = lax.broadcasted_iota(jnp.int32, rows.shape, 1)
        noise = jnp.sum(jnp.where(lane == column, rows, 0.0), axis=1, keepdims=True)
        timestep = 1000.0 * (noise + 1.0) / STEPS
        place = lax.broadcasted_iota(jnp.int32, (2, half), 1).astype(jnp.float32)
        angles = timestep * jnp.exp(-math.log(10000.0) * place / half)
        features = jnp.concatenate([jnp.cos(angles), jnp.sin(angles)], axis=1)
        gates = jnp.dot(
            features,
            weight_ref[...].astype(jnp.float32),
            precision=lax.Precision.HIGHEST,
            preferred_element_type=jnp.float32,
        )
        here_ref[...] = gates[:1]
        next_ref[...] = gates[1:]

    return pl.pallas_call(
        kernel,
        out_shape=[jax.ShapeDtypeStruct((1, columns), jnp.float32)] * 2,
        in_specs=whole_in_vmem(2),
        out_specs=whole_in_vmem(2),
        compiler_params=roomy(),
        name="gates_of",
    )(notes, time_weight)


def frame_rows(k, pairs, tokens):
    core = (lax.axis_index("head") % 2) ^ k
    return [pl.ds(pl.multiple_of((2 * p + core) * tokens, 16), tokens) for p in range(pairs)]


def join(partial, table, arrived, k, pairs, residual=None, gate=None):
    rows, columns = partial[0].shape
    tokens = rows // pairs
    step = math.gcd(columns, 256)
    slots = sorted(set(table))
    extras = [] if residual is None else [residual, gate]

    def kernel(*refs):
        own_refs, refs = (refs[: len(slots)], refs[len(slots) :])
        arrived_refs, refs = (refs[: len(arrived)], refs[len(arrived) :])
        out_ref = refs[-1]
        here = lax.axis_index("tm")
        places = frame_rows(k, pairs, tokens)
        for slot, own_ref in zip(slots, own_refs):

            @pl.when(pick([entry == slot for entry in table], here))
            def _(own_ref=own_ref):
                for p, place in enumerate(places):
                    inner = slice(p * tokens, (p + 1) * tokens)
                    for start in range(0, columns, step):
                        part = slice(start, start + step)
                        total = own_ref[inner, part]
                        for ref in arrived_refs:
                            total += ref[inner, part].astype(jnp.float32)
                        if extras:
                            kept = refs[0][place, part].astype(jnp.float32)
                            total = kept + refs[1][:, part] * total
                        out_ref[inner, part] = total.astype(jnp.bfloat16)

    operands = [partial[slot] for slot in slots] + list(arrived) + extras
    return pl.pallas_call(
        kernel,
        out_shape=jax.ShapeDtypeStruct((rows, columns), jnp.bfloat16),
        in_specs=whole_in_vmem(len(operands)),
        out_specs=whole_in_vmem(1)[0],
        compiler_params=roomy(),
        name="join",
    )(*operands)


def finish(k, arrived, partial, below, gate, fresh_frame, pairs, started=None):
    rows, columns = partial.shape
    tokens = rows // pairs
    step = math.gcd(columns, 256)

    def kernel(*refs):
        arrived_ref, partial_ref, below_ref, gate_ref, fresh_ref = refs[:5]
        out_ref, done, sems = refs[-3:]
        last = lax.axis_index("tm") == lax.axis_size("tm") - 1
        places = frame_rows(k, pairs, tokens)

        @pl.when(last)
        def _():
            for p, place in enumerate(places):
                done[p * tokens : (p + 1) * tokens, :] = fresh_ref[place, :]

        @pl.when(jnp.logical_not(last))
        def _():
            for p in range(pairs):
                inner = slice(p * tokens, (p + 1) * tokens)
                for start in range(0, columns, step):
                    part = slice(start, start + step)
                    total = partial_ref[inner, part] + below_ref[inner, part].astype(jnp.float32)
                    total = gate_ref[:, part] * total
                    total += arrived_ref[inner, part].astype(jnp.float32)
                    done[inner, part] = total.astype(jnp.bfloat16)

        copies = [
            pltpu.make_async_copy(
                done.at[p * tokens : (p + 1) * tokens, :], out_ref.at[place, :], sems.at[p]
            )
            for p, place in enumerate(places)
        ]
        for copy in copies:
            copy.start()
        for copy in copies:
            copy.wait()

    operands = [arrived, partial, below, gate, fresh_frame]
    specs = whole_in_vmem(5)
    aliases = {}
    if started is not None:
        operands.append(started)
        specs = specs + in_hbm(1)
        aliases = {5: 0}
    return pl.pallas_call(
        kernel,
        out_shape=jax.ShapeDtypeStruct(fresh_frame.shape, jnp.bfloat16),
        in_specs=specs,
        out_specs=in_hbm(1)[0],
        scratch_shapes=[
            pltpu.VMEM((rows, columns), jnp.bfloat16),
            pltpu.SemaphoreType.DMA((pairs,)),
        ],
        input_output_aliases=aliases,
        compiler_params=roomy(),
        name="finish",
    )(*operands)


def line_schedule(frames):
    steps = []
    for step in range(frames - 1):
        down = {z: step + 1 - (frames - 1 - z) for z in range(1, frames)}
        up = {z: frames - 1 - step + z for z in range(frames)}
        down = {z: f for z, f in down.items() if 1 <= f <= z}
        up = {z: f for z, f in up.items() if z + 2 <= f < frames}
        steps.append((down, up))
    order = []
    for z in range(frames):
        sent = [f for down, up in steps for f in (down.get(z), up.get(z)) if f is not None]
        order.append((sent + [z + 1])[: frames - 1])
    return steps, order


def head_plan(
    queries, keys, values, residual, fresh_frame, out_weight, time_weight, noise_steps, frame_mask
):
    frames, across = (lax.axis_size("tm"), lax.axis_size("head"))
    pairs = across // 2
    width = queries.shape[2] // (frames * pairs)
    everywhere = range(frames)

    def swap(array, j):
        return lax.ppermute(array, "head", [(h, h ^ j) for h in range(across)])

    def gather(part, meanwhile=None):
        near = [part]
        for move in range(1, pairs):
            piece = swap(part, 2 * move)
            if meanwhile is not None:
                piece, meanwhile = lax.optimization_barrier((piece, meanwhile))
            near.append(piece)
        return ([near, [swap(piece, 1) for piece in near]], meanwhile)

    far = [(a, b) for b in range(pairs) for a in reversed(everywhere[2:])]
    near = [(1, pairs - 1)] + [(0, b) for b in range(1, pairs)] + [(1, b) for b in range(pairs - 1)]
    moves = far + near + [(0, 0)]
    packed = []
    for some in (moves[: len(far) + 1], moves[len(far) + 1 :]):
        packed += pack(
            queries[0], keys[0], values[0], frame_mask, noise_steps, some, pairs, width
        )
    first = len(far)
    own = []
    for piece, (a, b) in zip(packed, moves):
        if (a, b) != (0, 0):
            if a == 0:
                piece, own[first] = lax.optimization_barrier((piece, own[first]))
            links = [
                (z * across + h, (z ^ a) * across + (h ^ (2 * b)))
                for z in everywhere
                for h in range(across)
            ]
            piece = lax.ppermute(piece, ("tm", "head"), links)
        own.append(piece)
    for number in range(first):
        own[number], own[first] = lax.optimization_barrier((own[number], own[first]))
    mine = moves.index((0, 0))
    (own[mine],), weight = (bring(own[mine]), out_weight)
    mate = [swap(piece, 1) for piece in own]

    steps, order = line_schedule(frames)

    named = [[order[z][slot] for z in everywhere] for slot in range(frames - 1)]
    (part,), held = attend(named[:1], own, mate, moves, pairs, frames, width)
    following = attend_again(named[1:], held)
    pieces, following = gather(part, following)
    partial, payload = ([[]], [])
    for rows in pieces:
        product, rounded = project([rows], weight, (jnp.float32, jnp.bfloat16))
        partial[0] += product
        payload += rounded
    following, payload[0] = lax.optimization_barrier((following, payload[0]))
    down, up = steps[0]
    links = [(z, z - 1) for z in down] + [(z, z + 1) for z in up]
    above = [lax.ppermute(part, "tm", links) for part in payload]
    below = above
    pieces, _ = gather(following)
    later = project(pieces, weight, (jnp.float32,), frames - 2)[0]
    partial += [later[2 * slot : 2 * slot + 2] for slot in range(frames - 2)]
    gates = gates_of(held[-1], time_weight, frame_mask.shape[1], frames)

    for number, (down, up) in enumerate(steps[1:], 1):
        sends = {**down, **up}
        table = [order[z].index(sends[z]) if z in sends else 0 for z in everywhere]
        final = number == len(steps) - 1
        extras = (residual[0], gates[0]) if final else ()
        payload = [
            join(
                [products[k] for products in partial],
                table,
                [above[k]] if final or above is below else [above[k], below[k]],
                k,
                pairs,
                *extras,
            )
            for k in range(2)
        ]
        above = [lax.ppermute(part, "tm", [(z, z - 1) for z in down]) for part in payload]
        if up:
            below = [lax.ppermute(part, "tm", [(z, z + 1) for z in up]) for part in payload]
    result = None
    for k in range(2):
        result = finish(
            k, above[k], partial[-1][k], below[k], gates[1], fresh_frame, pairs, result
        )
    return result[None]


def power_of_two(number):
    return number & (number - 1) == 0


def suits_line(frames, window):
    apart = all(not set(down) & set(up) for down, up in line_schedule(frames)[0])
    return 2 < frames <= window and power_of_two(frames) and apart


def on_device(queries, *others):
    frames, across = (lax.axis_size("tm"), lax.axis_size("head"))
    heads = queries.shape[2] // HD
    even = across % 2 == 0 and power_of_two(across)
    even = even and queries.shape[1] % 16 == 0
    if even and suits_line(frames, others[-1].shape[1]) and heads % (frames * across // 2) == 0:
        return head_plan(queries, *others)
    return frame_plan(queries, *others)


def solution(mesh):
    placed = (
        P(("groups", "tm"), "head", None),
        P(("groups", "tm"), "head", None),
        P(("groups", "tm"), "head", None),
        P(("groups", "tm"), None, "head"),
        P("groups", "head"),
        P("tm", "head"),
        P(None, "head"),
        P(("groups", "tm")),
        P(("groups", "tm"), None),
    )
    return jax.shard_map(
        on_device,
        mesh=mesh,
        in_specs=placed,
        out_specs=P(("groups", "tm"), None, "head"),
        check_vma=False,
    )
```
